32 devices in a mesh: grp: 2 (over y), ep: 4 (over z), et: 4 (over x, core).
Axes of the slice: x: 2, y: 2, z: 4, core: 2. Of those that a mesh axis runs over, the one named last changes fastest.
Arguments:
- tokens: bfloat16 [256, 4096], P(('grp', 'ep')), parts along dimension 0, may hold values from -6 to 6
- modulation: float32 [2, 2, 4096], replicated, may hold values from -3 to 3
- router: bfloat16 [4096, 4], replicated, may hold values from -0.25 to 0.25
- gate_weight: bfloat16 [4, 4096, 1536], P('ep', None, 'et'), may hold values from -0.09375 to 0.09375
- up_weight: bfloat16 [4, 4096, 1536], P('ep', None, 'et'), may hold values from -0.09375 to 0.09375
- down_weight: bfloat16 [4, 1536, 4096], P('ep', 'et'), may hold values from -0.15625 to 0.15625
- expert_ids: int32 [2, 256, 2], P(None, ('grp', 'ep')), parts along dimension 1, may hold values from 0 to 3, all different within a row; in each aligned block of 32 rows (0 to 31, 32 to 63, ..., all dimensions but the last counted through in order) at most 24 rows name the same one
Outputs:
- latents: bfloat16 [256, 4096], P(('grp', 'ep'), 'et'), parts along dimension 0
- velocity: bfloat16 [256, 4096], P(('grp', 'ep'), 'et'), parts along dimension 0
The draws below stay inside these ranges and needn't reach their ends.
There are 2 independent parts, one for each index of `grp`. The reference program is written for one: setup_inputs(seed, part) draws one part's arguments, and reference() takes and returns one part's arrays. A program takes and returns all parts, laid end to end along the dimension named above; an argument that names none is the same for every part. Nothing has to cross between parts.
Inputs may be any that keep to these rules, and one draw needn't show every extreme that they name: `expert_ids`: each row names 2 different experts. In each section, among the 32 rows of one ep index, no expert is named by more than 24 rows, and in each section some expert is named by exactly 24 rows of some ep index.
All inputs are finite; a program needn't handle non-finite values.
Results may differ from the reference program's by a relative error of at most 0.017.
Values may be sent and summed in bfloat16 or wider, within the bound.
No kernel may reach another device: no remote copies, remote signals or barrier semaphores. Data moves between devices by JAX's collectives and lax.ppermute only.
A program may use at most 64 MiB of HBM per device.

```python
import math
import jax
import jax.numpy as jnp
import numpy as np
from jax import lax

D = 4096
FFW = 1536
TOK_DEV = 32
SECTIONS = 2
EXPERTS = 4
TOPK = 2
SLOT = 24
TOKENS = 128
N_EP = 4
N_ET = 4


def level_of(rng, extent, split, least, top_value):
    gain, own = 1.0, jax.random.fold_in(rng, 6)
    for position, blocks in split:
        heights = jnp.exp(jax.random.uniform(jax.random.fold_in(own, position), (blocks,), jnp.float32, least / len(split), top_value / len(split)))
        gain = gain * jnp.repeat(heights, extent[position] // blocks).reshape([-1 if axis == position else 1 for axis in range(len(extent))])
    return gain


def assign_block(stream_key, own, number, rows, number_of, top, bound, skew):
    ranking = jax.random.permutation(stream_key, number_of)
    heavy_load, usual = shares(number_of, rows * top, bound, skew, True), shares(number_of, rows * top, bound, skew, False)
    places = jnp.arange(number_of)

    def named(tallies, rotation):
        used = int((tallies > 0).sum())
        fixed = max(1, used // 4)
        moved = fixed + (places - fixed + rotation * (used - fixed)) % max(1, number_of - fixed)
        return jnp.zeros((number_of,), jnp.int32).at[ranking[jnp.where(places < fixed, places, moved)]].set(jnp.asarray(tallies, jnp.int32))

    tallies = jnp.where(number % 4 == 0, named(heavy_load, number // 4), named(usual, number - number // 4 - 1))
    mixed = jax.random.permutation(jax.random.fold_in(own, 3), number_of)
    giver, receiver = mixed[0:number_of // 2 * 2:2], mixed[1:number_of // 2 * 2:2]
    slack = jnp.minimum(tallies[giver] - 1, bound - tallies[receiver]) // 2
    slack = jnp.where((giver == ranking[0]) | (receiver == ranking[0]) | (tallies[receiver] == 0), 0, jnp.maximum(slack, 0))
    moved = jax.random.randint(jax.random.fold_in(own, 4), (number_of // 2,), 0, 1 << 20) % (slack + 1)
    tallies = tallies.at[giver].add(-moved).at[receiver].add(moved)
    items = jnp.searchsorted(jnp.cumsum(tallies), jnp.arange(rows * top), side="right").astype(jnp.int32)
    table = items.reshape(top, rows).T
    table = table[jax.random.permutation(jax.random.fold_in(own, 1), rows)]
    rotation = jax.random.randint(jax.random.fold_in(own, 2), (rows, 1), 0, top)
    return jnp.take_along_axis(table, (jnp.arange(top)[None, :] + rotation) % top, axis=1)


def shares(amount, total, most, lean, full):
    portions = [(1 << 20) // math.isqrt(rank ** lean) + 1 for rank in range(1, amount + 1)]
    largest = most if full else min(most, max(-(-total // amount), total * portions[0] // sum(portions)))
    least = 1 if total - largest >= amount - 1 else 0
    counts, rest = [largest] + [least] * (amount - 1), total - largest - least * (amount - 1)
    while rest > 0:
        candidates = [i for i in range(1, amount) if counts[i] < largest] or [i for i in range(1, amount) if counts[i] < most]
        mass, remaining = sum([portions[i] for i in candidates]), rest
        for i in candidates:
            more = min(most - counts[i], max(1, remaining * portions[i] // mass), rest)
            counts[i] = counts[i] + more
            rest = rest - more
    return np.array(counts)


def noise(key, shape, scale, most, split=(), kind=jnp.bfloat16):
    gain = level_of(key, shape, split, -0.22, 0.18) if split else 1.0
    entries = jax.random.normal(key, shape, jnp.float32) * scale * gain
    return jnp.minimum(jnp.maximum(entries, -most), most).astype(kind)


def setup_inputs(seed: int = 0, part: int = 0) -> dict:
    arg_keys = jax.random.split(jax.random.key(seed), 8)
    part_splits = jax.random.split(jax.random.fold_in(arg_keys[7], part), 8)
    tokens = noise(part_splits[0], (TOKENS, D), 1.0, 6.0, ((0, 4),))
    modulation = noise(arg_keys[1], (SECTIONS, 2, D), 0.5, 3.0, (), jnp.float32)
    router = noise(arg_keys[2], (D, EXPERTS), (D // 9) ** -0.5, 0.25)
    gate_weight = noise(arg_keys[3], (EXPERTS, D, FFW), D ** -0.5, 0.09375, ((0, 4), (2, 4)))
    up_weight = noise(arg_keys[4], (EXPERTS, D, FFW), D ** -0.5, 0.09375, ((0, 4), (2, 4)))
    down_weight = noise(arg_keys[5], (EXPERTS, FFW, D), FFW ** -0.5, 0.15625, ((0, 4), (1, 4)))
    expert_ids_keys = jax.random.split(jax.random.fold_in(part_splits[6], 1), SECTIONS * TOKENS // TOK_DEV)
    expert_ids_turns = jax.random.permutation(jax.random.fold_in(part_splits[6], 3), SECTIONS * TOKENS // TOK_DEV)
    expert_ids = jax.vmap(lambda own, number: assign_block(jax.random.fold_in(part_splits[6], 2), own, number, TOK_DEV, EXPERTS, TOPK, SLOT, 2))(expert_ids_keys, expert_ids_turns).reshape((SECTIONS, TOKENS, TOPK))
    return {"tokens": tokens, "modulation": modulation, "router": router, "gate_weight": gate_weight, "up_weight": up_weight, "down_weight": down_weight, "expert_ids": expert_ids}


def normalize(x, mod):
    xf = x.astype(jnp.float32)
    scaled = xf * lax.rsqrt(lax.optimization_barrier(jnp.mean(xf * xf, axis=-1, keepdims=True)) + 1e-06)
    return (scaled * (1.0 + mod[0]) + mod[1]).astype(jnp.bfloat16)

def slot_numbers(ids):
    blocks = ids.reshape(N_EP, TOK_DEV * TOPK)
    onehot = (blocks[:, :, None] == jnp.arange(EXPERTS, dtype=jnp.int32)).astype(jnp.int32)
    counted = jnp.cumsum(onehot, axis=1)
    slot = lax.optimization_barrier(jnp.sum(onehot * (counted - 1), axis=-1))
    source = jnp.arange(N_EP, dtype=jnp.int32)[:, None]
    return (source * SLOT + slot).reshape(-1).astype(jnp.int32)

def run_expert(args):
    rows, w_gate, w_up, w_down = args
    part = FFW // N_ET
    total = jnp.zeros((rows.shape[0], D), jnp.float32)
    for quarter in range(N_ET):
        lo = quarter * part
        gate = jnp.dot(rows, w_gate[:, lo:lo + part], preferred_element_type=jnp.float32)
        upper = jnp.dot(rows, w_up[:, lo:lo + part], preferred_element_type=jnp.float32)
        hidden = (jax.nn.silu(gate) * upper).astype(jnp.bfloat16)
        term = jnp.dot(hidden, w_down[lo:lo + part, :], preferred_element_type=jnp.float32).astype(jnp.bfloat16)
        term = lax.optimization_barrier(term)
        total = total + term.astype(jnp.float32)
    return total.astype(jnp.bfloat16)

def one_section(x, mod, ids, router, gate_weight, up_weight, down_weight):
    normed = normalize(x, mod)
    logits = jnp.dot(normed, router, preferred_element_type=jnp.float32)
    chosen = jax.nn.sigmoid(jnp.take_along_axis(logits, ids, axis=1))
    weight = chosen / lax.optimization_barrier(jnp.sum(chosen, axis=1, keepdims=True))
    flat_e = ids.reshape(-1)
    flat_p = slot_numbers(ids)
    token_of = jnp.arange(TOKENS * TOPK, dtype=jnp.int32) // TOPK
    buffer = jnp.zeros((EXPERTS, N_EP * SLOT, D), jnp.bfloat16).at[flat_e, flat_p].set(normed[token_of])
    outputs = lax.map(run_expert, (buffer, gate_weight, up_weight, down_weight))
    picked = outputs[flat_e, flat_p].astype(jnp.float32).reshape(TOKENS, TOPK, D)
    velocity = lax.optimization_barrier(jnp.sum(picked * weight[:, :, None], axis=1))
    moved = (x.astype(jnp.float32) - 0.5 * velocity).astype(jnp.bfloat16)
    return (moved, velocity)

def reference(tokens, modulation, router, gate_weight, up_weight, down_weight, expert_ids):
    first, _ = one_section(tokens, modulation[0], expert_ids[0], router, gate_weight, up_weight, down_weight)
    second, velocity = one_section(first, modulation[1], expert_ids[1], router, gate_weight, up_weight, down_weight)
    return (second, velocity.astype(jnp.bfloat16))
```

```python
import jax
import jax.numpy as jnp
from jax import lax
from jax.sharding import PartitionSpec as P


def normalize(x, mod):
    xf = x.astype(jnp.float32)
    scaled = xf * lax.rsqrt(jnp.mean(xf * xf, axis=-1, keepdims=True) + 1e-06)
    return (scaled * (1.0 + mod[0]) + mod[1]).astype(jnp.bfloat16)


def routed_section(x_full, x_cols, mod, ids, router, gate_weight, up_weight, down_weight):
    tok_rows = x_full.shape[0]
    width = x_full.shape[1]
    experts = router.shape[1]
    picks = ids.shape[1]
    n_peers = lax.axis_size("ep")
    quarter = width // lax.axis_size("et")
    slot_count = 3 * tok_rows * picks // (2 * experts)
    normed = normalize(x_full, mod)
    logits = jnp.dot(normed, router, preferred_element_type=jnp.float32)
    chosen = jax.nn.sigmoid(jnp.take_along_axis(logits, ids, axis=1))
    weight = chosen / jnp.sum(chosen, axis=1, keepdims=True)
    flat_e = ids.reshape(-1)
    onehot = (flat_e[:, None] == jnp.arange(experts, dtype=jnp.int32)).astype(jnp.int32)
    counted = jnp.cumsum(onehot, axis=0)
    slot = jnp.sum(onehot * (counted - 1), axis=1)
    repeated = jnp.repeat(normed, picks, axis=0)
    outbox = jnp.zeros((experts, slot_count, width), jnp.bfloat16).at[flat_e, slot].set(repeated)
    arrived = lax.all_to_all(outbox, "ep", split_axis=0, concat_axis=0, tiled=True)
    in_rows = arrived.reshape(n_peers * slot_count, width)
    gate = jnp.dot(in_rows, gate_weight[0], preferred_element_type=jnp.float32)
    upper = jnp.dot(in_rows, up_weight[0], preferred_element_type=jnp.float32)
    hidden = (jax.nn.silu(gate) * upper).astype(jnp.bfloat16)
    partial_out = jnp.dot(hidden, down_weight[0], preferred_element_type=jnp.float32)
    summed = lax.psum_scatter(
        partial_out.astype(jnp.bfloat16), "et", scatter_dimension=1, tiled=True
    )
    returned = lax.all_to_all(
        summed.reshape(n_peers, slot_count, quarter), "ep", split_axis=0, concat_axis=0, tiled=True
    )
    picked = returned[flat_e, slot].astype(jnp.float32).reshape(tok_rows, picks, quarter)
    velocity = jnp.sum(picked * weight[:, :, None], axis=1)
    moved = (x_cols.astype(jnp.float32) - 0.5 * velocity).astype(jnp.bfloat16)
    return (moved, velocity)


def routed_body(tokens, modulation, router, gate_weight, up_weight, down_weight, expert_ids):
    quarter = tokens.shape[1] // lax.axis_size("et")
    column_start = lax.axis_index("et") * quarter
    cols = lax.dynamic_slice_in_dim(tokens, column_start, quarter, 1)
    weights = (router, gate_weight, up_weight, down_weight)
    first, _ = routed_section(tokens, cols, modulation[0], expert_ids[0], *weights)
    full = lax.all_gather(first, "et", axis=1, tiled=True)
    second, velocity = routed_section(full, first, modulation[1], expert_ids[1], *weights)
    return (second, velocity.astype(jnp.bfloat16))


def swap(x, axis, bit):
    size = lax.axis_size(axis)
    return lax.ppermute(x, axis, [(i, i ^ bit) for i in range(size)])


def both(mine, other, bit_set, axis):
    low = jnp.where(bit_set, other, mine)
    high = jnp.where(bit_set, mine, other)
    return jnp.concatenate([low, high], axis=axis)


def gather_ep(x):
    return [x] + [swap(x, "ep", k) for k in range(1, lax.axis_size("ep"))]


def take_half(x, bit_set, axis):
    half = x.shape[axis] // 2
    start = jnp.where(bit_set, half, 0)
    return lax.dynamic_slice_in_dim(x, start, half, axis)


def add_halves(x, y):
    return (x.astype(jnp.float32) + y.astype(jnp.float32)).astype(jnp.bfloat16)


def partial_sum(x, mod, ids, router, w_gate, w_up, w_down):
    experts = router.shape[1]
    normed = normalize(x, mod)
    logits = jnp.dot(normed, router, preferred_element_type=jnp.float32)
    numbers = jnp.arange(experts, dtype=jnp.int32)
    named = jnp.any(ids[:, :, None] == numbers, axis=1)
    chosen = jnp.where(named, jax.nn.sigmoid(logits), 0.0)
    weight = chosen / jnp.sum(chosen, axis=1, keepdims=True)
    mine = numbers == lax.axis_index("ep")
    weight = jnp.sum(jnp.where(mine, weight, 0.0), axis=1, keepdims=True)
    gate = jnp.dot(normed, w_gate, preferred_element_type=jnp.float32)
    upper = jnp.dot(normed, w_up, preferred_element_type=jnp.float32)
    hidden = (jax.nn.silu(gate) * upper * weight).astype(jnp.bfloat16)
    return jnp.dot(hidden, w_down, preferred_element_type=jnp.float32).astype(jnp.bfloat16)


def scatter_sum(part, core, side):
    rows = part.shape[0] // lax.axis_size("ep")
    width = part.shape[1]
    part = part.reshape(part.shape[0], 2, 2, width // 4)
    keep = jnp.where(core, part[:, :, 1], part[:, :, 0])
    send = jnp.where(core, part[:, :, 0], part[:, :, 1])
    part = add_halves(keep, swap(send, "et", 1))
    keep = jnp.where(side, part[:, 1], part[:, 0])
    send = jnp.where(side, part[:, 0], part[:, 1])
    part = add_halves(keep, swap(send, "et", 2))
    total = part[:rows].astype(jnp.float32)
    for k in range(1, lax.axis_size("ep")):
        total += swap(part[k * rows : (k + 1) * rows], "ep", k).astype(jnp.float32)
    return total


def dense_body(tokens, modulation, router, gate_weight, up_weight, down_weight, expert_ids):
    rows, width = tokens.shape
    quarter = width // lax.axis_size("et")
    where_et = lax.axis_index("et")
    core = where_et % 2 == 1
    side = where_et // 2 == 1
    weights = (router, gate_weight[0], up_weight[0], down_weight[0])
    own = lax.dynamic_slice_in_dim(tokens, where_et * quarter, quarter, 1)

    sections, _, picks = expert_ids.shape
    flat_ids = expert_ids.transpose(1, 0, 2).reshape(rows, sections * picks)
    half = take_half(tokens, core, 1)
    flags = jnp.pad(flat_ids.astype(jnp.bfloat16), ((0, 0), (0, 128 - sections * picks)))
    blocks = gather_ep(jnp.concatenate([half, flags], axis=1))
    gathered = jnp.concatenate(blocks, axis=0)
    ids = gathered[:, width // 2 : width // 2 + sections * picks].astype(jnp.int32)
    ids = ids.reshape(-1, sections, picks)
    mine = gathered[rows:, : width // 2]
    others = both(mine, swap(mine, "et", 1), core, 1)
    x = jnp.concatenate([tokens, others], axis=0)

    part = partial_sum(x, modulation[0], ids[:, 0], *weights)
    velocity = scatter_sum(part, core, side)
    own = (own.astype(jnp.float32) - 0.5 * velocity).astype(jnp.bfloat16)

    x = jnp.concatenate(gather_ep(own), axis=0)
    far = swap(x, "et", 2)
    x = jnp.stack([jnp.where(side, far, x), jnp.where(side, x, far)], axis=1)
    near = swap(x, "et", 1)
    x = jnp.stack([jnp.where(core, near, x), jnp.where(core, x, near)], axis=2)
    x = x.reshape(-1, width)

    part = partial_sum(x, modulation[1], ids[:, 1], *weights)
    velocity = scatter_sum(part, core, side)
    own = (own.astype(jnp.float32) - 0.5 * velocity).astype(jnp.bfloat16)
    return (own, velocity.astype(jnp.bfloat16))


def solution(mesh):
    in_specs = (
        P(("grp", "ep"), None),
        P(),
        P(),
        P("ep", None, "et"),
        P("ep", None, "et"),
        P("ep", "et", None),
        P(None, ("grp", "ep"), None),
    )
    out_specs = (P(("grp", "ep"), "et"), P(("grp", "ep"), "et"))

    def body(*args):
        experts, picks = args[2].shape[1], args[6].shape[2]
        chosen = dense_body if experts <= 2 * picks else routed_body
        return chosen(*args)

    return jax.shard_map(body, mesh=mesh, in_specs=in_specs, out_specs=out_specs, check_vma=False)
```

```python
import functools

import jax
import jax.numpy as jnp
from jax import lax
from jax.experimental import pallas as pl
from jax.experimental.pallas import tpu as pltpu
from jax.sharding import PartitionSpec as P


def normalize(x, mod):
    xf = x.astype(jnp.float32)
    scaled = xf * lax.rsqrt(jnp.mean(xf * xf, axis=-1, keepdims=True) + 1e-06)
    return (scaled * (1.0 + mod[0]) + mod[1]).astype(jnp.bfloat16)


def routed_section(x_full, x_cols, mod, ids, router, gate_weight, up_weight, down_weight):
    tok_rows = x_full.shape[0]
    width = x_full.shape[1]
    experts = router.shape[1]
    picks = ids.shape[1]
    n_peers = lax.axis_size("ep")
    quarter = width // lax.axis_size("et")
    slot_count = 3 * tok_rows * picks // (2 * experts)
    normed = normalize(x_full, mod)
    logits = jnp.dot(normed, router, preferred_element_type=jnp.float32)
    chosen = jax.nn.sigmoid(jnp.take_along_axis(logits, ids, axis=1))
    weight = chosen / jnp.sum(chosen, axis=1, keepdims=True)
    flat_e = ids.reshape(-1)
    onehot = (flat_e[:, None] == jnp.arange(experts, dtype=jnp.int32)).astype(jnp.int32)
    counted = jnp.cumsum(onehot, axis=0)
    slot = jnp.sum(onehot * (counted - 1), axis=1)
    repeated = jnp.repeat(normed, picks, axis=0)
    outbox = jnp.zeros((experts, slot_count, width), jnp.bfloat16).at[flat_e, slot].set(repeated)
    arrived = lax.all_to_all(outbox, "ep", split_axis=0, concat_axis=0, tiled=True)
    in_rows = arrived.reshape(n_peers * slot_count, width)
    gate = jnp.dot(in_rows, gate_weight[0], preferred_element_type=jnp.float32)
    upper = jnp.dot(in_rows, up_weight[0], preferred_element_type=jnp.float32)
    hidden = (jax.nn.silu(gate) * upper).astype(jnp.bfloat16)
    partial_out = jnp.dot(hidden, down_weight[0], preferred_element_type=jnp.float32)
    summed = lax.psum_scatter(
        partial_out.astype(jnp.bfloat16), "et", scatter_dimension=1, tiled=True
    )
    returned = lax.all_to_all(
        summed.reshape(n_peers, slot_count, quarter), "ep", split_axis=0, concat_axis=0, tiled=True
    )
    picked = returned[flat_e, slot].astype(jnp.float32).reshape(tok_rows, picks, quarter)
    velocity = jnp.sum(picked * weight[:, :, None], axis=1)
    moved = (x_cols.astype(jnp.float32) - 0.5 * velocity).astype(jnp.bfloat16)
    return (moved, velocity)


def routed_body(tokens, modulation, router, gate_weight, up_weight, down_weight, expert_ids):
    quarter = tokens.shape[1] // lax.axis_size("et")
    column_start = lax.axis_index("et") * quarter
    cols = lax.dynamic_slice_in_dim(tokens, column_start, quarter, 1)
    weights = (router, gate_weight, up_weight, down_weight)
    first, _ = routed_section(tokens, cols, modulation[0], expert_ids[0], *weights)
    full = lax.all_gather(first, "et", axis=1, tiled=True)
    second, velocity = routed_section(full, first, modulation[1], expert_ids[1], *weights)
    return (second, velocity.astype(jnp.bfloat16))


def swap(x, axis, bit):
    size = lax.axis_size(axis)
    return lax.ppermute(x, axis, [(i, i ^ bit) for i in range(size)])


LANES = 128
VMEM_LIMIT = 40 * 1024 * 1024


def params():
    return pltpu.CompilerParams(vmem_limit_bytes=VMEM_LIMIT)


def whole(shape):
    return pl.BlockSpec(shape, lambda *_: (0,) * len(shape))


def aligned(index, size):
    return pl.ds(pl.multiple_of(index * size, size), size)


def pack_kernel(place, tokens_ref, ids_ref, out_ref, own_ref):
    half = tokens_ref.shape[1] // 2
    quarter = half // 2
    out_ref[:, :half] = tokens_ref[:, aligned(place[0] & 1, half)]
    own_ref[...] = tokens_ref[:, aligned(place[0], quarter)]
    experts = place[2]
    lane = lax.broadcasted_iota(jnp.int32, (tokens_ref.shape[0], LANES), 1)
    flags = jnp.zeros(lane.shape, jnp.float32)
    for s in range(ids_ref.shape[0]):
        for k in range(ids_ref.shape[2]):
            flags += jnp.where(ids_ref[s][:, k : k + 1] + s * experts == lane, 1.0, 0.0)
    out_ref[:, half:] = flags.astype(jnp.bfloat16)


def pack(place, tokens, ids):
    rows, width = tokens.shape
    shapes = [(rows, width // 2 + LANES), (rows, width // 4)]
    return pl.pallas_call(
        pack_kernel,
        grid_spec=pltpu.PrefetchScalarGridSpec(
            num_scalar_prefetch=1,
            grid=(1,),
            in_specs=[whole(tokens.shape), whole(ids.shape)],
            out_specs=[whole(s) for s in shapes],
        ),
        out_shape=[jax.ShapeDtypeStruct(s, jnp.bfloat16) for s in shapes],
        compiler_params=params(),
        name="pack",
    )(place, tokens, ids)


def front_kernel(pieces, section, experts, n_flags, place, *refs):
    n = len(pieces)
    x_refs, flag_refs = refs[:n], refs[n : n + n_flags]
    mod_ref, router_ref, gate_ref, up_ref, out_ref, normed_ref, gate_acc, up_acc, weight_ref = refs[n + n_flags :]
    step = pl.program_id(0)
    depth = gate_ref.shape[1]
    width = normed_ref.shape[1]

    @pl.when(step == 0)
    def _():
        groups = sorted({row for row, _, _, _ in pieces})
        for row in groups:
            members = [i for i in range(n) if pieces[i][0] == row]
            rows = pieces[members[0]][1]
            total = jnp.zeros((rows, 1), jnp.float32)
            for i in members:
                xf = x_refs[i][:, : pieces[i][2]].astype(jnp.float32)
                total += jnp.sum(xf * xf, axis=1, keepdims=True)
            scale = lax.rsqrt(total / width + 1e-06)
            for i in members:
                cols = pieces[i][2]
                where = aligned(pieces[i][3](place[0]), cols)
                xf = x_refs[i][:, :cols].astype(jnp.float32)
                normed_ref[row : row + rows, where] = (
                    xf * scale * (1.0 + mod_ref[0:1, where]) + mod_ref[1:2, where]
                ).astype(jnp.bfloat16)
        logits = lax.dot_general(
            normed_ref[...], router_ref[...], (((1,), (1,)), ((), ())), preferred_element_type=jnp.float32
        )
        count = logits.shape[1]
        lane = lax.broadcasted_iota(jnp.int32, logits.shape, 1)
        flags = jnp.concatenate([f[:, :count] for f in flag_refs], axis=0).astype(jnp.float32)
        here = (lane >= section * experts) & (lane < (section + 1) * experts) & (flags > 0.5)
        chosen = jnp.where(here, jax.nn.sigmoid(logits), 0.0)
        mine = jnp.where(lane == section * experts + place[1], chosen, 0.0)
        weight_ref[...] = jnp.sum(mine, axis=1, keepdims=True) / jnp.sum(chosen, axis=1, keepdims=True)
        gate_acc[...] = jnp.zeros_like(gate_acc)
        up_acc[...] = jnp.zeros_like(up_acc)

    block = normed_ref[:, aligned(step, depth)]
    gate_acc[...] += jnp.dot(block, gate_ref[0], preferred_element_type=jnp.float32)
    up_acc[...] += jnp.dot(block, up_ref[0], preferred_element_type=jnp.float32)

    @pl.when(step == pl.num_programs(0) - 1)
    def _():
        gate = gate_acc[...]
        out_ref[...] = (gate / (1.0 + jnp.exp(-gate)) * up_acc[...] * weight_ref[...]).astype(jnp.bfloat16)


def front(place, xs, pieces, flags, half, section, experts, mod, routers, w_gate, w_up):
    _, width, hidden = w_gate.shape
    rows = sum(f.shape[0] for f in flags)
    steps = 4
    depth = width // steps
    flag_spec = pl.BlockSpec((flags[0].shape[0], LANES), lambda k, p: (0, half // LANES))
    weight_spec = pl.BlockSpec((1, depth, hidden), lambda k, p: (0, k, 0))
    return pl.pallas_call(
        functools.partial(front_kernel, pieces, section, experts, len(flags)),
        grid_spec=pltpu.PrefetchScalarGridSpec(
            num_scalar_prefetch=1,
            grid=(steps,),
            in_specs=[whole(x.shape) for x in xs]
            + [flag_spec] * len(flags)
            + [whole(mod.shape), whole(routers.shape), weight_spec, weight_spec],
            out_specs=whole((rows, hidden)),
            scratch_shapes=[
                pltpu.VMEM((rows, width), jnp.bfloat16),
                pltpu.VMEM((rows, hidden), jnp.float32),
                pltpu.VMEM((rows, hidden), jnp.float32),
                pltpu.VMEM((rows, 1), jnp.float32),
            ],
        ),
        out_shape=jax.ShapeDtypeStruct((rows, hidden), jnp.bfloat16),
        compiler_params=params(),
        cost_estimate=pl.CostEstimate(
            flops=4 * rows * width * hidden, bytes_accessed=4 * width * hidden, transcendentals=0
        ),
        name="front",
    )(place, *xs, *flags, mod, routers, w_gate, w_up)


def down_kernel(place, hidden_ref, down_ref, *refs):
    product = jnp.dot(hidden_ref[...], down_ref[0], preferred_element_type=jnp.float32)
    for ref in refs[:-1]:
        product += ref[...].astype(jnp.float32)
    refs[-1][...] = product.astype(refs[-1].dtype)


def down(place, hidden, w_down, flip, adds=(), dtype=jnp.bfloat16):
    _, units, width = w_down.shape
    rows = hidden.shape[0]
    quarter = width // 4
    steps = 2
    cols = quarter // steps
    out_spec = pl.BlockSpec((rows, cols), lambda j, p: (0, j))
    return pl.pallas_call(
        down_kernel,
        grid_spec=pltpu.PrefetchScalarGridSpec(
            num_scalar_prefetch=1,
            grid=(steps,),
            in_specs=[
                whole(hidden.shape),
                pl.BlockSpec((1, units, cols), lambda j, p: (0, 0, (p[0] ^ flip) * steps + j)),
            ]
            + [out_spec] * len(adds),
            out_specs=out_spec,
        ),
        out_shape=jax.ShapeDtypeStruct((rows, quarter), dtype),
        compiler_params=params(),
        cost_estimate=pl.CostEstimate(
            flops=2 * rows * units * quarter, bytes_accessed=2 * units * quarter, transcendentals=0
        ),
        name="down",
    )(place, hidden, w_down, *adds)


def split_kernel(keep_ref, came_ref, *out_refs):
    rows = out_refs[0].shape[0]
    for k, out in enumerate(out_refs):
        part = slice(k * rows, (k + 1) * rows)
        out[...] = (keep_ref[part, :] + came_ref[part, :].astype(jnp.float32)).astype(out.dtype)


def split(keep, came, blocks):
    rows, cols = keep.shape
    shape = (rows // blocks, cols)
    dtypes = [jnp.float32] + [jnp.bfloat16] * (blocks - 1)
    return pl.pallas_call(
        split_kernel,
        out_shape=[jax.ShapeDtypeStruct(shape, t) for t in dtypes],
        compiler_params=params(),
        name="split",
    )(keep, came)


def move_kernel(own_ref, total_ref, *refs):
    came, (next_ref, velocity_ref) = refs[:-2], refs[-2:]
    velocity = total_ref[...]
    for ref in came:
        velocity += ref[...].astype(jnp.float32)
    next_ref[...] = (own_ref[...].astype(jnp.float32) - 0.5 * velocity).astype(jnp.bfloat16)
    velocity_ref[...] = velocity.astype(jnp.bfloat16)


def move(own, total, came):
    return pl.pallas_call(
        move_kernel,
        out_shape=[jax.ShapeDtypeStruct(own.shape, jnp.bfloat16)] * 2,
        compiler_params=params(),
        name="move",
    )(own, total, *came)


def sum_back(place, hidden, w_down, own):
    peers = lax.axis_size("ep")
    far = swap(down(place, hidden, w_down, 3), "et", 1)
    near = swap(down(place, hidden, w_down, 1), "et", 1)
    came = swap(down(place, hidden, w_down, 2, (far,)), "et", 2)
    keep = down(place, hidden, w_down, 0, (near,), jnp.float32)
    total, *blocks = split(keep, came, peers)
    return move(own, total, [swap(b, "ep", k + 1) for k, b in enumerate(blocks)])


def dense_body(tokens, modulation, router, gate_weight, up_weight, down_weight, expert_ids):
    rows, width = tokens.shape
    half, quarter = width // 2, width // 4
    experts = router.shape[1]
    peers = range(1, lax.axis_size("ep"))
    place = jnp.stack([lax.axis_index("et"), lax.axis_index("ep"), jnp.int32(experts)]).astype(jnp.int32)
    routers = jnp.concatenate([router.T] * expert_ids.shape[0], axis=0)
    expert = (routers, gate_weight, up_weight)

    packed, own = pack(place, tokens, expert_ids)
    flags = [packed] + [swap(packed, "ep", k) for k in peers]
    xs, pieces = [tokens], [(0, rows, width, lambda et: 0)]
    for k in peers:
        xs += [flags[k], swap(flags[k], "et", 1)]
        pieces += [
            (k * rows, rows, half, lambda et: et & 1),
            (k * rows, rows, half, lambda et: 1 - (et & 1)),
        ]
    hidden = front(place, xs, pieces, flags, half, 0, experts, modulation[0], *expert)
    own, _ = sum_back(place, hidden, down_weight, own)

    gathered = jnp.concatenate([own] + [swap(own, "ep", k) for k in peers], axis=0)
    side = swap(gathered, "et", 2)
    xs = [gathered, side, swap(gathered, "et", 1), swap(side, "et", 1)]
    flips = [0, 2, 1, 3]
    pieces = [(0, gathered.shape[0], quarter, functools.partial(lambda f, et: et ^ f, f)) for f in flips]
    hidden = front(place, xs, pieces, flags, half, 1, experts, modulation[1], *expert)
    return tuple(sum_back(place, hidden, down_weight, own))


def solution(mesh):
    in_specs = (
        P(("grp", "ep"), None),
        P(),
        P(),
        P("ep", None, "et"),
        P("ep", None, "et"),
        P("ep", "et", None),
        P(None, ("grp", "ep"), None),
    )
    out_specs = (P(("grp", "ep"), "et"), P(("grp", "ep"), "et"))

    def body(*args):
        experts, picks = args[2].shape[1], args[6].shape[2]
        peers = lax.axis_size("ep")
        fits = lax.axis_size("et") == 4 and peers & (peers - 1) == 0
        chosen = dense_body if fits and experts <= 2 * picks else routed_body
        return chosen(*args)

    return jax.shard_map(body, mesh=mesh, in_specs=in_specs, out_specs=out_specs, check_vma=False)
```

```python
import functools

import jax
import jax.numpy as jnp
from jax import lax
from jax.experimental import pallas as pl
from jax.experimental.pallas import tpu as pltpu
from jax.sharding import PartitionSpec as P


def normalize(x, mod):
    xf = x.astype(jnp.float32)
    scaled = xf * lax.rsqrt(jnp.mean(xf * xf, axis=-1, keepdims=True) + 1e-06)
    return (scaled * (1.0 + mod[0]) + mod[1]).astype(jnp.bfloat16)


def routed_section(x_full, x_cols, mod, ids, router, gate_weight, up_weight, down_weight):
    tok_rows = x_full.shape[0]
    width = x_full.shape[1]
    experts = router.shape[1]
    picks = ids.shape[1]
    n_peers = lax.axis_size("ep")
    quarter = width // lax.axis_size("et")
    slot_count = 3 * tok_rows * picks // (2 * experts)
    normed = normalize(x_full, mod)
    logits = jnp.dot(normed, router, preferred_element_type=jnp.float32)
    chosen = jax.nn.sigmoid(jnp.take_along_axis(logits, ids, axis=1))
    weight = chosen / jnp.sum(chosen, axis=1, keepdims=True)
    flat_e = ids.reshape(-1)
    onehot = (flat_e[:, None] == jnp.arange(experts, dtype=jnp.int32)).astype(jnp.int32)
    counted = jnp.cumsum(onehot, axis=0)
    slot = jnp.sum(onehot * (counted - 1), axis=1)
    repeated = jnp.repeat(normed, picks, axis=0)
    outbox = jnp.zeros((experts, slot_count, width), jnp.bfloat16).at[flat_e, slot].set(repeated)
    arrived = lax.all_to_all(outbox, "ep", split_axis=0, concat_axis=0, tiled=True)
    in_rows = arrived.reshape(n_peers * slot_count, width)
    gate = jnp.dot(in_rows, gate_weight[0], preferred_element_type=jnp.float32)
    upper = jnp.dot(in_rows, up_weight[0], preferred_element_type=jnp.float32)
    hidden = (jax.nn.silu(gate) * upper).astype(jnp.bfloat16)
    partial_out = jnp.dot(hidden, down_weight[0], preferred_element_type=jnp.float32)
    summed = lax.psum_scatter(
        partial_out.astype(jnp.bfloat16), "et", scatter_dimension=1, tiled=True
    )
    returned = lax.all_to_all(
        summed.reshape(n_peers, slot_count, quarter), "ep", split_axis=0, concat_axis=0, tiled=True
    )
    picked = returned[flat_e, slot].astype(jnp.float32).reshape(tok_rows, picks, quarter)
    velocity = jnp.sum(picked * weight[:, :, None], axis=1)
    moved = (x_cols.astype(jnp.float32) - 0.5 * velocity).astype(jnp.bfloat16)
    return (moved, velocity)


def routed_body(tokens, modulation, router, gate_weight, up_weight, down_weight, expert_ids):
    quarter = tokens.shape[1] // lax.axis_size("et")
    column_start = lax.axis_index("et") * quarter
    cols = lax.dynamic_slice_in_dim(tokens, column_start, quarter, 1)
    weights = (router, gate_weight, up_weight, down_weight)
    first, _ = routed_section(tokens, cols, modulation[0], expert_ids[0], *weights)
    full = lax.all_gather(first, "et", axis=1, tiled=True)
    second, velocity = routed_section(full, first, modulation[1], expert_ids[1], *weights)
    return (second, velocity.astype(jnp.bfloat16))


def swap(x, axis, bit):
    size = lax.axis_size(axis)
    return lax.ppermute(x, axis, [(i, i ^ bit) for i in range(size)])


LANES = 128
VMEM_LIMIT = 32 * 1024 * 1024
VMEM = pl.BlockSpec(memory_space=pltpu.VMEM)
SMEM = pl.BlockSpec(memory_space=pltpu.SMEM)
ANY = pl.BlockSpec(memory_space=pl.ANY)


def params():
    return pltpu.CompilerParams(vmem_limit_bytes=VMEM_LIMIT)


def aligned(index, size):
    return pl.ds(pl.multiple_of(index * size, size), size)


def load_kernel(gate_ref, up_ref, down_ref, pair_ref, out_ref, sems):
    hidden = gate_ref.shape[2]
    copies = [
        pltpu.make_async_copy(gate_ref.at[0], pair_ref.at[:, :hidden], sems.at[0]),
        pltpu.make_async_copy(up_ref.at[0], pair_ref.at[:, hidden:], sems.at[1]),
        pltpu.make_async_copy(down_ref.at[0], out_ref, sems.at[2]),
    ]
    for copy in copies:
        copy.start()
    for copy in copies:
        copy.wait()


def load(gate, up, down):
    _, width, hidden = gate.shape
    return pl.pallas_call(
        load_kernel,
        in_specs=[ANY] * 3,
        out_specs=[VMEM] * 2,
        out_shape=[
            pltpu.VMEM((width, 2 * hidden), jnp.bfloat16),
            pltpu.VMEM((hidden, width), jnp.bfloat16),
        ],
        scratch_shapes=[pltpu.SemaphoreType.DMA((3,))],
        compiler_params=params(),
        cost_estimate=pl.CostEstimate(flops=0, bytes_accessed=12 * width * hidden, transcendentals=0),
        name="load",
    )(gate, up, down)


def pack_kernel(experts, place, tokens_ref, ids_ref, out_ref, own_ref):
    quarter = tokens_ref.shape[1] // 4
    own = tokens_ref[:, aligned(place[0], quarter)]
    own_ref[...] = own
    out_ref[:, :quarter] = own
    lane = lax.broadcasted_iota(jnp.int32, (tokens_ref.shape[0], LANES), 1)
    flags = jnp.zeros(lane.shape, jnp.float32)
    for s in range(ids_ref.shape[0]):
        for k in range(ids_ref.shape[2]):
            flags += jnp.where(ids_ref[s][:, k : k + 1] + s * experts == lane, 1.0, 0.0)
    out_ref[:, quarter:] = flags.astype(jnp.bfloat16)


def pack(place, tokens, ids, experts):
    rows, width = tokens.shape
    shapes = [(rows, width // 4 + LANES), (rows, width // 4)]
    return pl.pallas_call(
        functools.partial(pack_kernel, experts),
        in_specs=[SMEM, VMEM, VMEM],
        out_shape=[jax.ShapeDtypeStruct(s, jnp.bfloat16) for s in shapes],
        compiler_params=params(),
        name="pack",
    )(place, tokens, ids)


def front_kernel(pieces, section, experts, n_flags, place, *refs):
    n = len(pieces)
    x_refs, flag_refs = refs[:n], refs[n : n + n_flags]
    mod_ref, router_ref, pair_ref, out_ref, normed_ref = refs[n + n_flags :]
    width = normed_ref.shape[1]
    hidden = out_ref.shape[1]
    for row in sorted({piece[0] for piece in pieces}):
        members = [i for i in range(n) if pieces[i][0] == row]
        rows = pieces[members[0]][1]
        total = jnp.zeros((rows, 1), jnp.float32)
        for i in members:
            xf = x_refs[i][:, : pieces[i][2]].astype(jnp.float32)
            total += jnp.sum(xf * xf, axis=1, keepdims=True)
        scale = lax.rsqrt(total / width + 1e-06)
        for i in members:
            cols = pieces[i][2]
            where = aligned(place[0] ^ pieces[i][3], cols) if cols < width else slice(None)
            xf = x_refs[i][:, :cols].astype(jnp.float32)
            normed_ref[row : row + rows, where] = (
                xf * scale * (1.0 + mod_ref[section, 0:1, where]) + mod_ref[section, 1:2, where]
            ).astype(jnp.bfloat16)
    normed = normed_ref[...]
    both = jnp.dot(normed, pair_ref[...], preferred_element_type=jnp.float32)
    logits = lax.dot_general(
        normed, router_ref[...], (((1,), (1,)), ((), ())), preferred_element_type=jnp.float32
    )
    count = logits.shape[1]
    lane = lax.broadcasted_iota(jnp.int32, logits.shape, 1)
    flags = jnp.concatenate([f[:, f.shape[1] - LANES :] for f in flag_refs], axis=0).astype(jnp.float32)
    flags = flags[:, section * experts : section * experts + count]
    chosen = jnp.where(flags > 0.5, jax.nn.sigmoid(logits), 0.0)
    mine = jnp.where(lane == place[1], chosen, 0.0)
    weight = jnp.sum(mine, axis=1, keepdims=True) / jnp.sum(chosen, axis=1, keepdims=True)
    gate, upper = both[:, :hidden], both[:, hidden:]
    out_ref[...] = (gate / (1.0 + jnp.exp(-gate)) * upper * weight).astype(jnp.bfloat16)


def front(place, xs, pieces, flags, section, mod, router, pair):
    width, hidden = pair.shape[0], pair.shape[1] // 2
    rows = sum(f.shape[0] for f in flags)
    experts = router.shape[0]
    return pl.pallas_call(
        functools.partial(front_kernel, pieces, section, experts, len(flags)),
        in_specs=[SMEM] + [VMEM] * (len(xs) + len(flags) + 3),
        scratch_shapes=[pltpu.VMEM((rows, width), jnp.bfloat16)],
        out_shape=jax.ShapeDtypeStruct((rows, hidden), jnp.bfloat16),
        compiler_params=params(),
        cost_estimate=pl.CostEstimate(
            flops=4 * rows * width * hidden, bytes_accessed=4 * width * hidden, transcendentals=0
        ),
        name="front",
    )(place, *xs, *flags, mod, router, pair)


def down_kernel(flip, n_adds, place, hidden_ref, down_ref, *refs):
    adds, outs = refs[:n_adds], refs[n_adds:]
    quarter = outs[0].shape[1]
    weights = down_ref[:, aligned(place[0] ^ flip, quarter)]
    product = jnp.dot(hidden_ref[...], weights, preferred_element_type=jnp.float32)
    for ref in adds:
        product += ref[...].astype(jnp.float32)
    rows = outs[0].shape[0]
    for k, out in enumerate(outs):
        out[...] = product[k * rows : (k + 1) * rows].astype(out.dtype)


def down(place, hidden, w_down, flip, blocks, adds=(), dtype=jnp.bfloat16):
    units, width = w_down.shape
    rows, quarter = hidden.shape[0], width // 4
    return pl.pallas_call(
        functools.partial(down_kernel, flip, len(adds)),
        in_specs=[SMEM] + [VMEM] * (2 + len(adds)),
        out_shape=[jax.ShapeDtypeStruct((rows // blocks, quarter), dtype)] * blocks,
        compiler_params=params(),
        cost_estimate=pl.CostEstimate(
            flops=2 * rows * units * quarter, bytes_accessed=2 * units * quarter, transcendentals=0
        ),
        name="down",
    )(place, hidden, w_down, *adds)


def add_kernel(keep_ref, came_ref, out_ref):
    out_ref[...] = (keep_ref[...] + came_ref[...].astype(jnp.float32)).astype(out_ref.dtype)


def add(keep, came):
    return pl.pallas_call(
        add_kernel,
        out_shape=jax.ShapeDtypeStruct(keep.shape, jnp.bfloat16),
        compiler_params=params(),
        name="add",
    )(keep, came)


def move_kernel(own_ref, total_ref, *refs):
    came, (next_ref, velocity_ref) = refs[:-2], refs[-2:]
    velocity = total_ref[...]
    for ref in came:
        velocity += ref[...].astype(jnp.float32)
    next_ref[...] = (own_ref[...].astype(jnp.float32) - 0.5 * velocity).astype(jnp.bfloat16)
    velocity_ref[...] = velocity.astype(jnp.bfloat16)


def move(own, total, came):
    return pl.pallas_call(
        move_kernel,
        out_shape=[jax.ShapeDtypeStruct(own.shape, jnp.bfloat16)] * 2,
        compiler_params=params(),
        name="move",
    )(own, total, *came)


def sum_back(place, hidden, w_down, own):
    peers = lax.axis_size("ep")
    far = swap(down(place, hidden, w_down, 3, 1)[0], "et", 1)
    near = swap(down(place, hidden, w_down, 1, 1)[0], "et", 1)
    parts = down(place, hidden, w_down, 2, peers, (far,))
    came = {k: swap(parts[k], "et", 2) for k in reversed(range(peers))}
    keep = down(place, hidden, w_down, 0, peers, (near,), jnp.float32)
    sent = [swap(add(keep[k], came[k]), "ep", k) for k in reversed(range(1, peers))]
    return move(own, keep[0], [came[0], *sent])


def gather(own):
    found = []
    for k in range(lax.axis_size("ep")):
        block = swap(own, "ep", k) if k else own
        side = swap(block, "et", 2)
        found.append([block, side, swap(block, "et", 1), swap(side, "et", 1)])
    return found


FLIPS = (0, 2, 1, 3)


def dense_body(tokens, modulation, router, gate_weight, up_weight, down_weight, expert_ids):
    rows, width = tokens.shape
    quarter = width // 4
    router = router.T
    place = jnp.stack([lax.axis_index("et"), lax.axis_index("ep")]).astype(jnp.int32)

    packed, own = pack(place, tokens, expert_ids, router.shape[0])
    found = gather(packed)
    flags = [blocks[0] for blocks in found]
    xs = [tokens] + sum(found[1:], [])
    pieces = [(0, rows, width, 0)]
    pieces += [(k * rows, rows, quarter, f) for k in range(1, len(found)) for f in FLIPS]
    pair, w_down = load(gate_weight, up_weight, down_weight)
    hidden = front(place, xs, pieces, flags, 0, modulation, router, pair)
    own, _ = sum_back(place, hidden, w_down, own)

    found = gather(own)
    pieces = [(k * rows, rows, quarter, f) for k in range(len(found)) for f in FLIPS]
    hidden = front(place, sum(found, []), pieces, flags, 1, modulation, router, pair)
    return tuple(sum_back(place, hidden, w_down, own))


def solution(mesh):
    in_specs = (
        P(("grp", "ep"), None),
        P(),
        P(),
        P("ep", None, "et"),
        P("ep", None, "et"),
        P("ep", "et", None),
        P(None, ("grp", "ep"), None),
    )
    out_specs = (P(("grp", "ep"), "et"), P(("grp", "ep"), "et"))

    def body(*args):
        experts, picks = args[2].shape[1], args[6].shape[2]
        peers = lax.axis_size("ep")
        fits = lax.axis_size("et") == 4 and peers & (peers - 1) == 0
        chosen = dense_body if fits and experts <= 2 * picks else routed_body
        return chosen(*args)

    return jax.shard_map(body, mesh=mesh, in_specs=in_specs, out_specs=out_specs, check_vma=False)
```

```python
import functools

import jax
import jax.numpy as jnp
from jax import lax
from jax.experimental import pallas as pl
from jax.experimental.pallas import tpu as pltpu
from jax.sharding import PartitionSpec as P


def normalize(x, mod):
    xf = x.astype(jnp.float32)
    scaled = xf * lax.rsqrt(jnp.mean(xf * xf, axis=-1, keepdims=True) + 1e-06)
    return (scaled * (1.0 + mod[0]) + mod[1]).astype(jnp.bfloat16)


def routed_section(x_full, x_cols, mod, ids, router, gate_weight, up_weight, down_weight):
    tok_rows = x_full.shape[0]
    width = x_full.shape[1]
    experts = router.shape[1]
    picks = ids.shape[1]
    n_peers = lax.axis_size("ep")
    quarter = width // lax.axis_size("et")
    slot_count = 3 * tok_rows * picks // (2 * experts)
    normed = normalize(x_full, mod)
    logits = jnp.dot(normed, router, preferred_element_type=jnp.float32)
    chosen = jax.nn.sigmoid(jnp.take_along_axis(logits, ids, axis=1))
    weight = chosen / jnp.sum(chosen, axis=1, keepdims=True)
    flat_e = ids.reshape(-1)
    onehot = (flat_e[:, None] == jnp.arange(experts, dtype=jnp.int32)).astype(jnp.int32)
    counted = jnp.cumsum(onehot, axis=0)
    slot = jnp.sum(onehot * (counted - 1), axis=1)
    repeated = jnp.repeat(normed, picks, axis=0)
    outbox = jnp.zeros((experts, slot_count, width), jnp.bfloat16).at[flat_e, slot].set(repeated)
    arrived = lax.all_to_all(outbox, "ep", split_axis=0, concat_axis=0, tiled=True)
    in_rows = arrived.reshape(n_peers * slot_count, width)
    gate = jnp.dot(in_rows, gate_weight[0], preferred_element_type=jnp.float32)
    upper = jnp.dot(in_rows, up_weight[0], preferred_element_type=jnp.float32)
    hidden = (jax.nn.silu(gate) * upper).astype(jnp.bfloat16)
    partial_out = jnp.dot(hidden, down_weight[0], preferred_element_type=jnp.float32)
    summed = lax.psum_scatter(
        partial_out.astype(jnp.bfloat16), "et", scatter_dimension=1, tiled=True
    )
    returned = lax.all_to_all(
        summed.reshape(n_peers, slot_count, quarter), "ep", split_axis=0, concat_axis=0, tiled=True
    )
    picked = returned[flat_e, slot].astype(jnp.float32).reshape(tok_rows, picks, quarter)
    velocity = jnp.sum(picked * weight[:, :, None], axis=1)
    moved = (x_cols.astype(jnp.float32) - 0.5 * velocity).astype(jnp.bfloat16)
    return (moved, velocity)


def routed_body(tokens, modulation, router, gate_weight, up_weight, down_weight, expert_ids):
    quarter = tokens.shape[1] // lax.axis_size("et")
    column_start = lax.axis_index("et") * quarter
    cols = lax.dynamic_slice_in_dim(tokens, column_start, quarter, 1)
    weights = (router, gate_weight, up_weight, down_weight)
    first, _ = routed_section(tokens, cols, modulation[0], expert_ids[0], *weights)
    full = lax.all_gather(first, "et", axis=1, tiled=True)
    second, velocity = routed_section(full, first, modulation[1], expert_ids[1], *weights)
    return (second, velocity.astype(jnp.bfloat16))


def swap(x, axis, bit):
    size = lax.axis_size(axis)
    return lax.ppermute(x, axis, [(i, i ^ bit) for i in range(size)])


LANES = 128
VMEM_LIMIT = 32 * 1024 * 1024
VMEM_MOST = 52 * 1024 * 1024
VMEM_ALL = 63 * 1024 * 1024
VMEM = pl.BlockSpec(memory_space=pltpu.VMEM)
ANY = pl.BlockSpec(memory_space=pl.ANY)


def params(limit=VMEM_LIMIT):
    return pltpu.CompilerParams(vmem_limit_bytes=limit)


def aligned(index, size):
    return pl.ds(pl.multiple_of(index * size, size), size)


def load_kernel(gate_ref, up_ref, down_ref, pair_ref, out_ref, done_ref, sems):
    hidden = gate_ref.shape[2]
    copies = [
        pltpu.make_async_copy(gate_ref.at[0], pair_ref.at[:, :hidden], sems.at[0]),
        pltpu.make_async_copy(up_ref.at[0], pair_ref.at[:, hidden:], sems.at[1]),
        pltpu.make_async_copy(down_ref.at[0], out_ref, sems.at[2]),
    ]
    for copy in copies:
        copy.start()
    for copy in copies:
        copy.wait()
    done_ref[...] = jnp.zeros_like(done_ref)


def load(gate, up, down):
    _, width, hidden = gate.shape
    return pl.pallas_call(
        load_kernel,
        in_specs=[ANY] * 3,
        out_specs=[VMEM] * 3,
        out_shape=[
            pltpu.VMEM((width, 2 * hidden), jnp.bfloat16),
            pltpu.VMEM((hidden, width), jnp.bfloat16),
            pltpu.VMEM((8, LANES), jnp.float32),
        ],
        scratch_shapes=[pltpu.SemaphoreType.DMA((3,))],
        compiler_params=params(VMEM_MOST),
        cost_estimate=pl.CostEstimate(flops=0, bytes_accessed=12 * width * hidden, transcendentals=0),
        name="load",
    )(gate, up, down)


def relay_kernel(block_ref, done_ref, out_ref):
    out_ref[...] = block_ref[:, : out_ref.shape[1]]


def relay(block, cols, done):
    return pl.pallas_call(
        relay_kernel,
        out_shape=jax.ShapeDtypeStruct((block.shape[0], cols), block.dtype),
        compiler_params=params(),
        name="relay",
    )(block, done)


def pack_kernel(experts, tokens_ref, ids_ref, wide_ref, out_ref, own_ref, sems):
    width = tokens_ref.shape[1]
    half, quarter = width // 2, width // 4
    where = lax.axis_index("et")
    copies = [
        pltpu.make_async_copy(tokens_ref.at[:, aligned(where & 1, half)], wide_ref.at[:, :half], sems.at[0]),
        pltpu.make_async_copy(tokens_ref.at[:, aligned(where, quarter)], own_ref, sems.at[1]),
    ]
    for copy in copies:
        copy.start()
    rows = tokens_ref.shape[0]
    lane = lax.broadcasted_iota(jnp.int32, (LANES, rows), 0)
    flags = jnp.zeros(lane.shape, jnp.float32)
    for s in range(ids_ref.shape[0]):
        for k in range(ids_ref.shape[1]):
            flags += jnp.where(ids_ref[s][k : k + 1, :] + s * experts == lane, 1.0, 0.0)
    flags = flags.T.astype(jnp.bfloat16)
    wide_ref[:, half:] = flags
    out_ref[:, quarter:] = flags
    for copy in copies:
        copy.wait()
    out_ref[:, :quarter] = own_ref[...]


def pack(tokens, ids, experts):
    rows, width = tokens.shape
    shapes = [(rows, width // 2 + LANES), (rows, width // 4 + LANES), (rows, width // 4)]
    return pl.pallas_call(
        functools.partial(pack_kernel, experts),
        in_specs=[ANY, VMEM],
        out_specs=[VMEM] * 3,
        out_shape=[pltpu.VMEM(s, jnp.bfloat16) for s in shapes],
        scratch_shapes=[pltpu.SemaphoreType.DMA((2,))],
        compiler_params=params(VMEM_ALL),
        name="pack",
    )(tokens, ids)


def front_kernel(pieces, section, experts, n_flags, *refs):
    n = len(pieces)
    x_refs, flag_refs = refs[:n], refs[n : n + n_flags]
    mod_ref, router_ref, pair_ref, out_ref, normed_ref = refs[n + n_flags :]
    width = normed_ref.shape[1]
    hidden = out_ref.shape[1]
    for row in sorted({piece[0] for piece in pieces}):
        members = [i for i in range(n) if pieces[i][0] == row]
        rows = pieces[members[0]][1]
        total = jnp.zeros((rows, 1), jnp.float32)
        for i in members:
            xf = x_refs[i][:, : pieces[i][2]].astype(jnp.float32)
            total += jnp.sum(xf * xf, axis=1, keepdims=True)
        scale = lax.rsqrt(total / width + 1e-06)
        for i in members:
            cols = pieces[i][2]
            place = (lax.axis_index("et") & (width // cols - 1)) ^ pieces[i][3]
            where = aligned(place, cols) if cols < width else slice(None)
            xf = x_refs[i][:, :cols].astype(jnp.float32)
            normed_ref[row : row + rows, where] = (
                xf * scale * (1.0 + mod_ref[section, 0:1, where]) + mod_ref[section, 1:2, where]
            ).astype(jnp.bfloat16)
    normed = normed_ref[...]
    both = jnp.dot(normed, pair_ref[...], preferred_element_type=jnp.float32)
    logits = lax.dot_general(
        normed, router_ref[...], (((1,), (1,)), ((), ())), preferred_element_type=jnp.float32
    )
    count = logits.shape[1]
    lane = lax.broadcasted_iota(jnp.int32, logits.shape, 1)
    flags = jnp.concatenate([f[:, f.shape[1] - LANES :] for f in flag_refs], axis=0).astype(jnp.float32)
    flags = flags[:, section * experts : section * experts + count]
    chosen = jnp.where(flags > 0.5, jax.nn.sigmoid(logits), 0.0)
    mine = jnp.where(lane == lax.axis_index("ep"), chosen, 0.0)
    weight = jnp.sum(mine, axis=1, keepdims=True) / jnp.sum(chosen, axis=1, keepdims=True)
    gate, upper = both[:, :hidden], both[:, hidden:]
    out_ref[...] = (gate / (1.0 + jnp.exp(-gate)) * upper * weight).astype(jnp.bfloat16)


def front(xs, pieces, flags, section, mod, router, pair):
    width, hidden = pair.shape[0], pair.shape[1] // 2
    rows = sum(f.shape[0] for f in flags)
    experts = router.shape[0]
    return pl.pallas_call(
        functools.partial(front_kernel, pieces, section, experts, len(flags)),
        in_specs=[VMEM] * (len(xs) + len(flags) + 3),
        scratch_shapes=[pltpu.VMEM((rows, width), jnp.bfloat16)],
        out_shape=jax.ShapeDtypeStruct((rows, hidden), jnp.bfloat16),
        compiler_params=params(),
        cost_estimate=pl.CostEstimate(
            flops=4 * rows * width * hidden, bytes_accessed=4 * width * hidden, transcendentals=0
        ),
        name="front",
    )(*xs, *flags, mod, router, pair)


def down_kernel(flip, n_adds, hidden_ref, down_ref, *refs):
    adds, outs = refs[:n_adds], refs[n_adds:]
    quarter = outs[0].shape[1]
    weights = down_ref[:, aligned(lax.axis_index("et") ^ flip, quarter)]
    product = jnp.dot(hidden_ref[...], weights, preferred_element_type=jnp.float32)
    for ref in adds:
        product += ref[...].astype(jnp.float32)
    rows = outs[0].shape[0]
    for k, out in enumerate(outs):
        out[...] = product[k * rows : (k + 1) * rows].astype(out.dtype)


def down(hidden, w_down, flip, blocks, adds=(), dtype=jnp.bfloat16):
    units, width = w_down.shape
    rows, quarter = hidden.shape[0], width // 4
    return pl.pallas_call(
        functools.partial(down_kernel, flip, len(adds)),
        in_specs=[VMEM] * (2 + len(adds)),
        out_shape=[jax.ShapeDtypeStruct((rows // blocks, quarter), dtype)] * blocks,
        compiler_params=params(),
        cost_estimate=pl.CostEstimate(
            flops=2 * rows * units * quarter, bytes_accessed=2 * units * quarter, transcendentals=0
        ),
        name="down",
    )(hidden, w_down, *adds)


def add_kernel(keep_ref, came_ref, *outs):
    for k, out in enumerate(outs):
        rows = slice(k * out.shape[0], (k + 1) * out.shape[0])
        out[...] = (keep_ref[rows, :] + came_ref[rows, :].astype(jnp.float32)).astype(out.dtype)


def add(keep, came, dtypes):
    shape = (keep.shape[0] // len(dtypes), keep.shape[1])
    return pl.pallas_call(
        add_kernel,
        out_shape=[jax.ShapeDtypeStruct(shape, t) for t in dtypes],
        compiler_params=params(),
        name="add",
    )(keep, came)


def move_kernel(n_outs, own_ref, total_ref, *refs):
    came, outs = refs[:-n_outs], refs[-n_outs:]
    velocity = total_ref[...]
    for ref in came:
        velocity += ref[...].astype(jnp.float32)
    outs[0][...] = (own_ref[...].astype(jnp.float32) - 0.5 * velocity).astype(jnp.bfloat16)
    if n_outs > 1:
        outs[1][...] = velocity.astype(jnp.bfloat16)


def move(own, total, came, n_outs):
    return pl.pallas_call(
        functools.partial(move_kernel, n_outs),
        out_shape=[jax.ShapeDtypeStruct(own.shape, jnp.bfloat16)] * n_outs,
        compiler_params=params(),
        name="move",
    )(own, total, *came)


def sum_back(hidden, w_down, own, n_outs):
    peers = lax.axis_size("ep")
    some = peers // 2
    far = swap(down(hidden, w_down, 3, 1)[0], "et", 1)
    near = swap(down(hidden, w_down, 1, 1)[0], "et", 1)
    first, last = down(hidden, w_down, 2, 2, (far,))
    last, first = swap(last, "et", 2), swap(first, "et", 2)
    keep_first, keep_last = down(hidden, w_down, 0, 2, (near,), jnp.float32)
    blocks = add(keep_last, last, [jnp.bfloat16] * (peers - some))
    total, *others = add(keep_first, first, [jnp.float32] + [jnp.bfloat16] * (some - 1))
    sent = [swap(b, "ep", k + 1) for k, b in enumerate(others + list(blocks))]
    return move(own, total, sent, n_outs)


QUARTERS = (0, 2, 1, 3)


def spread(block):
    side = swap(block, "et", 2)
    return [block, side, swap(block, "et", 1), swap(side, "et", 1)]


def dense_body(tokens, modulation, router, gate_weight, up_weight, down_weight, expert_ids):
    rows, width = tokens.shape
    quarter = width // 4
    router = router.T
    peers = lax.axis_size("ep")

    wide, packed, own = pack(tokens, expert_ids.transpose(0, 2, 1), router.shape[0])
    pair, w_down, done = load(gate_weight, up_weight, down_weight)
    flags = [packed, swap(wide, "ep", 1)] + [swap(packed, "ep", k) for k in range(2, peers)]
    xs = [tokens, flags[1], swap(flags[1], "et", 1)]
    pieces = [(0, rows, width, 0), (rows, rows, width // 2, 0), (rows, rows, width // 2, 1)]
    for k in range(2, peers):
        xs += spread(relay(flags[k], quarter, done))
        pieces += [(k * rows, rows, quarter, f) for f in QUARTERS]
    hidden = front(xs, pieces, flags, 0, modulation, router, pair)
    (own,) = sum_back(hidden, w_down, own, 1)

    xs, pieces = [], []
    for k in range(peers):
        xs += spread(swap(own, "ep", k) if k else own)
        pieces += [(k * rows, rows, quarter, f) for f in QUARTERS]
    hidden = front(xs, pieces, flags, 1, modulation, router, pair)
    return tuple(sum_back(hidden, w_down, own, 2))


def solution(mesh):
    in_specs = (
        P(("grp", "ep"), None),
        P(),
        P(),
        P("ep", None, "et"),
        P("ep", None, "et"),
        P("ep", "et", None),
        P(None, ("grp", "ep"), None),
    )
    out_specs = (P(("grp", "ep"), "et"), P(("grp", "ep"), "et"))

    def body(*args):
        experts, picks = args[2].shape[1], args[6].shape[2]
        peers = lax.axis_size("ep")
        fits = lax.axis_size("et") == 4 and peers & (peers - 1) == 0
        chosen = dense_body if fits and experts <= 2 * picks else routed_body
        return chosen(*args)

    return jax.shard_map(body, mesh=mesh, in_specs=in_specs, out_specs=out_specs, check_vma=False)
```

```python
import functools

import jax
import jax.numpy as jnp
from jax import lax
from jax.experimental import pallas as pl
from jax.experimental.pallas import tpu as pltpu
from jax.sharding import PartitionSpec as P


def normalize(x, mod):
    xf = x.astype(jnp.float32)
    scaled = xf * lax.rsqrt(jnp.mean(xf * xf, axis=-1, keepdims=True) + 1e-06)
    return (scaled * (1.0 + mod[0]) + mod[1]).astype(jnp.bfloat16)


def routed_section(x_full, x_cols, mod, ids, router, gate_weight, up_weight, down_weight):
    tok_rows = x_full.shape[0]
    width = x_full.shape[1]
    experts = router.shape[1]
    picks = ids.shape[1]
    n_peers = lax.axis_size("ep")
    quarter = width // lax.axis_size("et")
    slot_count = 3 * tok_rows * picks // (2 * experts)
    normed = normalize(x_full, mod)
    logits = jnp.dot(normed, router, preferred_element_type=jnp.float32)
    chosen = jax.nn.sigmoid(jnp.take_along_axis(logits, ids, axis=1))
    weight = chosen / jnp.sum(chosen, axis=1, keepdims=True)
    flat_e = ids.reshape(-1)
    onehot = (flat_e[:, None] == jnp.arange(experts, dtype=jnp.int32)).astype(jnp.int32)
    counted = jnp.cumsum(onehot, axis=0)
    slot = jnp.sum(onehot * (counted - 1), axis=1)
    repeated = jnp.repeat(normed, picks, axis=0)
    outbox = jnp.zeros((experts, slot_count, width), jnp.bfloat16).at[flat_e, slot].set(repeated)
    arrived = lax.all_to_all(outbox, "ep", split_axis=0, concat_axis=0, tiled=True)
    in_rows = arrived.reshape(n_peers * slot_count, width)
    gate = jnp.dot(in_rows, gate_weight[0], preferred_element_type=jnp.float32)
    upper = jnp.dot(in_rows, up_weight[0], preferred_element_type=jnp.float32)
    hidden = (jax.nn.silu(gate) * upper).astype(jnp.bfloat16)
    partial_out = jnp.dot(hidden, down_weight[0], preferred_element_type=jnp.float32)
    summed = lax.psum_scatter(
        partial_out.astype(jnp.bfloat16), "et", scatter_dimension=1, tiled=True
    )
    returned = lax.all_to_all(
        summed.reshape(n_peers, slot_count, quarter), "ep", split_axis=0, concat_axis=0, tiled=True
    )
    picked = returned[flat_e, slot].astype(jnp.float32).reshape(tok_rows, picks, quarter)
    velocity = jnp.sum(picked * weight[:, :, None], axis=1)
    moved = (x_cols.astype(jnp.float32) - 0.5 * velocity).astype(jnp.bfloat16)
    return (moved, velocity)


def routed_body(tokens, modulation, router, gate_weight, up_weight, down_weight, expert_ids):
    quarter = tokens.shape[1] // lax.axis_size("et")
    column_start = lax.axis_index("et") * quarter
    cols = lax.dynamic_slice_in_dim(tokens, column_start, quarter, 1)
    weights = (router, gate_weight, up_weight, down_weight)
    first, _ = routed_section(tokens, cols, modulation[0], expert_ids[0], *weights)
    full = lax.all_gather(first, "et", axis=1, tiled=True)
    second, velocity = routed_section(full, first, modulation[1], expert_ids[1], *weights)
    return (second, velocity.astype(jnp.bfloat16))


def swap(x, axis, bit):
    size = lax.axis_size(axis)
    return lax.ppermute(x, axis, [(i, i ^ bit) for i in range(size)])


LANES = 128
VMEM_LIMIT = 32 * 1024 * 1024
VMEM_MOST = 52 * 1024 * 1024
VMEM_ALL = 63 * 1024 * 1024
VMEM = pl.BlockSpec(memory_space=pltpu.VMEM)
ANY = pl.BlockSpec(memory_space=pl.ANY)


def params(limit=VMEM_LIMIT):
    return pltpu.CompilerParams(vmem_limit_bytes=limit)


def aligned(index, size):
    return pl.ds(pl.multiple_of(index * size, size), size)


def load_kernel(gate_ref, up_ref, down_ref, pair_ref, out_ref, done_ref, sems):
    hidden = gate_ref.shape[2]
    copies = [
        pltpu.make_async_copy(gate_ref.at[0], pair_ref.at[:, :hidden], sems.at[0]),
        pltpu.make_async_copy(up_ref.at[0], pair_ref.at[:, hidden:], sems.at[1]),
        pltpu.make_async_copy(down_ref.at[0], out_ref, sems.at[2]),
    ]
    for copy in copies:
        copy.start()
    for copy in copies:
        copy.wait()
    done_ref[...] = jnp.zeros_like(done_ref)


def load(gate, up, down):
    _, width, hidden = gate.shape
    return pl.pallas_call(
        load_kernel,
        in_specs=[ANY] * 3,
        out_specs=[VMEM] * 3,
        out_shape=[
            pltpu.VMEM((width, 2 * hidden), jnp.bfloat16),
            pltpu.VMEM((hidden, width), jnp.bfloat16),
            pltpu.VMEM((8, LANES), jnp.float32),
        ],
        scratch_shapes=[pltpu.SemaphoreType.DMA((3,))],
        compiler_params=params(VMEM_MOST),
        cost_estimate=pl.CostEstimate(flops=0, bytes_accessed=12 * width * hidden, transcendentals=0),
        name="load",
    )(gate, up, down)


def relay_kernel(block_ref, done_ref, out_ref):
    out_ref[...] = block_ref[:, : out_ref.shape[1]]


def relay(block, cols, done):
    return pl.pallas_call(
        relay_kernel,
        out_shape=jax.ShapeDtypeStruct((block.shape[0], cols), block.dtype),
        compiler_params=params(),
        name="relay",
    )(block, done)


def choose(ids, expert, slots):
    picks, rows = ids.shape
    named = jnp.zeros((1, rows), jnp.float32)
    for k in range(picks):
        named += jnp.where(ids[k : k + 1, :] == expert, 1.0, 0.0)
    named = jnp.broadcast_to(named, (slots, rows))
    earlier = lax.broadcasted_iota(jnp.int32, (rows, rows), 0) < lax.broadcasted_iota(jnp.int32, (rows, rows), 1)
    ahead = jnp.dot(
        named.astype(jnp.bfloat16),
        jnp.where(earlier, 1.0, 0.0).astype(jnp.bfloat16),
        preferred_element_type=jnp.float32,
    )
    slot = lax.broadcasted_iota(jnp.int32, (slots, rows), 0)
    return jnp.where((ahead.astype(jnp.int32) == slot) & (named > 0.5), 1.0, 0.0)


def select(one_hot, values):
    one_hot = one_hot.astype(jnp.bfloat16)
    return jnp.dot(one_hot, values, preferred_element_type=jnp.float32).astype(jnp.bfloat16)


def flags_of(ids, section, experts):
    picks, rows = ids.shape
    lane = lax.broadcasted_iota(jnp.int32, (LANES, rows), 0)
    flags = jnp.zeros(lane.shape, jnp.float32)
    for k in range(picks):
        flags += jnp.where(ids[k : k + 1, :] + section * experts == lane, 1.0, 0.0)
    return flags.T.astype(jnp.bfloat16)


def chosen_flags(ids, peer, experts, slots):
    picked = [choose(one, lax.axis_index("ep") ^ peer, slots) for one in ids]
    parts = [select(p, flags_of(one, s, experts)) for s, (p, one) in enumerate(zip(picked, ids))]
    return sum(part.astype(jnp.float32) for part in parts).astype(jnp.bfloat16), picked[0]


def pack_kernel(experts, tokens_ref, ids_ref, *refs):
    wide_ref, *out_refs, own_ref, half_ref, held_ref, sems = refs
    width = tokens_ref.shape[1]
    half, quarter = width // 2, width // 4
    where = lax.axis_index("et")
    copies = [
        pltpu.make_async_copy(ids_ref, held_ref, sems.at[0]),
        pltpu.make_async_copy(tokens_ref.at[:, aligned(where & 1, quarter)], half_ref.at[:, :quarter], sems.at[1]),
        pltpu.make_async_copy(tokens_ref.at[:, aligned(where & 1 | 2, quarter)], half_ref.at[:, quarter:], sems.at[2]),
    ]
    for copy in copies:
        copy.start()
    copies[0].wait()
    ids = [held_ref[s] for s in range(held_ref.shape[0])]
    slots = wide_ref.shape[0]
    made = [chosen_flags(ids, k + 1, experts, slots) for k in range(1 + len(out_refs))]
    copies[1].wait()
    copies[2].wait()
    own_ref[...] = half_ref[:, aligned(where >> 1, quarter)]
    wide_ref[:, :half] = select(made[0][1], half_ref[...])
    wide_ref[:, half:] = made[0][0]
    for (flags, picked), out_ref in zip(made[1:], out_refs):
        out_ref[:, :quarter] = select(picked, own_ref[...])
        out_ref[:, quarter:] = flags


def pack(tokens, ids, experts, slots):
    rows, width = tokens.shape
    far = lax.axis_size("ep") - 2
    shapes = [(slots, width // 2 + LANES)] + [(slots, width // 4 + LANES)] * far + [(rows, width // 4)]
    return pl.pallas_call(
        functools.partial(pack_kernel, experts),
        in_specs=[ANY] * 2,
        out_specs=[VMEM] * len(shapes),
        out_shape=[pltpu.VMEM(s, jnp.bfloat16) for s in shapes],
        scratch_shapes=[
            pltpu.VMEM((rows, width // 2), jnp.bfloat16),
            pltpu.VMEM(ids.shape, jnp.int32),
            pltpu.SemaphoreType.DMA((3,)),
        ],
        compiler_params=params(VMEM_ALL),
        name="pack",
    )(tokens, ids)


def own_kernel(experts, tokens_ref, ids_ref, out_ref, flags_ref):
    ids = [ids_ref[s] for s in range(ids_ref.shape[0])]
    flags_ref[...], picked = chosen_flags(ids, 0, experts, out_ref.shape[0])
    out_ref[...] = select(picked, tokens_ref[...])


def own_rows(tokens, ids, experts, slots):
    shapes = [(slots, tokens.shape[1]), (slots, LANES)]
    return pl.pallas_call(
        functools.partial(own_kernel, experts),
        out_shape=[jax.ShapeDtypeStruct(s, jnp.bfloat16) for s in shapes],
        compiler_params=params(),
        name="own_rows",
    )(tokens, ids)


def front_kernel(layout, section, experts, n_flags, *refs):
    n = sum(len(block) for block in layout)
    x_refs, flag_refs = list(refs[:n]), refs[n : n + n_flags]
    mod_ref, router_ref, pair_ref, out_ref, normed_ref = refs[n + n_flags :]
    width = normed_ref.shape[1]
    hidden = out_ref.shape[1]
    quarter = width // 4
    et = lax.axis_index("et")
    blocks = []
    for block in layout:
        blocks.append([(x_refs.pop(0), cols, flip) for cols, flip in block])

    def part(block, flip):
        for ref, cols, at in block:
            if cols == quarter and at == flip:
                return ref[...].astype(jnp.float32)
            if cols == 2 * quarter and at == flip & 1:
                return ref[:, aligned((et ^ flip) >> 1, quarter)].astype(jnp.float32)
            if cols == width:
                return ref[:, aligned(et ^ flip, quarter)].astype(jnp.float32)

    parts = [jnp.concatenate([part(block, flip) for block in blocks], axis=0) for flip in range(4)]
    total = sum(jnp.sum(xf * xf, axis=1, keepdims=True) for xf in parts)
    scale = lax.rsqrt(total / width + 1e-06)
    for flip, xf in enumerate(parts):
        where = aligned(et ^ flip, quarter)
        normed_ref[:, where] = (
            xf * scale * (1.0 + mod_ref[section, 0:1, where]) + mod_ref[section, 1:2, where]
        ).astype(jnp.bfloat16)
    normed = normed_ref[...]
    both = jnp.dot(normed, pair_ref[...], preferred_element_type=jnp.float32)
    logits = lax.dot_general(
        normed, router_ref[...], (((1,), (1,)), ((), ())), preferred_element_type=jnp.float32
    )
    count = logits.shape[1]
    lane = lax.broadcasted_iota(jnp.int32, logits.shape, 1)
    flags = [f[:, f.shape[1] - LANES :].astype(jnp.float32) for f in flag_refs]
    flags = jnp.concatenate(flags, axis=0)[:, section * experts : section * experts + count]
    chosen = jnp.where(flags > 0.5, jax.nn.sigmoid(logits), 0.0)
    mine = jnp.sum(jnp.where(lane == lax.axis_index("ep"), chosen, 0.0), axis=1, keepdims=True)
    used = jnp.max(flags, axis=1, keepdims=True) > 0.5
    weight = jnp.where(used, mine / jnp.sum(chosen, axis=1, keepdims=True), 0.0)
    gate, upper = both[:, :hidden], both[:, hidden:]
    units = jnp.where(used, gate / (1.0 + jnp.exp(-gate)) * upper * weight, 0.0)
    out_ref[...] = units.astype(jnp.bfloat16)


def front(blocks, flags, section, mod, router, pair):
    width, hidden = pair.shape[0], pair.shape[1] // 2
    rows = sum(f.shape[0] for f in flags)
    experts = router.shape[0]
    xs = [x for block in blocks for x, _, _ in block]
    layout = [[piece[1:] for piece in block] for block in blocks]
    return pl.pallas_call(
        functools.partial(front_kernel, layout, section, experts, len(flags)),
        in_specs=[VMEM] * (len(xs) + len(flags) + 3),
        scratch_shapes=[pltpu.VMEM((rows, width), jnp.bfloat16)],
        out_shape=jax.ShapeDtypeStruct((rows, hidden), jnp.bfloat16),
        compiler_params=params(),
        cost_estimate=pl.CostEstimate(
            flops=4 * rows * width * hidden, bytes_accessed=4 * width * hidden, transcendentals=0
        ),
        name="front",
    )(*xs, *flags, mod, router, pair)


def down_kernel(flip, n_adds, hidden_ref, down_ref, *refs):
    adds, outs = refs[:n_adds], refs[n_adds:]
    quarter = outs[0].shape[1]
    weights = down_ref[:, aligned(lax.axis_index("et") ^ flip, quarter)]
    product = jnp.dot(hidden_ref[...], weights, preferred_element_type=jnp.float32)
    for ref in adds:
        product += ref[...].astype(jnp.float32)
    rows = outs[0].shape[0]
    for k, out in enumerate(outs):
        out[...] = product[k * rows : (k + 1) * rows].astype(out.dtype)


def down(hidden, w_down, flip, blocks, adds=(), dtype=jnp.bfloat16):
    units, width = w_down.shape
    rows, quarter = hidden.shape[0], width // 4
    return pl.pallas_call(
        functools.partial(down_kernel, flip, len(adds)),
        in_specs=[VMEM] * (2 + len(adds)),
        out_shape=[jax.ShapeDtypeStruct((rows // blocks, quarter), dtype)] * blocks,
        compiler_params=params(),
        cost_estimate=pl.CostEstimate(
            flops=2 * rows * units * quarter, bytes_accessed=2 * units * quarter, transcendentals=0
        ),
        name="down",
    )(hidden, w_down, *adds)


def add_kernel(keep_ref, came_ref, *outs):
    total = keep_ref[...] + came_ref[...].astype(jnp.float32)
    rows = outs[0].shape[0]
    for k, out in enumerate(outs):
        out[...] = total[k * rows : (k + 1) * rows].astype(out.dtype)


def add(keep, came, count):
    shape = (keep.shape[0] // count, keep.shape[1])
    return pl.pallas_call(
        add_kernel,
        out_shape=[jax.ShapeDtypeStruct(shape, jnp.bfloat16)] * count,
        compiler_params=params(),
        name="add",
    )(keep, came)


def move_kernel(section, n_came, own_ref, ids_ref, *refs):
    came, outs = refs[:n_came], refs[n_came:]
    peer = lax.axis_index("ep")
    slots = came[0].shape[0]
    velocity = jnp.zeros(own_ref.shape, jnp.float32)
    for k, ref in enumerate(came):
        back = choose(ids_ref[section], peer ^ k, slots).T.astype(jnp.bfloat16)
        velocity += jnp.dot(back, ref[...], preferred_element_type=jnp.float32)
    moved = (own_ref[...].astype(jnp.float32) - 0.5 * velocity).astype(jnp.bfloat16)
    outs[0][...] = moved
    if len(outs) == 2:
        outs[1][...] = velocity.astype(jnp.bfloat16)
    else:
        for k, out in enumerate(outs[1:]):
            out[...] = select(choose(ids_ref[section + 1], peer ^ k, slots), moved)


def move(section, own, ids, came):
    shapes = [own.shape] + ([own.shape] if section + 1 == ids.shape[0] else [c.shape for c in came])
    return pl.pallas_call(
        functools.partial(move_kernel, section, len(came)),
        out_shape=[jax.ShapeDtypeStruct(s, jnp.bfloat16) for s in shapes],
        compiler_params=params(),
        name="move",
    )(own, ids, *came)


def sum_back(section, hidden, w_down, own, ids):
    peers = lax.axis_size("ep")
    some = peers // 2
    far = swap(down(hidden, w_down, 3, 1)[0], "et", 1)
    near = swap(down(hidden, w_down, 1, 1)[0], "et", 1)
    first, last = down(hidden, w_down, 2, 2, (far,))
    last, first = swap(last, "et", 2), swap(first, "et", 2)
    keep_first, keep_last = down(hidden, w_down, 0, 2, (near,), jnp.float32)
    later = add(keep_last, last, peers - some)
    blocks = add(keep_first, first, some) + later
    return move(section, own, ids, [swap(b, "ep", k) if k else b for k, b in enumerate(blocks)])


def spread(block, quarter):
    side = swap(block, "et", 2)
    near, far = swap(block, "et", 1), swap(side, "et", 1)
    return [(block, quarter, 0), (side, quarter, 2), (near, quarter, 1), (far, quarter, 3)]


def dense_body(tokens, modulation, router, gate_weight, up_weight, down_weight, expert_ids):
    rows, width = tokens.shape
    half, quarter = width // 2, width // 4
    router = router.T
    experts = router.shape[0]
    peers = lax.axis_size("ep")
    slots = 3 * rows * expert_ids.shape[2] // (2 * experts)
    ids = expert_ids.transpose(0, 2, 1)

    wide, *packed, own = pack(tokens, ids, experts, slots)
    pair, w_down, done = load(gate_weight, up_weight, down_weight)
    mine, flags = own_rows(tokens, ids, experts, slots)
    flags = [flags, swap(wide, "ep", 1)] + [swap(p, "ep", k + 2) for k, p in enumerate(packed)]
    blocks = [[(mine, width, 0)], [(flags[1], half, 0), (swap(flags[1], "et", 1), half, 1)]]
    blocks += [spread(relay(f, quarter, done), quarter) for f in flags[2:]]
    hidden = front(blocks, flags, 0, modulation, router, pair)
    own, *sent = sum_back(0, hidden, w_down, own, ids)

    blocks = [spread(swap(b, "ep", k) if k else b, quarter) for k, b in enumerate(sent)]
    hidden = front(blocks, flags, 1, modulation, router, pair)
    return tuple(sum_back(1, hidden, w_down, own, ids))


def solution(mesh):
    in_specs = (
        P(("grp", "ep"), None),
        P(),
        P(),
        P("ep", None, "et"),
        P("ep", None, "et"),
        P("ep", "et", None),
        P(None, ("grp", "ep"), None),
    )
    out_specs = (P(("grp", "ep"), "et"), P(("grp", "ep"), "et"))

    def body(*args):
        experts, picks = args[2].shape[1], args[6].shape[2]
        peers = lax.axis_size("ep")
        fits = lax.axis_size("et") == 4 and peers & (peers - 1) == 0
        chosen = dense_body if fits and experts <= 2 * picks else routed_body
        return chosen(*args)

    return jax.shard_map(body, mesh=mesh, in_specs=in_specs, out_specs=out_specs, check_vma=False)
```

```python
import functools

import jax
import jax.numpy as jnp
from jax import lax
from jax.experimental import pallas as pl
from jax.experimental.pallas import tpu as pltpu
from jax.sharding import PartitionSpec as P


def normalize(x, mod):
    xf = x.astype(jnp.float32)
    scaled = xf * lax.rsqrt(jnp.mean(xf * xf, axis=-1, keepdims=True) + 1e-06)
    return (scaled * (1.0 + mod[0]) + mod[1]).astype(jnp.bfloat16)


def routed_section(x_full, x_cols, mod, ids, router, gate_weight, up_weight, down_weight):
    tok_rows = x_full.shape[0]
    width = x_full.shape[1]
    experts = router.shape[1]
    picks = ids.shape[1]
    n_peers = lax.axis_size("ep")
    quarter = width // lax.axis_size("et")
    slot_count = 3 * tok_rows * picks // (2 * experts)
    normed = normalize(x_full, mod)
    logits = jnp.dot(normed, router, preferred_element_type=jnp.float32)
    chosen = jax.nn.sigmoid(jnp.take_along_axis(logits, ids, axis=1))
    weight = chosen / jnp.sum(chosen, axis=1, keepdims=True)
    flat_e = ids.reshape(-1)
    onehot = (flat_e[:, None] == jnp.arange(experts, dtype=jnp.int32)).astype(jnp.int32)
    counted = jnp.cumsum(onehot, axis=0)
    slot = jnp.sum(onehot * (counted - 1), axis=1)
    repeated = jnp.repeat(normed, picks, axis=0)
    outbox = jnp.zeros((experts, slot_count, width), jnp.bfloat16).at[flat_e, slot].set(repeated)
    arrived = lax.all_to_all(outbox, "ep", split_axis=0, concat_axis=0, tiled=True)
    in_rows = arrived.reshape(n_peers * slot_count, width)
    gate = jnp.dot(in_rows, gate_weight[0], preferred_element_type=jnp.float32)
    upper = jnp.dot(in_rows, up_weight[0], preferred_element_type=jnp.float32)
    hidden = (jax.nn.silu(gate) * upper).astype(jnp.bfloat16)
    partial_out = jnp.dot(hidden, down_weight[0], preferred_element_type=jnp.float32)
    summed = lax.psum_scatter(
        partial_out.astype(jnp.bfloat16), "et", scatter_dimension=1, tiled=True
    )
    returned = lax.all_to_all(
        summed.reshape(n_peers, slot_count, quarter), "ep", split_axis=0, concat_axis=0, tiled=True
    )
    picked = returned[flat_e, slot].astype(jnp.float32).reshape(tok_rows, picks, quarter)
    velocity = jnp.sum(picked * weight[:, :, None], axis=1)
    moved = (x_cols.astype(jnp.float32) - 0.5 * velocity).astype(jnp.bfloat16)
    return (moved, velocity)


def routed_body(tokens, modulation, router, gate_weight, up_weight, down_weight, expert_ids):
    quarter = tokens.shape[1] // lax.axis_size("et")
    column_start = lax.axis_index("et") * quarter
    cols = lax.dynamic_slice_in_dim(tokens, column_start, quarter, 1)
    weights = (router, gate_weight, up_weight, down_weight)
    first, _ = routed_section(tokens, cols, modulation[0], expert_ids[0], *weights)
    full = lax.all_gather(first, "et", axis=1, tiled=True)
    second, velocity = routed_section(full, first, modulation[1], expert_ids[1], *weights)
    return (second, velocity.astype(jnp.bfloat16))


def swap(x, axis, bit):
    size = lax.axis_size(axis)
    return lax.ppermute(x, axis, [(i, i ^ bit) for i in range(size)])


LANES = 128
VMEM_LIMIT = 32 * 1024 * 1024
VMEM_MOST = 52 * 1024 * 1024
VMEM_ALL = 63 * 1024 * 1024
VMEM = pl.BlockSpec(memory_space=pltpu.VMEM)
ANY = pl.BlockSpec(memory_space=pl.ANY)


def params(limit=VMEM_LIMIT):
    return pltpu.CompilerParams(vmem_limit_bytes=limit)


def aligned(index, size):
    return pl.ds(pl.multiple_of(index * size, size), size)


def load_kernel(gate_ref, up_ref, down_ref, pair_ref, out_ref, done_ref, sems):
    hidden = gate_ref.shape[2]
    copies = [
        pltpu.make_async_copy(gate_ref.at[0], pair_ref.at[:, :hidden], sems.at[0]),
        pltpu.make_async_copy(up_ref.at[0], pair_ref.at[:, hidden:], sems.at[1]),
        pltpu.make_async_copy(down_ref.at[0], out_ref, sems.at[2]),
    ]
    for copy in copies:
        copy.start()
    for copy in copies:
        copy.wait()
    done_ref[...] = jnp.zeros_like(done_ref)


def load(gate, up, down):
    _, width, hidden = gate.shape
    return pl.pallas_call(
        load_kernel,
        in_specs=[ANY] * 3,
        out_specs=[VMEM] * 3,
        out_shape=[
            pltpu.VMEM((width, 2 * hidden), jnp.bfloat16),
            pltpu.VMEM((hidden, width), jnp.bfloat16),
            pltpu.VMEM((8, LANES), jnp.float32),
        ],
        scratch_shapes=[pltpu.SemaphoreType.DMA((3,))],
        compiler_params=params(VMEM_MOST),
        cost_estimate=pl.CostEstimate(flops=0, bytes_accessed=12 * width * hidden, transcendentals=0),
        name="load",
    )(gate, up, down)


def relay_kernel(block_ref, done_ref, out_ref):
    out_ref[...] = block_ref[:, : out_ref.shape[1]]


def relay(block, cols, done):
    return pl.pallas_call(
        relay_kernel,
        out_shape=jax.ShapeDtypeStruct((block.shape[0], cols), block.dtype),
        compiler_params=params(),
        name="relay",
    )(block, done)


def choices(ids, peers, slots):
    rows = ids[0].shape[1]
    me = lax.axis_index("ep")
    named = []
    for one in ids:
        for k in range(peers):
            hits = [jnp.where(one[p : p + 1, :] == me ^ k, 1.0, 0.0) for p in range(one.shape[0])]
            named.append(sum(hits))
    earlier = lax.broadcasted_iota(jnp.int32, (rows, rows), 0) < lax.broadcasted_iota(jnp.int32, (rows, rows), 1)
    ahead = jnp.dot(
        jnp.concatenate(named, axis=0).astype(jnp.bfloat16),
        jnp.where(earlier, 1.0, 0.0).astype(jnp.bfloat16),
        preferred_element_type=jnp.float32,
    ).astype(jnp.int32)
    slot = lax.broadcasted_iota(jnp.int32, (slots, rows), 0)
    holds = [jnp.where((ahead[i : i + 1, :] == slot) & (row > 0.5), 1.0, 0.0) for i, row in enumerate(named)]
    return [jnp.concatenate(holds[s * peers : (s + 1) * peers], axis=0) for s in range(len(ids))]


def narrow(x):
    return x.astype(jnp.bfloat16)


def product(x, y):
    return jnp.dot(narrow(x), narrow(y), preferred_element_type=jnp.float32)


def named_experts(ids, held, experts):
    rows = ids[0].shape[1]
    flags = []
    for s, one in enumerate(ids):
        lane = lax.broadcasted_iota(jnp.int32, (LANES, rows), 0)
        hits = [jnp.where(one[p : p + 1, :] + s * experts == lane, 1.0, 0.0) for p in range(one.shape[0])]
        flags.append(product(held[s], sum(hits).T))
    return sum(flags)


def pack_kernel(experts, tokens_ref, ids_ref, *refs):
    *out_refs, own_ref, half_ref, held_ref, sems = refs
    quarter = tokens_ref.shape[1] // 4
    half = 2 * quarter
    where = lax.axis_index("et")
    copies = [
        pltpu.make_async_copy(ids_ref, held_ref, sems.at[0]),
        pltpu.make_async_copy(tokens_ref.at[:, aligned(where & 1, quarter)], half_ref.at[:, :quarter], sems.at[1]),
        pltpu.make_async_copy(tokens_ref.at[:, aligned(where & 1 | 2, quarter)], half_ref.at[:, quarter:], sems.at[2]),
    ]
    for copy in copies:
        copy.start()
    copies[0].wait()
    ids = [held_ref[s] for s in range(held_ref.shape[0])]
    slots, peers = out_refs[0].shape[0], 1 + len(out_refs)
    held = choices(ids, peers, slots)
    flags = named_experts(ids, held, experts)
    copies[1].wait()
    copies[2].wait()
    own_ref[...] = half_ref[:, aligned(where >> 1, quarter)]
    picked = product(held[0][slots:], half_ref[...])
    for k, out_ref in enumerate(out_refs):
        out_ref[:, :half] = narrow(picked[k * slots : (k + 1) * slots])
        out_ref[:, half:] = narrow(flags[(k + 1) * slots : (k + 2) * slots])


def pack(tokens, ids, experts, slots):
    rows, width = tokens.shape
    others = lax.axis_size("ep") - 1
    shapes = [(slots, width // 2 + LANES)] * others + [(rows, width // 4)]
    return pl.pallas_call(
        functools.partial(pack_kernel, experts),
        in_specs=[ANY] * 2,
        out_specs=[VMEM] * len(shapes),
        out_shape=[pltpu.VMEM(s, jnp.bfloat16) for s in shapes],
        scratch_shapes=[
            pltpu.VMEM((rows, width // 2), jnp.bfloat16),
            pltpu.VMEM(ids.shape, jnp.int32),
            pltpu.SemaphoreType.DMA((3,)),
        ],
        compiler_params=params(VMEM_ALL),
        name="pack",
    )(tokens, ids)


def own_kernel(experts, tokens_ref, ids_ref, out_ref, flags_ref, *choice_refs):
    ids = [ids_ref[s] for s in range(ids_ref.shape[0])]
    slots = out_ref.shape[0]
    held = choices(ids, choice_refs[0].shape[0] // slots, slots)
    flags_ref[...] = narrow(named_experts(ids, held, experts)[:slots])
    out_ref[...] = narrow(product(held[0][:slots], tokens_ref[...]))
    for s, one in enumerate(held):
        choice_refs[2 * s][...] = narrow(one)
        choice_refs[2 * s + 1][...] = narrow(one.T)


def own_rows(tokens, ids, experts, slots):
    rows, width = tokens.shape
    total = lax.axis_size("ep") * slots
    shapes = [(slots, width), (slots, LANES)] + [(total, rows), (rows, total)] * ids.shape[0]
    return pl.pallas_call(
        functools.partial(own_kernel, experts),
        out_shape=[jax.ShapeDtypeStruct(s, jnp.bfloat16) for s in shapes],
        compiler_params=params(),
        name="own_rows",
    )(tokens, ids)


def front_kernel(layout, section, experts, n_flags, *refs):
    n = sum(len(block) for block in layout)
    x_refs, flag_refs = list(refs[:n]), refs[n : n + n_flags]
    mod_ref, router_ref, pair_ref, out_ref, normed_ref = refs[n + n_flags :]
    width = normed_ref.shape[1]
    hidden = out_ref.shape[1]
    quarter = width // 4
    et = lax.axis_index("et")
    blocks = []
    for block in layout:
        blocks.append([(x_refs.pop(0), cols, flip) for cols, flip in block])

    def part(block, flip):
        for ref, cols, at in block:
            if cols == quarter and at == flip:
                return ref[...].astype(jnp.float32)
            if cols == 2 * quarter and at == flip & 1:
                return ref[:, aligned((et ^ flip) >> 1, quarter)].astype(jnp.float32)
            if cols == width:
                return ref[:, aligned(et ^ flip, quarter)].astype(jnp.float32)

    parts = [jnp.concatenate([part(block, flip) for block in blocks], axis=0) for flip in range(4)]
    total = sum(jnp.sum(xf * xf, axis=1, keepdims=True) for xf in parts)
    scale = lax.rsqrt(total / width + 1e-06)
    for flip, xf in enumerate(parts):
        where = aligned(et ^ flip, quarter)
        normed_ref[:, where] = (
            xf * scale * (1.0 + mod_ref[section, 0:1, where]) + mod_ref[section, 1:2, where]
        ).astype(jnp.bfloat16)
    normed = normed_ref[...]
    both = jnp.dot(normed, pair_ref[...], preferred_element_type=jnp.float32)
    logits = lax.dot_general(
        normed, router_ref[...], (((1,), (1,)), ((), ())), preferred_element_type=jnp.float32
    )
    count = logits.shape[1]
    lane = lax.broadcasted_iota(jnp.int32, logits.shape, 1)
    flags = [f[:, f.shape[1] - LANES :].astype(jnp.float32) for f in flag_refs]
    flags = jnp.concatenate(flags, axis=0)[:, section * experts : section * experts + count]
    chosen = jnp.where(flags > 0.5, jax.nn.sigmoid(logits), 0.0)
    mine = jnp.sum(jnp.where(lane == lax.axis_index("ep"), chosen, 0.0), axis=1, keepdims=True)
    used = jnp.max(flags, axis=1, keepdims=True) > 0.5
    weight = jnp.where(used, mine / jnp.sum(chosen, axis=1, keepdims=True), 0.0)
    gate, upper = both[:, :hidden], both[:, hidden:]
    units = jnp.where(used, gate / (1.0 + jnp.exp(-gate)) * upper * weight, 0.0)
    out_ref[...] = units.astype(jnp.bfloat16)


def front(blocks, flags, section, mod, router, pair):
    width, hidden = pair.shape[0], pair.shape[1] // 2
    rows = sum(f.shape[0] for f in flags)
    experts = router.shape[0]
    xs = [x for block in blocks for x, _, _ in block]
    layout = [[piece[1:] for piece in block] for block in blocks]
    return pl.pallas_call(
        functools.partial(front_kernel, layout, section, experts, len(flags)),
        in_specs=[VMEM] * (len(xs) + len(flags) + 3),
        scratch_shapes=[pltpu.VMEM((rows, width), jnp.bfloat16)],
        out_shape=jax.ShapeDtypeStruct((rows, hidden), jnp.bfloat16),
        compiler_params=params(),
        cost_estimate=pl.CostEstimate(
            flops=4 * rows * width * hidden, bytes_accessed=4 * width * hidden, transcendentals=0
        ),
        name="front",
    )(*xs, *flags, mod, router, pair)


def down_kernel(flip, n_adds, hidden_ref, down_ref, *refs):
    adds, outs = refs[:n_adds], refs[n_adds:]
    quarter = outs[0].shape[1]
    weights = down_ref[:, aligned(lax.axis_index("et") ^ flip, quarter)]
    product = jnp.dot(hidden_ref[...], weights, preferred_element_type=jnp.float32)
    for ref in adds:
        product += ref[...].astype(jnp.float32)
    rows = outs[0].shape[0]
    for k, out in enumerate(outs):
        out[...] = product[k * rows : (k + 1) * rows].astype(out.dtype)


def down(hidden, w_down, flip, blocks, adds=(), dtype=jnp.bfloat16):
    units, width = w_down.shape
    rows, quarter = hidden.shape[0], width // 4
    return pl.pallas_call(
        functools.partial(down_kernel, flip, len(adds)),
        in_specs=[VMEM] * (2 + len(adds)),
        out_shape=[jax.ShapeDtypeStruct((rows // blocks, quarter), dtype)] * blocks,
        compiler_params=params(),
        cost_estimate=pl.CostEstimate(
            flops=2 * rows * units * quarter, bytes_accessed=2 * units * quarter, transcendentals=0
        ),
        name="down",
    )(hidden, w_down, *adds)


def add_kernel(keep_ref, came_ref, *outs):
    total = keep_ref[...] + came_ref[...].astype(jnp.float32)
    rows = outs[0].shape[0]
    for k, out in enumerate(outs):
        out[...] = total[k * rows : (k + 1) * rows].astype(out.dtype)


def add(keep, came, count):
    shape = (keep.shape[0] // count, keep.shape[1])
    return pl.pallas_call(
        add_kernel,
        out_shape=[jax.ShapeDtypeStruct(shape, jnp.bfloat16)] * count,
        compiler_params=params(),
        name="add",
    )(keep, came)


def move_kernel(n_came, last, own_ref, back_ref, pick_ref, *refs):
    came, outs = refs[:n_came], refs[n_came:]
    rows = [ref[...].astype(jnp.float32) for ref in came]
    velocity = product(back_ref[...], jnp.concatenate(rows, axis=0))
    moved = narrow(own_ref[...].astype(jnp.float32) - 0.5 * velocity)
    outs[0][...] = moved
    if last:
        outs[1][...] = narrow(velocity)
    else:
        slots = came[0].shape[0]
        picked = product(pick_ref[...], moved)
        for k, out in enumerate(outs[1:]):
            out[...] = narrow(picked[k * slots : (k + 1) * slots])


def move(own, back, pick, came, last):
    shapes = [own.shape] + ([own.shape] if last else [c.shape for c in came])
    return pl.pallas_call(
        functools.partial(move_kernel, len(came), last),
        out_shape=[jax.ShapeDtypeStruct(s, jnp.bfloat16) for s in shapes],
        compiler_params=params(),
        name="move",
    )(own, back, pick, *came)


def sum_back(hidden, w_down, own, back, pick, last_section):
    peers = lax.axis_size("ep")
    some = peers // 2
    far = swap(down(hidden, w_down, 3, 1)[0], "et", 1)
    near = swap(down(hidden, w_down, 1, 1)[0], "et", 1)
    first, last = down(hidden, w_down, 2, 2, (far,))
    last, first = swap(last, "et", 2), swap(first, "et", 2)
    keep_first, keep_last = down(hidden, w_down, 0, 2, (near,), jnp.float32)
    later = add(keep_last, last, peers - some)
    blocks = add(keep_first, first, some) + later
    came = [swap(b, "ep", k) if k else b for k, b in enumerate(blocks)]
    return move(own, back, pick, came, last_section)


def spread(block, quarter):
    side = swap(block, "et", 2)
    near, far = swap(block, "et", 1), swap(side, "et", 1)
    return [(block, quarter, 0), (side, quarter, 2), (near, quarter, 1), (far, quarter, 3)]


def dense_body(tokens, modulation, router, gate_weight, up_weight, down_weight, expert_ids):
    rows, width = tokens.shape
    half, quarter = width // 2, width // 4
    router = router.T
    experts = router.shape[0]
    peers = lax.axis_size("ep")
    slots = 3 * rows * expert_ids.shape[2] // (2 * experts)
    ids = expert_ids.transpose(0, 2, 1)

    *packed, own = pack(tokens, ids, experts, slots)
    pair, w_down, done = load(gate_weight, up_weight, down_weight)
    mine, flags, *choice = own_rows(tokens, ids, experts, slots)
    pick, back = choice[2], choice[1::2]
    flags = [flags] + [swap(p, "ep", k + 1) for k, p in enumerate(packed)]
    blocks = [[(mine, width, 0)]]
    for f in flags[1:]:
        f = relay(f, half, done)
        blocks.append([(f, half, 0), (swap(f, "et", 1), half, 1)])
    hidden = front(blocks, flags, 0, modulation, router, pair)
    own, *sent = sum_back(hidden, w_down, own, back[0], pick, False)

    blocks = [spread(swap(b, "ep", k) if k else b, quarter) for k, b in enumerate(sent)]
    hidden = front(blocks, flags, 1, modulation, router, pair)
    return tuple(sum_back(hidden, w_down, own, back[1], pick, True))


def solution(mesh):
    in_specs = (
        P(("grp", "ep"), None),
        P(),
        P(),
        P("ep", None, "et"),
        P("ep", None, "et"),
        P("ep", "et", None),
        P(None, ("grp", "ep"), None),
    )
    out_specs = (P(("grp", "ep"), "et"), P(("grp", "ep"), "et"))

    def body(*args):
        experts, picks = args[2].shape[1], args[6].shape[2]
        peers = lax.axis_size("ep")
        fits = lax.axis_size("et") == 4 and peers & (peers - 1) == 0
        chosen = dense_body if fits and experts <= 2 * picks else routed_body
        return chosen(*args)

    return jax.shard_map(body, mesh=mesh, in_specs=in_specs, out_specs=out_specs, check_vma=False)
```

```python
import functools

import jax
import jax.numpy as jnp
from jax import lax
from jax.experimental import pallas as pl
from jax.experimental.pallas import tpu as pltpu
from jax.sharding import PartitionSpec as P


def normalize(x, mod):
    xf = x.astype(jnp.float32)
    scaled = xf * lax.rsqrt(jnp.mean(xf * xf, axis=-1, keepdims=True) + 1e-06)
    return (scaled * (1.0 + mod[0]) + mod[1]).astype(jnp.bfloat16)


def routed_section(x_full, x_cols, mod, ids, router, gate_weight, up_weight, down_weight):
    tok_rows = x_full.shape[0]
    width = x_full.shape[1]
    experts = router.shape[1]
    picks = ids.shape[1]
    n_peers = lax.axis_size("ep")
    quarter = width // lax.axis_size("et")
    slot_count = 3 * tok_rows * picks // (2 * experts)
    normed = normalize(x_full, mod)
    logits = jnp.dot(normed, router, preferred_element_type=jnp.float32)
    chosen = jax.nn.sigmoid(jnp.take_along_axis(logits, ids, axis=1))
    weight = chosen / jnp.sum(chosen, axis=1, keepdims=True)
    flat_e = ids.reshape(-1)
    onehot = (flat_e[:, None] == jnp.arange(experts, dtype=jnp.int32)).astype(jnp.int32)
    counted = jnp.cumsum(onehot, axis=0)
    slot = jnp.sum(onehot * (counted - 1), axis=1)
    repeated = jnp.repeat(normed, picks, axis=0)
    outbox = jnp.zeros((experts, slot_count, width), jnp.bfloat16).at[flat_e, slot].set(repeated)
    arrived = lax.all_to_all(outbox, "ep", split_axis=0, concat_axis=0, tiled=True)
    in_rows = arrived.reshape(n_peers * slot_count, width)
    gate = jnp.dot(in_rows, gate_weight[0], preferred_element_type=jnp.float32)
    upper = jnp.dot(in_rows, up_weight[0], preferred_element_type=jnp.float32)
    hidden = (jax.nn.silu(gate) * upper).astype(jnp.bfloat16)
    partial_out = jnp.dot(hidden, down_weight[0], preferred_element_type=jnp.float32)
    summed = lax.psum_scatter(
        partial_out.astype(jnp.bfloat16), "et", scatter_dimension=1, tiled=True
    )
    returned = lax.all_to_all(
        summed.reshape(n_peers, slot_count, quarter), "ep", split_axis=0, concat_axis=0, tiled=True
    )
    picked = returned[flat_e, slot].astype(jnp.float32).reshape(tok_rows, picks, quarter)
    velocity = jnp.sum(picked * weight[:, :, None], axis=1)
    moved = (x_cols.astype(jnp.float32) - 0.5 * velocity).astype(jnp.bfloat16)
    return (moved, velocity)


def routed_body(tokens, modulation, router, gate_weight, up_weight, down_weight, expert_ids):
    quarter = tokens.shape[1] // lax.axis_size("et")
    column_start = lax.axis_index("et") * quarter
    cols = lax.dynamic_slice_in_dim(tokens, column_start, quarter, 1)
    weights = (router, gate_weight, up_weight, down_weight)
    first, _ = routed_section(tokens, cols, modulation[0], expert_ids[0], *weights)
    full = lax.all_gather(first, "et", axis=1, tiled=True)
    second, velocity = routed_section(full, first, modulation[1], expert_ids[1], *weights)
    return (second, velocity.astype(jnp.bfloat16))


def swap(x, axis, bit):
    size = lax.axis_size(axis)
    return lax.ppermute(x, axis, [(i, i ^ bit) for i in range(size)])


LANES = 128
VMEM_LIMIT = 32 * 1024 * 1024
VMEM_MOST = 52 * 1024 * 1024
VMEM_ALL = 63 * 1024 * 1024
VMEM = pl.BlockSpec(memory_space=pltpu.VMEM)
ANY = pl.BlockSpec(memory_space=pl.ANY)


def params(limit=VMEM_LIMIT):
    return pltpu.CompilerParams(vmem_limit_bytes=limit)


def aligned(index, size):
    return pl.ds(pl.multiple_of(index * size, size), size)


def load_kernel(gate_ref, up_ref, down_ref, pair_ref, out_ref, done_ref, sems):
    hidden = gate_ref.shape[2]
    copies = [
        pltpu.make_async_copy(gate_ref.at[0], pair_ref.at[:, :hidden], sems.at[0]),
        pltpu.make_async_copy(up_ref.at[0], pair_ref.at[:, hidden:], sems.at[1]),
        pltpu.make_async_copy(down_ref.at[0], out_ref, sems.at[2]),
    ]
    for copy in copies:
        copy.start()
    for copy in copies:
        copy.wait()
    done_ref[...] = jnp.zeros_like(done_ref)


def load(gate, up, down):
    _, width, hidden = gate.shape
    return pl.pallas_call(
        load_kernel,
        in_specs=[ANY] * 3,
        out_specs=[VMEM] * 3,
        out_shape=[
            pltpu.VMEM((width, 2 * hidden), jnp.bfloat16),
            pltpu.VMEM((hidden, width), jnp.bfloat16),
            pltpu.VMEM((8, LANES), jnp.float32),
        ],
        scratch_shapes=[pltpu.SemaphoreType.DMA((3,))],
        compiler_params=params(VMEM_MOST),
        cost_estimate=pl.CostEstimate(flops=0, bytes_accessed=12 * width * hidden, transcendentals=0),
        name="load",
    )(gate, up, down)


def relay_kernel(block_ref, done_ref, out_ref):
    out_ref[...] = block_ref[:, : out_ref.shape[1]]


def relay(block, cols, done):
    return pl.pallas_call(
        relay_kernel,
        out_shape=jax.ShapeDtypeStruct((block.shape[0], cols), block.dtype),
        compiler_params=params(),
        name="relay",
    )(block, done)


def choices(ids, peers, slots):
    rows = ids[0].shape[1]
    me = lax.axis_index("ep")
    named = []
    for one in ids:
        for k in range(peers):
            hits = [jnp.where(one[p : p + 1, :] == me ^ k, 1.0, 0.0) for p in range(one.shape[0])]
            named.append(sum(hits))
    earlier = lax.broadcasted_iota(jnp.int32, (rows, rows), 0) < lax.broadcasted_iota(jnp.int32, (rows, rows), 1)
    ahead = jnp.dot(
        jnp.concatenate(named, axis=0).astype(jnp.bfloat16),
        jnp.where(earlier, 1.0, 0.0).astype(jnp.bfloat16),
        preferred_element_type=jnp.float32,
    ).astype(jnp.int32)
    slot = lax.broadcasted_iota(jnp.int32, (slots, rows), 0)
    holds = [jnp.where((ahead[i : i + 1, :] == slot) & (row > 0.5), 1.0, 0.0) for i, row in enumerate(named)]
    return [jnp.concatenate(holds[s * peers : (s + 1) * peers], axis=0) for s in range(len(ids))]


def narrow(x):
    return x.astype(jnp.bfloat16)


def product(x, y):
    return jnp.dot(narrow(x), narrow(y), preferred_element_type=jnp.float32)


def named_experts(ids, held, experts):
    rows = ids[0].shape[1]
    flags = []
    for s, one in enumerate(ids):
        lane = lax.broadcasted_iota(jnp.int32, (LANES, rows), 0)
        hits = [jnp.where(one[p : p + 1, :] + s * experts == lane, 1.0, 0.0) for p in range(one.shape[0])]
        flags.append(product(held[s], sum(hits).T))
    return sum(flags)


def pack_kernel(experts, tokens_ref, ids_ref, *refs):
    *out_refs, own_ref, half_ref, held_ref, sems = refs
    quarter = tokens_ref.shape[1] // 4
    half = 2 * quarter
    where = lax.axis_index("et")
    copies = [
        pltpu.make_async_copy(ids_ref, held_ref, sems.at[0]),
        pltpu.make_async_copy(tokens_ref.at[:, aligned(where & 1, quarter)], half_ref.at[:, :quarter], sems.at[1]),
        pltpu.make_async_copy(tokens_ref.at[:, aligned(where & 1 | 2, quarter)], half_ref.at[:, quarter:], sems.at[2]),
    ]
    for copy in copies:
        copy.start()
    copies[0].wait()
    ids = [held_ref[s] for s in range(held_ref.shape[0])]
    slots, peers = out_refs[0].shape[0], 1 + len(out_refs)
    held = choices(ids, peers, slots)
    flags = named_experts(ids, held, experts)
    copies[1].wait()
    copies[2].wait()
    own_ref[...] = half_ref[:, aligned(where >> 1, quarter)]
    picked = product(held[0][slots:], half_ref[...])
    for k, out_ref in enumerate(out_refs):
        out_ref[:, :half] = narrow(picked[k * slots : (k + 1) * slots])
        out_ref[:, half:] = narrow(flags[(k + 1) * slots : (k + 2) * slots])


def pack(tokens, ids, experts, slots):
    rows, width = tokens.shape
    others = lax.axis_size("ep") - 1
    shapes = [(slots, width // 2 + LANES)] * others + [(rows, width // 4)]
    return pl.pallas_call(
        functools.partial(pack_kernel, experts),
        in_specs=[ANY] * 2,
        out_specs=[VMEM] * len(shapes),
        out_shape=[pltpu.VMEM(s, jnp.bfloat16) for s in shapes],
        scratch_shapes=[
            pltpu.VMEM((rows, width // 2), jnp.bfloat16),
            pltpu.VMEM(ids.shape, jnp.int32),
            pltpu.SemaphoreType.DMA((3,)),
        ],
        compiler_params=params(VMEM_ALL),
        name="pack",
    )(tokens, ids)


def own_kernel(experts, tokens_ref, ids_ref, out_ref, flags_ref, *choice_refs):
    ids = [ids_ref[s] for s in range(ids_ref.shape[0])]
    slots = out_ref.shape[0]
    held = choices(ids, choice_refs[0].shape[0] // slots, slots)
    flags_ref[...] = narrow(named_experts(ids, held, experts)[:slots])
    out_ref[...] = narrow(product(held[0][:slots], tokens_ref[...]))
    for s, one in enumerate(held):
        choice_refs[2 * s][...] = narrow(one)
        choice_refs[2 * s + 1][...] = narrow(one.T)


def own_rows(tokens, ids, experts, slots):
    rows, width = tokens.shape
    total = lax.axis_size("ep") * slots
    shapes = [(slots, width), (slots, LANES)] + [(total, rows), (rows, total)] * ids.shape[0]
    return pl.pallas_call(
        functools.partial(own_kernel, experts),
        out_shape=[jax.ShapeDtypeStruct(s, jnp.bfloat16) for s in shapes],
        compiler_params=params(),
        name="own_rows",
    )(tokens, ids)


def front_kernel(layout, section, experts, n_x, *refs):
    x_refs, flag_refs = refs[:n_x], refs[n_x : n_x + len(layout)]
    mod_ref, router_ref, pair_ref, out_ref, normed_ref = refs[n_x + len(layout) :]
    slots = flag_refs[0].shape[0]
    width = normed_ref.shape[1]
    hidden = out_ref.shape[1]
    quarter = width // 4
    et = lax.axis_index("et")

    def part(block, flip):
        index, place = block[flip]
        ref = x_refs[index]
        if place is None:
            cols = aligned((et ^ flip) & (ref.shape[1] // quarter - 1), quarter)
        elif place == "high":
            cols = aligned((et ^ flip) >> 1, quarter)
        else:
            cols = pl.ds(place * quarter, quarter)
        return ref[:, cols].astype(jnp.float32)[:slots]

    blocks = layout
    parts = [jnp.concatenate([part(block, flip) for block in blocks], axis=0) for flip in range(4)]
    total = sum(jnp.sum(xf * xf, axis=1, keepdims=True) for xf in parts)
    scale = lax.rsqrt(total / width + 1e-06)
    for flip, xf in enumerate(parts):
        where = aligned(et ^ flip, quarter)
        normed_ref[:, where] = (
            xf * scale * (1.0 + mod_ref[section, 0:1, where]) + mod_ref[section, 1:2, where]
        ).astype(jnp.bfloat16)
    normed = normed_ref[...]
    both = jnp.dot(normed, pair_ref[...], preferred_element_type=jnp.float32)
    logits = lax.dot_general(
        normed, router_ref[...], (((1,), (1,)), ((), ())), preferred_element_type=jnp.float32
    )
    count = logits.shape[1]
    lane = lax.broadcasted_iota(jnp.int32, logits.shape, 1)
    flags = [f[:, f.shape[1] - LANES :].astype(jnp.float32) for f in flag_refs]
    flags = jnp.concatenate(flags, axis=0)[:, section * experts : section * experts + count]
    chosen = jnp.where(flags > 0.5, jax.nn.sigmoid(logits), 0.0)
    mine = jnp.sum(jnp.where(lane == lax.axis_index("ep"), chosen, 0.0), axis=1, keepdims=True)
    used = jnp.max(flags, axis=1, keepdims=True) > 0.5
    weight = jnp.where(used, mine / jnp.sum(chosen, axis=1, keepdims=True), 0.0)
    gate, upper = both[:, :hidden], both[:, hidden:]
    units = jnp.where(used, gate / (1.0 + jnp.exp(-gate)) * upper * weight, 0.0)
    out_ref[...] = units.astype(jnp.bfloat16)


def front(blocks, flags, section, mod, router, pair):
    width, hidden = pair.shape[0], pair.shape[1] // 2
    rows = sum(f.shape[0] for f in flags)
    experts = router.shape[0]
    xs, layout = [], []
    for block in blocks:
        layout.append([])
        for x, place in block:
            known = [i for i, other in enumerate(xs) if other is x]
            layout[-1].append((known[0] if known else len(xs), place))
            if not known:
                xs.append(x)
    return pl.pallas_call(
        functools.partial(front_kernel, layout, section, experts, len(xs)),
        in_specs=[VMEM] * (len(xs) + len(flags) + 3),
        scratch_shapes=[pltpu.VMEM((rows, width), jnp.bfloat16)],
        out_shape=jax.ShapeDtypeStruct((rows, hidden), jnp.bfloat16),
        compiler_params=params(),
        cost_estimate=pl.CostEstimate(
            flops=4 * rows * width * hidden, bytes_accessed=4 * width * hidden, transcendentals=0
        ),
        name="front",
    )(*xs, *flags, mod, router, pair)


def down_kernel(flip, n_adds, hidden_ref, down_ref, *refs):
    adds, outs = refs[:n_adds], refs[n_adds:]
    quarter = down_ref.shape[1] // 4
    weights = down_ref[:, aligned(lax.axis_index("et") ^ flip, quarter)]
    product = jnp.dot(hidden_ref[...], weights, preferred_element_type=jnp.float32)
    rows = 0
    for ref in adds:
        if ref.shape[0] == product.shape[0]:
            product += ref[...].astype(jnp.float32)
    for out in outs:
        out[:, :quarter] = product[rows : rows + out.shape[0]].astype(out.dtype)
        rows += out.shape[0]
        if out.shape[1] > quarter:
            out[:, quarter:] = adds[-1][...]


def down(hidden, w_down, flip, outs, adds=()):
    units, width = w_down.shape
    rows, quarter = hidden.shape[0], width // 4
    return pl.pallas_call(
        functools.partial(down_kernel, flip, len(adds)),
        in_specs=[VMEM] * (2 + len(adds)),
        out_shape=[jax.ShapeDtypeStruct((r, quarter * wide), t) for r, wide, t in outs],
        compiler_params=params(),
        cost_estimate=pl.CostEstimate(
            flops=2 * rows * units * quarter, bytes_accessed=2 * units * quarter, transcendentals=0
        ),
        name="down",
    )(hidden, w_down, *adds)


def add_kernel(keep_ref, came_ref, *outs):
    total = keep_ref[...] + came_ref[...].astype(jnp.float32)
    rows = outs[0].shape[0]
    for k, out in enumerate(outs):
        out[...] = total[k * rows : (k + 1) * rows].astype(out.dtype)


def add(keep, came, count):
    shape = (keep.shape[0] // count, keep.shape[1])
    return pl.pallas_call(
        add_kernel,
        out_shape=[jax.ShapeDtypeStruct(shape, jnp.bfloat16)] * count,
        compiler_params=params(),
        name="add",
    )(keep, came)


def fold_kernel(back_ref, mine_ref, came_ref, out_ref):
    cols = mine_ref.shape[1]
    rows = [mine_ref[...].astype(jnp.float32), came_ref[:, cols:].astype(jnp.float32)]
    rows = jnp.concatenate(rows, axis=0)
    out_ref[...] = narrow(product(back_ref[:, : rows.shape[0]], rows))


def fold(back, mine, came):
    return pl.pallas_call(
        fold_kernel,
        out_shape=jax.ShapeDtypeStruct((back.shape[0], mine.shape[1]), jnp.bfloat16),
        compiler_params=params(),
        name="fold",
    )(back, mine, came)


def move_kernel(n_came, last, own_ref, back_ref, pick_ref, cross_ref, *refs):
    came, outs = refs[:n_came], refs[n_came:]
    cols = own_ref.shape[1]
    rows = [ref[:, :cols].astype(jnp.float32) for ref in came]
    velocity = product(back_ref[...], jnp.concatenate(rows, axis=0)) + cross_ref[...].astype(jnp.float32)
    moved = narrow(own_ref[...].astype(jnp.float32) - 0.5 * velocity)
    outs[0][...] = moved
    if last:
        outs[1][...] = narrow(velocity)
    else:
        picked, at = product(pick_ref[...], moved), 0
        for out in outs[1:]:
            out[...] = narrow(picked[at : at + out.shape[0]])
            at += out.shape[0]


def move(own, back, pick, cross, came, last):
    slots = came[0].shape[0]
    counts = [2] + [1] * (len(came) - 2)
    shapes = [own.shape] + ([own.shape] if last else [(slots * c, own.shape[1]) for c in counts])
    return pl.pallas_call(
        functools.partial(move_kernel, len(came), last),
        out_shape=[jax.ShapeDtypeStruct(s, jnp.bfloat16) for s in shapes],
        compiler_params=params(),
        name="move",
    )(own, back, pick, cross, *came)


def sum_back(hidden, w_down, own, back, pick, last):
    peers = lax.axis_size("ep")
    slots = hidden.shape[0] // peers
    far_rows = slots * (peers - 2)
    narrow_type, wide_type = jnp.bfloat16, jnp.float32
    whole = [(hidden.shape[0], 1, narrow_type)]
    far = swap(down(hidden, w_down, 3, whole)[0], "et", 1)
    near = swap(down(hidden, w_down, 1, whole)[0], "et", 1)
    cuts = [(slots, 1, narrow_type), (slots, 1, narrow_type), (far_rows, 1, narrow_type)]
    own_cross, next_cross, sent = down(hidden, w_down, 2, cuts, (far,))
    cuts = [(slots, 1, wide_type), (slots, 2, narrow_type), (far_rows, 1, wide_type)]
    kept, beside, kept_far = down(hidden, w_down, 0, cuts, (near, next_cross))
    came = swap(beside, "ep", 1)
    blocks = add(kept_far, swap(sent, "et", 2), peers - 2)
    cross = swap(fold(back, own_cross, came), "et", 2)
    blocks = [kept, came] + [swap(b, "ep", k + 2) for k, b in enumerate(blocks)]
    return move(own, back, pick, cross, blocks, last)


def spread(block, place=0):
    side = swap(block, "et", 2)
    near, far = swap(block, "et", 1), swap(side, "et", 1)
    return [(block, place), (near, place), (side, place), (far, place)]


def join_kernel(block_ref, side_ref, out_ref):
    rows, cols = out_ref.shape[0], block_ref.shape[1]
    out_ref[:, :cols] = narrow(block_ref[...].astype(jnp.float32)[rows:])
    out_ref[:, cols:] = narrow(side_ref[...].astype(jnp.float32)[rows:])


def join(block, side):
    return pl.pallas_call(
        join_kernel,
        out_shape=jax.ShapeDtypeStruct((block.shape[0] // 2, 2 * block.shape[1]), block.dtype),
        compiler_params=params(),
        name="join",
    )(block, side)


def dense_body(tokens, modulation, router, gate_weight, up_weight, down_weight, expert_ids):
    rows, width = tokens.shape
    half = width // 2
    router = router.T
    experts = router.shape[0]
    slots = 3 * rows * expert_ids.shape[2] // (2 * experts)
    ids = expert_ids.transpose(0, 2, 1)

    *packed, own = pack(tokens, ids, experts, slots)
    pair, w_down, done = load(gate_weight, up_weight, down_weight)
    mine, flags, *choice = own_rows(tokens, ids, experts, slots)
    pick, back = choice[2], choice[1::2]
    flags = [flags] + [swap(p, "ep", k + 1) for k, p in enumerate(packed)]
    blocks = [[(mine, None)] * 4]
    for f in flags[1:]:
        f = relay(f, half, done)
        other = swap(f, "et", 1)
        blocks.append([(f, "high"), (other, "high")] * 2)
    hidden = front(blocks, flags, 0, modulation, router, pair)
    own, near, *far = sum_back(hidden, w_down, own, back[0], pick, False)

    first = spread(near)
    beside = swap(join(near, first[2][0]), "ep", 1)
    other = swap(beside, "et", 1)
    blocks = [first, [(beside, 0), (other, 0), (beside, 1), (other, 1)]]
    blocks += [spread(swap(b, "ep", k + 2)) for k, b in enumerate(far)]
    hidden = front(blocks, flags, 1, modulation, router, pair)
    return tuple(sum_back(hidden, w_down, own, back[1], pick, True))


def solution(mesh):
    in_specs = (
        P(("grp", "ep"), None),
        P(),
        P(),
        P("ep", None, "et"),
        P("ep", None, "et"),
        P("ep", "et", None),
        P(None, ("grp", "ep"), None),
    )
    out_specs = (P(("grp", "ep"), "et"), P(("grp", "ep"), "et"))

    def body(*args):
        experts, picks = args[2].shape[1], args[6].shape[2]
        peers = lax.axis_size("ep")
        fits = lax.axis_size("et") == 4 and peers >= 4 and peers & (peers - 1) == 0
        chosen = dense_body if fits and experts <= 2 * picks else routed_body
        return chosen(*args)

    return jax.shard_map(body, mesh=mesh, in_specs=in_specs, out_specs=out_specs, check_vma=False)
```

```python
import functools

import jax
import jax.numpy as jnp
from jax import lax
from jax.experimental import pallas as pl
from jax.experimental.pallas import tpu as pltpu
from jax.sharding import PartitionSpec as P


def normalize(x, mod):
    xf = x.astype(jnp.float32)
    scaled = xf * lax.rsqrt(jnp.mean(xf * xf, axis=-1, keepdims=True) + 1e-06)
    return (scaled * (1.0 + mod[0]) + mod[1]).astype(jnp.bfloat16)


def routed_section(x_full, x_cols, mod, ids, router, gate_weight, up_weight, down_weight):
    tok_rows = x_full.shape[0]
    width = x_full.shape[1]
    experts = router.shape[1]
    picks = ids.shape[1]
    n_peers = lax.axis_size("ep")
    quarter = width // lax.axis_size("et")
    slot_count = 3 * tok_rows * picks // (2 * experts)
    normed = normalize(x_full, mod)
    logits = jnp.dot(normed, router, preferred_element_type=jnp.float32)
    chosen = jax.nn.sigmoid(jnp.take_along_axis(logits, ids, axis=1))
    weight = chosen / jnp.sum(chosen, axis=1, keepdims=True)
    flat_e = ids.reshape(-1)
    onehot = (flat_e[:, None] == jnp.arange(experts, dtype=jnp.int32)).astype(jnp.int32)
    counted = jnp.cumsum(onehot, axis=0)
    slot = jnp.sum(onehot * (counted - 1), axis=1)
    repeated = jnp.repeat(normed, picks, axis=0)
    outbox = jnp.zeros((experts, slot_count, width), jnp.bfloat16).at[flat_e, slot].set(repeated)
    arrived = lax.all_to_all(outbox, "ep", split_axis=0, concat_axis=0, tiled=True)
    in_rows = arrived.reshape(n_peers * slot_count, width)
    gate = jnp.dot(in_rows, gate_weight[0], preferred_element_type=jnp.float32)
    upper = jnp.dot(in_rows, up_weight[0], preferred_element_type=jnp.float32)
    hidden = (jax.nn.silu(gate) * upper).astype(jnp.bfloat16)
    partial_out = jnp.dot(hidden, down_weight[0], preferred_element_type=jnp.float32)
    summed = lax.psum_scatter(
        partial_out.astype(jnp.bfloat16), "et", scatter_dimension=1, tiled=True
    )
    returned = lax.all_to_all(
        summed.reshape(n_peers, slot_count, quarter), "ep", split_axis=0, concat_axis=0, tiled=True
    )
    picked = returned[flat_e, slot].astype(jnp.float32).reshape(tok_rows, picks, quarter)
    velocity = jnp.sum(picked * weight[:, :, None], axis=1)
    moved = (x_cols.astype(jnp.float32) - 0.5 * velocity).astype(jnp.bfloat16)
    return (moved, velocity)


def routed_body(tokens, modulation, router, gate_weight, up_weight, down_weight, expert_ids):
    quarter = tokens.shape[1] // lax.axis_size("et")
    column_start = lax.axis_index("et") * quarter
    cols = lax.dynamic_slice_in_dim(tokens, column_start, quarter, 1)
    weights = (router, gate_weight, up_weight, down_weight)
    first, _ = routed_section(tokens, cols, modulation[0], expert_ids[0], *weights)
    full = lax.all_gather(first, "et", axis=1, tiled=True)
    second, velocity = routed_section(full, first, modulation[1], expert_ids[1], *weights)
    return (second, velocity.astype(jnp.bfloat16))


def swap(x, axis, bit):
    size = lax.axis_size(axis)
    return lax.ppermute(x, axis, [(i, i ^ bit) for i in range(size)])


LANES = 128
VMEM_LIMIT = 32 * 1024 * 1024
VMEM_MOST = 52 * 1024 * 1024
VMEM_ALL = 63 * 1024 * 1024
VMEM = pl.BlockSpec(memory_space=pltpu.VMEM)
ANY = pl.BlockSpec(memory_space=pl.ANY)


def params(limit=VMEM_LIMIT):
    return pltpu.CompilerParams(vmem_limit_bytes=limit)


def aligned(index, size):
    return pl.ds(pl.multiple_of(index * size, size), size)


def load_kernel(gate_ref, up_ref, down_ref, pair_ref, out_ref, done_ref, sems):
    hidden = gate_ref.shape[2]
    copies = [
        pltpu.make_async_copy(gate_ref.at[0], pair_ref.at[:, :hidden], sems.at[0]),
        pltpu.make_async_copy(up_ref.at[0], pair_ref.at[:, hidden:], sems.at[1]),
        pltpu.make_async_copy(down_ref.at[0], out_ref, sems.at[2]),
    ]
    for copy in copies:
        copy.start()
    for copy in copies:
        copy.wait()
    done_ref[...] = jnp.zeros_like(done_ref)


def load(gate, up, down):
    _, width, hidden = gate.shape
    return pl.pallas_call(
        load_kernel,
        in_specs=[ANY] * 3,
        out_specs=[VMEM] * 3,
        out_shape=[
            pltpu.VMEM((width, 2 * hidden), jnp.bfloat16),
            pltpu.VMEM((hidden, width), jnp.bfloat16),
            pltpu.VMEM((8, LANES), jnp.float32),
        ],
        scratch_shapes=[pltpu.SemaphoreType.DMA((3,))],
        compiler_params=params(VMEM_MOST),
        cost_estimate=pl.CostEstimate(flops=0, bytes_accessed=12 * width * hidden, transcendentals=0),
        name="load",
    )(gate, up, down)


def relay_kernel(block_ref, done_ref, out_ref):
    out_ref[...] = block_ref[:, : out_ref.shape[1]]


def relay(block, cols, done):
    return pl.pallas_call(
        relay_kernel,
        out_shape=jax.ShapeDtypeStruct((block.shape[0], cols), block.dtype),
        compiler_params=params(),
        name="relay",
    )(block, done)


def choices(ids, peers, slots):
    rows = ids[0].shape[1]
    me = lax.axis_index("ep")
    named = []
    for one in ids:
        for k in range(peers):
            hits = [jnp.where(one[p : p + 1, :] == me ^ k, 1.0, 0.0) for p in range(one.shape[0])]
            named.append(sum(hits))
    earlier = lax.broadcasted_iota(jnp.int32, (rows, rows), 0) < lax.broadcasted_iota(jnp.int32, (rows, rows), 1)
    ahead = jnp.dot(
        jnp.concatenate(named, axis=0).astype(jnp.bfloat16),
        jnp.where(earlier, 1.0, 0.0).astype(jnp.bfloat16),
        preferred_element_type=jnp.float32,
    ).astype(jnp.int32)
    slot = lax.broadcasted_iota(jnp.int32, (slots, rows), 0)
    holds = [jnp.where((ahead[i : i + 1, :] == slot) & (row > 0.5), 1.0, 0.0) for i, row in enumerate(named)]
    return [jnp.concatenate(holds[s * peers : (s + 1) * peers], axis=0) for s in range(len(ids))]


def narrow(x):
    return x.astype(jnp.bfloat16)


def product(x, y):
    return jnp.dot(narrow(x), narrow(y), preferred_element_type=jnp.float32)


def named_experts(ids, held, experts):
    rows = ids[0].shape[1]
    flags = []
    for s, one in enumerate(ids):
        lane = lax.broadcasted_iota(jnp.int32, (LANES, rows), 0)
        hits = [jnp.where(one[p : p + 1, :] + s * experts == lane, 1.0, 0.0) for p in range(one.shape[0])]
        flags.append(product(held[s], sum(hits).T))
    return sum(flags)


def pack_kernel(experts, tokens_ref, ids_ref, *refs):
    *out_refs, own_ref, half_ref, held_ref, sems = refs
    quarter = tokens_ref.shape[1] // 4
    half = 2 * quarter
    where = lax.axis_index("et")
    copies = [
        pltpu.make_async_copy(ids_ref, held_ref, sems.at[0]),
        pltpu.make_async_copy(tokens_ref.at[:, aligned(where & 1, quarter)], half_ref.at[:, :quarter], sems.at[1]),
        pltpu.make_async_copy(tokens_ref.at[:, aligned(where & 1 | 2, quarter)], half_ref.at[:, quarter:], sems.at[2]),
    ]
    for copy in copies:
        copy.start()
    copies[0].wait()
    ids = [held_ref[s] for s in range(held_ref.shape[0])]
    slots, peers = out_refs[0].shape[0], 1 + len(out_refs)
    held = choices(ids, peers, slots)
    flags = named_experts(ids, held, experts)
    copies[1].wait()
    copies[2].wait()
    own_ref[...] = half_ref[:, aligned(where >> 1, quarter)]
    picked = product(held[0][slots:], half_ref[...])
    for k, out_ref in enumerate(out_refs):
        out_ref[:, :half] = narrow(picked[k * slots : (k + 1) * slots])
        out_ref[:, half:] = narrow(flags[(k + 1) * slots : (k + 2) * slots])


def pack(tokens, ids, experts, slots):
    rows, width = tokens.shape
    others = lax.axis_size("ep") - 1
    shapes = [(slots, width // 2 + LANES)] * others + [(rows, width // 4)]
    return pl.pallas_call(
        functools.partial(pack_kernel, experts),
        in_specs=[ANY] * 2,
        out_specs=[VMEM] * len(shapes),
        out_shape=[pltpu.VMEM(s, jnp.bfloat16) for s in shapes],
        scratch_shapes=[
            pltpu.VMEM((rows, width // 2), jnp.bfloat16),
            pltpu.VMEM(ids.shape, jnp.int32),
            pltpu.SemaphoreType.DMA((3,)),
        ],
        compiler_params=params(VMEM_ALL),
        name="pack",
    )(tokens, ids)


def own_kernel(experts, tokens_ref, ids_ref, out_ref, flags_ref, *choice_refs):
    ids = [ids_ref[s] for s in range(ids_ref.shape[0])]
    slots = out_ref.shape[0]
    held = choices(ids, choice_refs[0].shape[0] // slots, slots)
    flags_ref[...] = narrow(named_experts(ids, held, experts)[:slots])
    out_ref[...] = narrow(product(held[0][:slots], tokens_ref[...]))
    for s, one in enumerate(held):
        choice_refs[2 * s][...] = narrow(one)
        choice_refs[2 * s + 1][...] = narrow(one.T)


def own_rows(tokens, ids, experts, slots):
    rows, width = tokens.shape
    total = lax.axis_size("ep") * slots
    shapes = [(slots, width), (slots, LANES)] + [(total, rows), (rows, total)] * ids.shape[0]
    return pl.pallas_call(
        functools.partial(own_kernel, experts),
        out_shape=[jax.ShapeDtypeStruct(s, jnp.bfloat16) for s in shapes],
        compiler_params=params(),
        name="own_rows",
    )(tokens, ids)


def front_kernel(layout, section, experts, n_x, *refs):
    x_refs, flag_refs = refs[:n_x], refs[n_x : n_x + len(layout)]
    mod_ref, router_ref, pair_ref, out_ref, normed_ref = refs[n_x + len(layout) :]
    slots = flag_refs[0].shape[0]
    width = normed_ref.shape[1]
    hidden = out_ref.shape[1]
    quarter = width // 4
    et = lax.axis_index("et")

    def part(block, flip):
        index, place = block[flip]
        ref = x_refs[index]
        if place is None:
            cols = aligned((et ^ flip) & (ref.shape[1] // quarter - 1), quarter)
        elif place == "high":
            cols = aligned((et ^ flip) >> 1, quarter)
        else:
            cols = pl.ds(place * quarter, quarter)
        return ref[:, cols].astype(jnp.float32)[:slots]

    blocks = layout
    parts = [jnp.concatenate([part(block, flip) for block in blocks], axis=0) for flip in range(4)]
    total = sum(jnp.sum(xf * xf, axis=1, keepdims=True) for xf in parts)
    scale = lax.rsqrt(total / width + 1e-06)
    for flip, xf in enumerate(parts):
        where = aligned(et ^ flip, quarter)
        normed_ref[:, where] = (
            xf * scale * (1.0 + mod_ref[section, 0:1, where]) + mod_ref[section, 1:2, where]
        ).astype(jnp.bfloat16)
    normed = normed_ref[...]
    both = jnp.dot(normed, pair_ref[...], preferred_element_type=jnp.float32)
    logits = lax.dot_general(
        normed, router_ref[...], (((1,), (1,)), ((), ())), preferred_element_type=jnp.float32
    )
    count = logits.shape[1]
    lane = lax.broadcasted_iota(jnp.int32, logits.shape, 1)
    flags = [f[:, f.shape[1] - LANES :].astype(jnp.float32) for f in flag_refs]
    flags = jnp.concatenate(flags, axis=0)[:, section * experts : section * experts + count]
    chosen = jnp.where(flags > 0.5, jax.nn.sigmoid(logits), 0.0)
    mine = jnp.sum(jnp.where(lane == lax.axis_index("ep"), chosen, 0.0), axis=1, keepdims=True)
    used = jnp.max(flags, axis=1, keepdims=True) > 0.5
    weight = jnp.where(used, mine / jnp.sum(chosen, axis=1, keepdims=True), 0.0)
    gate, upper = both[:, :hidden], both[:, hidden:]
    units = jnp.where(used, gate / (1.0 + jnp.exp(-gate)) * upper * weight, 0.0)
    out_ref[...] = units.astype(jnp.bfloat16)


def front(blocks, flags, section, mod, router, pair):
    width, hidden = pair.shape[0], pair.shape[1] // 2
    rows = sum(f.shape[0] for f in flags)
    experts = router.shape[0]
    xs, layout = [], []
    for block in blocks:
        layout.append([])
        for x, place in block:
            known = [i for i, other in enumerate(xs) if other is x]
            layout[-1].append((known[0] if known else len(xs), place))
            if not known:
                xs.append(x)
    return pl.pallas_call(
        functools.partial(front_kernel, layout, section, experts, len(xs)),
        in_specs=[VMEM] * (len(xs) + len(flags) + 3),
        scratch_shapes=[pltpu.VMEM((rows, width), jnp.bfloat16)],
        out_shape=jax.ShapeDtypeStruct((rows, hidden), jnp.bfloat16),
        compiler_params=params(),
        cost_estimate=pl.CostEstimate(
            flops=4 * rows * width * hidden, bytes_accessed=4 * width * hidden, transcendentals=0
        ),
        name="front",
    )(*xs, *flags, mod, router, pair)


def down_kernel(flip, n_adds, hidden_ref, down_ref, *refs):
    adds, outs = refs[:n_adds], refs[n_adds:]
    quarter = down_ref.shape[1] // 4
    weights = down_ref[:, aligned(lax.axis_index("et") ^ flip, quarter)]
    product = jnp.dot(hidden_ref[...], weights, preferred_element_type=jnp.float32)
    rows = 0
    for ref in adds:
        if ref.shape[0] == product.shape[0]:
            product += ref[...].astype(jnp.float32)
    for out in outs:
        out[:, :quarter] = product[rows : rows + out.shape[0]].astype(out.dtype)
        rows += out.shape[0]
        if out.shape[1] > quarter:
            out[:, quarter:] = adds[-1][...]


def down(hidden, w_down, flip, outs, adds=()):
    units, width = w_down.shape
    rows, quarter = hidden.shape[0], width // 4
    return pl.pallas_call(
        functools.partial(down_kernel, flip, len(adds)),
        in_specs=[VMEM] * (2 + len(adds)),
        out_shape=[jax.ShapeDtypeStruct((r, quarter * wide), t) for r, wide, t in outs],
        compiler_params=params(),
        cost_estimate=pl.CostEstimate(
            flops=2 * rows * units * quarter, bytes_accessed=2 * units * quarter, transcendentals=0
        ),
        name="down",
    )(hidden, w_down, *adds)


def add_kernel(keep_ref, came_ref, *outs):
    total = keep_ref[...] + came_ref[...].astype(jnp.float32)
    rows = outs[0].shape[0]
    for k, out in enumerate(outs):
        out[...] = total[k * rows : (k + 1) * rows].astype(out.dtype)


def add(keep, came, count):
    shape = (keep.shape[0] // count, keep.shape[1])
    return pl.pallas_call(
        add_kernel,
        out_shape=[jax.ShapeDtypeStruct(shape, jnp.bfloat16)] * count,
        compiler_params=params(),
        name="add",
    )(keep, came)


def fold_kernel(back_ref, mine_ref, came_ref, after_ref, out_ref):
    cols = mine_ref.shape[1]
    rows = [mine_ref[...].astype(jnp.float32), came_ref[:, cols:].astype(jnp.float32)]
    rows = jnp.concatenate(rows, axis=0)
    out_ref[...] = narrow(product(back_ref[:, : rows.shape[0]], rows))


def fold(back, mine, came, after):
    return pl.pallas_call(
        fold_kernel,
        out_shape=jax.ShapeDtypeStruct((back.shape[0], mine.shape[1]), jnp.bfloat16),
        compiler_params=params(),
        name="fold",
    )(back, mine, came, after)


def move_kernel(n_came, last, own_ref, back_ref, pick_ref, cross_ref, *refs):
    came, outs = refs[:n_came], refs[n_came:]
    cols = own_ref.shape[1]
    rows = [ref[:, :cols].astype(jnp.float32) for ref in came]
    velocity = product(back_ref[...], jnp.concatenate(rows, axis=0)) + cross_ref[...].astype(jnp.float32)
    moved = narrow(own_ref[...].astype(jnp.float32) - 0.5 * velocity)
    outs[0][...] = moved
    if last:
        outs[1][...] = narrow(velocity)
    else:
        picked, at = product(pick_ref[...], moved), 0
        for out in outs[1:]:
            out[...] = narrow(picked[at : at + out.shape[0]])
            at += out.shape[0]


def move(own, back, pick, cross, came, last):
    slots = came[0].shape[0]
    shapes = [own.shape] + ([own.shape] if last else [(slots, own.shape[1])] * len(came))
    return pl.pallas_call(
        functools.partial(move_kernel, len(came), last),
        out_shape=[jax.ShapeDtypeStruct(s, jnp.bfloat16) for s in shapes],
        compiler_params=params(),
        name="move",
    )(own, back, pick, cross, *came)


def sum_back(hidden, w_down, own, back, pick, last):
    peers = lax.axis_size("ep")
    slots = hidden.shape[0] // peers
    far_rows = slots * (peers - 2)
    narrow_type, wide_type = jnp.bfloat16, jnp.float32
    whole = [(hidden.shape[0], 1, narrow_type)]
    far = swap(down(hidden, w_down, 3, whole)[0], "et", 1)
    near = swap(down(hidden, w_down, 1, whole)[0], "et", 1)
    cuts = [(slots, 1, narrow_type), (slots, 1, narrow_type), (far_rows, 1, narrow_type)]
    own_cross, next_cross, sent = down(hidden, w_down, 2, cuts, (far,))
    cuts = [(slots, 1, wide_type), (slots, 2, narrow_type), (far_rows, 1, wide_type)]
    kept, beside, kept_far = down(hidden, w_down, 0, cuts, (near, next_cross))
    came = swap(beside, "ep", 1)
    blocks = add(kept_far, swap(sent, "et", 2), peers - 2)
    cross = swap(fold(back, own_cross, came, blocks[-1]), "et", 2)
    blocks = [kept, came] + [swap(b, "ep", k + 2) for k, b in enumerate(blocks)]
    return move(own, back, pick, cross, blocks, last)


def spread(block, place=0):
    side = swap(block, "et", 2)
    near, far = swap(block, "et", 1), swap(side, "et", 1)
    return [(block, place), (near, place), (side, place), (far, place)]


def dense_body(tokens, modulation, router, gate_weight, up_weight, down_weight, expert_ids):
    rows, width = tokens.shape
    half = width // 2
    router = router.T
    experts = router.shape[0]
    slots = 3 * rows * expert_ids.shape[2] // (2 * experts)
    ids = expert_ids.transpose(0, 2, 1)

    *packed, own = pack(tokens, ids, experts, slots)
    pair, w_down, done = load(gate_weight, up_weight, down_weight)
    mine, flags, *choice = own_rows(tokens, ids, experts, slots)
    pick, back = choice[2], choice[1::2]
    flags = [flags] + [swap(p, "ep", k + 1) for k, p in enumerate(packed)]
    blocks = [[(mine, None)] * 4]
    for f in flags[1:]:
        f = relay(f, half, done)
        other = swap(f, "et", 1)
        blocks.append([(f, "high"), (other, "high")] * 2)
    hidden = front(blocks, flags, 0, modulation, router, pair)
    own, *sent = sum_back(hidden, w_down, own, back[0], pick, False)

    blocks = [spread(swap(b, "ep", k) if k else b) for k, b in enumerate(sent)]
    hidden = front(blocks, flags, 1, modulation, router, pair)
    return tuple(sum_back(hidden, w_down, own, back[1], pick, True))


def solution(mesh):
    in_specs = (
        P(("grp", "ep"), None),
        P(),
        P(),
        P("ep", None, "et"),
        P("ep", None, "et"),
        P("ep", "et", None),
        P(None, ("grp", "ep"), None),
    )
    out_specs = (P(("grp", "ep"), "et"), P(("grp", "ep"), "et"))

    def body(*args):
        experts, picks = args[2].shape[1], args[6].shape[2]
        peers = lax.axis_size("ep")
        fits = lax.axis_size("et") == 4 and peers >= 4 and peers & (peers - 1) == 0
        chosen = dense_body if fits and experts <= 2 * picks else routed_body
        return chosen(*args)

    return jax.shard_map(body, mesh=mesh, in_specs=in_specs, out_specs=out_specs, check_vma=False)
```

```python
import functools

import jax
import jax.numpy as jnp
from jax import lax
from jax.experimental import pallas as pl
from jax.experimental.pallas import tpu as pltpu
from jax.sharding import PartitionSpec as P


def normalize(x, mod):
    xf = x.astype(jnp.float32)
    scaled = xf * lax.rsqrt(jnp.mean(xf * xf, axis=-1, keepdims=True) + 1e-06)
    return (scaled * (1.0 + mod[0]) + mod[1]).astype(jnp.bfloat16)


def routed_section(x_full, x_cols, mod, ids, router, gate_weight, up_weight, down_weight):
    tok_rows = x_full.shape[0]
    width = x_full.shape[1]
    experts = router.shape[1]
    picks = ids.shape[1]
    n_peers = lax.axis_size("ep")
    quarter = width // lax.axis_size("et")
    slot_count = 3 * tok_rows * picks // (2 * experts)
    normed = normalize(x_full, mod)
    logits = jnp.dot(normed, router, preferred_element_type=jnp.float32)
    chosen = jax.nn.sigmoid(jnp.take_along_axis(logits, ids, axis=1))
    weight = chosen / jnp.sum(chosen, axis=1, keepdims=True)
    flat_e = ids.reshape(-1)
    onehot = (flat_e[:, None] == jnp.arange(experts, dtype=jnp.int32)).astype(jnp.int32)
    counted = jnp.cumsum(onehot, axis=0)
    slot = jnp.sum(onehot * (counted - 1), axis=1)
    repeated = jnp.repeat(normed, picks, axis=0)
    outbox = jnp.zeros((experts, slot_count, width), jnp.bfloat16).at[flat_e, slot].set(repeated)
    arrived = lax.all_to_all(outbox, "ep", split_axis=0, concat_axis=0, tiled=True)
    in_rows = arrived.reshape(n_peers * slot_count, width)
    gate = jnp.dot(in_rows, gate_weight[0], preferred_element_type=jnp.float32)
    upper = jnp.dot(in_rows, up_weight[0], preferred_element_type=jnp.float32)
    hidden = (jax.nn.silu(gate) * upper).astype(jnp.bfloat16)
    partial_out = jnp.dot(hidden, down_weight[0], preferred_element_type=jnp.float32)
    summed = lax.psum_scatter(
        partial_out.astype(jnp.bfloat16), "et", scatter_dimension=1, tiled=True
    )
    returned = lax.all_to_all(
        summed.reshape(n_peers, slot_count, quarter), "ep", split_axis=0, concat_axis=0, tiled=True
    )
    picked = returned[flat_e, slot].astype(jnp.float32).reshape(tok_rows, picks, quarter)
    velocity = jnp.sum(picked * weight[:, :, None], axis=1)
    moved = (x_cols.astype(jnp.float32) - 0.5 * velocity).astype(jnp.bfloat16)
    return (moved, velocity)


def routed_body(tokens, modulation, router, gate_weight, up_weight, down_weight, expert_ids):
    quarter = tokens.shape[1] // lax.axis_size("et")
    column_start = lax.axis_index("et") * quarter
    cols = lax.dynamic_slice_in_dim(tokens, column_start, quarter, 1)
    weights = (router, gate_weight, up_weight, down_weight)
    first, _ = routed_section(tokens, cols, modulation[0], expert_ids[0], *weights)
    full = lax.all_gather(first, "et", axis=1, tiled=True)
    second, velocity = routed_section(full, first, modulation[1], expert_ids[1], *weights)
    return (second, velocity.astype(jnp.bfloat16))


def swap(x, axis, bit):
    size = lax.axis_size(axis)
    return lax.ppermute(x, axis, [(i, i ^ bit) for i in range(size)])


LANES = 128
VMEM_LIMIT = 32 * 1024 * 1024
VMEM_MOST = 52 * 1024 * 1024
VMEM_ALL = 63 * 1024 * 1024
VMEM = pl.BlockSpec(memory_space=pltpu.VMEM)
ANY = pl.BlockSpec(memory_space=pl.ANY)


def params(limit=VMEM_LIMIT):
    return pltpu.CompilerParams(vmem_limit_bytes=limit)


def aligned(index, size):
    return pl.ds(pl.multiple_of(index * size, size), size)


def load_kernel(gate_ref, up_ref, down_ref, pair_ref, out_ref, done_ref, sems):
    hidden = gate_ref.shape[2]
    copies = [
        pltpu.make_async_copy(gate_ref.at[0], pair_ref.at[:, :hidden], sems.at[0]),
        pltpu.make_async_copy(up_ref.at[0], pair_ref.at[:, hidden:], sems.at[1]),
        pltpu.make_async_copy(down_ref.at[0], out_ref, sems.at[2]),
    ]
    for copy in copies:
        copy.start()
    for copy in copies:
        copy.wait()
    done_ref[...] = jnp.zeros_like(done_ref)


def load(gate, up, down):
    _, width, hidden = gate.shape
    return pl.pallas_call(
        load_kernel,
        in_specs=[ANY] * 3,
        out_specs=[VMEM] * 3,
        out_shape=[
            pltpu.VMEM((width, 2 * hidden), jnp.bfloat16),
            pltpu.VMEM((hidden, width), jnp.bfloat16),
            pltpu.VMEM((8, LANES), jnp.float32),
        ],
        scratch_shapes=[pltpu.SemaphoreType.DMA((3,))],
        compiler_params=params(VMEM_MOST),
        cost_estimate=pl.CostEstimate(flops=0, bytes_accessed=12 * width * hidden, transcendentals=0),
        name="load",
    )(gate, up, down)


def relay_kernel(block_ref, done_ref, out_ref):
    out_ref[...] = block_ref[:, : out_ref.shape[1]]


def relay(block, cols, done):
    return pl.pallas_call(
        relay_kernel,
        out_shape=jax.ShapeDtypeStruct((block.shape[0], cols), block.dtype),
        compiler_params=params(),
        name="relay",
    )(block, done)


def choices(ids, peers, slots):
    rows = ids[0].shape[1]
    me = lax.axis_index("ep")
    named = []
    for one in ids:
        for k in range(peers):
            hits = [jnp.where(one[p : p + 1, :] == me ^ k, 1.0, 0.0) for p in range(one.shape[0])]
            named.append(sum(hits))
    earlier = lax.broadcasted_iota(jnp.int32, (rows, rows), 0) < lax.broadcasted_iota(jnp.int32, (rows, rows), 1)
    ahead = jnp.dot(
        jnp.concatenate(named, axis=0).astype(jnp.bfloat16),
        jnp.where(earlier, 1.0, 0.0).astype(jnp.bfloat16),
        preferred_element_type=jnp.float32,
    ).astype(jnp.int32)
    slot = lax.broadcasted_iota(jnp.int32, (slots, rows), 0)
    holds = [jnp.where((ahead[i : i + 1, :] == slot) & (row > 0.5), 1.0, 0.0) for i, row in enumerate(named)]
    return [jnp.concatenate(holds[s * peers : (s + 1) * peers], axis=0) for s in range(len(ids))]


def narrow(x):
    return x.astype(jnp.bfloat16)


def product(x, y):
    return jnp.dot(narrow(x), narrow(y), preferred_element_type=jnp.float32)


def named_experts(ids, held, experts):
    rows = ids[0].shape[1]
    flags = []
    for s, one in enumerate(ids):
        lane = lax.broadcasted_iota(jnp.int32, (LANES, rows), 0)
        hits = [jnp.where(one[p : p + 1, :] + s * experts == lane, 1.0, 0.0) for p in range(one.shape[0])]
        flags.append(product(held[s], sum(hits).T))
    return sum(flags)


def pack_kernel(experts, tokens_ref, ids_ref, *refs):
    *out_refs, own_ref, half_ref, held_ref, sems = refs
    quarter = tokens_ref.shape[1] // 4
    half = 2 * quarter
    where = lax.axis_index("et")
    copies = [
        pltpu.make_async_copy(ids_ref, held_ref, sems.at[0]),
        pltpu.make_async_copy(tokens_ref.at[:, aligned(where & 1, quarter)], half_ref.at[:, :quarter], sems.at[1]),
        pltpu.make_async_copy(tokens_ref.at[:, aligned(where & 1 | 2, quarter)], half_ref.at[:, quarter:], sems.at[2]),
    ]
    for copy in copies:
        copy.start()
    copies[0].wait()
    ids = [held_ref[s] for s in range(held_ref.shape[0])]
    slots, peers = out_refs[0].shape[0], 1 + len(out_refs)
    held = choices(ids, peers, slots)
    flags = named_experts(ids, held, experts)
    copies[1].wait()
    copies[2].wait()
    own_ref[...] = half_ref[:, aligned(where >> 1, quarter)]
    picked = product(held[0][slots:], half_ref[...])
    for k, out_ref in enumerate(out_refs):
        out_ref[:, :half] = narrow(picked[k * slots : (k + 1) * slots])
        out_ref[:, half:] = narrow(flags[(k + 1) * slots : (k + 2) * slots])


def pack(tokens, ids, experts, slots):
    rows, width = tokens.shape
    others = lax.axis_size("ep") - 1
    shapes = [(slots, width // 2 + LANES)] * others + [(rows, width // 4)]
    return pl.pallas_call(
        functools.partial(pack_kernel, experts),
        in_specs=[ANY] * 2,
        out_specs=[VMEM] * len(shapes),
        out_shape=[pltpu.VMEM(s, jnp.bfloat16) for s in shapes],
        scratch_shapes=[
            pltpu.VMEM((rows, width // 2), jnp.bfloat16),
            pltpu.VMEM(ids.shape, jnp.int32),
            pltpu.SemaphoreType.DMA((3,)),
        ],
        compiler_params=params(VMEM_ALL),
        name="pack",
    )(tokens, ids)


def own_kernel(experts, tokens_ref, ids_ref, out_ref, flags_ref, *choice_refs):
    ids = [ids_ref[s] for s in range(ids_ref.shape[0])]
    slots = out_ref.shape[0]
    held = choices(ids, choice_refs[0].shape[0] // slots, slots)
    flags_ref[...] = narrow(named_experts(ids, held, experts)[:slots])
    out_ref[...] = narrow(product(held[0][:slots], tokens_ref[...]))
    for s, one in enumerate(held):
        choice_refs[2 * s][...] = narrow(one)
        choice_refs[2 * s + 1][...] = narrow(one.T)


def own_rows(tokens, ids, experts, slots):
    rows, width = tokens.shape
    total = lax.axis_size("ep") * slots
    shapes = [(slots, width), (slots, LANES)] + [(total, rows), (rows, total)] * ids.shape[0]
    return pl.pallas_call(
        functools.partial(own_kernel, experts),
        out_shape=[jax.ShapeDtypeStruct(s, jnp.bfloat16) for s in shapes],
        compiler_params=params(),
        name="own_rows",
    )(tokens, ids)


def front_kernel(layout, order, section, experts, n_flags, *refs):
    n = sum(len(block) for block in layout)
    x_refs, flag_refs = list(refs[:n]), refs[n : n + n_flags]
    flag_refs = [flag_refs[order.index(k)] for k in range(n_flags)]
    mod_ref, router_ref, pair_ref, out_ref, normed_ref = refs[n + n_flags :]
    width = normed_ref.shape[1]
    hidden = out_ref.shape[1]
    quarter = width // 4
    et = lax.axis_index("et")
    blocks = {}
    for k in order:
        blocks[k] = [(x_refs.pop(0), cols, flip) for cols, flip in layout[k]]
    blocks = [blocks[k] for k in range(len(layout))]

    def part(block, flip):
        for ref, cols, at in block:
            if cols == quarter and at == flip:
                return ref[...].astype(jnp.float32)
            if cols == 2 * quarter and at == flip & 1:
                return ref[:, aligned((et ^ flip) >> 1, quarter)].astype(jnp.float32)
            if cols == width:
                return ref[:, aligned(et ^ flip, quarter)].astype(jnp.float32)

    parts = [jnp.concatenate([part(block, flip) for block in blocks], axis=0) for flip in range(4)]
    total = sum(jnp.sum(xf * xf, axis=1, keepdims=True) for xf in parts)
    scale = lax.rsqrt(total / width + 1e-06)
    for flip, xf in enumerate(parts):
        where = aligned(et ^ flip, quarter)
        normed_ref[:, where] = (
            xf * scale * (1.0 + mod_ref[section, 0:1, where]) + mod_ref[section, 1:2, where]
        ).astype(jnp.bfloat16)
    normed = normed_ref[...]
    both = jnp.dot(normed, pair_ref[...], preferred_element_type=jnp.float32)
    logits = lax.dot_general(
        normed, router_ref[...], (((1,), (1,)), ((), ())), preferred_element_type=jnp.float32
    )
    count = logits.shape[1]
    lane = lax.broadcasted_iota(jnp.int32, logits.shape, 1)
    flags = [f[:, f.shape[1] - LANES :].astype(jnp.float32) for f in flag_refs]
    flags = jnp.concatenate(flags, axis=0)[:, section * experts : section * experts + count]
    chosen = jnp.where(flags > 0.5, jax.nn.sigmoid(logits), 0.0)
    mine = jnp.sum(jnp.where(lane == lax.axis_index("ep"), chosen, 0.0), axis=1, keepdims=True)
    used = jnp.max(flags, axis=1, keepdims=True) > 0.5
    weight = jnp.where(used, mine / jnp.sum(chosen, axis=1, keepdims=True), 0.0)
    gate, upper = both[:, :hidden], both[:, hidden:]
    units = jnp.where(used, gate / (1.0 + jnp.exp(-gate)) * upper * weight, 0.0)
    out_ref[...] = units.astype(jnp.bfloat16)


def front(blocks, flags, order, section, mod, router, pair):
    width, hidden = pair.shape[0], pair.shape[1] // 2
    rows = sum(f.shape[0] for f in flags)
    experts = router.shape[0]
    xs = [x for k in order for x, _, _ in blocks[k]]
    flags = [flags[k] for k in order]
    layout = [[piece[1:] for piece in block] for block in blocks]
    return pl.pallas_call(
        functools.partial(front_kernel, layout, order, section, experts, len(flags)),
        in_specs=[VMEM] * (len(xs) + len(flags) + 3),
        scratch_shapes=[pltpu.VMEM((rows, width), jnp.bfloat16)],
        out_shape=jax.ShapeDtypeStruct((rows, hidden), jnp.bfloat16),
        compiler_params=params(),
        cost_estimate=pl.CostEstimate(
            flops=4 * rows * width * hidden, bytes_accessed=4 * width * hidden, transcendentals=0
        ),
        name="front",
    )(*xs, *flags, mod, router, pair)


def down_kernel(flip, n_adds, hidden_ref, down_ref, *refs):
    adds, outs = refs[:n_adds], refs[n_adds:]
    quarter = outs[0].shape[1]
    weights = down_ref[:, aligned(lax.axis_index("et") ^ flip, quarter)]
    product = jnp.dot(hidden_ref[...], weights, preferred_element_type=jnp.float32)
    for ref in adds:
        product += ref[...].astype(jnp.float32)
    rows = outs[0].shape[0]
    for k, out in enumerate(outs):
        out[...] = product[k * rows : (k + 1) * rows].astype(out.dtype)


def down(hidden, w_down, flip, blocks, adds=(), dtype=jnp.bfloat16):
    units, width = w_down.shape
    rows, quarter = hidden.shape[0], width // 4
    return pl.pallas_call(
        functools.partial(down_kernel, flip, len(adds)),
        in_specs=[VMEM] * (2 + len(adds)),
        out_shape=[jax.ShapeDtypeStruct((rows // blocks, quarter), dtype)] * blocks,
        compiler_params=params(),
        cost_estimate=pl.CostEstimate(
            flops=2 * rows * units * quarter, bytes_accessed=2 * units * quarter, transcendentals=0
        ),
        name="down",
    )(hidden, w_down, *adds)


def add_kernel(keep_ref, came_ref, *outs):
    total = keep_ref[...] + came_ref[...].astype(jnp.float32)
    rows = outs[0].shape[0]
    for k, out in enumerate(outs):
        out[...] = total[k * rows : (k + 1) * rows].astype(out.dtype)


def add(keep, came, count):
    shape = (keep.shape[0] // count, keep.shape[1])
    return pl.pallas_call(
        add_kernel,
        out_shape=[jax.ShapeDtypeStruct(shape, jnp.bfloat16)] * count,
        compiler_params=params(),
        name="add",
    )(keep, came)


def move_kernel(n_came, last, own_ref, back_ref, pick_ref, *refs):
    came, outs = refs[:n_came], refs[n_came:]
    rows = [ref[...].astype(jnp.float32) for ref in came]
    velocity = product(back_ref[...], jnp.concatenate(rows, axis=0))
    moved = narrow(own_ref[...].astype(jnp.float32) - 0.5 * velocity)
    outs[0][...] = moved
    if last:
        outs[1][...] = narrow(velocity)
    else:
        slots = came[0].shape[0]
        picked = product(pick_ref[...], moved)
        for k, out in enumerate(outs[1:]):
            out[...] = narrow(picked[k * slots : (k + 1) * slots])


def move(own, back, pick, came, last):
    shapes = [own.shape] + ([own.shape] if last else [c.shape for c in came])
    return pl.pallas_call(
        functools.partial(move_kernel, len(came), last),
        out_shape=[jax.ShapeDtypeStruct(s, jnp.bfloat16) for s in shapes],
        compiler_params=params(),
        name="move",
    )(own, back, pick, *came)


def sum_back(hidden, w_down, own, back, pick, last_section):
    peers = lax.axis_size("ep")
    some = peers // 2
    far = swap(down(hidden, w_down, 3, 1)[0], "et", 1)
    near = swap(down(hidden, w_down, 1, 1)[0], "et", 1)
    first, last = add(down(hidden, w_down, 2, 1, (), jnp.float32)[0], far, 2)
    last, first = swap(last, "et", 2), swap(first, "et", 2)
    keep_first, keep_last = down(hidden, w_down, 0, 2, (near,), jnp.float32)
    later = add(keep_last, last, peers - some)
    blocks = add(keep_first, first, some) + later
    came = [swap(b, "ep", k) if k else b for k, b in enumerate(blocks)]
    return move(own, back, pick, came, last_section)


def spread(block, quarter):
    side = swap(block, "et", 2)
    near, far = swap(block, "et", 1), swap(side, "et", 1)
    return [(block, quarter, 0), (side, quarter, 2), (near, quarter, 1), (far, quarter, 3)]


def dense_body(tokens, modulation, router, gate_weight, up_weight, down_weight, expert_ids):
    rows, width = tokens.shape
    half, quarter = width // 2, width // 4
    router = router.T
    experts = router.shape[0]
    peers = lax.axis_size("ep")
    slots = 3 * rows * expert_ids.shape[2] // (2 * experts)
    ids = expert_ids.transpose(0, 2, 1)

    *packed, own = pack(tokens, ids, experts, slots)
    pair, w_down, done = load(gate_weight, up_weight, down_weight)
    mine, flags, *choice = own_rows(tokens, ids, experts, slots)
    pick, back = choice[2], choice[1::2]
    order = [*range(2, len(packed) + 1), 1]
    came = {k: swap(packed[k - 1], "ep", k) for k in order}
    halves = {k: relay(came[k], half, done) for k in order}
    others = {k: swap(halves[k], "et", 1) for k in order}
    flags = [flags] + [came[k] for k in sorted(order)]
    blocks = [[(mine, width, 0)]] + [[(halves[k], half, 0), (others[k], half, 1)] for k in sorted(order)]
    hidden = front(blocks, flags, order + [0], 0, modulation, router, pair)
    own, *sent = sum_back(hidden, w_down, own, back[0], pick, False)

    blocks = [spread(swap(b, "ep", k) if k else b, quarter) for k, b in enumerate(sent)]
    hidden = front(blocks, flags, sorted(order + [0]), 1, modulation, router, pair)
    return tuple(sum_back(hidden, w_down, own, back[1], pick, True))


def solution(mesh):
    in_specs = (
        P(("grp", "ep"), None),
        P(),
        P(),
        P("ep", None, "et"),
        P("ep", None, "et"),
        P("ep", "et", None),
        P(None, ("grp", "ep"), None),
    )
    out_specs = (P(("grp", "ep"), "et"), P(("grp", "ep"), "et"))

    def body(*args):
        experts, picks = args[2].shape[1], args[6].shape[2]
        peers = lax.axis_size("ep")
        fits = lax.axis_size("et") == 4 and peers & (peers - 1) == 0
        chosen = dense_body if fits and experts <= 2 * picks else routed_body
        return chosen(*args)

    return jax.shard_map(body, mesh=mesh, in_specs=in_specs, out_specs=out_specs, check_vma=False)
```

```python
import functools

import jax
import jax.numpy as jnp
from jax import lax
from jax.experimental import pallas as pl
from jax.experimental.pallas import tpu as pltpu
from jax.sharding import PartitionSpec as P


def normalize(x, mod):
    xf = x.astype(jnp.float32)
    scaled = xf * lax.rsqrt(jnp.mean(xf * xf, axis=-1, keepdims=True) + 1e-06)
    return (scaled * (1.0 + mod[0]) + mod[1]).astype(jnp.bfloat16)


def routed_section(x_full, x_cols, mod, ids, router, gate_weight, up_weight, down_weight):
    tok_rows = x_full.shape[0]
    width = x_full.shape[1]
    experts = router.shape[1]
    picks = ids.shape[1]
    n_peers = lax.axis_size("ep")
    quarter = width // lax.axis_size("et")
    slot_count = 3 * tok_rows * picks // (2 * experts)
    normed = normalize(x_full, mod)
    logits = jnp.dot(normed, router, preferred_element_type=jnp.float32)
    chosen = jax.nn.sigmoid(jnp.take_along_axis(logits, ids, axis=1))
    weight = chosen / jnp.sum(chosen, axis=1, keepdims=True)
    flat_e = ids.reshape(-1)
    onehot = (flat_e[:, None] == jnp.arange(experts, dtype=jnp.int32)).astype(jnp.int32)
    counted = jnp.cumsum(onehot, axis=0)
    slot = jnp.sum(onehot * (counted - 1), axis=1)
    repeated = jnp.repeat(normed, picks, axis=0)
    outbox = jnp.zeros((experts, slot_count, width), jnp.bfloat16).at[flat_e, slot].set(repeated)
    arrived = lax.all_to_all(outbox, "ep", split_axis=0, concat_axis=0, tiled=True)
    in_rows = arrived.reshape(n_peers * slot_count, width)
    gate = jnp.dot(in_rows, gate_weight[0], preferred_element_type=jnp.float32)
    upper = jnp.dot(in_rows, up_weight[0], preferred_element_type=jnp.float32)
    hidden = (jax.nn.silu(gate) * upper).astype(jnp.bfloat16)
    partial_out = jnp.dot(hidden, down_weight[0], preferred_element_type=jnp.float32)
    summed = lax.psum_scatter(
        partial_out.astype(jnp.bfloat16), "et", scatter_dimension=1, tiled=True
    )
    returned = lax.all_to_all(
        summed.reshape(n_peers, slot_count, quarter), "ep", split_axis=0, concat_axis=0, tiled=True
    )
    picked = returned[flat_e, slot].astype(jnp.float32).reshape(tok_rows, picks, quarter)
    velocity = jnp.sum(picked * weight[:, :, None], axis=1)
    moved = (x_cols.astype(jnp.float32) - 0.5 * velocity).astype(jnp.bfloat16)
    return (moved, velocity)


def routed_body(tokens, modulation, router, gate_weight, up_weight, down_weight, expert_ids):
    quarter = tokens.shape[1] // lax.axis_size("et")
    column_start = lax.axis_index("et") * quarter
    cols = lax.dynamic_slice_in_dim(tokens, column_start, quarter, 1)
    weights = (router, gate_weight, up_weight, down_weight)
    first, _ = routed_section(tokens, cols, modulation[0], expert_ids[0], *weights)
    full = lax.all_gather(first, "et", axis=1, tiled=True)
    second, velocity = routed_section(full, first, modulation[1], expert_ids[1], *weights)
    return (second, velocity.astype(jnp.bfloat16))


def swap(x, axis, bit):
    size = lax.axis_size(axis)
    return lax.ppermute(x, axis, [(i, i ^ bit) for i in range(size)])


LANES = 128
VMEM_LIMIT = 32 * 1024 * 1024
VMEM_MOST = 52 * 1024 * 1024
VMEM_ALL = 63 * 1024 * 1024
VMEM = pl.BlockSpec(memory_space=pltpu.VMEM)
ANY = pl.BlockSpec(memory_space=pl.ANY)


def params(limit=VMEM_LIMIT):
    return pltpu.CompilerParams(vmem_limit_bytes=limit)


def aligned(index, size):
    return pl.ds(pl.multiple_of(index * size, size), size)


def load_kernel(gate_ref, up_ref, down_ref, pair_ref, out_ref, done_ref, sems):
    hidden = gate_ref.shape[2]
    copies = [
        pltpu.make_async_copy(gate_ref.at[0], pair_ref.at[:, :hidden], sems.at[0]),
        pltpu.make_async_copy(up_ref.at[0], pair_ref.at[:, hidden:], sems.at[1]),
        pltpu.make_async_copy(down_ref.at[0], out_ref, sems.at[2]),
    ]
    for copy in copies:
        copy.start()
    for copy in copies:
        copy.wait()
    done_ref[...] = jnp.zeros_like(done_ref)


def load(gate, up, down):
    _, width, hidden = gate.shape
    return pl.pallas_call(
        load_kernel,
        in_specs=[ANY] * 3,
        out_specs=[VMEM] * 3,
        out_shape=[
            pltpu.VMEM((width, 2 * hidden), jnp.bfloat16),
            pltpu.VMEM((hidden, width), jnp.bfloat16),
            pltpu.VMEM((8, LANES), jnp.float32),
        ],
        scratch_shapes=[pltpu.SemaphoreType.DMA((3,))],
        compiler_params=params(VMEM_MOST),
        cost_estimate=pl.CostEstimate(flops=0, bytes_accessed=12 * width * hidden, transcendentals=0),
        name="load",
    )(gate, up, down)


def relay_kernel(block_ref, done_ref, out_ref):
    out_ref[...] = block_ref[:, : out_ref.shape[1]]


def relay(block, cols, done):
    return pl.pallas_call(
        relay_kernel,
        out_shape=jax.ShapeDtypeStruct((block.shape[0], cols), block.dtype),
        compiler_params=params(),
        name="relay",
    )(block, done)


def choices(ids, peers, slots):
    rows = ids[0].shape[1]
    me = lax.axis_index("ep")
    named = []
    for one in ids:
        for k in range(peers):
            hits = [jnp.where(one[p : p + 1, :] == me ^ k, 1.0, 0.0) for p in range(one.shape[0])]
            named.append(sum(hits))
    earlier = lax.broadcasted_iota(jnp.int32, (rows, rows), 0) < lax.broadcasted_iota(jnp.int32, (rows, rows), 1)
    ahead = jnp.dot(
        jnp.concatenate(named, axis=0).astype(jnp.bfloat16),
        jnp.where(earlier, 1.0, 0.0).astype(jnp.bfloat16),
        preferred_element_type=jnp.float32,
    ).astype(jnp.int32)
    slot = lax.broadcasted_iota(jnp.int32, (slots, rows), 0)
    holds = [jnp.where((ahead[i : i + 1, :] == slot) & (row > 0.5), 1.0, 0.0) for i, row in enumerate(named)]
    return [jnp.concatenate(holds[s * peers : (s + 1) * peers], axis=0) for s in range(len(ids))]


def narrow(x):
    return x.astype(jnp.bfloat16)


def product(x, y):
    return jnp.dot(narrow(x), narrow(y), preferred_element_type=jnp.float32)


def named_experts(ids, held, experts):
    rows = ids[0].shape[1]
    flags = []
    for s, one in enumerate(ids):
        lane = lax.broadcasted_iota(jnp.int32, (LANES, rows), 0)
        hits = [jnp.where(one[p : p + 1, :] + s * experts == lane, 1.0, 0.0) for p in range(one.shape[0])]
        flags.append(product(held[s], sum(hits).T))
    return sum(flags)


def pack_kernel(experts, tokens_ref, ids_ref, *refs):
    *out_refs, own_ref, half_ref, held_ref, sems = refs
    quarter = tokens_ref.shape[1] // 4
    half = 2 * quarter
    where = lax.axis_index("et")
    copies = [
        pltpu.make_async_copy(ids_ref, held_ref, sems.at[0]),
        pltpu.make_async_copy(tokens_ref.at[:, aligned(where & 1, quarter)], half_ref.at[:, :quarter], sems.at[1]),
        pltpu.make_async_copy(tokens_ref.at[:, aligned(where & 1 | 2, quarter)], half_ref.at[:, quarter:], sems.at[2]),
    ]
    for copy in copies:
        copy.start()
    copies[0].wait()
    ids = [held_ref[s] for s in range(held_ref.shape[0])]
    slots, peers = out_refs[0].shape[0], 1 + len(out_refs)
    held = choices(ids, peers, slots)
    flags = named_experts(ids, held, experts)
    copies[1].wait()
    copies[2].wait()
    own_ref[...] = half_ref[:, aligned(where >> 1, quarter)]
    picked = product(held[0][slots:], half_ref[...])
    for k, out_ref in enumerate(out_refs):
        out_ref[:, :half] = narrow(picked[k * slots : (k + 1) * slots])
        out_ref[:, half:] = narrow(flags[(k + 1) * slots : (k + 2) * slots])


def pack(tokens, ids, experts, slots):
    rows, width = tokens.shape
    others = lax.axis_size("ep") - 1
    shapes = [(slots, width // 2 + LANES)] * others + [(rows, width // 4)]
    return pl.pallas_call(
        functools.partial(pack_kernel, experts),
        in_specs=[ANY] * 2,
        out_specs=[VMEM] * len(shapes),
        out_shape=[pltpu.VMEM(s, jnp.bfloat16) for s in shapes],
        scratch_shapes=[
            pltpu.VMEM((rows, width // 2), jnp.bfloat16),
            pltpu.VMEM(ids.shape, jnp.int32),
            pltpu.SemaphoreType.DMA((3,)),
        ],
        compiler_params=params(VMEM_ALL),
        name="pack",
    )(tokens, ids)


def own_kernel(experts, tokens_ref, ids_ref, out_ref, flags_ref, *choice_refs):
    ids = [ids_ref[s] for s in range(ids_ref.shape[0])]
    slots = out_ref.shape[0]
    held = choices(ids, choice_refs[0].shape[0] // slots, slots)
    flags_ref[...] = narrow(named_experts(ids, held, experts)[:slots])
    out_ref[...] = narrow(product(held[0][:slots], tokens_ref[...]))
    for s, one in enumerate(held):
        choice_refs[2 * s][...] = narrow(one)
        choice_refs[2 * s + 1][...] = narrow(one.T)


def own_rows(tokens, ids, experts, slots):
    rows, width = tokens.shape
    total = lax.axis_size("ep") * slots
    shapes = [(slots, width), (slots, LANES)] + [(total, rows), (rows, total)] * ids.shape[0]
    return pl.pallas_call(
        functools.partial(own_kernel, experts),
        out_shape=[jax.ShapeDtypeStruct(s, jnp.bfloat16) for s in shapes],
        compiler_params=params(),
        name="own_rows",
    )(tokens, ids)


def front_kernel(layout, order, section, experts, n_flags, *refs):
    n = sum(len(block) for block in layout)
    x_refs, flag_refs = list(refs[:n]), refs[n : n + n_flags]
    flag_refs = [flag_refs[order.index(k)] for k in range(n_flags)]
    mod_ref, router_ref, pair_ref, out_ref, normed_ref = refs[n + n_flags :]
    width = normed_ref.shape[1]
    hidden = out_ref.shape[1]
    quarter = width // 4
    et = lax.axis_index("et")
    blocks = {}
    for k in order:
        blocks[k] = [(x_refs.pop(0), cols, flip) for cols, flip in layout[k]]
    blocks = [blocks[k] for k in range(len(layout))]

    def part(block, flip):
        for ref, cols, at in block:
            if cols == quarter and at == flip:
                return ref[...].astype(jnp.float32)
            if cols == 2 * quarter and at == flip & 1:
                return ref[:, aligned((et ^ flip) >> 1, quarter)].astype(jnp.float32)
            if cols == width:
                return ref[:, aligned(et ^ flip, quarter)].astype(jnp.float32)

    parts = [jnp.concatenate([part(block, flip) for block in blocks], axis=0) for flip in range(4)]
    total = sum(jnp.sum(xf * xf, axis=1, keepdims=True) for xf in parts)
    scale = lax.rsqrt(total / width + 1e-06)
    for flip, xf in enumerate(parts):
        where = aligned(et ^ flip, quarter)
        normed_ref[:, where] = (
            xf * scale * (1.0 + mod_ref[section, 0:1, where]) + mod_ref[section, 1:2, where]
        ).astype(jnp.bfloat16)
    normed = normed_ref[...]
    both = jnp.dot(normed, pair_ref[...], preferred_element_type=jnp.float32)
    logits = lax.dot_general(
        normed, router_ref[...], (((1,), (1,)), ((), ())), preferred_element_type=jnp.float32
    )
    count = logits.shape[1]
    lane = lax.broadcasted_iota(jnp.int32, logits.shape, 1)
    flags = [f[:, f.shape[1] - LANES :].astype(jnp.float32) for f in flag_refs]
    flags = jnp.concatenate(flags, axis=0)[:, section * experts : section * experts + count]
    chosen = jnp.where(flags > 0.5, jax.nn.sigmoid(logits), 0.0)
    mine = jnp.sum(jnp.where(lane == lax.axis_index("ep"), chosen, 0.0), axis=1, keepdims=True)
    used = jnp.max(flags, axis=1, keepdims=True) > 0.5
    weight = jnp.where(used, mine / jnp.sum(chosen, axis=1, keepdims=True), 0.0)
    gate, upper = both[:, :hidden], both[:, hidden:]
    units = jnp.where(used, gate / (1.0 + jnp.exp(-gate)) * upper * weight, 0.0)
    out_ref[...] = units.astype(jnp.bfloat16)


def front(blocks, flags, order, section, mod, router, pair):
    width, hidden = pair.shape[0], pair.shape[1] // 2
    rows = sum(f.shape[0] for f in flags)
    experts = router.shape[0]
    xs = [x for k in order for x, _, _ in blocks[k]]
    flags = [flags[k] for k in order]
    layout = [[piece[1:] for piece in block] for block in blocks]
    return pl.pallas_call(
        functools.partial(front_kernel, layout, order, section, experts, len(flags)),
        in_specs=[VMEM] * (len(xs) + len(flags) + 3),
        scratch_shapes=[pltpu.VMEM((rows, width), jnp.bfloat16)],
        out_shape=jax.ShapeDtypeStruct((rows, hidden), jnp.bfloat16),
        compiler_params=params(),
        cost_estimate=pl.CostEstimate(
            flops=4 * rows * width * hidden, bytes_accessed=4 * width * hidden, transcendentals=0
        ),
        name="front",
    )(*xs, *flags, mod, router, pair)


def store_blocks(total, groups, outs):
    rows = total.shape[0] // sum(len(group) for group in groups)
    for group, out in zip(groups, outs):
        blocks = [total[k * rows : (k + 1) * rows] for k in group]
        out[...] = jnp.concatenate(blocks, axis=0).astype(out.dtype)


def shapes_of(rows, cols, groups, types):
    slots = rows // sum(len(group) for group in groups)
    return [jax.ShapeDtypeStruct((slots * len(group), cols), t) for group, t in zip(groups, types)]


def down_kernel(flip, n_adds, groups, hidden_ref, down_ref, *refs):
    adds, outs = refs[:n_adds], refs[n_adds:]
    quarter = outs[0].shape[1]
    weights = down_ref[:, aligned(lax.axis_index("et") ^ flip, quarter)]
    total = jnp.dot(hidden_ref[...], weights, preferred_element_type=jnp.float32)
    for ref in adds:
        total += ref[...].astype(jnp.float32)
    store_blocks(total, groups, outs)


def down(hidden, w_down, flip, adds=(), groups=((0,),), types=(jnp.bfloat16,)):
    units, width = w_down.shape
    rows, quarter = hidden.shape[0], width // 4
    return pl.pallas_call(
        functools.partial(down_kernel, flip, len(adds), groups),
        in_specs=[VMEM] * (2 + len(adds)),
        out_shape=shapes_of(rows, quarter, groups, types),
        compiler_params=params(),
        cost_estimate=pl.CostEstimate(
            flops=2 * rows * units * quarter, bytes_accessed=2 * units * quarter, transcendentals=0
        ),
        name="down",
    )(hidden, w_down, *adds)


def add_kernel(groups, keep_ref, came_ref, *outs):
    store_blocks(keep_ref[...] + came_ref[...].astype(jnp.float32), groups, outs)


def add(keep, came, groups):
    return pl.pallas_call(
        functools.partial(add_kernel, groups),
        out_shape=shapes_of(*keep.shape, groups, [jnp.bfloat16] * len(groups)),
        compiler_params=params(),
        name="add",
    )(keep, came)


def diagonal(x, k, flip):
    n_ep, n_et = lax.axis_size("ep"), lax.axis_size("et")
    pairs = [(e * n_et + t, (e ^ k) * n_et + (t ^ flip)) for e in range(n_ep) for t in range(n_et)]
    return lax.ppermute(x, ("ep", "et"), pairs)


def move_kernel(n_came, last, own_ref, back_ref, pick_ref, extra_ref, *refs):
    came, outs = refs[:n_came], refs[n_came:]
    rows = [ref[...].astype(jnp.float32) for ref in came]
    rows[DIRECT] += extra_ref[...].astype(jnp.float32)
    velocity = product(back_ref[...], jnp.concatenate(rows, axis=0))
    moved = narrow(own_ref[...].astype(jnp.float32) - 0.5 * velocity)
    outs[0][...] = moved
    if last:
        outs[1][...] = narrow(velocity)
    else:
        slots = came[0].shape[0]
        picked = product(pick_ref[...], moved)
        for k, out in enumerate(outs[1:]):
            out[...] = narrow(picked[k * slots : (k + 1) * slots])


def move(own, back, pick, extra, came, last):
    shapes = [own.shape] + ([own.shape] if last else [c.shape for c in came])
    return pl.pallas_call(
        functools.partial(move_kernel, len(came), last),
        out_shape=[jax.ShapeDtypeStruct(s, jnp.bfloat16) for s in shapes],
        compiler_params=params(),
        name="move",
    )(own, back, pick, extra, *came)


DIRECT = 2


def sum_back(hidden, w_down, own, back, pick, last):
    peers = lax.axis_size("ep")
    rest = tuple(k for k in range(peers) if k != DIRECT)
    groups = (rest, (DIRECT,))
    (far,), (near,) = down(hidden, w_down, 3), down(hidden, w_down, 1)
    far, near = swap(far, "et", 1), swap(near, "et", 1)
    (crossing,) = down(hidden, w_down, 2, types=[jnp.float32])
    crossing, beside = add(crossing, far, groups)
    crossed, extra = swap(crossing, "et", 2), diagonal(beside, DIRECT, 2)
    kept, straight = down(hidden, w_down, 0, (near,), groups, [jnp.float32, jnp.bfloat16])
    blocks = dict(zip(rest, add(kept, crossed, [(i,) for i in range(len(rest))])))
    blocks[DIRECT] = straight
    came = [swap(blocks[k], "ep", k) if k else blocks[k] for k in range(peers)]
    return move(own, back, pick, extra, came, last)


def spread(block, quarter):
    side = swap(block, "et", 2)
    near, far = swap(block, "et", 1), swap(side, "et", 1)
    return [(block, quarter, 0), (side, quarter, 2), (near, quarter, 1), (far, quarter, 3)]


def dense_body(tokens, modulation, router, gate_weight, up_weight, down_weight, expert_ids):
    rows, width = tokens.shape
    half, quarter = width // 2, width // 4
    router = router.T
    experts = router.shape[0]
    peers = lax.axis_size("ep")
    slots = 3 * rows * expert_ids.shape[2] // (2 * experts)
    ids = expert_ids.transpose(0, 2, 1)

    *packed, own = pack(tokens, ids, experts, slots)
    pair, w_down, done = load(gate_weight, up_weight, down_weight)
    mine, flags, *choice = own_rows(tokens, ids, experts, slots)
    pick, back = choice[2], choice[1::2]
    order = [*range(2, len(packed) + 1), 1]
    came = {k: swap(packed[k - 1], "ep", k) for k in order}
    halves = {k: relay(came[k], half, done) for k in order}
    others = {k: swap(halves[k], "et", 1) for k in order}
    flags = [flags] + [came[k] for k in sorted(order)]
    blocks = [[(mine, width, 0)]] + [[(halves[k], half, 0), (others[k], half, 1)] for k in sorted(order)]
    hidden = front(blocks, flags, order + [0], 0, modulation, router, pair)
    own, *sent = sum_back(hidden, w_down, own, back[0], pick, False)

    blocks = [spread(swap(b, "ep", k) if k else b, quarter) for k, b in enumerate(sent)]
    hidden = front(blocks, flags, sorted(order + [0]), 1, modulation, router, pair)
    return tuple(sum_back(hidden, w_down, own, back[1], pick, True))


def solution(mesh):
    in_specs = (
        P(("grp", "ep"), None),
        P(),
        P(),
        P("ep", None, "et"),
        P("ep", None, "et"),
        P("ep", "et", None),
        P(None, ("grp", "ep"), None),
    )
    out_specs = (P(("grp", "ep"), "et"), P(("grp", "ep"), "et"))

    def body(*args):
        experts, picks = args[2].shape[1], args[6].shape[2]
        peers = lax.axis_size("ep")
        fits = lax.axis_size("et") == 4 and peers >= 4 and peers & (peers - 1) == 0
        chosen = dense_body if fits and experts <= 2 * picks else routed_body
        return chosen(*args)

    return jax.shard_map(body, mesh=mesh, in_specs=in_specs, out_specs=out_specs, check_vma=False)
```

```python
import functools

import jax
import jax.numpy as jnp
from jax import lax
from jax.experimental import pallas as pl
from jax.experimental.pallas import tpu as pltpu
from jax.sharding import PartitionSpec as P


def normalize(x, mod):
    xf = x.astype(jnp.float32)
    scaled = xf * lax.rsqrt(jnp.mean(xf * xf, axis=-1, keepdims=True) + 1e-06)
    return (scaled * (1.0 + mod[0]) + mod[1]).astype(jnp.bfloat16)


def routed_section(x_full, x_cols, mod, ids, router, gate_weight, up_weight, down_weight):
    tok_rows = x_full.shape[0]
    width = x_full.shape[1]
    experts = router.shape[1]
    picks = ids.shape[1]
    n_peers = lax.axis_size("ep")
    quarter = width // lax.axis_size("et")
    slot_count = 3 * tok_rows * picks // (2 * experts)
    normed = normalize(x_full, mod)
    logits = jnp.dot(normed, router, preferred_element_type=jnp.float32)
    chosen = jax.nn.sigmoid(jnp.take_along_axis(logits, ids, axis=1))
    weight = chosen / jnp.sum(chosen, axis=1, keepdims=True)
    flat_e = ids.reshape(-1)
    onehot = (flat_e[:, None] == jnp.arange(experts, dtype=jnp.int32)).astype(jnp.int32)
    counted = jnp.cumsum(onehot, axis=0)
    slot = jnp.sum(onehot * (counted - 1), axis=1)
    repeated = jnp.repeat(normed, picks, axis=0)
    outbox = jnp.zeros((experts, slot_count, width), jnp.bfloat16).at[flat_e, slot].set(repeated)
    arrived = lax.all_to_all(outbox, "ep", split_axis=0, concat_axis=0, tiled=True)
    in_rows = arrived.reshape(n_peers * slot_count, width)
    gate = jnp.dot(in_rows, gate_weight[0], preferred_element_type=jnp.float32)
    upper = jnp.dot(in_rows, up_weight[0], preferred_element_type=jnp.float32)
    hidden = (jax.nn.silu(gate) * upper).astype(jnp.bfloat16)
    partial_out = jnp.dot(hidden, down_weight[0], preferred_element_type=jnp.float32)
    summed = lax.psum_scatter(
        partial_out.astype(jnp.bfloat16), "et", scatter_dimension=1, tiled=True
    )
    returned = lax.all_to_all(
        summed.reshape(n_peers, slot_count, quarter), "ep", split_axis=0, concat_axis=0, tiled=True
    )
    picked = returned[flat_e, slot].astype(jnp.float32).reshape(tok_rows, picks, quarter)
    velocity = jnp.sum(picked * weight[:, :, None], axis=1)
    moved = (x_cols.astype(jnp.float32) - 0.5 * velocity).astype(jnp.bfloat16)
    return (moved, velocity)


def routed_body(tokens, modulation, router, gate_weight, up_weight, down_weight, expert_ids):
    quarter = tokens.shape[1] // lax.axis_size("et")
    column_start = lax.axis_index("et") * quarter
    cols = lax.dynamic_slice_in_dim(tokens, column_start, quarter, 1)
    weights = (router, gate_weight, up_weight, down_weight)
    first, _ = routed_section(tokens, cols, modulation[0], expert_ids[0], *weights)
    full = lax.all_gather(first, "et", axis=1, tiled=True)
    second, velocity = routed_section(full, first, modulation[1], expert_ids[1], *weights)
    return (second, velocity.astype(jnp.bfloat16))


def swap(x, axis, bit):
    size = lax.axis_size(axis)
    return lax.ppermute(x, axis, [(i, i ^ bit) for i in range(size)])


LANES = 128
VMEM_LIMIT = 32 * 1024 * 1024
VMEM_MOST = 52 * 1024 * 1024
VMEM_ALL = 63 * 1024 * 1024
VMEM = pl.BlockSpec(memory_space=pltpu.VMEM)
ANY = pl.BlockSpec(memory_space=pl.ANY)


def params(limit=VMEM_LIMIT):
    return pltpu.CompilerParams(vmem_limit_bytes=limit)


def aligned(index, size):
    return pl.ds(pl.multiple_of(index * size, size), size)


def load_kernel(gate_ref, up_ref, down_ref, pair_ref, out_ref, done_ref, sems):
    hidden = gate_ref.shape[2]
    copies = [
        pltpu.make_async_copy(gate_ref.at[0], pair_ref.at[:, :hidden], sems.at[0]),
        pltpu.make_async_copy(up_ref.at[0], pair_ref.at[:, hidden:], sems.at[1]),
        pltpu.make_async_copy(down_ref.at[0], out_ref, sems.at[2]),
    ]
    for copy in copies:
        copy.start()
    for copy in copies:
        copy.wait()
    done_ref[...] = jnp.zeros_like(done_ref)


def load(gate, up, down):
    _, width, hidden = gate.shape
    return pl.pallas_call(
        load_kernel,
        in_specs=[ANY] * 3,
        out_specs=[VMEM] * 3,
        out_shape=[
            pltpu.VMEM((width, 2 * hidden), jnp.bfloat16),
            pltpu.VMEM((hidden, width), jnp.bfloat16),
            pltpu.VMEM((8, LANES), jnp.float32),
        ],
        scratch_shapes=[pltpu.SemaphoreType.DMA((3,))],
        compiler_params=params(VMEM_MOST),
        cost_estimate=pl.CostEstimate(flops=0, bytes_accessed=12 * width * hidden, transcendentals=0),
        name="load",
    )(gate, up, down)


def relay_kernel(block_ref, done_ref, out_ref):
    out_ref[...] = block_ref[:, : out_ref.shape[1]]


def relay(block, cols, done):
    return pl.pallas_call(
        relay_kernel,
        out_shape=jax.ShapeDtypeStruct((block.shape[0], cols), block.dtype),
        compiler_params=params(),
        name="relay",
    )(block, done)


def choices(ids, peers, slots):
    rows = ids[0].shape[1]
    me = lax.axis_index("ep")
    named = []
    for one in ids:
        for k in range(peers):
            hits = [jnp.where(one[p : p + 1, :] == me ^ k, 1.0, 0.0) for p in range(one.shape[0])]
            named.append(sum(hits))
    earlier = lax.broadcasted_iota(jnp.int32, (rows, rows), 0) < lax.broadcasted_iota(jnp.int32, (rows, rows), 1)
    ahead = jnp.dot(
        jnp.concatenate(named, axis=0).astype(jnp.bfloat16),
        jnp.where(earlier, 1.0, 0.0).astype(jnp.bfloat16),
        preferred_element_type=jnp.float32,
    ).astype(jnp.int32)
    slot = lax.broadcasted_iota(jnp.int32, (slots, rows), 0)
    holds = [jnp.where((ahead[i : i + 1, :] == slot) & (row > 0.5), 1.0, 0.0) for i, row in enumerate(named)]
    return [jnp.concatenate(holds[s * peers : (s + 1) * peers], axis=0) for s in range(len(ids))]


def narrow(x):
    return x.astype(jnp.bfloat16)


def product(x, y):
    return jnp.dot(narrow(x), narrow(y), preferred_element_type=jnp.float32)


def named_experts(ids, held, experts):
    rows = ids[0].shape[1]
    flags = []
    for s, one in enumerate(ids):
        lane = lax.broadcasted_iota(jnp.int32, (LANES, rows), 0)
        hits = [jnp.where(one[p : p + 1, :] + s * experts == lane, 1.0, 0.0) for p in range(one.shape[0])]
        flags.append(product(held[s], sum(hits).T))
    return sum(flags)


def pack_kernel(experts, tokens_ref, ids_ref, *refs):
    *out_refs, own_ref, half_ref, held_ref, sems = refs
    quarter = tokens_ref.shape[1] // 4
    half = 2 * quarter
    where = lax.axis_index("et")
    copies = [
        pltpu.make_async_copy(ids_ref, held_ref, sems.at[0]),
        pltpu.make_async_copy(tokens_ref.at[:, aligned(where & 1, quarter)], half_ref.at[:, :quarter], sems.at[1]),
        pltpu.make_async_copy(tokens_ref.at[:, aligned(where & 1 | 2, quarter)], half_ref.at[:, quarter:], sems.at[2]),
    ]
    for copy in copies:
        copy.start()
    copies[0].wait()
    ids = [held_ref[s] for s in range(held_ref.shape[0])]
    slots, peers = out_refs[0].shape[0], 1 + len(out_refs)
    held = choices(ids, peers, slots)
    flags = named_experts(ids, held, experts)
    copies[1].wait()
    copies[2].wait()
    own_ref[...] = half_ref[:, aligned(where >> 1, quarter)]
    picked = product(held[0][slots:], half_ref[...])
    for k, out_ref in enumerate(out_refs):
        out_ref[:, :half] = narrow(picked[k * slots : (k + 1) * slots])
        out_ref[:, half:] = narrow(flags[(k + 1) * slots : (k + 2) * slots])


def pack(tokens, ids, experts, slots):
    rows, width = tokens.shape
    others = lax.axis_size("ep") - 1
    shapes = [(slots, width // 2 + LANES)] * others + [(rows, width // 4)]
    return pl.pallas_call(
        functools.partial(pack_kernel, experts),
        in_specs=[ANY] * 2,
        out_specs=[VMEM] * len(shapes),
        out_shape=[pltpu.VMEM(s, jnp.bfloat16) for s in shapes],
        scratch_shapes=[
            pltpu.VMEM((rows, width // 2), jnp.bfloat16),
            pltpu.VMEM(ids.shape, jnp.int32),
            pltpu.SemaphoreType.DMA((3,)),
        ],
        compiler_params=params(VMEM_ALL),
        name="pack",
    )(tokens, ids)


def own_kernel(experts, tokens_ref, ids_ref, out_ref, flags_ref, *choice_refs):
    ids = [ids_ref[s] for s in range(ids_ref.shape[0])]
    slots = out_ref.shape[0]
    held = choices(ids, choice_refs[0].shape[0] // slots, slots)
    flags_ref[...] = narrow(named_experts(ids, held, experts)[:slots])
    out_ref[...] = narrow(product(held[0][:slots], tokens_ref[...]))
    for s, one in enumerate(held):
        choice_refs[2 * s][...] = narrow(one)
        choice_refs[2 * s + 1][...] = narrow(one.T)


def own_rows(tokens, ids, experts, slots):
    rows, width = tokens.shape
    total = lax.axis_size("ep") * slots
    shapes = [(slots, width), (slots, LANES)] + [(total, rows), (rows, total)] * ids.shape[0]
    return pl.pallas_call(
        functools.partial(own_kernel, experts),
        out_shape=[jax.ShapeDtypeStruct(s, jnp.bfloat16) for s in shapes],
        compiler_params=params(),
        name="own_rows",
    )(tokens, ids)


def front_kernel(layout, order, section, experts, n_flags, *refs):
    n = sum(len(block) for block in layout)
    x_refs, flag_refs = list(refs[:n]), refs[n : n + n_flags]
    flag_refs = [flag_refs[order.index(k)] for k in range(n_flags)]
    mod_ref, router_ref, pair_ref, out_ref, normed_ref = refs[n + n_flags :]
    width = normed_ref.shape[1]
    hidden = out_ref.shape[1]
    quarter = width // 4
    et = lax.axis_index("et")
    blocks = {}
    for k in order:
        blocks[k] = [(x_refs.pop(0), cols, flip) for cols, flip in layout[k]]
    blocks = [blocks[k] for k in range(len(layout))]

    def part(block, flip):
        for ref, cols, at in block:
            if cols == quarter and at == flip:
                return ref[...].astype(jnp.float32)
            if cols == 2 * quarter and at == flip & 1:
                return ref[:, aligned((et ^ flip) >> 1, quarter)].astype(jnp.float32)
            if cols == width:
                return ref[:, aligned(et ^ flip, quarter)].astype(jnp.float32)

    parts = [jnp.concatenate([part(block, flip) for block in blocks], axis=0) for flip in range(4)]
    total = sum(jnp.sum(xf * xf, axis=1, keepdims=True) for xf in parts)
    scale = lax.rsqrt(total / width + 1e-06)
    for flip, xf in enumerate(parts):
        where = aligned(et ^ flip, quarter)
        normed_ref[:, where] = (
            xf * scale * (1.0 + mod_ref[section, 0:1, where]) + mod_ref[section, 1:2, where]
        ).astype(jnp.bfloat16)
    normed = normed_ref[...]
    both = jnp.dot(normed, pair_ref[...], preferred_element_type=jnp.float32)
    logits = lax.dot_general(
        normed, router_ref[...], (((1,), (1,)), ((), ())), preferred_element_type=jnp.float32
    )
    count = logits.shape[1]
    lane = lax.broadcasted_iota(jnp.int32, logits.shape, 1)
    flags = [f[:, f.shape[1] - LANES :].astype(jnp.float32) for f in flag_refs]
    flags = jnp.concatenate(flags, axis=0)[:, section * experts : section * experts + count]
    chosen = jnp.where(flags > 0.5, jax.nn.sigmoid(logits), 0.0)
    mine = jnp.sum(jnp.where(lane == lax.axis_index("ep"), chosen, 0.0), axis=1, keepdims=True)
    used = jnp.max(flags, axis=1, keepdims=True) > 0.5
    weight = jnp.where(used, mine / jnp.sum(chosen, axis=1, keepdims=True), 0.0)
    gate, upper = both[:, :hidden], both[:, hidden:]
    units = jnp.where(used, gate / (1.0 + jnp.exp(-gate)) * upper * weight, 0.0)
    out_ref[...] = units.astype(jnp.bfloat16)


def front(blocks, flags, order, section, mod, router, pair):
    width, hidden = pair.shape[0], pair.shape[1] // 2
    rows = sum(f.shape[0] for f in flags)
    experts = router.shape[0]
    xs = [x for k in order for x, _, _ in blocks[k]]
    flags = [flags[k] for k in order]
    layout = [[piece[1:] for piece in block] for block in blocks]
    return pl.pallas_call(
        functools.partial(front_kernel, layout, order, section, experts, len(flags)),
        in_specs=[VMEM] * (len(xs) + len(flags) + 3),
        scratch_shapes=[pltpu.VMEM((rows, width), jnp.bfloat16)],
        out_shape=jax.ShapeDtypeStruct((rows, hidden), jnp.bfloat16),
        compiler_params=params(),
        cost_estimate=pl.CostEstimate(
            flops=4 * rows * width * hidden, bytes_accessed=4 * width * hidden, transcendentals=0
        ),
        name="front",
    )(*xs, *flags, mod, router, pair)


def down_kernel(flip, n_adds, hidden_ref, down_ref, *refs):
    adds, outs = refs[:n_adds], refs[n_adds:]
    quarter = outs[0].shape[1]
    weights = down_ref[:, aligned(lax.axis_index("et") ^ flip, quarter)]
    product = jnp.dot(hidden_ref[...], weights, preferred_element_type=jnp.float32)
    for ref in adds:
        product += ref[...].astype(jnp.float32)
    rows = outs[0].shape[0]
    for k, out in enumerate(outs):
        out[...] = product[k * rows : (k + 1) * rows].astype(out.dtype)


def down(hidden, w_down, flip, blocks, adds=(), dtype=jnp.bfloat16):
    units, width = w_down.shape
    rows, quarter = hidden.shape[0], width // 4
    return pl.pallas_call(
        functools.partial(down_kernel, flip, len(adds)),
        in_specs=[VMEM] * (2 + len(adds)),
        out_shape=[jax.ShapeDtypeStruct((rows // blocks, quarter), dtype)] * blocks,
        compiler_params=params(),
        cost_estimate=pl.CostEstimate(
            flops=2 * rows * units * quarter, bytes_accessed=2 * units * quarter, transcendentals=0
        ),
        name="down",
    )(hidden, w_down, *adds)


def add_kernel(keep_ref, came_ref, *outs):
    total = keep_ref[...] + came_ref[...].astype(jnp.float32)
    rows = outs[0].shape[0]
    for k, out in enumerate(outs):
        out[...] = total[k * rows : (k + 1) * rows].astype(out.dtype)


def add(keep, came, count):
    shape = (keep.shape[0] // count, keep.shape[1])
    return pl.pallas_call(
        add_kernel,
        out_shape=[jax.ShapeDtypeStruct(shape, jnp.bfloat16)] * count,
        compiler_params=params(),
        name="add",
    )(keep, came)


def move_kernel(n_came, last, own_ref, back_ref, pick_ref, *refs):
    came, outs = refs[:n_came], refs[n_came:]
    rows = [ref[...].astype(jnp.float32) for ref in came]
    velocity = product(back_ref[...], jnp.concatenate(rows, axis=0))
    moved = narrow(own_ref[...].astype(jnp.float32) - 0.5 * velocity)
    outs[0][...] = moved
    if last:
        outs[1][...] = narrow(velocity)
    else:
        slots = came[0].shape[0]
        picked = product(pick_ref[...], moved)
        for k, out in enumerate(outs[1:]):
            out[...] = narrow(picked[k * slots : (k + 1) * slots])


def move(own, back, pick, came, last):
    shapes = [own.shape] + ([own.shape] if last else [c.shape for c in came])
    return pl.pallas_call(
        functools.partial(move_kernel, len(came), last),
        out_shape=[jax.ShapeDtypeStruct(s, jnp.bfloat16) for s in shapes],
        compiler_params=params(),
        name="move",
    )(own, back, pick, *came)


def sum_back(hidden, w_down, own, back, pick, last_section):
    peers = lax.axis_size("ep")
    some = peers // 2
    far = swap(down(hidden, w_down, 3, 1)[0], "et", 1)
    near = swap(down(hidden, w_down, 1, 1)[0], "et", 1)
    first, last = add(down(hidden, w_down, 2, 1, (), jnp.float32)[0], far, 2)
    last, first = swap(last, "et", 2), swap(first, "et", 2)
    keep_first, keep_last = down(hidden, w_down, 0, 2, (near,), jnp.float32)
    later = add(keep_last, last, peers - some)
    blocks = add(keep_first, first, some) + later
    came = [swap(b, "ep", k) if k else b for k, b in enumerate(blocks)]
    return move(own, back, pick, came, last_section)


def spread(block, quarter):
    side = swap(block, "et", 2)
    near, far = swap(block, "et", 1), swap(side, "et", 1)
    return [(block, quarter, 0), (side, quarter, 2), (near, quarter, 1), (far, quarter, 3)]


def dense_body(tokens, modulation, router, gate_weight, up_weight, down_weight, expert_ids):
    rows, width = tokens.shape
    half, quarter = width // 2, width // 4
    router = router.T
    experts = router.shape[0]
    peers = lax.axis_size("ep")
    slots = 3 * rows * expert_ids.shape[2] // (2 * experts)
    ids = expert_ids.transpose(0, 2, 1)

    *packed, own = pack(tokens, ids, experts, slots)
    pair, w_down, done = load(gate_weight, up_weight, down_weight)
    mine, flags, *choice = own_rows(tokens, ids, experts, slots)
    pick, back = choice[2], choice[1::2]
    order = [*range(2, len(packed) + 1), 1]
    came = {k: swap(packed[k - 1], "ep", k) for k in order}
    halves = {k: relay(came[k], half, done) for k in order}
    others = {k: swap(halves[k], "et", 1) for k in order}
    flags = [flags] + [came[k] for k in sorted(order)]
    blocks = [[(mine, width, 0)]] + [[(halves[k], half, 0), (others[k], half, 1)] for k in sorted(order)]
    hidden = front(blocks, flags, order + [0], 0, modulation, router, pair)
    own, *sent = sum_back(hidden, w_down, own, back[0], pick, False)

    blocks = [spread(swap(b, "ep", k) if k else b, quarter) for k, b in enumerate(sent)]
    hidden = front(blocks, flags, order + [0], 1, modulation, router, pair)
    return tuple(sum_back(hidden, w_down, own, back[1], pick, True))


def solution(mesh):
    in_specs = (
        P(("grp", "ep"), None),
        P(),
        P(),
        P("ep", None, "et"),
        P("ep", None, "et"),
        P("ep", "et", None),
        P(None, ("grp", "ep"), None),
    )
    out_specs = (P(("grp", "ep"), "et"), P(("grp", "ep"), "et"))

    def body(*args):
        experts, picks = args[2].shape[1], args[6].shape[2]
        peers = lax.axis_size("ep")
        fits = lax.axis_size("et") == 4 and peers & (peers - 1) == 0
        chosen = dense_body if fits and experts <= 2 * picks else routed_body
        return chosen(*args)

    return jax.shard_map(body, mesh=mesh, in_specs=in_specs, out_specs=out_specs, check_vma=False)
```

```python
import functools

import jax
import jax.numpy as jnp
from jax import lax
from jax.experimental import pallas as pl
from jax.experimental.pallas import tpu as pltpu
from jax.sharding import PartitionSpec as P


def normalize(x, mod):
    xf = x.astype(jnp.float32)
    scaled = xf * lax.rsqrt(jnp.mean(xf * xf, axis=-1, keepdims=True) + 1e-06)
    return (scaled * (1.0 + mod[0]) + mod[1]).astype(jnp.bfloat16)


def routed_section(x_full, x_cols, mod, ids, router, gate_weight, up_weight, down_weight):
    tok_rows = x_full.shape[0]
    width = x_full.shape[1]
    experts = router.shape[1]
    picks = ids.shape[1]
    n_peers = lax.axis_size("ep")
    quarter = width // lax.axis_size("et")
    slot_count = 3 * tok_rows * picks // (2 * experts)
    normed = normalize(x_full, mod)
    logits = jnp.dot(normed, router, preferred_element_type=jnp.float32)
    chosen = jax.nn.sigmoid(jnp.take_along_axis(logits, ids, axis=1))
    weight = chosen / jnp.sum(chosen, axis=1, keepdims=True)
    flat_e = ids.reshape(-1)
    onehot = (flat_e[:, None] == jnp.arange(experts, dtype=jnp.int32)).astype(jnp.int32)
    counted = jnp.cumsum(onehot, axis=0)
    slot = jnp.sum(onehot * (counted - 1), axis=1)
    repeated = jnp.repeat(normed, picks, axis=0)
    outbox = jnp.zeros((experts, slot_count, width), jnp.bfloat16).at[flat_e, slot].set(repeated)
    arrived = lax.all_to_all(outbox, "ep", split_axis=0, concat_axis=0, tiled=True)
    in_rows = arrived.reshape(n_peers * slot_count, width)
    gate = jnp.dot(in_rows, gate_weight[0], preferred_element_type=jnp.float32)
    upper = jnp.dot(in_rows, up_weight[0], preferred_element_type=jnp.float32)
    hidden = (jax.nn.silu(gate) * upper).astype(jnp.bfloat16)
    partial_out = jnp.dot(hidden, down_weight[0], preferred_element_type=jnp.float32)
    summed = lax.psum_scatter(
        partial_out.astype(jnp.bfloat16), "et", scatter_dimension=1, tiled=True
    )
    returned = lax.all_to_all(
        summed.reshape(n_peers, slot_count, quarter), "ep", split_axis=0, concat_axis=0, tiled=True
    )
    picked = returned[flat_e, slot].astype(jnp.float32).reshape(tok_rows, picks, quarter)
    velocity = jnp.sum(picked * weight[:, :, None], axis=1)
    moved = (x_cols.astype(jnp.float32) - 0.5 * velocity).astype(jnp.bfloat16)
    return (moved, velocity)


def routed_body(tokens, modulation, router, gate_weight, up_weight, down_weight, expert_ids):
    quarter = tokens.shape[1] // lax.axis_size("et")
    column_start = lax.axis_index("et") * quarter
    cols = lax.dynamic_slice_in_dim(tokens, column_start, quarter, 1)
    weights = (router, gate_weight, up_weight, down_weight)
    first, _ = routed_section(tokens, cols, modulation[0], expert_ids[0], *weights)
    full = lax.all_gather(first, "et", axis=1, tiled=True)
    second, velocity = routed_section(full, first, modulation[1], expert_ids[1], *weights)
    return (second, velocity.astype(jnp.bfloat16))


def swap(x, axis, bit):
    size = lax.axis_size(axis)
    return lax.ppermute(x, axis, [(i, i ^ bit) for i in range(size)])


LANES = 128
VMEM_LIMIT = 32 * 1024 * 1024
VMEM_MOST = 52 * 1024 * 1024
VMEM_ALL = 63 * 1024 * 1024
VMEM = pl.BlockSpec(memory_space=pltpu.VMEM)
ANY = pl.BlockSpec(memory_space=pl.ANY)


def params(limit=VMEM_LIMIT):
    return pltpu.CompilerParams(vmem_limit_bytes=limit)


def aligned(index, size):
    return pl.ds(pl.multiple_of(index * size, size), size)


def load_kernel(gate_ref, up_ref, down_ref, pair_ref, out_ref, done_ref, sems):
    hidden = gate_ref.shape[2]
    copies = [
        pltpu.make_async_copy(gate_ref.at[0], pair_ref.at[:, :hidden], sems.at[0]),
        pltpu.make_async_copy(up_ref.at[0], pair_ref.at[:, hidden:], sems.at[1]),
        pltpu.make_async_copy(down_ref.at[0], out_ref, sems.at[2]),
    ]
    for copy in copies:
        copy.start()
    for copy in copies:
        copy.wait()
    done_ref[...] = jnp.zeros_like(done_ref)


def load(gate, up, down):
    _, width, hidden = gate.shape
    return pl.pallas_call(
        load_kernel,
        in_specs=[ANY] * 3,
        out_specs=[VMEM] * 3,
        out_shape=[
            pltpu.VMEM((width, 2 * hidden), jnp.bfloat16),
            pltpu.VMEM((hidden, width), jnp.bfloat16),
            pltpu.VMEM((8, LANES), jnp.float32),
        ],
        scratch_shapes=[pltpu.SemaphoreType.DMA((3,))],
        compiler_params=params(VMEM_MOST),
        cost_estimate=pl.CostEstimate(flops=0, bytes_accessed=12 * width * hidden, transcendentals=0),
        name="load",
    )(gate, up, down)


def relay_kernel(block_ref, done_ref, out_ref):
    out_ref[...] = block_ref[:, : out_ref.shape[1]]


def relay(block, cols, done):
    return pl.pallas_call(
        relay_kernel,
        out_shape=jax.ShapeDtypeStruct((block.shape[0], cols), block.dtype),
        compiler_params=params(),
        name="relay",
    )(block, done)


def choices(ids, peers, slots):
    rows = ids[0].shape[1]
    me = lax.axis_index("ep")
    named = []
    for one in ids:
        for k in range(peers):
            hits = [jnp.where(one[p : p + 1, :] == me ^ k, 1.0, 0.0) for p in range(one.shape[0])]
            named.append(sum(hits))
    earlier = lax.broadcasted_iota(jnp.int32, (rows, rows), 0) < lax.broadcasted_iota(jnp.int32, (rows, rows), 1)
    ahead = jnp.dot(
        jnp.concatenate(named, axis=0).astype(jnp.bfloat16),
        jnp.where(earlier, 1.0, 0.0).astype(jnp.bfloat16),
        preferred_element_type=jnp.float32,
    ).astype(jnp.int32)
    slot = lax.broadcasted_iota(jnp.int32, (slots, rows), 0)
    holds = [jnp.where((ahead[i : i + 1, :] == slot) & (row > 0.5), 1.0, 0.0) for i, row in enumerate(named)]
    return [jnp.concatenate(holds[s * peers : (s + 1) * peers], axis=0) for s in range(len(ids))]


def narrow(x):
    return x.astype(jnp.bfloat16)


def product(x, y):
    return jnp.dot(narrow(x), narrow(y), preferred_element_type=jnp.float32)


def named_experts(ids, held, experts):
    rows = ids[0].shape[1]
    flags = []
    for s, one in enumerate(ids):
        lane = lax.broadcasted_iota(jnp.int32, (LANES, rows), 0)
        hits = [jnp.where(one[p : p + 1, :] + s * experts == lane, 1.0, 0.0) for p in range(one.shape[0])]
        flags.append(product(held[s], sum(hits).T))
    return sum(flags)


def pack_kernel(experts, tokens_ref, ids_ref, *refs):
    *out_refs, own_ref, half_ref, held_ref, sems = refs
    quarter = tokens_ref.shape[1] // 4
    half = 2 * quarter
    where = lax.axis_index("et")
    copies = [
        pltpu.make_async_copy(ids_ref, held_ref, sems.at[0]),
        pltpu.make_async_copy(tokens_ref.at[:, aligned(where & 1, quarter)], half_ref.at[:, :quarter], sems.at[1]),
        pltpu.make_async_copy(tokens_ref.at[:, aligned(where & 1 | 2, quarter)], half_ref.at[:, quarter:], sems.at[2]),
    ]
    for copy in copies:
        copy.start()
    copies[0].wait()
    ids = [held_ref[s] for s in range(held_ref.shape[0])]
    slots, peers = out_refs[0].shape[0], 1 + len(out_refs)
    held = choices(ids, peers, slots)
    flags = named_experts(ids, held, experts)
    copies[1].wait()
    copies[2].wait()
    own_ref[...] = half_ref[:, aligned(where >> 1, quarter)]
    picked = product(held[0][slots:], half_ref[...])
    for k, out_ref in enumerate(out_refs):
        out_ref[:, :half] = narrow(picked[k * slots : (k + 1) * slots])
        out_ref[:, half:] = narrow(flags[(k + 1) * slots : (k + 2) * slots])


def pack(tokens, ids, experts, slots):
    rows, width = tokens.shape
    others = lax.axis_size("ep") - 1
    shapes = [(slots, width // 2 + LANES)] * others + [(rows, width // 4)]
    return pl.pallas_call(
        functools.partial(pack_kernel, experts),
        in_specs=[ANY] * 2,
        out_specs=[VMEM] * len(shapes),
        out_shape=[pltpu.VMEM(s, jnp.bfloat16) for s in shapes],
        scratch_shapes=[
            pltpu.VMEM((rows, width // 2), jnp.bfloat16),
            pltpu.VMEM(ids.shape, jnp.int32),
            pltpu.SemaphoreType.DMA((3,)),
        ],
        compiler_params=params(VMEM_ALL),
        name="pack",
    )(tokens, ids)


def own_kernel(experts, tokens_ref, ids_ref, done_ref, out_ref, flags_ref, *choice_refs):
    ids = [ids_ref[s] for s in range(ids_ref.shape[0])]
    slots = out_ref.shape[0]
    held = choices(ids, choice_refs[0].shape[0] // slots, slots)
    flags_ref[...] = narrow(named_experts(ids, held, experts)[:slots])
    out_ref[...] = narrow(product(held[0][:slots], tokens_ref[...]))
    for s, one in enumerate(held):
        choice_refs[2 * s][...] = narrow(one)
        choice_refs[2 * s + 1][...] = narrow(one.T)


def own_rows(tokens, ids, experts, slots, done):
    rows, width = tokens.shape
    total = lax.axis_size("ep") * slots
    shapes = [(slots, width), (slots, LANES)] + [(total, rows), (rows, total)] * ids.shape[0]
    return pl.pallas_call(
        functools.partial(own_kernel, experts),
        out_shape=[jax.ShapeDtypeStruct(s, jnp.bfloat16) for s in shapes],
        compiler_params=params(),
        name="own_rows",
    )(tokens, ids, done)


def front_kernel(layout, order, flips, section, experts, *refs):
    n = sum(len(block) for block in layout)
    x_refs = list(refs[:n])
    mod_ref, router_ref, pair_ref, *rest = refs[n:]
    width = pair_ref.shape[0]
    quarter = width // 4
    et = lax.axis_index("et")
    blocks = {}
    for k in order:
        blocks[k] = [(x_refs.pop(0), cols, flip) for cols, flip in layout[k]]

    def part(block, flip):
        for ref, cols, at in block:
            if cols == quarter and at == flip:
                return ref[...].astype(jnp.float32)
            if cols == 2 * quarter and at == flip & 1:
                return ref[:, aligned((et ^ flip) >> 1, quarter)].astype(jnp.float32)
            if cols == width:
                return ref[:, aligned(et ^ flip, quarter)].astype(jnp.float32)

    units, logits, squares = 0.0, 0.0, 0.0
    for flip in flips:
        xf = jnp.concatenate([part(blocks[k], flip) for k in range(len(layout))], axis=0)
        squares += jnp.sum(xf * xf, axis=1, keepdims=True)
        where = aligned(et ^ flip, quarter)
        shift = mod_ref[section, 1:2, where]
        head = narrow(shift).astype(jnp.float32)
        blank = jnp.zeros((6, quarter), jnp.float32)
        lhs = [xf * (1.0 + mod_ref[section, 0:1, where]), head, shift - head, blank]
        lhs = narrow(jnp.concatenate(lhs, axis=0))
        units += jnp.dot(lhs, pair_ref[where, :], preferred_element_type=jnp.float32)
        logits += lax.dot_general(
            lhs, router_ref[:, where], (((1,), (1,)), ((), ())), preferred_element_type=jnp.float32
        )
    if len(rest) == 3:
        rest[0][...], rest[1][...], rest[2][...] = units, logits, squares
        return
    *flag_refs, units_ref, logits_ref, squares_ref, out_ref = rest
    rows, hidden = out_ref.shape
    scale = lax.rsqrt((squares + squares_ref[...]) / width + 1e-06)

    def scaled(x):
        return x[:rows] * scale + (x[rows : rows + 1] + x[rows + 1 : rows + 2])

    units, logits = scaled(units + units_ref[...]), scaled(logits + logits_ref[...])
    count = logits.shape[1]
    lane = lax.broadcasted_iota(jnp.int32, logits.shape, 1)
    flags = [flag_refs[order.index(k)] for k in range(len(layout))]
    flags = [f[:, f.shape[1] - LANES :].astype(jnp.float32) for f in flags]
    flags = jnp.concatenate(flags, axis=0)[:, section * experts : section * experts + count]
    chosen = jnp.where(flags > 0.5, jax.nn.sigmoid(logits), 0.0)
    mine = jnp.sum(jnp.where(lane == lax.axis_index("ep"), chosen, 0.0), axis=1, keepdims=True)
    used = jnp.max(flags, axis=1, keepdims=True) > 0.5
    weight = jnp.where(used, mine / jnp.sum(chosen, axis=1, keepdims=True), 0.0)
    gate, upper = units[:, :hidden], units[:, hidden:]
    out = jnp.where(used, gate / (1.0 + jnp.exp(-gate)) * upper * weight, 0.0)
    out_ref[...] = narrow(out)


def half_front(blocks, flips, extra, shapes, order, section, mod, router, pair):
    xs = [x for k in order for x, _, _ in blocks[k]]
    layout = [[piece[1:] for piece in block] for block in blocks]
    rows, (width, units) = shapes[0].shape[0], pair.shape
    return pl.pallas_call(
        functools.partial(front_kernel, layout, order, flips, section, router.shape[0]),
        in_specs=[VMEM] * (len(xs) + 3 + len(extra)),
        out_shape=shapes,
        compiler_params=params(),
        cost_estimate=pl.CostEstimate(
            flops=rows * width * units, bytes_accessed=width * units, transcendentals=0
        ),
        name="front",
    )(*xs, mod, router, pair, *extra)


def front(blocks, flags, order, section, mod, router, pair):
    rows = sum(f.shape[0] for f in flags)
    units, experts = pair.shape[1], router.shape[0]
    width = pair.shape[0]
    common = (order, section, mod, router, pair)
    here = [[p for p in block if p[1] == width or p[2] & 1 == 0] for block in blocks]
    there = [[p for p in block if p[1] == width or p[2] & 1] for block in blocks]
    shapes = [jax.ShapeDtypeStruct(s, jnp.float32) for s in ((rows + 8, units), (rows + 8, experts), (rows, 1))]
    sums = half_front(here, (0, 2), [], shapes, *common)
    shapes = [jax.ShapeDtypeStruct((rows, units // 2), jnp.bfloat16)]
    return half_front(there, (1, 3), [flags[k] for k in order] + list(sums), shapes, *common)[0]


def down_kernel(flip, n_adds, hidden_ref, down_ref, *refs):
    adds, outs = refs[:n_adds], refs[n_adds:]
    quarter = outs[0].shape[1]
    weights = down_ref[:, aligned(lax.axis_index("et") ^ flip, quarter)]
    product = jnp.dot(hidden_ref[...], weights, preferred_element_type=jnp.float32)
    for ref in adds:
        product += ref[...].astype(jnp.float32)
    rows = outs[0].shape[0]
    for k, out in enumerate(outs):
        out[...] = product[k * rows : (k + 1) * rows].astype(out.dtype)


def down(hidden, w_down, flip, blocks, adds=(), dtype=jnp.bfloat16):
    units, width = w_down.shape
    rows, quarter = hidden.shape[0], width // 4
    return pl.pallas_call(
        functools.partial(down_kernel, flip, len(adds)),
        in_specs=[VMEM] * (2 + len(adds)),
        out_shape=[jax.ShapeDtypeStruct((rows // blocks, quarter), dtype)] * blocks,
        compiler_params=params(),
        cost_estimate=pl.CostEstimate(
            flops=2 * rows * units * quarter, bytes_accessed=2 * units * quarter, transcendentals=0
        ),
        name="down",
    )(hidden, w_down, *adds)


def add_kernel(keep_ref, came_ref, *outs):
    total = keep_ref[...] + came_ref[...].astype(jnp.float32)
    rows = outs[0].shape[0]
    for k, out in enumerate(outs):
        out[...] = total[k * rows : (k + 1) * rows].astype(out.dtype)


def add(keep, came, count):
    shape = (keep.shape[0] // count, keep.shape[1])
    return pl.pallas_call(
        add_kernel,
        out_shape=[jax.ShapeDtypeStruct(shape, jnp.bfloat16)] * count,
        compiler_params=params(),
        name="add",
    )(keep, came)


def move_kernel(n_came, last, own_ref, back_ref, pick_ref, *refs):
    came, outs = refs[:n_came], refs[n_came:]
    rows = [ref[...].astype(jnp.float32) for ref in came]
    velocity = product(back_ref[...], jnp.concatenate(rows, axis=0))
    moved = narrow(own_ref[...].astype(jnp.float32) - 0.5 * velocity)
    outs[0][...] = moved
    if last:
        outs[1][...] = narrow(velocity)
    else:
        slots = came[0].shape[0]
        picked = product(pick_ref[...], moved)
        for k, out in enumerate(outs[1:]):
            out[...] = narrow(picked[k * slots : (k + 1) * slots])


def move(own, back, pick, came, last):
    shapes = [own.shape] + ([own.shape] if last else [c.shape for c in came])
    return pl.pallas_call(
        functools.partial(move_kernel, len(came), last),
        out_shape=[jax.ShapeDtypeStruct(s, jnp.bfloat16) for s in shapes],
        compiler_params=params(),
        name="move",
    )(own, back, pick, *came)


def sum_back(hidden, w_down, own, back, pick, last_section):
    peers = lax.axis_size("ep")
    some = peers // 2
    far = swap(down(hidden, w_down, 3, 1)[0], "et", 1)
    near = swap(down(hidden, w_down, 1, 1)[0], "et", 1)
    first, last = add(down(hidden, w_down, 2, 1, (), jnp.float32)[0], far, 2)
    last, first = swap(last, "et", 2), swap(first, "et", 2)
    keep_first, keep_last = down(hidden, w_down, 0, 2, (near,), jnp.float32)
    later = add(keep_last, last, peers - some)
    blocks = add(keep_first, first, some) + later
    came = [swap(b, "ep", k) if k else b for k, b in enumerate(blocks)]
    return move(own, back, pick, came, last_section)


def spread(block, quarter):
    side = swap(block, "et", 2)
    near, far = swap(block, "et", 1), swap(side, "et", 1)
    return [(block, quarter, 0), (side, quarter, 2), (near, quarter, 1), (far, quarter, 3)]


def dense_body(tokens, modulation, router, gate_weight, up_weight, down_weight, expert_ids):
    rows, width = tokens.shape
    half, quarter = width // 2, width // 4
    router = router.T
    experts = router.shape[0]
    peers = lax.axis_size("ep")
    slots = 3 * rows * expert_ids.shape[2] // (2 * experts)
    ids = expert_ids.transpose(0, 2, 1)

    *packed, own = pack(tokens, ids, experts, slots)
    pair, w_down, done = load(gate_weight, up_weight, down_weight)
    mine, flags, *choice = own_rows(tokens, ids, experts, slots, done)
    pick, back = choice[2], choice[1::2]
    order = [*range(2, len(packed) + 1), 1]
    came = {k: swap(packed[k - 1], "ep", k) for k in order}
    halves = {k: relay(came[k], half, flags) for k in order}
    others = {k: swap(halves[k], "et", 1) for k in order}
    flags = [flags] + [came[k] for k in sorted(order)]
    blocks = [[(mine, width, 0)]] + [[(halves[k], half, 0), (others[k], half, 1)] for k in sorted(order)]
    hidden = front(blocks, flags, order + [0], 0, modulation, router, pair)
    own, *sent = sum_back(hidden, w_down, own, back[0], pick, False)

    blocks = [spread(swap(b, "ep", k) if k else b, quarter) for k, b in enumerate(sent)]
    hidden = front(blocks, flags, order + [0], 1, modulation, router, pair)
    return tuple(sum_back(hidden, w_down, own, back[1], pick, True))


def solution(mesh):
    in_specs = (
        P(("grp", "ep"), None),
        P(),
        P(),
        P("ep", None, "et"),
        P("ep", None, "et"),
        P("ep", "et", None),
        P(None, ("grp", "ep"), None),
    )
    out_specs = (P(("grp", "ep"), "et"), P(("grp", "ep"), "et"))

    def body(*args):
        experts, picks = args[2].shape[1], args[6].shape[2]
        peers = lax.axis_size("ep")
        fits = lax.axis_size("et") == 4 and peers & (peers - 1) == 0
        chosen = dense_body if fits and experts <= 2 * picks else routed_body
        return chosen(*args)

    return jax.shard_map(body, mesh=mesh, in_specs=in_specs, out_specs=out_specs, check_vma=False)
```

```python
import functools

import jax
import jax.numpy as jnp
from jax import lax
from jax.experimental import pallas as pl
from jax.experimental.pallas import tpu as pltpu
from jax.sharding import PartitionSpec as P


def normalize(x, mod):
    xf = x.astype(jnp.float32)
    scaled = xf * lax.rsqrt(jnp.mean(xf * xf, axis=-1, keepdims=True) + 1e-06)
    return (scaled * (1.0 + mod[0]) + mod[1]).astype(jnp.bfloat16)


def routed_section(x_full, x_cols, mod, ids, router, gate_weight, up_weight, down_weight):
    tok_rows = x_full.shape[0]
    width = x_full.shape[1]
    experts = router.shape[1]
    picks = ids.shape[1]
    n_peers = lax.axis_size("ep")
    quarter = width // lax.axis_size("et")
    slot_count = 3 * tok_rows * picks // (2 * experts)
    normed = normalize(x_full, mod)
    logits = jnp.dot(normed, router, preferred_element_type=jnp.float32)
    chosen = jax.nn.sigmoid(jnp.take_along_axis(logits, ids, axis=1))
    weight = chosen / jnp.sum(chosen, axis=1, keepdims=True)
    flat_e = ids.reshape(-1)
    onehot = (flat_e[:, None] == jnp.arange(experts, dtype=jnp.int32)).astype(jnp.int32)
    counted = jnp.cumsum(onehot, axis=0)
    slot = jnp.sum(onehot * (counted - 1), axis=1)
    repeated = jnp.repeat(normed, picks, axis=0)
    outbox = jnp.zeros((experts, slot_count, width), jnp.bfloat16).at[flat_e, slot].set(repeated)
    arrived = lax.all_to_all(outbox, "ep", split_axis=0, concat_axis=0, tiled=True)
    in_rows = arrived.reshape(n_peers * slot_count, width)
    gate = jnp.dot(in_rows, gate_weight[0], preferred_element_type=jnp.float32)
    upper = jnp.dot(in_rows, up_weight[0], preferred_element_type=jnp.float32)
    hidden = (jax.nn.silu(gate) * upper).astype(jnp.bfloat16)
    partial_out = jnp.dot(hidden, down_weight[0], preferred_element_type=jnp.float32)
    summed = lax.psum_scatter(
        partial_out.astype(jnp.bfloat16), "et", scatter_dimension=1, tiled=True
    )
    returned = lax.all_to_all(
        summed.reshape(n_peers, slot_count, quarter), "ep", split_axis=0, concat_axis=0, tiled=True
    )
    picked = returned[flat_e, slot].astype(jnp.float32).reshape(tok_rows, picks, quarter)
    velocity = jnp.sum(picked * weight[:, :, None], axis=1)
    moved = (x_cols.astype(jnp.float32) - 0.5 * velocity).astype(jnp.bfloat16)
    return (moved, velocity)


def routed_body(tokens, modulation, router, gate_weight, up_weight, down_weight, expert_ids):
    quarter = tokens.shape[1] // lax.axis_size("et")
    column_start = lax.axis_index("et") * quarter
    cols = lax.dynamic_slice_in_dim(tokens, column_start, quarter, 1)
    weights = (router, gate_weight, up_weight, down_weight)
    first, _ = routed_section(tokens, cols, modulation[0], expert_ids[0], *weights)
    full = lax.all_gather(first, "et", axis=1, tiled=True)
    second, velocity = routed_section(full, first, modulation[1], expert_ids[1], *weights)
    return (second, velocity.astype(jnp.bfloat16))


def swap(x, axis, bit):
    size = lax.axis_size(axis)
    return lax.ppermute(x, axis, [(i, i ^ bit) for i in range(size)])


LANES = 128
VMEM_LIMIT = 32 * 1024 * 1024
VMEM_MOST = 52 * 1024 * 1024
VMEM_REST = 48 * 1024 * 1024
VMEM_ALL = 63 * 1024 * 1024
VMEM = pl.BlockSpec(memory_space=pltpu.VMEM)
ANY = pl.BlockSpec(memory_space=pl.ANY)


def params(limit=VMEM_LIMIT):
    return pltpu.CompilerParams(vmem_limit_bytes=limit)


def aligned(index, size):
    return pl.ds(pl.multiple_of(index * size, size), size)


def load_kernel(n, *refs):
    in_refs, (out_ref, done_ref, sems) = refs[:n], refs[-3:]
    cols = out_ref.shape[1] // n
    copies = []
    for i, ref in enumerate(in_refs):
        to = out_ref.at[:, i * cols : (i + 1) * cols]
        copies.append(pltpu.make_async_copy(ref.at[0], to, sems.at[i]))
    for copy in copies:
        copy.start()
    for copy in copies:
        copy.wait()
    done_ref[...] = jnp.zeros_like(done_ref)


def load(*weights, after=()):
    _, rows, cols = weights[0].shape
    n = len(weights)
    return pl.pallas_call(
        functools.partial(load_kernel, n),
        in_specs=[ANY] * n + [VMEM] * len(after),
        out_specs=[VMEM] * 2,
        out_shape=[pltpu.VMEM((rows, n * cols), jnp.bfloat16), pltpu.VMEM((8, LANES), jnp.float32)],
        scratch_shapes=[pltpu.SemaphoreType.DMA((n,))],
        compiler_params=params(VMEM_MOST if n > 1 else VMEM_REST),
        cost_estimate=pl.CostEstimate(flops=0, bytes_accessed=4 * n * rows * cols, transcendentals=0),
        name="load",
    )(*weights, *after)


def relay_kernel(block_ref, done_ref, out_ref):
    out_ref[...] = block_ref[:, : out_ref.shape[1]]


def relay(block, cols, done):
    return pl.pallas_call(
        relay_kernel,
        out_shape=jax.ShapeDtypeStruct((block.shape[0], cols), block.dtype),
        compiler_params=params(),
        name="relay",
    )(block, done)


def choices(ids, peers, slots):
    rows = ids[0].shape[1]
    me = lax.axis_index("ep")
    named = []
    for one in ids:
        for k in range(peers):
            hits = [jnp.where(one[p : p + 1, :] == me ^ k, 1.0, 0.0) for p in range(one.shape[0])]
            named.append(sum(hits))
    earlier = lax.broadcasted_iota(jnp.int32, (rows, rows), 0) < lax.broadcasted_iota(jnp.int32, (rows, rows), 1)
    ahead = jnp.dot(
        jnp.concatenate(named, axis=0).astype(jnp.bfloat16),
        jnp.where(earlier, 1.0, 0.0).astype(jnp.bfloat16),
        preferred_element_type=jnp.float32,
    ).astype(jnp.int32)
    slot = lax.broadcasted_iota(jnp.int32, (slots, rows), 0)
    holds = [jnp.where((ahead[i : i + 1, :] == slot) & (row > 0.5), 1.0, 0.0) for i, row in enumerate(named)]
    return [jnp.concatenate(holds[s * peers : (s + 1) * peers], axis=0) for s in range(len(ids))]


def narrow(x):
    return x.astype(jnp.bfloat16)


def product(x, y):
    return jnp.dot(narrow(x), narrow(y), preferred_element_type=jnp.float32)


def named_experts(ids, held, experts):
    rows = ids[0].shape[1]
    flags = []
    for s, one in enumerate(ids):
        lane = lax.broadcasted_iota(jnp.int32, (LANES, rows), 0)
        hits = [jnp.where(one[p : p + 1, :] + s * experts == lane, 1.0, 0.0) for p in range(one.shape[0])]
        flags.append(product(held[s], sum(hits).T))
    return sum(flags)


CROSSING = 3


def pack_kernel(experts, tokens_ref, ids_ref, *refs):
    *out_refs, own_ref, half_ref, held_ref, sems = refs
    quarter = tokens_ref.shape[1] // 4
    half = 2 * quarter
    where = lax.axis_index("et")
    copies = [
        pltpu.make_async_copy(ids_ref, held_ref, sems.at[0]),
        pltpu.make_async_copy(tokens_ref.at[:, aligned(where & 1, quarter)], half_ref.at[:, :quarter], sems.at[1]),
        pltpu.make_async_copy(tokens_ref.at[:, aligned(where & 1 | 2, quarter)], half_ref.at[:, quarter:], sems.at[2]),
    ]
    for copy in copies:
        copy.start()
    copies[0].wait()
    ids = [held_ref[s] for s in range(held_ref.shape[0])]
    slots, peers = out_refs[0].shape[0], 1 + len(out_refs)
    held = choices(ids, peers, slots)
    flags = named_experts(ids, held, experts)
    copies[1].wait()
    copies[2].wait()
    own_ref[...] = half_ref[:, aligned(where >> 1, quarter)]
    picked = product(held[0][slots:], half_ref[...])
    for k, out_ref in enumerate(out_refs):
        cols = out_ref.shape[1] - LANES
        part = picked[k * slots : (k + 1) * slots]
        if cols < half:
            part = product(held[0][(k + 1) * slots : (k + 2) * slots], own_ref[...])
        out_ref[:, :cols] = narrow(part)
        out_ref[:, cols:] = narrow(flags[(k + 1) * slots : (k + 2) * slots])


def pack(tokens, ids, experts, slots):
    rows, width = tokens.shape
    parts = [4 if k == CROSSING else 2 for k in range(1, lax.axis_size("ep"))]
    shapes = [(slots, width // part + LANES) for part in parts] + [(rows, width // 4)]
    return pl.pallas_call(
        functools.partial(pack_kernel, experts),
        in_specs=[ANY] * 2,
        out_specs=[VMEM] * len(shapes),
        out_shape=[pltpu.VMEM(s, jnp.bfloat16) for s in shapes],
        scratch_shapes=[
            pltpu.VMEM((rows, width // 2), jnp.bfloat16),
            pltpu.VMEM(ids.shape, jnp.int32),
            pltpu.SemaphoreType.DMA((3,)),
        ],
        compiler_params=params(VMEM_ALL),
        name="pack",
    )(tokens, ids)


def own_kernel(experts, tokens_ref, ids_ref, done_ref, out_ref, flags_ref, *choice_refs):
    ids = [ids_ref[s] for s in range(ids_ref.shape[0])]
    slots = out_ref.shape[0]
    held = choices(ids, choice_refs[0].shape[0] // slots, slots)
    flags_ref[...] = narrow(named_experts(ids, held, experts)[:slots])
    out_ref[...] = narrow(product(held[0][:slots], tokens_ref[...]))
    for s, one in enumerate(held):
        choice_refs[2 * s][...] = narrow(one)
        choice_refs[2 * s + 1][...] = narrow(one.T)


def own_rows(tokens, ids, experts, slots, done):
    rows, width = tokens.shape
    total = lax.axis_size("ep") * slots
    shapes = [(slots, width), (slots, LANES)] + [(total, rows), (rows, total)] * ids.shape[0]
    return pl.pallas_call(
        functools.partial(own_kernel, experts),
        out_shape=[jax.ShapeDtypeStruct(s, jnp.bfloat16) for s in shapes],
        compiler_params=params(),
        name="own_rows",
    )(tokens, ids, done)


def front_kernel(layout, order, flips, section, experts, *refs):
    n = sum(len(block) for block in layout)
    x_refs = list(refs[:n])
    mod_ref, router_ref, pair_ref, *rest = refs[n:]
    width = pair_ref.shape[0]
    quarter = width // 4
    et = lax.axis_index("et")
    blocks = {}
    for k in order:
        blocks[k] = [(x_refs.pop(0), cols, flip) for cols, flip in layout[k]]

    def part(block, flip):
        for ref, cols, at in block:
            if cols == quarter and at == flip:
                return ref[...].astype(jnp.float32)
            if cols == 2 * quarter and at == flip & 1:
                return ref[:, aligned((et ^ flip) >> 1, quarter)].astype(jnp.float32)
            if cols == width:
                return ref[:, aligned(et ^ flip, quarter)].astype(jnp.float32)

    units, logits, squares = 0.0, 0.0, 0.0
    for flip in flips:
        xf = jnp.concatenate([part(blocks[k], flip) for k in range(len(layout))], axis=0)
        squares += jnp.sum(xf * xf, axis=1, keepdims=True)
        where = aligned(et ^ flip, quarter)
        shift = mod_ref[section, 1:2, where]
        head = narrow(shift).astype(jnp.float32)
        blank = jnp.zeros((6, quarter), jnp.float32)
        lhs = [xf * (1.0 + mod_ref[section, 0:1, where]), head, shift - head, blank]
        lhs = narrow(jnp.concatenate(lhs, axis=0))
        units += jnp.dot(lhs, pair_ref[where, :], preferred_element_type=jnp.float32)
        logits += lax.dot_general(
            lhs, router_ref[:, where], (((1,), (1,)), ((), ())), preferred_element_type=jnp.float32
        )
    if len(rest) == 3:
        rest[0][...], rest[1][...], rest[2][...] = units, logits, squares
        return
    *flag_refs, units_ref, logits_ref, squares_ref, out_ref = rest
    rows, hidden = out_ref.shape
    scale = lax.rsqrt((squares + squares_ref[...]) / width + 1e-06)

    def scaled(x):
        return x[:rows] * scale + (x[rows : rows + 1] + x[rows + 1 : rows + 2])

    units, logits = scaled(units + units_ref[...]), scaled(logits + logits_ref[...])
    count = logits.shape[1]
    lane = lax.broadcasted_iota(jnp.int32, logits.shape, 1)
    flags = [flag_refs[order.index(k)] for k in range(len(layout))]
    flags = [f[:, f.shape[1] - LANES :].astype(jnp.float32) for f in flags]
    flags = jnp.concatenate(flags, axis=0)[:, section * experts : section * experts + count]
    chosen = jnp.where(flags > 0.5, jax.nn.sigmoid(logits), 0.0)
    mine = jnp.sum(jnp.where(lane == lax.axis_index("ep"), chosen, 0.0), axis=1, keepdims=True)
    used = jnp.max(flags, axis=1, keepdims=True) > 0.5
    weight = jnp.where(used, mine / jnp.sum(chosen, axis=1, keepdims=True), 0.0)
    gate, upper = units[:, :hidden], units[:, hidden:]
    out = jnp.where(used, gate / (1.0 + jnp.exp(-gate)) * upper * weight, 0.0)
    out_ref[...] = narrow(out)


def half_front(blocks, flips, extra, shapes, order, section, mod, router, pair):
    xs = [x for k in order for x, _, _ in blocks[k]]
    layout = [[piece[1:] for piece in block] for block in blocks]
    rows, (width, units) = shapes[0].shape[0], pair.shape
    return pl.pallas_call(
        functools.partial(front_kernel, layout, order, flips, section, router.shape[0]),
        in_specs=[VMEM] * (len(xs) + 3 + len(extra)),
        out_shape=shapes,
        compiler_params=params(),
        cost_estimate=pl.CostEstimate(
            flops=rows * width * units, bytes_accessed=width * units, transcendentals=0
        ),
        name="front",
    )(*xs, mod, router, pair, *extra)


def front(blocks, flags, order, section, mod, router, pair):
    rows = sum(f.shape[0] for f in flags)
    units, experts = pair.shape[1], router.shape[0]
    width = pair.shape[0]
    common = (order, section, mod, router, pair)
    here = [[p for p in block if p[1] == width or p[2] & 1 == 0] for block in blocks]
    there = [[p for p in block if p[1] == width or p[2] & 1] for block in blocks]
    shapes = [jax.ShapeDtypeStruct(s, jnp.float32) for s in ((rows + 8, units), (rows + 8, experts), (rows, 1))]
    sums = half_front(here, (0, 2), [], shapes, *common)
    shapes = [jax.ShapeDtypeStruct((rows, units // 2), jnp.bfloat16)]
    return half_front(there, (1, 3), [flags[k] for k in order] + list(sums), shapes, *common)[0]


def down_kernel(flip, n_adds, hidden_ref, down_ref, *refs):
    adds, outs = refs[:n_adds], refs[n_adds:]
    quarter = outs[0].shape[1]
    weights = down_ref[:, aligned(lax.axis_index("et") ^ flip, quarter)]
    product = jnp.dot(hidden_ref[...], weights, preferred_element_type=jnp.float32)
    for ref in adds:
        product += ref[...].astype(jnp.float32)
    rows = outs[0].shape[0]
    for k, out in enumerate(outs):
        out[...] = product[k * rows : (k + 1) * rows].astype(out.dtype)


def down(hidden, w_down, flip, blocks, adds=(), dtype=jnp.bfloat16):
    units, width = w_down.shape
    rows, quarter = hidden.shape[0], width // 4
    return pl.pallas_call(
        functools.partial(down_kernel, flip, len(adds)),
        in_specs=[VMEM] * (2 + len(adds)),
        out_shape=[jax.ShapeDtypeStruct((rows // blocks, quarter), dtype)] * blocks,
        compiler_params=params(),
        cost_estimate=pl.CostEstimate(
            flops=2 * rows * units * quarter, bytes_accessed=2 * units * quarter, transcendentals=0
        ),
        name="down",
    )(hidden, w_down, *adds)


def add_kernel(keep_ref, came_ref, *outs):
    total = keep_ref[...] + came_ref[...].astype(jnp.float32)
    rows = outs[0].shape[0]
    for k, out in enumerate(outs):
        out[...] = total[k * rows : (k + 1) * rows].astype(out.dtype)


def add(keep, came, count):
    shape = (keep.shape[0] // count, keep.shape[1])
    return pl.pallas_call(
        add_kernel,
        out_shape=[jax.ShapeDtypeStruct(shape, jnp.bfloat16)] * count,
        compiler_params=params(),
        name="add",
    )(keep, came)


def move_kernel(n_came, last, own_ref, back_ref, pick_ref, *refs):
    came, outs = refs[:n_came], refs[n_came:]
    rows = [ref[...].astype(jnp.float32) for ref in came]
    velocity = product(back_ref[...], jnp.concatenate(rows, axis=0))
    moved = narrow(own_ref[...].astype(jnp.float32) - 0.5 * velocity)
    outs[0][...] = moved
    if last:
        outs[1][...] = narrow(velocity)
    else:
        slots = came[0].shape[0]
        picked = product(pick_ref[...], moved)
        for k, out in enumerate(outs[1:]):
            out[...] = narrow(picked[k * slots : (k + 1) * slots])


def move(own, back, pick, came, last):
    shapes = [own.shape] + ([own.shape] if last else [c.shape for c in came])
    return pl.pallas_call(
        functools.partial(move_kernel, len(came), last),
        out_shape=[jax.ShapeDtypeStruct(s, jnp.bfloat16) for s in shapes],
        compiler_params=params(),
        name="move",
    )(own, back, pick, *came)


def sum_back(hidden, w_down, own, back, pick, last_section):
    peers = lax.axis_size("ep")
    some = peers // 2
    far = swap(down(hidden, w_down, 3, 1)[0], "et", 1)
    near = swap(down(hidden, w_down, 1, 1)[0], "et", 1)
    first, last = add(down(hidden, w_down, 2, 1, (), jnp.float32)[0], far, 2)
    last, first = swap(last, "et", 2), swap(first, "et", 2)
    keep_first, keep_last = down(hidden, w_down, 0, 2, (near,), jnp.float32)
    later = add(keep_last, last, peers - some)
    blocks = add(keep_first, first, some) + later
    came = [swap(b, "ep", k) if k else b for k, b in enumerate(blocks)]
    return move(own, back, pick, came, last_section)


def spread(block, quarter):
    side = swap(block, "et", 2)
    near, far = swap(block, "et", 1), swap(side, "et", 1)
    return [(block, quarter, 0), (side, quarter, 2), (near, quarter, 1), (far, quarter, 3)]


def dense_body(tokens, modulation, router, gate_weight, up_weight, down_weight, expert_ids):
    rows, width = tokens.shape
    half, quarter = width // 2, width // 4
    router = router.T
    experts = router.shape[0]
    peers = lax.axis_size("ep")
    slots = 3 * rows * expert_ids.shape[2] // (2 * experts)
    ids = expert_ids.transpose(0, 2, 1)

    *packed, own = pack(tokens, ids, experts, slots)
    pair, pair_done = load(gate_weight, up_weight)
    order = [*range(1, len(packed) + 1)]
    came = {k: swap(packed[k - 1], "ep", k) for k in order}
    crossing = relay(came[CROSSING], quarter, pair_done)
    w_down, down_done = load(down_weight, after=(crossing,))
    mine, flags, *choice = own_rows(tokens, ids, experts, slots, down_done)
    pick, back = choice[2], choice[1::2]
    pieces = {0: [(mine, width, 0)], CROSSING: spread(crossing, quarter)}
    for k in order:
        if k != CROSSING:
            f = relay(came[k], half, flags)
            pieces[k] = [(f, half, 0), (swap(f, "et", 1), half, 1)]
    flags = [flags] + [came[k] for k in sorted(order)]
    blocks = [pieces[k] for k in sorted(pieces)]
    hidden = front(blocks, flags, order + [0], 0, modulation, router, pair)
    own, *sent = sum_back(hidden, w_down, own, back[0], pick, False)

    blocks = [spread(swap(b, "ep", k) if k else b, quarter) for k, b in enumerate(sent)]
    hidden = front(blocks, flags, order[1:] + [1, 0], 1, modulation, router, pair)
    return tuple(sum_back(hidden, w_down, own, back[1], pick, True))


def solution(mesh):
    in_specs = (
        P(("grp", "ep"), None),
        P(),
        P(),
        P("ep", None, "et"),
        P("ep", None, "et"),
        P("ep", "et", None),
        P(None, ("grp", "ep"), None),
    )
    out_specs = (P(("grp", "ep"), "et"), P(("grp", "ep"), "et"))

    def body(*args):
        experts, picks = args[2].shape[1], args[6].shape[2]
        peers = lax.axis_size("ep")
        fits = lax.axis_size("et") == 4 and peers >= 4 and peers & (peers - 1) == 0
        chosen = dense_body if fits and experts <= 2 * picks else routed_body
        return chosen(*args)

    return jax.shard_map(body, mesh=mesh, in_specs=in_specs, out_specs=out_specs, check_vma=False)
```

```python
import functools

import jax
import jax.numpy as jnp
from jax import lax
from jax.experimental import pallas as pl
from jax.experimental.pallas import tpu as pltpu
from jax.sharding import PartitionSpec as P


def normalize(x, mod):
    xf = x.astype(jnp.float32)
    scaled = xf * lax.rsqrt(jnp.mean(xf * xf, axis=-1, keepdims=True) + 1e-06)
    return (scaled * (1.0 + mod[0]) + mod[1]).astype(jnp.bfloat16)


def routed_section(x_full, x_cols, mod, ids, router, gate_weight, up_weight, down_weight):
    tok_rows = x_full.shape[0]
    width = x_full.shape[1]
    experts = router.shape[1]
    picks = ids.shape[1]
    n_peers = lax.axis_size("ep")
    quarter = width // lax.axis_size("et")
    slot_count = 3 * tok_rows * picks // (2 * experts)
    normed = normalize(x_full, mod)
    logits = jnp.dot(normed, router, preferred_element_type=jnp.float32)
    chosen = jax.nn.sigmoid(jnp.take_along_axis(logits, ids, axis=1))
    weight = chosen / jnp.sum(chosen, axis=1, keepdims=True)
    flat_e = ids.reshape(-1)
    onehot = (flat_e[:, None] == jnp.arange(experts, dtype=jnp.int32)).astype(jnp.int32)
    counted = jnp.cumsum(onehot, axis=0)
    slot = jnp.sum(onehot * (counted - 1), axis=1)
    repeated = jnp.repeat(normed, picks, axis=0)
    outbox = jnp.zeros((experts, slot_count, width), jnp.bfloat16).at[flat_e, slot].set(repeated)
    arrived = lax.all_to_all(outbox, "ep", split_axis=0, concat_axis=0, tiled=True)
    in_rows = arrived.reshape(n_peers * slot_count, width)
    gate = jnp.dot(in_rows, gate_weight[0], preferred_element_type=jnp.float32)
    upper = jnp.dot(in_rows, up_weight[0], preferred_element_type=jnp.float32)
    hidden = (jax.nn.silu(gate) * upper).astype(jnp.bfloat16)
    partial_out = jnp.dot(hidden, down_weight[0], preferred_element_type=jnp.float32)
    summed = lax.psum_scatter(
        partial_out.astype(jnp.bfloat16), "et", scatter_dimension=1, tiled=True
    )
    returned = lax.all_to_all(
        summed.reshape(n_peers, slot_count, quarter), "ep", split_axis=0, concat_axis=0, tiled=True
    )
    picked = returned[flat_e, slot].astype(jnp.float32).reshape(tok_rows, picks, quarter)
    velocity = jnp.sum(picked * weight[:, :, None], axis=1)
    moved = (x_cols.astype(jnp.float32) - 0.5 * velocity).astype(jnp.bfloat16)
    return (moved, velocity)


def routed_body(tokens, modulation, router, gate_weight, up_weight, down_weight, expert_ids):
    quarter = tokens.shape[1] // lax.axis_size("et")
    column_start = lax.axis_index("et") * quarter
    cols = lax.dynamic_slice_in_dim(tokens, column_start, quarter, 1)
    weights = (router, gate_weight, up_weight, down_weight)
    first, _ = routed_section(tokens, cols, modulation[0], expert_ids[0], *weights)
    full = lax.all_gather(first, "et", axis=1, tiled=True)
    second, velocity = routed_section(full, first, modulation[1], expert_ids[1], *weights)
    return (second, velocity.astype(jnp.bfloat16))


def swap(x, axis, bit):
    size = lax.axis_size(axis)
    return lax.ppermute(x, axis, [(i, i ^ bit) for i in range(size)])


LANES = 128
VMEM_LIMIT = 32 * 1024 * 1024
VMEM_MOST = 52 * 1024 * 1024
VMEM_ALL = 63 * 1024 * 1024
VMEM = pl.BlockSpec(memory_space=pltpu.VMEM)
ANY = pl.BlockSpec(memory_space=pl.ANY)


def params(limit=VMEM_LIMIT):
    return pltpu.CompilerParams(vmem_limit_bytes=limit)


def aligned(index, size):
    return pl.ds(pl.multiple_of(index * size, size), size)


def load_kernel(gate_ref, up_ref, down_ref, pair_ref, out_ref, done_ref, sems):
    hidden = gate_ref.shape[2]
    copies = [
        pltpu.make_async_copy(gate_ref.at[0], pair_ref.at[:, :hidden], sems.at[0]),
        pltpu.make_async_copy(up_ref.at[0], pair_ref.at[:, hidden:], sems.at[1]),
        pltpu.make_async_copy(down_ref.at[0], out_ref, sems.at[2]),
    ]
    for copy in copies:
        copy.start()
    for copy in copies:
        copy.wait()
    done_ref[...] = jnp.zeros_like(done_ref)


def load(gate, up, down):
    _, width, hidden = gate.shape
    return pl.pallas_call(
        load_kernel,
        in_specs=[ANY] * 3,
        out_specs=[VMEM] * 3,
        out_shape=[
            pltpu.VMEM((width, 2 * hidden), jnp.bfloat16),
            pltpu.VMEM((hidden, width), jnp.bfloat16),
            pltpu.VMEM((8, LANES), jnp.float32),
        ],
        scratch_shapes=[pltpu.SemaphoreType.DMA((3,))],
        compiler_params=params(VMEM_MOST),
        cost_estimate=pl.CostEstimate(flops=0, bytes_accessed=12 * width * hidden, transcendentals=0),
        name="load",
    )(gate, up, down)


def relay_kernel(block_ref, done_ref, out_ref):
    out_ref[...] = block_ref[:, : out_ref.shape[1]]


def relay(block, cols, done):
    return pl.pallas_call(
        relay_kernel,
        out_shape=jax.ShapeDtypeStruct((block.shape[0], cols), block.dtype),
        compiler_params=params(),
        name="relay",
    )(block, done)


def choices(ids, peers, slots):
    rows = ids[0].shape[1]
    me = lax.axis_index("ep")
    named = []
    for one in ids:
        for k in range(peers):
            hits = [jnp.where(one[p : p + 1, :] == me ^ k, 1.0, 0.0) for p in range(one.shape[0])]
            named.append(sum(hits))
    earlier = lax.broadcasted_iota(jnp.int32, (rows, rows), 0) < lax.broadcasted_iota(jnp.int32, (rows, rows), 1)
    ahead = jnp.dot(
        jnp.concatenate(named, axis=0).astype(jnp.bfloat16),
        jnp.where(earlier, 1.0, 0.0).astype(jnp.bfloat16),
        preferred_element_type=jnp.float32,
    ).astype(jnp.int32)
    slot = lax.broadcasted_iota(jnp.int32, (slots, rows), 0)
    holds = [jnp.where((ahead[i : i + 1, :] == slot) & (row > 0.5), 1.0, 0.0) for i, row in enumerate(named)]
    return [jnp.concatenate(holds[s * peers : (s + 1) * peers], axis=0) for s in range(len(ids))]


def narrow(x):
    return x.astype(jnp.bfloat16)


def product(x, y):
    return jnp.dot(narrow(x), narrow(y), preferred_element_type=jnp.float32)


def named_experts(ids, held, experts):
    rows = ids[0].shape[1]
    flags = []
    for s, one in enumerate(ids):
        lane = lax.broadcasted_iota(jnp.int32, (LANES, rows), 0)
        hits = [jnp.where(one[p : p + 1, :] + s * experts == lane, 1.0, 0.0) for p in range(one.shape[0])]
        flags.append(product(held[s], sum(hits).T))
    return sum(flags)


def pack_kernel(experts, tokens_ref, ids_ref, *refs):
    *out_refs, own_ref, half_ref, held_ref, sems = refs
    quarter = tokens_ref.shape[1] // 4
    half = 2 * quarter
    where = lax.axis_index("et")
    copies = [
        pltpu.make_async_copy(ids_ref, held_ref, sems.at[0]),
        pltpu.make_async_copy(tokens_ref.at[:, aligned(where & 1, quarter)], half_ref.at[:, :quarter], sems.at[1]),
        pltpu.make_async_copy(tokens_ref.at[:, aligned(where & 1 | 2, quarter)], half_ref.at[:, quarter:], sems.at[2]),
    ]
    for copy in copies:
        copy.start()
    copies[0].wait()
    ids = [held_ref[s] for s in range(held_ref.shape[0])]
    slots, peers = out_refs[0].shape[0], 1 + len(out_refs)
    held = choices(ids, peers, slots)
    flags = named_experts(ids, held, experts)
    copies[1].wait()
    copies[2].wait()
    own_ref[...] = half_ref[:, aligned(where >> 1, quarter)]
    picked = product(held[0][slots:], half_ref[...])
    for k, out_ref in enumerate(out_refs):
        out_ref[:, :half] = narrow(picked[k * slots : (k + 1) * slots])
        out_ref[:, half:] = narrow(flags[(k + 1) * slots : (k + 2) * slots])


def pack(tokens, ids, experts, slots):
    rows, width = tokens.shape
    others = lax.axis_size("ep") - 1
    shapes = [(slots, width // 2 + LANES)] * others + [(rows, width // 4)]
    return pl.pallas_call(
        functools.partial(pack_kernel, experts),
        in_specs=[ANY] * 2,
        out_specs=[VMEM] * len(shapes),
        out_shape=[pltpu.VMEM(s, jnp.bfloat16) for s in shapes],
        scratch_shapes=[
            pltpu.VMEM((rows, width // 2), jnp.bfloat16),
            pltpu.VMEM(ids.shape, jnp.int32),
            pltpu.SemaphoreType.DMA((3,)),
        ],
        compiler_params=params(VMEM_ALL),
        name="pack",
    )(tokens, ids)


def own_kernel(experts, tokens_ref, ids_ref, done_ref, out_ref, flags_ref, *choice_refs):
    ids = [ids_ref[s] for s in range(ids_ref.shape[0])]
    slots = out_ref.shape[0]
    held = choices(ids, choice_refs[0].shape[0] // slots, slots)
    flags_ref[...] = narrow(named_experts(ids, held, experts)[:slots])
    out_ref[...] = narrow(product(held[0][:slots], tokens_ref[...]))
    for s, one in enumerate(held):
        choice_refs[2 * s][...] = narrow(one)
        choice_refs[2 * s + 1][...] = narrow(one.T)


def own_rows(tokens, ids, experts, slots, done):
    rows, width = tokens.shape
    total = lax.axis_size("ep") * slots
    shapes = [(slots, width), (slots, LANES)] + [(total, rows), (rows, total)] * ids.shape[0]
    return pl.pallas_call(
        functools.partial(own_kernel, experts),
        out_shape=[jax.ShapeDtypeStruct(s, jnp.bfloat16) for s in shapes],
        compiler_params=params(),
        name="own_rows",
    )(tokens, ids, done)


def front_kernel(layout, order, flips, section, experts, *refs):
    n = sum(len(block) for block in layout)
    x_refs = list(refs[:n])
    mod_ref, router_ref, pair_ref, *rest = refs[n:]
    width = pair_ref.shape[0]
    quarter = width // 4
    et = lax.axis_index("et")
    blocks = {}
    for k in order:
        blocks[k] = [(x_refs.pop(0), cols, flip) for cols, flip in layout[k]]

    def part(block, flip):
        for ref, cols, at in block:
            if cols == quarter and at == flip:
                return ref[...].astype(jnp.float32)
            if cols == 2 * quarter and at == flip & 1:
                return ref[:, aligned((et ^ flip) >> 1, quarter)].astype(jnp.float32)
            if cols == width:
                return ref[:, aligned(et ^ flip, quarter)].astype(jnp.float32)

    units, logits, squares = 0.0, 0.0, 0.0
    for flip in flips:
        xf = jnp.concatenate([part(blocks[k], flip) for k in range(len(layout))], axis=0)
        squares += jnp.sum(xf * xf, axis=1, keepdims=True)
        where = aligned(et ^ flip, quarter)
        shift = mod_ref[section, 1:2, where]
        head = narrow(shift).astype(jnp.float32)
        blank = jnp.zeros((6, quarter), jnp.float32)
        lhs = [xf * (1.0 + mod_ref[section, 0:1, where]), head, shift - head, blank]
        lhs = narrow(jnp.concatenate(lhs, axis=0))
        units += jnp.dot(lhs, pair_ref[where, :], preferred_element_type=jnp.float32)
        logits += lax.dot_general(
            lhs, router_ref[:, where], (((1,), (1,)), ((), ())), preferred_element_type=jnp.float32
        )
    if len(rest) == 3:
        rest[0][...], rest[1][...], rest[2][...] = units, logits, squares
        return
    *flag_refs, units_ref, logits_ref, squares_ref, out_ref = rest
    rows, hidden = out_ref.shape
    scale = lax.rsqrt((squares + squares_ref[...]) / width + 1e-06)

    def scaled(x):
        return x[:rows] * scale + (x[rows : rows + 1] + x[rows + 1 : rows + 2])

    units, logits = scaled(units + units_ref[...]), scaled(logits + logits_ref[...])
    count = logits.shape[1]
    lane = lax.broadcasted_iota(jnp.int32, logits.shape, 1)
    flags = [flag_refs[order.index(k)] for k in range(len(layout))]
    flags = [f[:, f.shape[1] - LANES :].astype(jnp.float32) for f in flags]
    flags = jnp.concatenate(flags, axis=0)[:, section * experts : section * experts + count]
    chosen = jnp.where(flags > 0.5, jax.nn.sigmoid(logits), 0.0)
    mine = jnp.sum(jnp.where(lane == lax.axis_index("ep"), chosen, 0.0), axis=1, keepdims=True)
    used = jnp.max(flags, axis=1, keepdims=True) > 0.5
    weight = jnp.where(used, mine / jnp.sum(chosen, axis=1, keepdims=True), 0.0)
    gate, upper = units[:, :hidden], units[:, hidden:]
    out = jnp.where(used, gate / (1.0 + jnp.exp(-gate)) * upper * weight, 0.0)
    out_ref[...] = narrow(out)


def half_front(blocks, flips, extra, shapes, order, section, mod, router, pair):
    xs = [x for k in order for x, _, _ in blocks[k]]
    layout = [[piece[1:] for piece in block] for block in blocks]
    rows, (width, units) = shapes[0].shape[0], pair.shape
    return pl.pallas_call(
        functools.partial(front_kernel, layout, order, flips, section, router.shape[0]),
        in_specs=[VMEM] * (len(xs) + 3 + len(extra)),
        out_shape=shapes,
        compiler_params=params(),
        cost_estimate=pl.CostEstimate(
            flops=rows * width * units, bytes_accessed=width * units, transcendentals=0
        ),
        name="front",
    )(*xs, mod, router, pair, *extra)


def front(blocks, flags, order, section, mod, router, pair):
    rows = sum(f.shape[0] for f in flags)
    units, experts = pair.shape[1], router.shape[0]
    width = pair.shape[0]
    common = (order, section, mod, router, pair)
    here = [[p for p in block if p[1] == width or p[2] & 1 == 0] for block in blocks]
    there = [[p for p in block if p[1] == width or p[2] & 1] for block in blocks]
    shapes = [jax.ShapeDtypeStruct(s, jnp.float32) for s in ((rows + 8, units), (rows + 8, experts), (rows, 1))]
    sums = half_front(here, (0, 2), [], shapes, *common)
    shapes = [jax.ShapeDtypeStruct((rows, units // 2), jnp.bfloat16)]
    return half_front(there, (1, 3), [flags[k] for k in order] + list(sums), shapes, *common)[0]


def store_blocks(total, groups, outs):
    rows = total.shape[0] // sum(len(group) for group in groups)
    for group, out in zip(groups, outs):
        blocks = [total[k * rows : (k + 1) * rows] for k in group]
        out[...] = jnp.concatenate(blocks, axis=0).astype(out.dtype)


def shapes_of(rows, cols, groups, types):
    slots = rows // sum(len(group) for group in groups)
    return [jax.ShapeDtypeStruct((slots * len(group), cols), t) for group, t in zip(groups, types)]


def down_kernel(flip, n_adds, groups, hidden_ref, down_ref, *refs):
    adds, outs = refs[:n_adds], refs[n_adds:]
    quarter = outs[0].shape[1]
    weights = down_ref[:, aligned(lax.axis_index("et") ^ flip, quarter)]
    total = jnp.dot(hidden_ref[...], weights, preferred_element_type=jnp.float32)
    for ref in adds:
        total += ref[...].astype(jnp.float32)
    store_blocks(total, groups, outs)


def down(hidden, w_down, flip, adds=(), groups=((0,),), types=(jnp.bfloat16,)):
    units, width = w_down.shape
    rows, quarter = hidden.shape[0], width // 4
    return pl.pallas_call(
        functools.partial(down_kernel, flip, len(adds), groups),
        in_specs=[VMEM] * (2 + len(adds)),
        out_shape=shapes_of(rows, quarter, groups, types),
        compiler_params=params(),
        cost_estimate=pl.CostEstimate(
            flops=2 * rows * units * quarter, bytes_accessed=2 * units * quarter, transcendentals=0
        ),
        name="down",
    )(hidden, w_down, *adds)


def add_kernel(groups, keep_ref, came_ref, *outs):
    store_blocks(keep_ref[...] + came_ref[...].astype(jnp.float32), groups, outs)


def add(keep, came, groups):
    return pl.pallas_call(
        functools.partial(add_kernel, groups),
        out_shape=shapes_of(*keep.shape, groups, [jnp.bfloat16] * len(groups)),
        compiler_params=params(),
        name="add",
    )(keep, came)


def diagonal(x, k, flip):
    n_ep, n_et = lax.axis_size("ep"), lax.axis_size("et")
    pairs = [(e * n_et + t, (e ^ k) * n_et + (t ^ flip)) for e in range(n_ep) for t in range(n_et)]
    return lax.ppermute(x, ("ep", "et"), pairs)


def move_kernel(order, last, own_ref, back_ref, pick_ref, extra_ref, *refs):
    came, outs = refs[: len(order)], refs[len(order) :]
    rows = [came[order.index(k)][...].astype(jnp.float32) for k in range(len(order))]
    rows[DIRECT] += extra_ref[...].astype(jnp.float32)
    velocity = product(back_ref[...], jnp.concatenate(rows, axis=0))
    moved = narrow(own_ref[...].astype(jnp.float32) - 0.5 * velocity)
    outs[0][...] = moved
    if last:
        outs[1][...] = narrow(velocity)
    else:
        slots = came[0].shape[0]
        picked = product(pick_ref[...], moved)
        for k, out in enumerate(outs[1:]):
            out[...] = narrow(picked[k * slots : (k + 1) * slots])


def move(own, back, pick, extra, came, order, last):
    shapes = [own.shape] + ([own.shape] if last else [c.shape for c in came])
    return pl.pallas_call(
        functools.partial(move_kernel, order, last),
        out_shape=[jax.ShapeDtypeStruct(s, jnp.bfloat16) for s in shapes],
        compiler_params=params(),
        name="move",
    )(own, back, pick, extra, *[came[k] for k in order])


DIRECT = 2


def sum_back(hidden, w_down, own, back, pick, last):
    peers = lax.axis_size("ep")
    rest = tuple(k for k in range(peers) if k != DIRECT)
    groups = (rest, (DIRECT,))
    (far,), (near,) = down(hidden, w_down, 3), down(hidden, w_down, 1)
    far, near = swap(far, "et", 1), swap(near, "et", 1)
    (crossing,) = down(hidden, w_down, 2, types=[jnp.float32])
    crossing, beside = add(crossing, far, groups)
    crossed, extra = swap(crossing, "et", 2), diagonal(beside, DIRECT, 2)
    kept, straight = down(hidden, w_down, 0, (near,), groups, [jnp.float32, jnp.bfloat16])
    blocks = dict(zip(rest, add(kept, crossed, [(i,) for i in range(len(rest))])))
    blocks[DIRECT] = straight
    came = [swap(blocks[k], "ep", k) if k else blocks[k] for k in range(peers)]
    order = [*range(2, peers), 1, 0]
    return move(own, back, pick, extra, came, order, last)


def spread(block, quarter):
    side = swap(block, "et", 2)
    near, far = swap(block, "et", 1), swap(side, "et", 1)
    return [(block, quarter, 0), (side, quarter, 2), (near, quarter, 1), (far, quarter, 3)]


def dense_body(tokens, modulation, router, gate_weight, up_weight, down_weight, expert_ids):
    rows, width = tokens.shape
    half, quarter = width // 2, width // 4
    router = router.T
    experts = router.shape[0]
    peers = lax.axis_size("ep")
    slots = 3 * rows * expert_ids.shape[2] // (2 * experts)
    ids = expert_ids.transpose(0, 2, 1)

    *packed, own = pack(tokens, ids, experts, slots)
    pair, w_down, done = load(gate_weight, up_weight, down_weight)
    mine, flags, *choice = own_rows(tokens, ids, experts, slots, done)
    pick, back = choice[2], choice[1::2]
    order = [*range(2, len(packed) + 1), 1]
    came = {k: swap(packed[k - 1], "ep", k) for k in order}
    halves = {k: relay(came[k], half, flags) for k in order}
    others = {k: swap(halves[k], "et", 1) for k in order}
    flags = [flags] + [came[k] for k in sorted(order)]
    blocks = [[(mine, width, 0)]] + [[(halves[k], half, 0), (others[k], half, 1)] for k in sorted(order)]
    hidden = front(blocks, flags, order + [0], 0, modulation, router, pair)
    own, *sent = sum_back(hidden, w_down, own, back[0], pick, False)

    blocks = [spread(swap(b, "ep", k) if k else b, quarter) for k, b in enumerate(sent)]
    hidden = front(blocks, flags, order + [0], 1, modulation, router, pair)
    return tuple(sum_back(hidden, w_down, own, back[1], pick, True))


def solution(mesh):
    in_specs = (
        P(("grp", "ep"), None),
        P(),
        P(),
        P("ep", None, "et"),
        P("ep", None, "et"),
        P("ep", "et", None),
        P(None, ("grp", "ep"), None),
    )
    out_specs = (P(("grp", "ep"), "et"), P(("grp", "ep"), "et"))

    def body(*args):
        experts, picks = args[2].shape[1], args[6].shape[2]
        peers = lax.axis_size("ep")
        fits = lax.axis_size("et") == 4 and peers >= 4 and peers & (peers - 1) == 0
        chosen = dense_body if fits and experts <= 2 * picks else routed_body
        return chosen(*args)

    return jax.shard_map(body, mesh=mesh, in_specs=in_specs, out_specs=out_specs, check_vma=False)
```

```python
import functools

import jax
import jax.numpy as jnp
from jax import lax
from jax.experimental import pallas as pl
from jax.experimental.pallas import tpu as pltpu
from jax.sharding import PartitionSpec as P


def normalize(x, mod):
    xf = x.astype(jnp.float32)
    scaled = xf * lax.rsqrt(jnp.mean(xf * xf, axis=-1, keepdims=True) + 1e-06)
    return (scaled * (1.0 + mod[0]) + mod[1]).astype(jnp.bfloat16)


def routed_section(x_full, x_cols, mod, ids, router, gate_weight, up_weight, down_weight):
    tok_rows = x_full.shape[0]
    width = x_full.shape[1]
    experts = router.shape[1]
    picks = ids.shape[1]
    n_peers = lax.axis_size("ep")
    quarter = width // lax.axis_size("et")
    slot_count = 3 * tok_rows * picks // (2 * experts)
    normed = normalize(x_full, mod)
    logits = jnp.dot(normed, router, preferred_element_type=jnp.float32)
    chosen = jax.nn.sigmoid(jnp.take_along_axis(logits, ids, axis=1))
    weight = chosen / jnp.sum(chosen, axis=1, keepdims=True)
    flat_e = ids.reshape(-1)
    onehot = (flat_e[:, None] == jnp.arange(experts, dtype=jnp.int32)).astype(jnp.int32)
    counted = jnp.cumsum(onehot, axis=0)
    slot = jnp.sum(onehot * (counted - 1), axis=1)
    repeated = jnp.repeat(normed, picks, axis=0)
    outbox = jnp.zeros((experts, slot_count, width), jnp.bfloat16).at[flat_e, slot].set(repeated)
    arrived = lax.all_to_all(outbox, "ep", split_axis=0, concat_axis=0, tiled=True)
    in_rows = arrived.reshape(n_peers * slot_count, width)
    gate = jnp.dot(in_rows, gate_weight[0], preferred_element_type=jnp.float32)
    upper = jnp.dot(in_rows, up_weight[0], preferred_element_type=jnp.float32)
    hidden = (jax.nn.silu(gate) * upper).astype(jnp.bfloat16)
    partial_out = jnp.dot(hidden, down_weight[0], preferred_element_type=jnp.float32)
    summed = lax.psum_scatter(
        partial_out.astype(jnp.bfloat16), "et", scatter_dimension=1, tiled=True
    )
    returned = lax.all_to_all(
        summed.reshape(n_peers, slot_count, quarter), "ep", split_axis=0, concat_axis=0, tiled=True
    )
    picked = returned[flat_e, slot].astype(jnp.float32).reshape(tok_rows, picks, quarter)
    velocity = jnp.sum(picked * weight[:, :, None], axis=1)
    moved = (x_cols.astype(jnp.float32) - 0.5 * velocity).astype(jnp.bfloat16)
    return (moved, velocity)


def routed_body(tokens, modulation, router, gate_weight, up_weight, down_weight, expert_ids):
    quarter = tokens.shape[1] // lax.axis_size("et")
    column_start = lax.axis_index("et") * quarter
    cols = lax.dynamic_slice_in_dim(tokens, column_start, quarter, 1)
    weights = (router, gate_weight, up_weight, down_weight)
    first, _ = routed_section(tokens, cols, modulation[0], expert_ids[0], *weights)
    full = lax.all_gather(first, "et", axis=1, tiled=True)
    second, velocity = routed_section(full, first, modulation[1], expert_ids[1], *weights)
    return (second, velocity.astype(jnp.bfloat16))


def swap(x, axis, bit):
    size = lax.axis_size(axis)
    return lax.ppermute(x, axis, [(i, i ^ bit) for i in range(size)])


LANES = 128
VMEM_LIMIT = 32 * 1024 * 1024
VMEM_MOST = 52 * 1024 * 1024
VMEM_ALL = 63 * 1024 * 1024
VMEM = pl.BlockSpec(memory_space=pltpu.VMEM)
ANY = pl.BlockSpec(memory_space=pl.ANY)


def params(limit=VMEM_LIMIT):
    return pltpu.CompilerParams(vmem_limit_bytes=limit)


def aligned(index, size):
    return pl.ds(pl.multiple_of(index * size, size), size)


def load_kernel(gate_ref, up_ref, down_ref, pair_ref, out_ref, done_ref, sems):
    hidden = gate_ref.shape[2]
    copies = [
        pltpu.make_async_copy(gate_ref.at[0], pair_ref.at[:, :hidden], sems.at[0]),
        pltpu.make_async_copy(up_ref.at[0], pair_ref.at[:, hidden:], sems.at[1]),
        pltpu.make_async_copy(down_ref.at[0], out_ref, sems.at[2]),
    ]
    for copy in copies:
        copy.start()
    for copy in copies:
        copy.wait()
    done_ref[...] = jnp.zeros_like(done_ref)


def load(gate, up, down):
    _, width, hidden = gate.shape
    return pl.pallas_call(
        load_kernel,
        in_specs=[ANY] * 3,
        out_specs=[VMEM] * 3,
        out_shape=[
            pltpu.VMEM((width, 2 * hidden), jnp.bfloat16),
            pltpu.VMEM((hidden, width), jnp.bfloat16),
            pltpu.VMEM((8, LANES), jnp.float32),
        ],
        scratch_shapes=[pltpu.SemaphoreType.DMA((3,))],
        compiler_params=params(VMEM_MOST),
        cost_estimate=pl.CostEstimate(flops=0, bytes_accessed=12 * width * hidden, transcendentals=0),
        name="load",
    )(gate, up, down)


def relay_kernel(block_ref, done_ref, out_ref):
    out_ref[...] = block_ref[:, : out_ref.shape[1]]


def relay(block, cols, done):
    return pl.pallas_call(
        relay_kernel,
        out_shape=jax.ShapeDtypeStruct((block.shape[0], cols), block.dtype),
        compiler_params=params(),
        name="relay",
    )(block, done)


def choices(ids, peers, slots):
    rows = ids[0].shape[1]
    me = lax.axis_index("ep")
    named = []
    for one in ids:
        for k in range(peers):
            hits = [jnp.where(one[p : p + 1, :] == me ^ k, 1.0, 0.0) for p in range(one.shape[0])]
            named.append(sum(hits))
    earlier = lax.broadcasted_iota(jnp.int32, (rows, rows), 0) < lax.broadcasted_iota(jnp.int32, (rows, rows), 1)
    ahead = jnp.dot(
        jnp.concatenate(named, axis=0).astype(jnp.bfloat16),
        jnp.where(earlier, 1.0, 0.0).astype(jnp.bfloat16),
        preferred_element_type=jnp.float32,
    ).astype(jnp.int32)
    slot = lax.broadcasted_iota(jnp.int32, (slots, rows), 0)
    holds = [jnp.where((ahead[i : i + 1, :] == slot) & (row > 0.5), 1.0, 0.0) for i, row in enumerate(named)]
    return [jnp.concatenate(holds[s * peers : (s + 1) * peers], axis=0) for s in range(len(ids))]


def narrow(x):
    return x.astype(jnp.bfloat16)


def product(x, y):
    return jnp.dot(narrow(x), narrow(y), preferred_element_type=jnp.float32)


def named_experts(ids, held, experts):
    rows = ids[0].shape[1]
    flags = []
    for s, one in enumerate(ids):
        lane = lax.broadcasted_iota(jnp.int32, (LANES, rows), 0)
        hits = [jnp.where(one[p : p + 1, :] + s * experts == lane, 1.0, 0.0) for p in range(one.shape[0])]
        flags.append(product(held[s], sum(hits).T))
    return sum(flags)


def pack_kernel(experts, tokens_ref, ids_ref, *refs):
    *out_refs, own_ref, half_ref, held_ref, sems = refs
    quarter = tokens_ref.shape[1] // 4
    half = 2 * quarter
    where = lax.axis_index("et")
    copies = [
        pltpu.make_async_copy(ids_ref, held_ref, sems.at[0]),
        pltpu.make_async_copy(tokens_ref.at[:, aligned(where & 1, quarter)], half_ref.at[:, :quarter], sems.at[1]),
        pltpu.make_async_copy(tokens_ref.at[:, aligned(where & 1 | 2, quarter)], half_ref.at[:, quarter:], sems.at[2]),
    ]
    for copy in copies:
        copy.start()
    copies[0].wait()
    ids = [held_ref[s] for s in range(held_ref.shape[0])]
    slots, peers = out_refs[0].shape[0], 1 + len(out_refs)
    held = choices(ids, peers, slots)
    flags = named_experts(ids, held, experts)
    copies[1].wait()
    copies[2].wait()
    own_ref[...] = half_ref[:, aligned(where >> 1, quarter)]
    picked = product(held[0][slots:], half_ref[...])
    for k, out_ref in enumerate(out_refs):
        out_ref[:, :half] = narrow(picked[k * slots : (k + 1) * slots])
        out_ref[:, half:] = narrow(flags[(k + 1) * slots : (k + 2) * slots])


def pack(tokens, ids, experts, slots):
    rows, width = tokens.shape
    others = lax.axis_size("ep") - 1
    shapes = [(slots, width // 2 + LANES)] * others + [(rows, width // 4)]
    return pl.pallas_call(
        functools.partial(pack_kernel, experts),
        in_specs=[ANY] * 2,
        out_specs=[VMEM] * len(shapes),
        out_shape=[pltpu.VMEM(s, jnp.bfloat16) for s in shapes],
        scratch_shapes=[
            pltpu.VMEM((rows, width // 2), jnp.bfloat16),
            pltpu.VMEM(ids.shape, jnp.int32),
            pltpu.SemaphoreType.DMA((3,)),
        ],
        compiler_params=params(VMEM_ALL),
        name="pack",
    )(tokens, ids)


def own_kernel(experts, tokens_ref, ids_ref, done_ref, out_ref, flags_ref, *choice_refs):
    ids = [ids_ref[s] for s in range(ids_ref.shape[0])]
    slots = out_ref.shape[0]
    held = choices(ids, choice_refs[0].shape[0] // slots, slots)
    flags_ref[...] = narrow(named_experts(ids, held, experts)[:slots])
    out_ref[...] = narrow(product(held[0][:slots], tokens_ref[...]))
    for s, one in enumerate(held):
        choice_refs[2 * s][...] = narrow(one)
        choice_refs[2 * s + 1][...] = narrow(one.T)


def own_rows(tokens, ids, experts, slots, done):
    rows, width = tokens.shape
    total = lax.axis_size("ep") * slots
    shapes = [(slots, width), (slots, LANES)] + [(total, rows), (rows, total)] * ids.shape[0]
    return pl.pallas_call(
        functools.partial(own_kernel, experts),
        out_shape=[jax.ShapeDtypeStruct(s, jnp.bfloat16) for s in shapes],
        compiler_params=params(),
        name="own_rows",
    )(tokens, ids, done)


def front_kernel(layout, order, flips, section, experts, *refs):
    n = sum(len(block) for block in layout)
    x_refs = list(refs[:n])
    mod_ref, router_ref, pair_ref, *rest = refs[n:]
    width = pair_ref.shape[0]
    quarter = width // 4
    et = lax.axis_index("et")
    blocks = {}
    for k in order:
        blocks[k] = [(x_refs.pop(0), cols, flip) for cols, flip in layout[k]]

    def part(block, flip):
        for ref, cols, at in block:
            if cols == quarter and at == flip:
                return ref[...].astype(jnp.float32)
            if cols == 2 * quarter and at == flip & 1:
                return ref[:, aligned((et ^ flip) >> 1, quarter)].astype(jnp.float32)
            if cols == width:
                return ref[:, aligned(et ^ flip, quarter)].astype(jnp.float32)

    units, logits, squares = 0.0, 0.0, 0.0
    for flip in flips:
        xf = jnp.concatenate([part(blocks[k], flip) for k in range(len(layout))], axis=0)
        squares += jnp.sum(xf * xf, axis=1, keepdims=True)
        where = aligned(et ^ flip, quarter)
        shift = mod_ref[section, 1:2, where]
        head = narrow(shift).astype(jnp.float32)
        blank = jnp.zeros((6, quarter), jnp.float32)
        lhs = [xf * (1.0 + mod_ref[section, 0:1, where]), head, shift - head, blank]
        lhs = narrow(jnp.concatenate(lhs, axis=0))
        units += jnp.dot(lhs, pair_ref[where, :], preferred_element_type=jnp.float32)
        logits += lax.dot_general(
            lhs, router_ref[:, where], (((1,), (1,)), ((), ())), preferred_element_type=jnp.float32
        )
    if len(rest) == 3:
        rest[0][...], rest[1][...], rest[2][...] = units, logits, squares
        return
    *flag_refs, units_ref, logits_ref, squares_ref, out_ref = rest
    rows, hidden = out_ref.shape
    scale = lax.rsqrt((squares + squares_ref[...]) / width + 1e-06)

    def scaled(x):
        return x[:rows] * scale + (x[rows : rows + 1] + x[rows + 1 : rows + 2])

    units, logits = scaled(units + units_ref[...]), scaled(logits + logits_ref[...])
    count = logits.shape[1]
    lane = lax.broadcasted_iota(jnp.int32, logits.shape, 1)
    flags = [flag_refs[order.index(k)] for k in range(len(layout))]
    flags = [f[:, f.shape[1] - LANES :].astype(jnp.float32) for f in flags]
    flags = jnp.concatenate(flags, axis=0)[:, section * experts : section * experts + count]
    chosen = jnp.where(flags > 0.5, jax.nn.sigmoid(logits), 0.0)
    mine = jnp.sum(jnp.where(lane == lax.axis_index("ep"), chosen, 0.0), axis=1, keepdims=True)
    used = jnp.max(flags, axis=1, keepdims=True) > 0.5
    weight = jnp.where(used, mine / jnp.sum(chosen, axis=1, keepdims=True), 0.0)
    gate, upper = units[:, :hidden], units[:, hidden:]
    out = jnp.where(used, gate / (1.0 + jnp.exp(-gate)) * upper * weight, 0.0)
    out_ref[...] = narrow(out)


def half_front(blocks, flips, extra, shapes, order, section, mod, router, pair):
    xs = [x for k in order for x, _, _ in blocks[k]]
    layout = [[piece[1:] for piece in block] for block in blocks]
    rows, (width, units) = shapes[0].shape[0], pair.shape
    return pl.pallas_call(
        functools.partial(front_kernel, layout, order, flips, section, router.shape[0]),
        in_specs=[VMEM] * (len(xs) + 3 + len(extra)),
        out_shape=shapes,
        compiler_params=params(),
        cost_estimate=pl.CostEstimate(
            flops=rows * width * units, bytes_accessed=width * units, transcendentals=0
        ),
        name="front",
    )(*xs, mod, router, pair, *extra)


def front(blocks, flags, order, section, mod, router, pair):
    rows = sum(f.shape[0] for f in flags)
    units, experts = pair.shape[1], router.shape[0]
    width = pair.shape[0]
    common = (order, section, mod, router, pair)
    here = [[p for p in block if p[1] == width or p[2] & 1 == 0] for block in blocks]
    there = [[p for p in block if p[1] == width or p[2] & 1] for block in blocks]
    shapes = [jax.ShapeDtypeStruct(s, jnp.float32) for s in ((rows + 8, units), (rows + 8, experts), (rows, 1))]
    sums = half_front(here, (0, 2), [], shapes, *common)
    shapes = [jax.ShapeDtypeStruct((rows, units // 2), jnp.bfloat16)]
    return half_front(there, (1, 3), [flags[k] for k in order] + list(sums), shapes, *common)[0]


def store_blocks(total, groups, outs):
    rows = total.shape[0] // sum(len(group) for group in groups)
    for group, out in zip(groups, outs):
        blocks = [total[k * rows : (k + 1) * rows] for k in group]
        out[...] = jnp.concatenate(blocks, axis=0).astype(out.dtype)


def shapes_of(rows, cols, groups, types):
    slots = rows // sum(len(group) for group in groups)
    return [jax.ShapeDtypeStruct((slots * len(group), cols), t) for group, t in zip(groups, types)]


def down_kernel(flip, n_adds, groups, hidden_ref, down_ref, *refs):
    adds, outs = refs[:n_adds], refs[n_adds:]
    quarter = outs[0].shape[1]
    weights = down_ref[:, aligned(lax.axis_index("et") ^ flip, quarter)]
    total = jnp.dot(hidden_ref[...], weights, preferred_element_type=jnp.float32)
    for ref in adds:
        total += ref[...].astype(jnp.float32)
    store_blocks(total, groups, outs)


def down(hidden, w_down, flip, adds=(), groups=((0,),), types=(jnp.bfloat16,)):
    units, width = w_down.shape
    rows, quarter = hidden.shape[0], width // 4
    return pl.pallas_call(
        functools.partial(down_kernel, flip, len(adds), groups),
        in_specs=[VMEM] * (2 + len(adds)),
        out_shape=shapes_of(rows, quarter, groups, types),
        compiler_params=params(),
        cost_estimate=pl.CostEstimate(
            flops=2 * rows * units * quarter, bytes_accessed=2 * units * quarter, transcendentals=0
        ),
        name="down",
    )(hidden, w_down, *adds)


def add_kernel(groups, keep_ref, came_ref, *outs):
    store_blocks(keep_ref[...] + came_ref[...].astype(jnp.float32), groups, outs)


def add(keep, came, groups):
    return pl.pallas_call(
        functools.partial(add_kernel, groups),
        out_shape=shapes_of(*keep.shape, groups, [jnp.bfloat16] * len(groups)),
        compiler_params=params(),
        name="add",
    )(keep, came)


def diagonal(x, k, flip):
    n_ep, n_et = lax.axis_size("ep"), lax.axis_size("et")
    pairs = [(e * n_et + t, (e ^ k) * n_et + (t ^ flip)) for e in range(n_ep) for t in range(n_et)]
    return lax.ppermute(x, ("ep", "et"), pairs)


def move_kernel(order, last, own_ref, back_ref, pick_ref, extra_ref, *refs):
    came, outs = refs[: len(order)], refs[len(order) :]
    rows = [came[order.index(k)][...].astype(jnp.float32) for k in range(len(order))]
    rows[DIRECT] += extra_ref[...].astype(jnp.float32)
    velocity = product(back_ref[...], jnp.concatenate(rows, axis=0))
    moved = narrow(own_ref[...].astype(jnp.float32) - 0.5 * velocity)
    outs[0][...] = moved
    if last:
        outs[1][...] = narrow(velocity)
    else:
        slots = came[0].shape[0]
        picked = product(pick_ref[...], moved)
        for k, out in enumerate(outs[1:]):
            out[...] = narrow(picked[k * slots : (k + 1) * slots])


def move(own, back, pick, extra, came, order, last):
    shapes = [own.shape] + ([own.shape] if last else [c.shape for c in came])
    return pl.pallas_call(
        functools.partial(move_kernel, order, last),
        out_shape=[jax.ShapeDtypeStruct(s, jnp.bfloat16) for s in shapes],
        compiler_params=params(),
        name="move",
    )(own, back, pick, extra, *[came[k] for k in order])


DIRECT = 2


def sum_back(hidden, w_down, own, back, pick, last):
    peers = lax.axis_size("ep")
    rest = tuple(k for k in range(peers) if k != DIRECT)
    groups = (rest, (DIRECT,))
    (far,), (near,) = down(hidden, w_down, 3), down(hidden, w_down, 1)
    far, near = swap(far, "et", 1), swap(near, "et", 1)
    (crossing,) = down(hidden, w_down, 2, types=[jnp.float32])
    crossing, beside = add(crossing, far, groups)
    crossed, extra = swap(crossing, "et", 2), diagonal(beside, DIRECT, 2)
    kept, straight = down(hidden, w_down, 0, (near,), groups, [jnp.float32, jnp.bfloat16])
    blocks = dict(zip(rest, add(kept, crossed, [(i,) for i in range(len(rest))])))
    blocks[DIRECT] = straight
    came = [swap(blocks[k], "ep", k) if k else blocks[k] for k in range(peers)]
    order = [*range(2, peers), 1, 0]
    return move(own, back, pick, extra, came, order, last)


def spread(block, quarter, side=None):
    side = swap(block, "et", 2) if side is None else side
    near, far = swap(block, "et", 1), swap(side, "et", 1)
    return [(block, quarter, 0), (side, quarter, 2), (near, quarter, 1), (far, quarter, 3)]


def dense_body(tokens, modulation, router, gate_weight, up_weight, down_weight, expert_ids):
    rows, width = tokens.shape
    half, quarter = width // 2, width // 4
    router = router.T
    experts = router.shape[0]
    peers = lax.axis_size("ep")
    slots = 3 * rows * expert_ids.shape[2] // (2 * experts)
    ids = expert_ids.transpose(0, 2, 1)

    *packed, own = pack(tokens, ids, experts, slots)
    pair, w_down, done = load(gate_weight, up_weight, down_weight)
    mine, flags, *choice = own_rows(tokens, ids, experts, slots, done)
    pick, back = choice[2], choice[1::2]
    order = [*range(2, len(packed) + 1), 1]
    came = {k: swap(packed[k - 1], "ep", k) for k in order}
    halves = {k: relay(came[k], half, flags) for k in order}
    others = {k: swap(halves[k], "et", 1) for k in order}
    flags = [flags] + [came[k] for k in sorted(order)]
    blocks = [[(mine, width, 0)]] + [[(halves[k], half, 0), (others[k], half, 1)] for k in sorted(order)]
    hidden = front(blocks, flags, order + [0], 0, modulation, router, pair)
    own, *sent = sum_back(hidden, w_down, own, back[0], pick, False)

    sides = {1: diagonal(sent[1], 1, 2)}
    blocks = [spread(swap(b, "ep", k) if k else b, quarter, sides.get(k)) for k, b in enumerate(sent)]
    hidden = front(blocks, flags, order + [0], 1, modulation, router, pair)
    return tuple(sum_back(hidden, w_down, own, back[1], pick, True))


def solution(mesh):
    in_specs = (
        P(("grp", "ep"), None),
        P(),
        P(),
        P("ep", None, "et"),
        P("ep", None, "et"),
        P("ep", "et", None),
        P(None, ("grp", "ep"), None),
    )
    out_specs = (P(("grp", "ep"), "et"), P(("grp", "ep"), "et"))

    def body(*args):
        experts, picks = args[2].shape[1], args[6].shape[2]
        peers = lax.axis_size("ep")
        fits = lax.axis_size("et") == 4 and peers >= 4 and peers & (peers - 1) == 0
        chosen = dense_body if fits and experts <= 2 * picks else routed_body
        return chosen(*args)

    return jax.shard_map(body, mesh=mesh, in_specs=in_specs, out_specs=out_specs, check_vma=False)
```

```python
import functools

import jax
import jax.numpy as jnp
from jax import lax
from jax.experimental import pallas as pl
from jax.experimental.pallas import tpu as pltpu
from jax.sharding import PartitionSpec as P


def normalize(x, mod):
    xf = x.astype(jnp.float32)
    scaled = xf * lax.rsqrt(jnp.mean(xf * xf, axis=-1, keepdims=True) + 1e-06)
    return (scaled * (1.0 + mod[0]) + mod[1]).astype(jnp.bfloat16)


def routed_section(x_full, x_cols, mod, ids, router, gate_weight, up_weight, down_weight):
    tok_rows = x_full.shape[0]
    width = x_full.shape[1]
    experts = router.shape[1]
    picks = ids.shape[1]
    n_peers = lax.axis_size("ep")
    quarter = width // lax.axis_size("et")
    slot_count = 3 * tok_rows * picks // (2 * experts)
    normed = normalize(x_full, mod)
    logits = jnp.dot(normed, router, preferred_element_type=jnp.float32)
    chosen = jax.nn.sigmoid(jnp.take_along_axis(logits, ids, axis=1))
    weight = chosen / jnp.sum(chosen, axis=1, keepdims=True)
    flat_e = ids.reshape(-1)
    onehot = (flat_e[:, None] == jnp.arange(experts, dtype=jnp.int32)).astype(jnp.int32)
    counted = jnp.cumsum(onehot, axis=0)
    slot = jnp.sum(onehot * (counted - 1), axis=1)
    repeated = jnp.repeat(normed, picks, axis=0)
    outbox = jnp.zeros((experts, slot_count, width), jnp.bfloat16).at[flat_e, slot].set(repeated)
    arrived = lax.all_to_all(outbox, "ep", split_axis=0, concat_axis=0, tiled=True)
    in_rows = arrived.reshape(n_peers * slot_count, width)
    gate = jnp.dot(in_rows, gate_weight[0], preferred_element_type=jnp.float32)
    upper = jnp.dot(in_rows, up_weight[0], preferred_element_type=jnp.float32)
    hidden = (jax.nn.silu(gate) * upper).astype(jnp.bfloat16)
    partial_out = jnp.dot(hidden, down_weight[0], preferred_element_type=jnp.float32)
    summed = lax.psum_scatter(
        partial_out.astype(jnp.bfloat16), "et", scatter_dimension=1, tiled=True
    )
    returned = lax.all_to_all(
        summed.reshape(n_peers, slot_count, quarter), "ep", split_axis=0, concat_axis=0, tiled=True
    )
    picked = returned[flat_e, slot].astype(jnp.float32).reshape(tok_rows, picks, quarter)
    velocity = jnp.sum(picked * weight[:, :, None], axis=1)
    moved = (x_cols.astype(jnp.float32) - 0.5 * velocity).astype(jnp.bfloat16)
    return (moved, velocity)


def routed_body(tokens, modulation, router, gate_weight, up_weight, down_weight, expert_ids):
    quarter = tokens.shape[1] // lax.axis_size("et")
    column_start = lax.axis_index("et") * quarter
    cols = lax.dynamic_slice_in_dim(tokens, column_start, quarter, 1)
    weights = (router, gate_weight, up_weight, down_weight)
    first, _ = routed_section(tokens, cols, modulation[0], expert_ids[0], *weights)
    full = lax.all_gather(first, "et", axis=1, tiled=True)
    second, velocity = routed_section(full, first, modulation[1], expert_ids[1], *weights)
    return (second, velocity.astype(jnp.bfloat16))


def swap(x, axis, bit):
    size = lax.axis_size(axis)
    return lax.ppermute(x, axis, [(i, i ^ bit) for i in range(size)])


LANES = 128
VMEM_LIMIT = 32 * 1024 * 1024
VMEM_MOST = 52 * 1024 * 1024
VMEM_ALL = 63 * 1024 * 1024
VMEM = pl.BlockSpec(memory_space=pltpu.VMEM)
ANY = pl.BlockSpec(memory_space=pl.ANY)


def params(limit=VMEM_LIMIT):
    return pltpu.CompilerParams(vmem_limit_bytes=limit)


def aligned(index, size):
    return pl.ds(pl.multiple_of(index * size, size), size)


def load_kernel(gate_ref, up_ref, down_ref, pair_ref, out_ref, done_ref, sems):
    hidden = gate_ref.shape[2]
    copies = [
        pltpu.make_async_copy(gate_ref.at[0], pair_ref.at[:, :hidden], sems.at[0]),
        pltpu.make_async_copy(up_ref.at[0], pair_ref.at[:, hidden:], sems.at[1]),
        pltpu.make_async_copy(down_ref.at[0], out_ref, sems.at[2]),
    ]
    for copy in copies:
        copy.start()
    for copy in copies:
        copy.wait()
    done_ref[...] = jnp.zeros_like(done_ref)


def load(gate, up, down):
    _, width, hidden = gate.shape
    return pl.pallas_call(
        load_kernel,
        in_specs=[ANY] * 3,
        out_specs=[VMEM] * 3,
        out_shape=[
            pltpu.VMEM((width, 2 * hidden), jnp.bfloat16),
            pltpu.VMEM((hidden, width), jnp.bfloat16),
            pltpu.VMEM((8, LANES), jnp.float32),
        ],
        scratch_shapes=[pltpu.SemaphoreType.DMA((3,))],
        compiler_params=params(VMEM_MOST),
        cost_estimate=pl.CostEstimate(flops=0, bytes_accessed=12 * width * hidden, transcendentals=0),
        name="load",
    )(gate, up, down)


def relay_kernel(block_ref, done_ref, out_ref):
    out_ref[...] = block_ref[:, : out_ref.shape[1]]


def relay(block, cols, done):
    return pl.pallas_call(
        relay_kernel,
        out_shape=jax.ShapeDtypeStruct((block.shape[0], cols), block.dtype),
        compiler_params=params(),
        name="relay",
    )(block, done)


def choices(ids, peers, slots):
    rows = ids[0].shape[1]
    me = lax.axis_index("ep")
    named = []
    for one in ids:
        for k in range(peers):
            hits = [jnp.where(one[p : p + 1, :] == me ^ k, 1.0, 0.0) for p in range(one.shape[0])]
            named.append(sum(hits))
    earlier = lax.broadcasted_iota(jnp.int32, (rows, rows), 0) < lax.broadcasted_iota(jnp.int32, (rows, rows), 1)
    ahead = jnp.dot(
        jnp.concatenate(named, axis=0).astype(jnp.bfloat16),
        jnp.where(earlier, 1.0, 0.0).astype(jnp.bfloat16),
        preferred_element_type=jnp.float32,
    ).astype(jnp.int32)
    slot = lax.broadcasted_iota(jnp.int32, (slots, rows), 0)
    holds = [jnp.where((ahead[i : i + 1, :] == slot) & (row > 0.5), 1.0, 0.0) for i, row in enumerate(named)]
    return [jnp.concatenate(holds[s * peers : (s + 1) * peers], axis=0) for s in range(len(ids))]


def narrow(x):
    return x.astype(jnp.bfloat16)


def product(x, y):
    return jnp.dot(narrow(x), narrow(y), preferred_element_type=jnp.float32)


def named_experts(ids, held, experts):
    rows = ids[0].shape[1]
    flags = []
    for s, one in enumerate(ids):
        lane = lax.broadcasted_iota(jnp.int32, (LANES, rows), 0)
        hits = [jnp.where(one[p : p + 1, :] + s * experts == lane, 1.0, 0.0) for p in range(one.shape[0])]
        flags.append(product(held[s], sum(hits).T))
    return sum(flags)


def pack_kernel(experts, tokens_ref, ids_ref, *refs):
    *out_refs, own_ref, half_ref, held_ref, sems = refs
    quarter = tokens_ref.shape[1] // 4
    half = 2 * quarter
    where = lax.axis_index("et")
    copies = [
        pltpu.make_async_copy(ids_ref, held_ref, sems.at[0]),
        pltpu.make_async_copy(tokens_ref.at[:, aligned(where & 1, quarter)], half_ref.at[:, :quarter], sems.at[1]),
        pltpu.make_async_copy(tokens_ref.at[:, aligned(where & 1 | 2, quarter)], half_ref.at[:, quarter:], sems.at[2]),
    ]
    for copy in copies:
        copy.start()
    copies[0].wait()
    ids = [held_ref[s] for s in range(held_ref.shape[0])]
    slots, peers = out_refs[0].shape[0], 1 + len(out_refs)
    held = choices(ids, peers, slots)
    flags = named_experts(ids, held, experts)
    copies[1].wait()
    copies[2].wait()
    own_ref[...] = half_ref[:, aligned(where >> 1, quarter)]
    picked = product(held[0][slots:], half_ref[...])
    for k, out_ref in enumerate(out_refs):
        out_ref[:, :half] = narrow(picked[k * slots : (k + 1) * slots])
        out_ref[:, half:] = narrow(flags[(k + 1) * slots : (k + 2) * slots])


def pack(tokens, ids, experts, slots):
    rows, width = tokens.shape
    others = lax.axis_size("ep") - 1
    shapes = [(slots, width // 2 + LANES)] * others + [(rows, width // 4)]
    return pl.pallas_call(
        functools.partial(pack_kernel, experts),
        in_specs=[ANY] * 2,
        out_specs=[VMEM] * len(shapes),
        out_shape=[pltpu.VMEM(s, jnp.bfloat16) for s in shapes],
        scratch_shapes=[
            pltpu.VMEM((rows, width // 2), jnp.bfloat16),
            pltpu.VMEM(ids.shape, jnp.int32),
            pltpu.SemaphoreType.DMA((3,)),
        ],
        compiler_params=params(VMEM_ALL),
        name="pack",
    )(tokens, ids)


def own_kernel(experts, tokens_ref, ids_ref, done_ref, out_ref, flags_ref, *choice_refs):
    ids = [ids_ref[s] for s in range(ids_ref.shape[0])]
    slots = out_ref.shape[0]
    held = choices(ids, choice_refs[0].shape[0] // slots, slots)
    flags_ref[...] = narrow(named_experts(ids, held, experts)[:slots])
    out_ref[...] = narrow(product(held[0][:slots], tokens_ref[...]))
    for s, one in enumerate(held):
        choice_refs[2 * s][...] = narrow(one)
        choice_refs[2 * s + 1][...] = narrow(one.T)


def own_rows(tokens, ids, experts, slots, done):
    rows, width = tokens.shape
    total = lax.axis_size("ep") * slots
    shapes = [(slots, width), (slots, LANES)] + [(total, rows), (rows, total)] * ids.shape[0]
    return pl.pallas_call(
        functools.partial(own_kernel, experts),
        out_shape=[jax.ShapeDtypeStruct(s, jnp.bfloat16) for s in shapes],
        compiler_params=params(),
        name="own_rows",
    )(tokens, ids, done)


def front_kernel(layout, order, flips, section, experts, *refs):
    n = sum(len(block) for block in layout)
    x_refs = list(refs[:n])
    mod_ref, router_ref, pair_ref, *rest = refs[n:]
    width = pair_ref.shape[0]
    quarter = width // 4
    et = lax.axis_index("et")
    blocks = {}
    for k in order:
        blocks[k] = [(x_refs.pop(0), cols, flip) for cols, flip in layout[k]]

    def part(block, flip):
        for ref, cols, at in block:
            if cols == quarter and at == flip:
                return ref[...].astype(jnp.float32)
            if cols == 2 * quarter and at == flip & 1:
                return ref[:, aligned((et ^ flip) >> 1, quarter)].astype(jnp.float32)
            if cols == width:
                return ref[:, aligned(et ^ flip, quarter)].astype(jnp.float32)

    units, logits, squares = 0.0, 0.0, 0.0
    for flip in flips:
        xf = jnp.concatenate([part(blocks[k], flip) for k in range(len(layout))], axis=0)
        squares += jnp.sum(xf * xf, axis=1, keepdims=True)
        where = aligned(et ^ flip, quarter)
        shift = mod_ref[section, 1:2, where]
        head = narrow(shift).astype(jnp.float32)
        blank = jnp.zeros((6, quarter), jnp.float32)
        lhs = [xf * (1.0 + mod_ref[section, 0:1, where]), head, shift - head, blank]
        lhs = narrow(jnp.concatenate(lhs, axis=0))
        units += jnp.dot(lhs, pair_ref[where, :], preferred_element_type=jnp.float32)
        logits += lax.dot_general(
            lhs, router_ref[:, where], (((1,), (1,)), ((), ())), preferred_element_type=jnp.float32
        )
    if len(rest) == 3:
        rest[0][...], rest[1][...], rest[2][...] = units, logits, squares
        return
    *flag_refs, units_ref, logits_ref, squares_ref, out_ref = rest
    rows, hidden = out_ref.shape
    scale = lax.rsqrt((squares + squares_ref[...]) / width + 1e-06)

    def scaled(x):
        return x[:rows] * scale + (x[rows : rows + 1] + x[rows + 1 : rows + 2])

    units, logits = scaled(units + units_ref[...]), scaled(logits + logits_ref[...])
    count = logits.shape[1]
    lane = lax.broadcasted_iota(jnp.int32, logits.shape, 1)
    flags = [flag_refs[order.index(k)] for k in range(len(layout))]
    flags = [f[:, f.shape[1] - LANES :].astype(jnp.float32) for f in flags]
    flags = jnp.concatenate(flags, axis=0)[:, section * experts : section * experts + count]
    chosen = jnp.where(flags > 0.5, jax.nn.sigmoid(logits), 0.0)
    mine = jnp.sum(jnp.where(lane == lax.axis_index("ep"), chosen, 0.0), axis=1, keepdims=True)
    used = jnp.max(flags, axis=1, keepdims=True) > 0.5
    weight = jnp.where(used, mine / jnp.sum(chosen, axis=1, keepdims=True), 0.0)
    gate, upper = units[:, :hidden], units[:, hidden:]
    out = jnp.where(used, gate / (1.0 + jnp.exp(-gate)) * upper * weight, 0.0)
    out_ref[...] = narrow(out)


def half_front(blocks, flips, extra, shapes, order, section, mod, router, pair):
    xs = [x for k in order for x, _, _ in blocks[k]]
    layout = [[piece[1:] for piece in block] for block in blocks]
    rows, (width, units) = shapes[0].shape[0], pair.shape
    return pl.pallas_call(
        functools.partial(front_kernel, layout, order, flips, section, router.shape[0]),
        in_specs=[VMEM] * (len(xs) + 3 + len(extra)),
        out_shape=shapes,
        compiler_params=params(),
        cost_estimate=pl.CostEstimate(
            flops=rows * width * units, bytes_accessed=width * units, transcendentals=0
        ),
        name="front",
    )(*xs, mod, router, pair, *extra)


def front(blocks, flags, order, section, mod, router, pair):
    rows = sum(f.shape[0] for f in flags)
    units, experts = pair.shape[1], router.shape[0]
    width = pair.shape[0]
    common = (order, section, mod, router, pair)
    here = [[p for p in block if p[1] == width or p[2] & 1 == 0] for block in blocks]
    there = [[p for p in block if p[1] == width or p[2] & 1] for block in blocks]
    shapes = [jax.ShapeDtypeStruct(s, jnp.float32) for s in ((rows + 8, units), (rows + 8, experts), (rows, 1))]
    sums = half_front(here, (0, 2), [], shapes, *common)
    shapes = [jax.ShapeDtypeStruct((rows, units // 2), jnp.bfloat16)]
    return half_front(there, (1, 3), [flags[k] for k in order] + list(sums), shapes, *common)[0]


def store_blocks(total, groups, outs):
    rows = total.shape[0] // sum(len(group) for group in groups)
    for group, out in zip(groups, outs):
        blocks = [total[k * rows : (k + 1) * rows] for k in group]
        out[...] = jnp.concatenate(blocks, axis=0).astype(out.dtype)


def shapes_of(rows, cols, groups, types):
    slots = rows // sum(len(group) for group in groups)
    return [jax.ShapeDtypeStruct((slots * len(group), cols), t) for group, t in zip(groups, types)]


def down_kernel(flip, n_adds, groups, hidden_ref, down_ref, *refs):
    adds, outs = refs[:n_adds], refs[n_adds:]
    quarter = outs[0].shape[1]
    weights = down_ref[:, aligned(lax.axis_index("et") ^ flip, quarter)]
    total = jnp.dot(hidden_ref[...], weights, preferred_element_type=jnp.float32)
    for ref in adds:
        total += ref[...].astype(jnp.float32)
    store_blocks(total, groups, outs)


def down(hidden, w_down, flip, adds=(), groups=((0,),), types=(jnp.bfloat16,)):
    units, width = w_down.shape
    rows, quarter = hidden.shape[0], width // 4
    return pl.pallas_call(
        functools.partial(down_kernel, flip, len(adds), groups),
        in_specs=[VMEM] * (2 + len(adds)),
        out_shape=shapes_of(rows, quarter, groups, types),
        compiler_params=params(),
        cost_estimate=pl.CostEstimate(
            flops=2 * rows * units * quarter, bytes_accessed=2 * units * quarter, transcendentals=0
        ),
        name="down",
    )(hidden, w_down, *adds)


def add_kernel(groups, keep_ref, came_ref, *outs):
    store_blocks(keep_ref[...] + came_ref[...].astype(jnp.float32), groups, outs)


def add(keep, came, groups):
    return pl.pallas_call(
        functools.partial(add_kernel, groups),
        out_shape=shapes_of(*keep.shape, groups, [jnp.bfloat16] * len(groups)),
        compiler_params=params(),
        name="add",
    )(keep, came)


def diagonal(x, k, flip):
    n_ep, n_et = lax.axis_size("ep"), lax.axis_size("et")
    pairs = [(e * n_et + t, (e ^ k) * n_et + (t ^ flip)) for e in range(n_ep) for t in range(n_et)]
    return lax.ppermute(x, ("ep", "et"), pairs)


def move_kernel(order, last, own_ref, back_ref, pick_ref, extra_ref, *refs):
    came, outs = refs[: len(order)], refs[len(order) :]
    rows = [came[order.index(k)][...].astype(jnp.float32) for k in range(len(order))]
    rows[DIRECT] += extra_ref[...].astype(jnp.float32)
    velocity = product(back_ref[...], jnp.concatenate(rows, axis=0))
    moved = narrow(own_ref[...].astype(jnp.float32) - 0.5 * velocity)
    outs[0][...] = moved
    if last:
        outs[1][...] = narrow(velocity)
    else:
        slots = came[0].shape[0]
        picked = product(pick_ref[...], moved)
        for k, out in enumerate(outs[1:]):
            out[...] = narrow(picked[k * slots : (k + 1) * slots])


def move(own, back, pick, extra, came, order, last):
    shapes = [own.shape] + ([own.shape] if last else [c.shape for c in came])
    return pl.pallas_call(
        functools.partial(move_kernel, order, last),
        out_shape=[jax.ShapeDtypeStruct(s, jnp.bfloat16) for s in shapes],
        compiler_params=params(),
        name="move",
    )(own, back, pick, extra, *[came[k] for k in order])


DIRECT = 3


def sum_back(hidden, w_down, own, back, pick, last):
    peers = lax.axis_size("ep")
    rest = tuple(k for k in range(peers) if k != DIRECT)
    groups = (rest, (DIRECT,))
    (far,), (near,) = down(hidden, w_down, 3), down(hidden, w_down, 1)
    far, near = swap(far, "et", 1), swap(near, "et", 1)
    (crossing,) = down(hidden, w_down, 2, types=[jnp.float32])
    crossing, beside = add(crossing, far, groups)
    crossed, extra = swap(crossing, "et", 2), diagonal(beside, DIRECT, 2)
    kept, straight = down(hidden, w_down, 0, (near,), groups, [jnp.float32, jnp.bfloat16])
    blocks = dict(zip(rest, add(kept, crossed, [(i,) for i in range(len(rest))])))
    blocks[DIRECT] = straight
    came = [swap(blocks[k], "ep", k) if k else blocks[k] for k in range(peers)]
    order = [*range(2, peers), 1, 0]
    return move(own, back, pick, extra, came, order, last)


def spread(block, quarter):
    side = swap(block, "et", 2)
    near, far = swap(block, "et", 1), swap(side, "et", 1)
    return [(block, quarter, 0), (side, quarter, 2), (near, quarter, 1), (far, quarter, 3)]


def dense_body(tokens, modulation, router, gate_weight, up_weight, down_weight, expert_ids):
    rows, width = tokens.shape
    half, quarter = width // 2, width // 4
    router = router.T
    experts = router.shape[0]
    peers = lax.axis_size("ep")
    slots = 3 * rows * expert_ids.shape[2] // (2 * experts)
    ids = expert_ids.transpose(0, 2, 1)

    *packed, own = pack(tokens, ids, experts, slots)
    pair, w_down, done = load(gate_weight, up_weight, down_weight)
    mine, flags, *choice = own_rows(tokens, ids, experts, slots, done)
    pick, back = choice[2], choice[1::2]
    order = [*range(2, len(packed) + 1), 1]
    came = {k: swap(packed[k - 1], "ep", k) for k in order}
    halves = {k: relay(came[k], half, flags) for k in order}
    others = {k: swap(halves[k], "et", 1) for k in order}
    flags = [flags] + [came[k] for k in sorted(order)]
    blocks = [[(mine, width, 0)]] + [[(halves[k], half, 0), (others[k], half, 1)] for k in sorted(order)]
    hidden = front(blocks, flags, order + [0], 0, modulation, router, pair)
    own, *sent = sum_back(hidden, w_down, own, back[0], pick, False)

    blocks = [spread(swap(b, "ep", k) if k else b, quarter) for k, b in enumerate(sent)]
    hidden = front(blocks, flags, order + [0], 1, modulation, router, pair)
    return tuple(sum_back(hidden, w_down, own, back[1], pick, True))


def solution(mesh):
    in_specs = (
        P(("grp", "ep"), None),
        P(),
        P(),
        P("ep", None, "et"),
        P("ep", None, "et"),
        P("ep", "et", None),
        P(None, ("grp", "ep"), None),
    )
    out_specs = (P(("grp", "ep"), "et"), P(("grp", "ep"), "et"))

    def body(*args):
        experts, picks = args[2].shape[1], args[6].shape[2]
        peers = lax.axis_size("ep")
        fits = lax.axis_size("et") == 4 and peers >= 4 and peers & (peers - 1) == 0
        chosen = dense_body if fits and experts <= 2 * picks else routed_body
        return chosen(*args)

    return jax.shard_map(body, mesh=mesh, in_specs=in_specs, out_specs=out_specs, check_vma=False)
```

```python
import functools

import jax
import jax.numpy as jnp
from jax import lax
from jax.experimental import pallas as pl
from jax.experimental.pallas import tpu as pltpu
from jax.sharding import PartitionSpec as P


def normalize(x, mod):
    xf = x.astype(jnp.float32)
    scaled = xf * lax.rsqrt(jnp.mean(xf * xf, axis=-1, keepdims=True) + 1e-06)
    return (scaled * (1.0 + mod[0]) + mod[1]).astype(jnp.bfloat16)


def routed_section(x_full, x_cols, mod, ids, router, gate_weight, up_weight, down_weight):
    tok_rows = x_full.shape[0]
    width = x_full.shape[1]
    experts = router.shape[1]
    picks = ids.shape[1]
    n_peers = lax.axis_size("ep")
    quarter = width // lax.axis_size("et")
    slot_count = 3 * tok_rows * picks // (2 * experts)
    normed = normalize(x_full, mod)
    logits = jnp.dot(normed, router, preferred_element_type=jnp.float32)
    chosen = jax.nn.sigmoid(jnp.take_along_axis(logits, ids, axis=1))
    weight = chosen / jnp.sum(chosen, axis=1, keepdims=True)
    flat_e = ids.reshape(-1)
    onehot = (flat_e[:, None] == jnp.arange(experts, dtype=jnp.int32)).astype(jnp.int32)
    counted = jnp.cumsum(onehot, axis=0)
    slot = jnp.sum(onehot * (counted - 1), axis=1)
    repeated = jnp.repeat(normed, picks, axis=0)
    outbox = jnp.zeros((experts, slot_count, width), jnp.bfloat16).at[flat_e, slot].set(repeated)
    arrived = lax.all_to_all(outbox, "ep", split_axis=0, concat_axis=0, tiled=True)
    in_rows = arrived.reshape(n_peers * slot_count, width)
    gate = jnp.dot(in_rows, gate_weight[0], preferred_element_type=jnp.float32)
    upper = jnp.dot(in_rows, up_weight[0], preferred_element_type=jnp.float32)
    hidden = (jax.nn.silu(gate) * upper).astype(jnp.bfloat16)
    partial_out = jnp.dot(hidden, down_weight[0], preferred_element_type=jnp.float32)
    summed = lax.psum_scatter(
        partial_out.astype(jnp.bfloat16), "et", scatter_dimension=1, tiled=True
    )
    returned = lax.all_to_all(
        summed.reshape(n_peers, slot_count, quarter), "ep", split_axis=0, concat_axis=0, tiled=True
    )
    picked = returned[flat_e, slot].astype(jnp.float32).reshape(tok_rows, picks, quarter)
    velocity = jnp.sum(picked * weight[:, :, None], axis=1)
    moved = (x_cols.astype(jnp.float32) - 0.5 * velocity).astype(jnp.bfloat16)
    return (moved, velocity)


def routed_body(tokens, modulation, router, gate_weight, up_weight, down_weight, expert_ids):
    quarter = tokens.shape[1] // lax.axis_size("et")
    column_start = lax.axis_index("et") * quarter
    cols = lax.dynamic_slice_in_dim(tokens, column_start, quarter, 1)
    weights = (router, gate_weight, up_weight, down_weight)
    first, _ = routed_section(tokens, cols, modulation[0], expert_ids[0], *weights)
    full = lax.all_gather(first, "et", axis=1, tiled=True)
    second, velocity = routed_section(full, first, modulation[1], expert_ids[1], *weights)
    return (second, velocity.astype(jnp.bfloat16))


def swap(x, axis, bit):
    size = lax.axis_size(axis)
    return lax.ppermute(x, axis, [(i, i ^ bit) for i in range(size)])


LANES = 128
VMEM_LIMIT = 32 * 1024 * 1024
VMEM_MOST = 52 * 1024 * 1024
VMEM_ALL = 63 * 1024 * 1024
VMEM = pl.BlockSpec(memory_space=pltpu.VMEM)
ANY = pl.BlockSpec(memory_space=pl.ANY)


def params(limit=VMEM_LIMIT):
    return pltpu.CompilerParams(vmem_limit_bytes=limit)


def aligned(index, size):
    return pl.ds(pl.multiple_of(index * size, size), size)


def load_kernel(gate_ref, up_ref, down_ref, pair_ref, out_ref, done_ref, sems):
    hidden = gate_ref.shape[2]
    copies = [
        pltpu.make_async_copy(gate_ref.at[0], pair_ref.at[:, :hidden], sems.at[0]),
        pltpu.make_async_copy(up_ref.at[0], pair_ref.at[:, hidden:], sems.at[1]),
        pltpu.make_async_copy(down_ref.at[0], out_ref, sems.at[2]),
    ]
    for copy in copies:
        copy.start()
    for copy in copies:
        copy.wait()
    done_ref[...] = jnp.zeros_like(done_ref)


def load(gate, up, down):
    _, width, hidden = gate.shape
    return pl.pallas_call(
        load_kernel,
        in_specs=[ANY] * 3,
        out_specs=[VMEM] * 3,
        out_shape=[
            pltpu.VMEM((width, 2 * hidden), jnp.bfloat16),
            pltpu.VMEM((hidden, width), jnp.bfloat16),
            pltpu.VMEM((8, LANES), jnp.float32),
        ],
        scratch_shapes=[pltpu.SemaphoreType.DMA((3,))],
        compiler_params=params(VMEM_MOST),
        cost_estimate=pl.CostEstimate(flops=0, bytes_accessed=12 * width * hidden, transcendentals=0),
        name="load",
    )(gate, up, down)


def relay_kernel(block_ref, done_ref, out_ref):
    out_ref[...] = block_ref[:, : out_ref.shape[1]]


def relay(block, cols, done):
    return pl.pallas_call(
        relay_kernel,
        out_shape=jax.ShapeDtypeStruct((block.shape[0], cols), block.dtype),
        compiler_params=params(),
        name="relay",
    )(block, done)


def choices(ids, peers, slots):
    rows = ids[0].shape[1]
    me = lax.axis_index("ep")
    named = []
    for one in ids:
        for k in range(peers):
            hits = [jnp.where(one[p : p + 1, :] == me ^ k, 1.0, 0.0) for p in range(one.shape[0])]
            named.append(sum(hits))
    earlier = lax.broadcasted_iota(jnp.int32, (rows, rows), 0) < lax.broadcasted_iota(jnp.int32, (rows, rows), 1)
    ahead = jnp.dot(
        jnp.concatenate(named, axis=0).astype(jnp.bfloat16),
        jnp.where(earlier, 1.0, 0.0).astype(jnp.bfloat16),
        preferred_element_type=jnp.float32,
    ).astype(jnp.int32)
    slot = lax.broadcasted_iota(jnp.int32, (slots, rows), 0)
    holds = [jnp.where((ahead[i : i + 1, :] == slot) & (row > 0.5), 1.0, 0.0) for i, row in enumerate(named)]
    return [jnp.concatenate(holds[s * peers : (s + 1) * peers], axis=0) for s in range(len(ids))]


def narrow(x):
    return x.astype(jnp.bfloat16)


def product(x, y):
    return jnp.dot(narrow(x), narrow(y), preferred_element_type=jnp.float32)


def named_experts(ids, held, experts):
    rows = ids[0].shape[1]
    flags = []
    for s, one in enumerate(ids):
        lane = lax.broadcasted_iota(jnp.int32, (LANES, rows), 0)
        hits = [jnp.where(one[p : p + 1, :] + s * experts == lane, 1.0, 0.0) for p in range(one.shape[0])]
        flags.append(product(held[s], sum(hits).T))
    return sum(flags)


def pack_kernel(experts, tokens_ref, ids_ref, *refs):
    *out_refs, own_ref, half_ref, held_ref, sems = refs
    quarter = tokens_ref.shape[1] // 4
    half = 2 * quarter
    where = lax.axis_index("et")
    copies = [
        pltpu.make_async_copy(ids_ref, held_ref, sems.at[0]),
        pltpu.make_async_copy(tokens_ref.at[:, aligned(where & 1, quarter)], half_ref.at[:, :quarter], sems.at[1]),
        pltpu.make_async_copy(tokens_ref.at[:, aligned(where & 1 | 2, quarter)], half_ref.at[:, quarter:], sems.at[2]),
    ]
    for copy in copies:
        copy.start()
    copies[0].wait()
    ids = [held_ref[s] for s in range(held_ref.shape[0])]
    slots, peers = out_refs[0].shape[0], 1 + len(out_refs)
    held = choices(ids, peers, slots)
    flags = named_experts(ids, held, experts)
    copies[1].wait()
    copies[2].wait()
    own_ref[...] = half_ref[:, aligned(where >> 1, quarter)]
    picked = product(held[0][slots:], half_ref[...])
    for k, out_ref in enumerate(out_refs):
        out_ref[:, :half] = narrow(picked[k * slots : (k + 1) * slots])
        out_ref[:, half:] = narrow(flags[(k + 1) * slots : (k + 2) * slots])


def pack(tokens, ids, experts, slots):
    rows, width = tokens.shape
    others = lax.axis_size("ep") - 1
    shapes = [(slots, width // 2 + LANES)] * others + [(rows, width // 4)]
    return pl.pallas_call(
        functools.partial(pack_kernel, experts),
        in_specs=[ANY] * 2,
        out_specs=[VMEM] * len(shapes),
        out_shape=[pltpu.VMEM(s, jnp.bfloat16) for s in shapes],
        scratch_shapes=[
            pltpu.VMEM((rows, width // 2), jnp.bfloat16),
            pltpu.VMEM(ids.shape, jnp.int32),
            pltpu.SemaphoreType.DMA((3,)),
        ],
        compiler_params=params(VMEM_ALL),
        name="pack",
    )(tokens, ids)


def own_kernel(experts, tokens_ref, ids_ref, done_ref, out_ref, flags_ref, *choice_refs):
    ids = [ids_ref[s] for s in range(ids_ref.shape[0])]
    slots = out_ref.shape[0]
    held = choices(ids, choice_refs[0].shape[0] // slots, slots)
    flags_ref[...] = narrow(named_experts(ids, held, experts)[:slots])
    out_ref[...] = narrow(product(held[0][:slots], tokens_ref[...]))
    for s, one in enumerate(held):
        choice_refs[2 * s][...] = narrow(one)
        choice_refs[2 * s + 1][...] = narrow(one.T)


def own_rows(tokens, ids, experts, slots, done):
    rows, width = tokens.shape
    total = lax.axis_size("ep") * slots
    shapes = [(slots, width), (slots, LANES)] + [(total, rows), (rows, total)] * ids.shape[0]
    return pl.pallas_call(
        functools.partial(own_kernel, experts),
        out_shape=[jax.ShapeDtypeStruct(s, jnp.bfloat16) for s in shapes],
        compiler_params=params(),
        name="own_rows",
    )(tokens, ids, done)


def front_kernel(layout, order, flips, section, experts, *refs):
    n = sum(len(block) for block in layout)
    x_refs = list(refs[:n])
    mod_ref, router_ref, pair_ref, *rest = refs[n:]
    width = pair_ref.shape[0]
    quarter = width // 4
    et = lax.axis_index("et")
    blocks = {}
    for k in order:
        blocks[k] = [(x_refs.pop(0), cols, flip) for cols, flip in layout[k]]

    def part(block, flip):
        for ref, cols, at in block:
            if cols == quarter and at == flip:
                return ref[...].astype(jnp.float32)
            if cols == 2 * quarter and at == flip & 1:
                return ref[:, aligned((et ^ flip) >> 1, quarter)].astype(jnp.float32)
            if cols == width:
                return ref[:, aligned(et ^ flip, quarter)].astype(jnp.float32)

    units, logits, squares = 0.0, 0.0, 0.0
    for flip in flips:
        xf = jnp.concatenate([part(blocks[k], flip) for k in range(len(layout))], axis=0)
        squares += jnp.sum(xf * xf, axis=1, keepdims=True)
        where = aligned(et ^ flip, quarter)
        shift = mod_ref[section, 1:2, where]
        head = narrow(shift).astype(jnp.float32)
        blank = jnp.zeros((6, quarter), jnp.float32)
        lhs = [xf * (1.0 + mod_ref[section, 0:1, where]), head, shift - head, blank]
        lhs = narrow(jnp.concatenate(lhs, axis=0))
        units += jnp.dot(lhs, pair_ref[where, :], preferred_element_type=jnp.float32)
        logits += lax.dot_general(
            lhs, router_ref[:, where], (((1,), (1,)), ((), ())), preferred_element_type=jnp.float32
        )
    if len(rest) == 3:
        rest[0][...], rest[1][...], rest[2][...] = units, logits, squares
        return
    *flag_refs, units_ref, logits_ref, squares_ref, out_ref = rest
    rows, hidden = out_ref.shape
    scale = lax.rsqrt((squares + squares_ref[...]) / width + 1e-06)

    def scaled(x):
        return x[:rows] * scale + (x[rows : rows + 1] + x[rows + 1 : rows + 2])

    units, logits = scaled(units + units_ref[...]), scaled(logits + logits_ref[...])
    count = logits.shape[1]
    lane = lax.broadcasted_iota(jnp.int32, logits.shape, 1)
    flags = [flag_refs[order.index(k)] for k in range(len(layout))]
    flags = [f[:, f.shape[1] - LANES :].astype(jnp.float32) for f in flags]
    flags = jnp.concatenate(flags, axis=0)[:, section * experts : section * experts + count]
    chosen = jnp.where(flags > 0.5, jax.nn.sigmoid(logits), 0.0)
    mine = jnp.sum(jnp.where(lane == lax.axis_index("ep"), chosen, 0.0), axis=1, keepdims=True)
    used = jnp.max(flags, axis=1, keepdims=True) > 0.5
    weight = jnp.where(used, mine / jnp.sum(chosen, axis=1, keepdims=True), 0.0)
    gate, upper = units[:, :hidden], units[:, hidden:]
    out = jnp.where(used, gate / (1.0 + jnp.exp(-gate)) * upper * weight, 0.0)
    out_ref[...] = narrow(out)


def half_front(blocks, flips, extra, shapes, order, section, mod, router, pair):
    xs = [x for k in order for x, _, _ in blocks[k]]
    layout = [[piece[1:] for piece in block] for block in blocks]
    rows, (width, units) = shapes[0].shape[0], pair.shape
    return pl.pallas_call(
        functools.partial(front_kernel, layout, order, flips, section, router.shape[0]),
        in_specs=[VMEM] * (len(xs) + 3 + len(extra)),
        out_shape=shapes,
        compiler_params=params(),
        cost_estimate=pl.CostEstimate(
            flops=rows * width * units, bytes_accessed=width * units, transcendentals=0
        ),
        name="front",
    )(*xs, mod, router, pair, *extra)


def front(blocks, flags, order, section, mod, router, pair):
    rows = sum(f.shape[0] for f in flags)
    units, experts = pair.shape[1], router.shape[0]
    width = pair.shape[0]
    common = (order, section, mod, router, pair)
    here = [[p for p in block if p[1] == width or p[2] & 1 == 0] for block in blocks]
    there = [[p for p in block if p[1] == width or p[2] & 1] for block in blocks]
    shapes = [jax.ShapeDtypeStruct(s, jnp.float32) for s in ((rows + 8, units), (rows + 8, experts), (rows, 1))]
    sums = half_front(here, (0, 2), [], shapes, *common)
    shapes = [jax.ShapeDtypeStruct((rows, units // 2), jnp.bfloat16)]
    return half_front(there, (1, 3), [flags[k] for k in order] + list(sums), shapes, *common)[0]


def store_blocks(total, groups, outs):
    rows = total.shape[0] // sum(len(group) for group in groups)
    for group, out in zip(groups, outs):
        blocks = [total[k * rows : (k + 1) * rows] for k in group]
        out[...] = jnp.concatenate(blocks, axis=0).astype(out.dtype)


def shapes_of(rows, cols, groups, types):
    slots = rows // sum(len(group) for group in groups)
    return [jax.ShapeDtypeStruct((slots * len(group), cols), t) for group, t in zip(groups, types)]


def down_kernel(flip, n_adds, groups, hidden_ref, down_ref, *refs):
    adds, outs = refs[:n_adds], refs[n_adds:]
    quarter = outs[0].shape[1]
    weights = down_ref[:, aligned(lax.axis_index("et") ^ flip, quarter)]
    total = jnp.dot(hidden_ref[...], weights, preferred_element_type=jnp.float32)
    for ref in adds:
        total += ref[...].astype(jnp.float32)
    store_blocks(total, groups, outs)


def down(hidden, w_down, flip, adds=(), groups=((0,),), types=(jnp.bfloat16,)):
    units, width = w_down.shape
    rows, quarter = hidden.shape[0], width // 4
    return pl.pallas_call(
        functools.partial(down_kernel, flip, len(adds), groups),
        in_specs=[VMEM] * (2 + len(adds)),
        out_shape=shapes_of(rows, quarter, groups, types),
        compiler_params=params(),
        cost_estimate=pl.CostEstimate(
            flops=2 * rows * units * quarter, bytes_accessed=2 * units * quarter, transcendentals=0
        ),
        name="down",
    )(hidden, w_down, *adds)


def add_kernel(groups, keep_ref, came_ref, *outs):
    store_blocks(keep_ref[...] + came_ref[...].astype(jnp.float32), groups, outs)


def add(keep, came, groups):
    return pl.pallas_call(
        functools.partial(add_kernel, groups),
        out_shape=shapes_of(*keep.shape, groups, [jnp.bfloat16] * len(groups)),
        compiler_params=params(),
        name="add",
    )(keep, came)


def diagonal(x, k, flip):
    n_ep, n_et = lax.axis_size("ep"), lax.axis_size("et")
    pairs = [(e * n_et + t, (e ^ k) * n_et + (t ^ flip)) for e in range(n_ep) for t in range(n_et)]
    return lax.ppermute(x, ("ep", "et"), pairs)


def move_kernel(order, last, own_ref, back_ref, pick_ref, extra_ref, *refs):
    came, outs = refs[: len(order)], refs[len(order) :]
    rows = [came[order.index(k)][...].astype(jnp.float32) for k in range(len(order))]
    rows[DIRECT] += extra_ref[...].astype(jnp.float32)
    velocity = product(back_ref[...], jnp.concatenate(rows, axis=0))
    moved = narrow(own_ref[...].astype(jnp.float32) - 0.5 * velocity)
    outs[0][...] = moved
    if last:
        outs[1][...] = narrow(velocity)
    else:
        slots = came[0].shape[0]
        picked = product(pick_ref[...], moved)
        for k, out in enumerate(outs[1:]):
            out[...] = narrow(picked[k * slots : (k + 1) * slots])


def move(own, back, pick, extra, came, order, last):
    shapes = [own.shape] + ([own.shape] if last else [c.shape for c in came])
    return pl.pallas_call(
        functools.partial(move_kernel, order, last),
        out_shape=[jax.ShapeDtypeStruct(s, jnp.bfloat16) for s in shapes],
        compiler_params=params(),
        name="move",
    )(own, back, pick, extra, *[came[k] for k in order])


DIRECT = 3


def sum_back(hidden, w_down, own, back, pick, last):
    peers = lax.axis_size("ep")
    rest = tuple(k for k in range(peers) if k != DIRECT)
    groups = (rest, (DIRECT,))
    (far,), (near,) = down(hidden, w_down, 3), down(hidden, w_down, 1)
    far, near = swap(far, "et", 1), swap(near, "et", 1)
    (crossing,) = down(hidden, w_down, 2, types=[jnp.float32])
    crossing, beside = add(crossing, far, groups)
    crossed, extra = swap(crossing, "et", 2), diagonal(beside, DIRECT, 2)
    kept, straight = down(hidden, w_down, 0, (near,), groups, [jnp.float32, jnp.bfloat16])
    blocks = dict(zip(rest, add(kept, crossed, [(i,) for i in range(len(rest))])))
    blocks[DIRECT] = straight
    came = [swap(blocks[k], "ep", k) if k else blocks[k] for k in range(peers)]
    order = [*range(2, peers), 1, 0]
    return move(own, back, pick, extra, came, order, last)


def spread(block, quarter, side=None):
    side = swap(block, "et", 2) if side is None else side
    near, far = swap(block, "et", 1), swap(side, "et", 1)
    return [(block, quarter, 0), (side, quarter, 2), (near, quarter, 1), (far, quarter, 3)]


def dense_body(tokens, modulation, router, gate_weight, up_weight, down_weight, expert_ids):
    rows, width = tokens.shape
    half, quarter = width // 2, width // 4
    router = router.T
    experts = router.shape[0]
    peers = lax.axis_size("ep")
    slots = 3 * rows * expert_ids.shape[2] // (2 * experts)
    ids = expert_ids.transpose(0, 2, 1)

    *packed, own = pack(tokens, ids, experts, slots)
    pair, w_down, done = load(gate_weight, up_weight, down_weight)
    mine, flags, *choice = own_rows(tokens, ids, experts, slots, done)
    pick, back = choice[2], choice[1::2]
    order = [*range(2, len(packed) + 1), 1]
    came = {k: swap(packed[k - 1], "ep", k) for k in order}
    halves = {k: relay(came[k], half, flags) for k in order}
    others = {k: swap(halves[k], "et", 1) for k in order}
    flags = [flags] + [came[k] for k in sorted(order)]
    blocks = [[(mine, width, 0)]] + [[(halves[k], half, 0), (others[k], half, 1)] for k in sorted(order)]
    hidden = front(blocks, flags, order + [0], 0, modulation, router, pair)
    own, *sent = sum_back(hidden, w_down, own, back[0], pick, False)

    sides = {DIRECT: diagonal(sent[DIRECT], DIRECT, 2)}
    blocks = [spread(swap(b, "ep", k) if k else b, quarter, sides.get(k)) for k, b in enumerate(sent)]
    hidden = front(blocks, flags, order + [0], 1, modulation, router, pair)
    return tuple(sum_back(hidden, w_down, own, back[1], pick, True))


def solution(mesh):
    in_specs = (
        P(("grp", "ep"), None),
        P(),
        P(),
        P("ep", None, "et"),
        P("ep", None, "et"),
        P("ep", "et", None),
        P(None, ("grp", "ep"), None),
    )
    out_specs = (P(("grp", "ep"), "et"), P(("grp", "ep"), "et"))

    def body(*args):
        experts, picks = args[2].shape[1], args[6].shape[2]
        peers = lax.axis_size("ep")
        fits = lax.axis_size("et") == 4 and peers >= 4 and peers & (peers - 1) == 0
        chosen = dense_body if fits and experts <= 2 * picks else routed_body
        return chosen(*args)

    return jax.shard_map(body, mesh=mesh, in_specs=in_specs, out_specs=out_specs, check_vma=False)
```

```python
import functools

import jax
import jax.numpy as jnp
from jax import lax
from jax.experimental import pallas as pl
from jax.experimental.pallas import tpu as pltpu
from jax.sharding import PartitionSpec as P


def normalize(x, mod):
    xf = x.astype(jnp.float32)
    scaled = xf * lax.rsqrt(jnp.mean(xf * xf, axis=-1, keepdims=True) + 1e-06)
    return (scaled * (1.0 + mod[0]) + mod[1]).astype(jnp.bfloat16)


def routed_section(x_full, x_cols, mod, ids, router, gate_weight, up_weight, down_weight):
    tok_rows = x_full.shape[0]
    width = x_full.shape[1]
    experts = router.shape[1]
    picks = ids.shape[1]
    n_peers = lax.axis_size("ep")
    quarter = width // lax.axis_size("et")
    slot_count = 3 * tok_rows * picks // (2 * experts)
    normed = normalize(x_full, mod)
    logits = jnp.dot(normed, router, preferred_element_type=jnp.float32)
    chosen = jax.nn.sigmoid(jnp.take_along_axis(logits, ids, axis=1))
    weight = chosen / jnp.sum(chosen, axis=1, keepdims=True)
    flat_e = ids.reshape(-1)
    onehot = (flat_e[:, None] == jnp.arange(experts, dtype=jnp.int32)).astype(jnp.int32)
    counted = jnp.cumsum(onehot, axis=0)
    slot = jnp.sum(onehot * (counted - 1), axis=1)
    repeated = jnp.repeat(normed, picks, axis=0)
    outbox = jnp.zeros((experts, slot_count, width), jnp.bfloat16).at[flat_e, slot].set(repeated)
    arrived = lax.all_to_all(outbox, "ep", split_axis=0, concat_axis=0, tiled=True)
    in_rows = arrived.reshape(n_peers * slot_count, width)
    gate = jnp.dot(in_rows, gate_weight[0], preferred_element_type=jnp.float32)
    upper = jnp.dot(in_rows, up_weight[0], preferred_element_type=jnp.float32)
    hidden = (jax.nn.silu(gate) * upper).astype(jnp.bfloat16)
    partial_out = jnp.dot(hidden, down_weight[0], preferred_element_type=jnp.float32)
    summed = lax.psum_scatter(
        partial_out.astype(jnp.bfloat16), "et", scatter_dimension=1, tiled=True
    )
    returned = lax.all_to_all(
        summed.reshape(n_peers, slot_count, quarter), "ep", split_axis=0, concat_axis=0, tiled=True
    )
    picked = returned[flat_e, slot].astype(jnp.float32).reshape(tok_rows, picks, quarter)
    velocity = jnp.sum(picked * weight[:, :, None], axis=1)
    moved = (x_cols.astype(jnp.float32) - 0.5 * velocity).astype(jnp.bfloat16)
    return (moved, velocity)


def routed_body(tokens, modulation, router, gate_weight, up_weight, down_weight, expert_ids):
    quarter = tokens.shape[1] // lax.axis_size("et")
    column_start = lax.axis_index("et") * quarter
    cols = lax.dynamic_slice_in_dim(tokens, column_start, quarter, 1)
    weights = (router, gate_weight, up_weight, down_weight)
    first, _ = routed_section(tokens, cols, modulation[0], expert_ids[0], *weights)
    full = lax.all_gather(first, "et", axis=1, tiled=True)
    second, velocity = routed_section(full, first, modulation[1], expert_ids[1], *weights)
    return (second, velocity.astype(jnp.bfloat16))


def swap(x, axis, bit):
    size = lax.axis_size(axis)
    return lax.ppermute(x, axis, [(i, i ^ bit) for i in range(size)])


LANES = 128
VMEM_LIMIT = 32 * 1024 * 1024
VMEM_MOST = 52 * 1024 * 1024
VMEM_ALL = 63 * 1024 * 1024
VMEM = pl.BlockSpec(memory_space=pltpu.VMEM)
ANY = pl.BlockSpec(memory_space=pl.ANY)


def params(limit=VMEM_LIMIT):
    return pltpu.CompilerParams(vmem_limit_bytes=limit)


def aligned(index, size):
    return pl.ds(pl.multiple_of(index * size, size), size)


def load_kernel(gate_ref, up_ref, down_ref, pair_ref, out_ref, done_ref, sems):
    hidden = gate_ref.shape[2]
    copies = [
        pltpu.make_async_copy(gate_ref.at[0], pair_ref.at[:, :hidden], sems.at[0]),
        pltpu.make_async_copy(up_ref.at[0], pair_ref.at[:, hidden:], sems.at[1]),
        pltpu.make_async_copy(down_ref.at[0], out_ref, sems.at[2]),
    ]
    for copy in copies:
        copy.start()
    for copy in copies:
        copy.wait()
    done_ref[...] = jnp.zeros_like(done_ref)


def load(gate, up, down):
    _, width, hidden = gate.shape
    return pl.pallas_call(
        load_kernel,
        in_specs=[ANY] * 3,
        out_specs=[VMEM] * 3,
        out_shape=[
            pltpu.VMEM((width, 2 * hidden), jnp.bfloat16),
            pltpu.VMEM((hidden, width), jnp.bfloat16),
            pltpu.VMEM((8, LANES), jnp.float32),
        ],
        scratch_shapes=[pltpu.SemaphoreType.DMA((3,))],
        compiler_params=params(VMEM_MOST),
        cost_estimate=pl.CostEstimate(flops=0, bytes_accessed=12 * width * hidden, transcendentals=0),
        name="load",
    )(gate, up, down)


def relay_kernel(block_ref, done_ref, out_ref):
    out_ref[...] = block_ref[:, : out_ref.shape[1]]


def relay(block, cols, done):
    return pl.pallas_call(
        relay_kernel,
        out_shape=jax.ShapeDtypeStruct((block.shape[0], cols), block.dtype),
        compiler_params=params(),
        name="relay",
    )(block, done)


def choices(ids, peers, slots):
    rows = ids[0].shape[1]
    me = lax.axis_index("ep")
    named = []
    for one in ids:
        for k in range(peers):
            hits = [jnp.where(one[p : p + 1, :] == me ^ k, 1.0, 0.0) for p in range(one.shape[0])]
            named.append(sum(hits))
    earlier = lax.broadcasted_iota(jnp.int32, (rows, rows), 0) < lax.broadcasted_iota(jnp.int32, (rows, rows), 1)
    ahead = jnp.dot(
        jnp.concatenate(named, axis=0).astype(jnp.bfloat16),
        jnp.where(earlier, 1.0, 0.0).astype(jnp.bfloat16),
        preferred_element_type=jnp.float32,
    ).astype(jnp.int32)
    slot = lax.broadcasted_iota(jnp.int32, (slots, rows), 0)
    holds = [jnp.where((ahead[i : i + 1, :] == slot) & (row > 0.5), 1.0, 0.0) for i, row in enumerate(named)]
    return [jnp.concatenate(holds[s * peers : (s + 1) * peers], axis=0) for s in range(len(ids))]


def narrow(x):
    return x.astype(jnp.bfloat16)


def product(x, y):
    return jnp.dot(narrow(x), narrow(y), preferred_element_type=jnp.float32)


def named_experts(ids, held, experts):
    rows = ids[0].shape[1]
    flags = []
    for s, one in enumerate(ids):
        lane = lax.broadcasted_iota(jnp.int32, (LANES, rows), 0)
        hits = [jnp.where(one[p : p + 1, :] + s * experts == lane, 1.0, 0.0) for p in range(one.shape[0])]
        flags.append(product(held[s], sum(hits).T))
    return sum(flags)


def pack_kernel(experts, tokens_ref, ids_ref, *refs):
    *out_refs, own_ref, half_ref, held_ref, sems = refs
    quarter = tokens_ref.shape[1] // 4
    half = 2 * quarter
    where = lax.axis_index("et")
    copies = [
        pltpu.make_async_copy(ids_ref, held_ref, sems.at[0]),
        pltpu.make_async_copy(tokens_ref.at[:, aligned(where & 1, quarter)], half_ref.at[:, :quarter], sems.at[1]),
        pltpu.make_async_copy(tokens_ref.at[:, aligned(where & 1 | 2, quarter)], half_ref.at[:, quarter:], sems.at[2]),
    ]
    for copy in copies:
        copy.start()
    copies[0].wait()
    ids = [held_ref[s] for s in range(held_ref.shape[0])]
    slots, peers = out_refs[0].shape[0], 1 + len(out_refs)
    held = choices(ids, peers, slots)
    flags = named_experts(ids, held, experts)
    copies[1].wait()
    copies[2].wait()
    own_ref[...] = half_ref[:, aligned(where >> 1, quarter)]
    picked = product(held[0][slots:], half_ref[...])
    for k, out_ref in enumerate(out_refs):
        out_ref[:, :half] = narrow(picked[k * slots : (k + 1) * slots])
        out_ref[:, half:] = narrow(flags[(k + 1) * slots : (k + 2) * slots])


def pack(tokens, ids, experts, slots):
    rows, width = tokens.shape
    others = lax.axis_size("ep") - 1
    shapes = [(slots, width // 2 + LANES)] * others + [(rows, width // 4)]
    return pl.pallas_call(
        functools.partial(pack_kernel, experts),
        in_specs=[ANY] * 2,
        out_specs=[VMEM] * len(shapes),
        out_shape=[pltpu.VMEM(s, jnp.bfloat16) for s in shapes],
        scratch_shapes=[
            pltpu.VMEM((rows, width // 2), jnp.bfloat16),
            pltpu.VMEM(ids.shape, jnp.int32),
            pltpu.SemaphoreType.DMA((3,)),
        ],
        compiler_params=params(VMEM_ALL),
        name="pack",
    )(tokens, ids)


def own_kernel(experts, tokens_ref, ids_ref, done_ref, out_ref, flags_ref, *choice_refs):
    ids = [ids_ref[s] for s in range(ids_ref.shape[0])]
    slots = out_ref.shape[0]
    held = choices(ids, choice_refs[0].shape[0] // slots, slots)
    flags_ref[...] = narrow(named_experts(ids, held, experts)[:slots])
    out_ref[...] = narrow(product(held[0][:slots], tokens_ref[...]))
    for s, one in enumerate(held):
        choice_refs[2 * s][...] = narrow(one)
        choice_refs[2 * s + 1][...] = narrow(one.T)


def own_rows(tokens, ids, experts, slots, done):
    rows, width = tokens.shape
    total = lax.axis_size("ep") * slots
    shapes = [(slots, width), (slots, LANES)] + [(total, rows), (rows, total)] * ids.shape[0]
    return pl.pallas_call(
        functools.partial(own_kernel, experts),
        out_shape=[jax.ShapeDtypeStruct(s, jnp.bfloat16) for s in shapes],
        compiler_params=params(),
        name="own_rows",
    )(tokens, ids, done)


def front_kernel(layout, order, flips, section, experts, *refs):
    n = sum(len(block) for block in layout)
    x_refs = list(refs[:n])
    mod_ref, router_ref, pair_ref, *rest = refs[n:]
    width = pair_ref.shape[0]
    quarter = width // 4
    et = lax.axis_index("et")
    blocks = {}
    for k in order:
        blocks[k] = [(x_refs.pop(0), cols, flip) for cols, flip in layout[k]]

    def part(block, flip):
        for ref, cols, at in block:
            if cols == quarter and at == flip:
                return ref[...].astype(jnp.float32)
            if cols == 2 * quarter and at == flip & 1:
                return ref[:, aligned((et ^ flip) >> 1, quarter)].astype(jnp.float32)
            if cols == width:
                return ref[:, aligned(et ^ flip, quarter)].astype(jnp.float32)

    units, logits, squares = 0.0, 0.0, 0.0
    for flip in flips:
        xf = jnp.concatenate([part(blocks[k], flip) for k in range(len(layout))], axis=0)
        squares += jnp.sum(xf * xf, axis=1, keepdims=True)
        where = aligned(et ^ flip, quarter)
        shift = mod_ref[section, 1:2, where]
        head = narrow(shift).astype(jnp.float32)
        blank = jnp.zeros((6, quarter), jnp.float32)
        lhs = [xf * (1.0 + mod_ref[section, 0:1, where]), head, shift - head, blank]
        lhs = narrow(jnp.concatenate(lhs, axis=0))
        units += jnp.dot(lhs, pair_ref[where, :], preferred_element_type=jnp.float32)
        logits += lax.dot_general(
            lhs, router_ref[:, where], (((1,), (1,)), ((), ())), preferred_element_type=jnp.float32
        )
    if len(rest) == 3:
        rest[0][...], rest[1][...], rest[2][...] = units, logits, squares
        return
    *flag_refs, units_ref, logits_ref, squares_ref, out_ref = rest
    rows, hidden = out_ref.shape
    scale = lax.rsqrt((squares + squares_ref[...]) / width + 1e-06)

    def scaled(x):
        return x[:rows] * scale + (x[rows : rows + 1] + x[rows + 1 : rows + 2])

    units, logits = scaled(units + units_ref[...]), scaled(logits + logits_ref[...])
    count = logits.shape[1]
    lane = lax.broadcasted_iota(jnp.int32, logits.shape, 1)
    flags = [flag_refs[order.index(k)] for k in range(len(layout))]
    flags = [f[:, f.shape[1] - LANES :].astype(jnp.float32) for f in flags]
    flags = jnp.concatenate(flags, axis=0)[:, section * experts : section * experts + count]
    chosen = jnp.where(flags > 0.5, jax.nn.sigmoid(logits), 0.0)
    mine = jnp.sum(jnp.where(lane == lax.axis_index("ep"), chosen, 0.0), axis=1, keepdims=True)
    used = jnp.max(flags, axis=1, keepdims=True) > 0.5
    weight = jnp.where(used, mine / jnp.sum(chosen, axis=1, keepdims=True), 0.0)
    gate, upper = units[:, :hidden], units[:, hidden:]
    out = jnp.where(used, gate / (1.0 + jnp.exp(-gate)) * upper * weight, 0.0)
    out_ref[...] = narrow(out)


def half_front(blocks, flips, extra, shapes, order, section, mod, router, pair):
    xs = [x for k in order for x, _, _ in blocks[k]]
    layout = [[piece[1:] for piece in block] for block in blocks]
    rows, (width, units) = shapes[0].shape[0], pair.shape
    return pl.pallas_call(
        functools.partial(front_kernel, layout, order, flips, section, router.shape[0]),
        in_specs=[VMEM] * (len(xs) + 3 + len(extra)),
        out_shape=shapes,
        compiler_params=params(),
        cost_estimate=pl.CostEstimate(
            flops=rows * width * units, bytes_accessed=width * units, transcendentals=0
        ),
        name="front",
    )(*xs, mod, router, pair, *extra)


def front(blocks, flags, order, section, mod, router, pair):
    rows = sum(f.shape[0] for f in flags)
    units, experts = pair.shape[1], router.shape[0]
    width = pair.shape[0]
    common = (order, section, mod, router, pair)
    here = [[p for p in block if p[1] == width or p[2] & 1 == 0] for block in blocks]
    there = [[p for p in block if p[1] == width or p[2] & 1] for block in blocks]
    shapes = [jax.ShapeDtypeStruct(s, jnp.float32) for s in ((rows + 8, units), (rows + 8, experts), (rows, 1))]
    sums = half_front(here, (0, 2), [], shapes, *common)
    shapes = [jax.ShapeDtypeStruct((rows, units // 2), jnp.bfloat16)]
    return half_front(there, (1, 3), [flags[k] for k in order] + list(sums), shapes, *common)[0]


def store_blocks(total, groups, outs):
    rows = total.shape[0] // sum(len(group) for group in groups)
    for group, out in zip(groups, outs):
        blocks = [total[k * rows : (k + 1) * rows] for k in group]
        out[...] = jnp.concatenate(blocks, axis=0).astype(out.dtype)


def shapes_of(rows, cols, groups, types):
    slots = rows // sum(len(group) for group in groups)
    return [jax.ShapeDtypeStruct((slots * len(group), cols), t) for group, t in zip(groups, types)]


def down_kernel(flip, n_adds, groups, hidden_ref, down_ref, *refs):
    adds, outs = refs[:n_adds], refs[n_adds:]
    quarter = outs[0].shape[1]
    weights = down_ref[:, aligned(lax.axis_index("et") ^ flip, quarter)]
    total = jnp.dot(hidden_ref[...], weights, preferred_element_type=jnp.float32)
    for ref in adds:
        total += ref[...].astype(jnp.float32)
    store_blocks(total, groups, outs)


def down(hidden, w_down, flip, adds=(), groups=((0,),), types=(jnp.bfloat16,)):
    units, width = w_down.shape
    rows, quarter = hidden.shape[0], width // 4
    return pl.pallas_call(
        functools.partial(down_kernel, flip, len(adds), groups),
        in_specs=[VMEM] * (2 + len(adds)),
        out_shape=shapes_of(rows, quarter, groups, types),
        compiler_params=params(),
        cost_estimate=pl.CostEstimate(
            flops=2 * rows * units * quarter, bytes_accessed=2 * units * quarter, transcendentals=0
        ),
        name="down",
    )(hidden, w_down, *adds)


def add_kernel(groups, keep_ref, came_ref, *outs):
    store_blocks(keep_ref[...] + came_ref[...].astype(jnp.float32), groups, outs)


def add(keep, came, groups):
    return pl.pallas_call(
        functools.partial(add_kernel, groups),
        out_shape=shapes_of(*keep.shape, groups, [jnp.bfloat16] * len(groups)),
        compiler_params=params(),
        name="add",
    )(keep, came)


def diagonal(x, k, flip):
    n_ep, n_et = lax.axis_size("ep"), lax.axis_size("et")
    pairs = [(e * n_et + t, (e ^ k) * n_et + (t ^ flip)) for e in range(n_ep) for t in range(n_et)]
    return lax.ppermute(x, ("ep", "et"), pairs)


def move_kernel(order, last, own_ref, back_ref, pick_ref, extra_ref, *refs):
    came, outs = refs[: len(order)], refs[len(order) :]
    rows = [came[order.index(k)][...].astype(jnp.float32) for k in range(len(order))]
    rows[DIRECT] += extra_ref[...].astype(jnp.float32)
    velocity = product(back_ref[...], jnp.concatenate(rows, axis=0))
    moved = narrow(own_ref[...].astype(jnp.float32) - 0.5 * velocity)
    outs[0][...] = moved
    if last:
        outs[1][...] = narrow(velocity)
    else:
        slots = came[0].shape[0]
        picked = product(pick_ref[...], moved)
        for k, out in enumerate(outs[1:]):
            out[...] = narrow(picked[k * slots : (k + 1) * slots])


def move(own, back, pick, extra, came, order, last):
    shapes = [own.shape] + ([own.shape] if last else [c.shape for c in came])
    return pl.pallas_call(
        functools.partial(move_kernel, order, last),
        out_shape=[jax.ShapeDtypeStruct(s, jnp.bfloat16) for s in shapes],
        compiler_params=params(),
        name="move",
    )(own, back, pick, extra, *[came[k] for k in order])


DIRECT = 3


def sum_back(hidden, w_down, own, back, pick, last):
    peers = lax.axis_size("ep")
    rest = tuple(k for k in range(peers) if k != DIRECT)
    groups = (rest, (DIRECT,))
    (far,), (near,) = down(hidden, w_down, 3), down(hidden, w_down, 1)
    far, near = swap(far, "et", 1), swap(near, "et", 1)
    (crossing,) = down(hidden, w_down, 2, types=[jnp.float32])
    crossing, beside = add(crossing, far, groups)
    crossed, extra = swap(crossing, "et", 2), diagonal(beside, DIRECT, 2)
    kept, straight = down(hidden, w_down, 0, (near,), groups, [jnp.float32, jnp.bfloat16])
    blocks = dict(zip(rest, add(kept, crossed, [(i,) for i in range(len(rest))])))
    blocks[DIRECT] = straight
    came = [swap(blocks[k], "ep", k) if k else blocks[k] for k in range(peers)]
    order = [*range(1, peers), 0]
    return move(own, back, pick, extra, came, order, last)


def spread(block, quarter):
    side = swap(block, "et", 2)
    near, far = swap(block, "et", 1), swap(side, "et", 1)
    return [(block, quarter, 0), (side, quarter, 2), (near, quarter, 1), (far, quarter, 3)]


def dense_body(tokens, modulation, router, gate_weight, up_weight, down_weight, expert_ids):
    rows, width = tokens.shape
    half, quarter = width // 2, width // 4
    router = router.T
    experts = router.shape[0]
    peers = lax.axis_size("ep")
    slots = 3 * rows * expert_ids.shape[2] // (2 * experts)
    ids = expert_ids.transpose(0, 2, 1)

    *packed, own = pack(tokens, ids, experts, slots)
    pair, w_down, done = load(gate_weight, up_weight, down_weight)
    mine, flags, *choice = own_rows(tokens, ids, experts, slots, done)
    pick, back = choice[2], choice[1::2]
    order = [*range(2, len(packed) + 1), 1]
    came = {k: swap(packed[k - 1], "ep", k) for k in order}
    halves = {k: relay(came[k], half, flags) for k in order}
    others = {k: swap(halves[k], "et", 1) for k in order}
    flags = [flags] + [came[k] for k in sorted(order)]
    blocks = [[(mine, width, 0)]] + [[(halves[k], half, 0), (others[k], half, 1)] for k in sorted(order)]
    hidden = front(blocks, flags, order + [0], 0, modulation, router, pair)
    own, *sent = sum_back(hidden, w_down, own, back[0], pick, False)

    blocks = [spread(swap(b, "ep", k) if k else b, quarter) for k, b in enumerate(sent)]
    hidden = front(blocks, flags, order + [0], 1, modulation, router, pair)
    return tuple(sum_back(hidden, w_down, own, back[1], pick, True))


def solution(mesh):
    in_specs = (
        P(("grp", "ep"), None),
        P(),
        P(),
        P("ep", None, "et"),
        P("ep", None, "et"),
        P("ep", "et", None),
        P(None, ("grp", "ep"), None),
    )
    out_specs = (P(("grp", "ep"), "et"), P(("grp", "ep"), "et"))

    def body(*args):
        experts, picks = args[2].shape[1], args[6].shape[2]
        peers = lax.axis_size("ep")
        fits = lax.axis_size("et") == 4 and peers >= 4 and peers & (peers - 1) == 0
        chosen = dense_body if fits and experts <= 2 * picks else routed_body
        return chosen(*args)

    return jax.shard_map(body, mesh=mesh, in_specs=in_specs, out_specs=out_specs, check_vma=False)
```

```python
import functools

import jax
import jax.numpy as jnp
from jax import lax
from jax.experimental import pallas as pl
from jax.experimental.pallas import tpu as pltpu
from jax.sharding import PartitionSpec as P


def normalize(x, mod):
    xf = x.astype(jnp.float32)
    scaled = xf * lax.rsqrt(jnp.mean(xf * xf, axis=-1, keepdims=True) + 1e-06)
    return (scaled * (1.0 + mod[0]) + mod[1]).astype(jnp.bfloat16)


def routed_section(x_full, x_cols, mod, ids, router, gate_weight, up_weight, down_weight):
    tok_rows = x_full.shape[0]
    width = x_full.shape[1]
    experts = router.shape[1]
    picks = ids.shape[1]
    n_peers = lax.axis_size("ep")
    quarter = width // lax.axis_size("et")
    slot_count = 3 * tok_rows * picks // (2 * experts)
    normed = normalize(x_full, mod)
    logits = jnp.dot(normed, router, preferred_element_type=jnp.float32)
    chosen = jax.nn.sigmoid(jnp.take_along_axis(logits, ids, axis=1))
    weight = chosen / jnp.sum(chosen, axis=1, keepdims=True)
    flat_e = ids.reshape(-1)
    onehot = (flat_e[:, None] == jnp.arange(experts, dtype=jnp.int32)).astype(jnp.int32)
    counted = jnp.cumsum(onehot, axis=0)
    slot = jnp.sum(onehot * (counted - 1), axis=1)
    repeated = jnp.repeat(normed, picks, axis=0)
    outbox = jnp.zeros((experts, slot_count, width), jnp.bfloat16).at[flat_e, slot].set(repeated)
    arrived = lax.all_to_all(outbox, "ep", split_axis=0, concat_axis=0, tiled=True)
    in_rows = arrived.reshape(n_peers * slot_count, width)
    gate = jnp.dot(in_rows, gate_weight[0], preferred_element_type=jnp.float32)
    upper = jnp.dot(in_rows, up_weight[0], preferred_element_type=jnp.float32)
    hidden = (jax.nn.silu(gate) * upper).astype(jnp.bfloat16)
    partial_out = jnp.dot(hidden, down_weight[0], preferred_element_type=jnp.float32)
    summed = lax.psum_scatter(
        partial_out.astype(jnp.bfloat16), "et", scatter_dimension=1, tiled=True
    )
    returned = lax.all_to_all(
        summed.reshape(n_peers, slot_count, quarter), "ep", split_axis=0, concat_axis=0, tiled=True
    )
    picked = returned[flat_e, slot].astype(jnp.float32).reshape(tok_rows, picks, quarter)
    velocity = jnp.sum(picked * weight[:, :, None], axis=1)
    moved = (x_cols.astype(jnp.float32) - 0.5 * velocity).astype(jnp.bfloat16)
    return (moved, velocity)


def routed_body(tokens, modulation, router, gate_weight, up_weight, down_weight, expert_ids):
    quarter = tokens.shape[1] // lax.axis_size("et")
    column_start = lax.axis_index("et") * quarter
    cols = lax.dynamic_slice_in_dim(tokens, column_start, quarter, 1)
    weights = (router, gate_weight, up_weight, down_weight)
    first, _ = routed_section(tokens, cols, modulation[0], expert_ids[0], *weights)
    full = lax.all_gather(first, "et", axis=1, tiled=True)
    second, velocity = routed_section(full, first, modulation[1], expert_ids[1], *weights)
    return (second, velocity.astype(jnp.bfloat16))


def swap(x, axis, bit):
    size = lax.axis_size(axis)
    return lax.ppermute(x, axis, [(i, i ^ bit) for i in range(size)])


LANES = 128
VMEM_LIMIT = 32 * 1024 * 1024
VMEM_MOST = 52 * 1024 * 1024
VMEM_ALL = 63 * 1024 * 1024
VMEM = pl.BlockSpec(memory_space=pltpu.VMEM)
ANY = pl.BlockSpec(memory_space=pl.ANY)


def params(limit=VMEM_LIMIT):
    return pltpu.CompilerParams(vmem_limit_bytes=limit)


def aligned(index, size):
    return pl.ds(pl.multiple_of(index * size, size), size)


def load_kernel(gate_ref, up_ref, down_ref, pair_ref, out_ref, done_ref, sems):
    hidden = gate_ref.shape[2]
    copies = [
        pltpu.make_async_copy(gate_ref.at[0], pair_ref.at[:, :hidden], sems.at[0]),
        pltpu.make_async_copy(up_ref.at[0], pair_ref.at[:, hidden:], sems.at[1]),
        pltpu.make_async_copy(down_ref.at[0], out_ref, sems.at[2]),
    ]
    for copy in copies:
        copy.start()
    for copy in copies:
        copy.wait()
    done_ref[...] = jnp.zeros_like(done_ref)


def load(gate, up, down):
    _, width, hidden = gate.shape
    return pl.pallas_call(
        load_kernel,
        in_specs=[ANY] * 3,
        out_specs=[VMEM] * 3,
        out_shape=[
            pltpu.VMEM((width, 2 * hidden), jnp.bfloat16),
            pltpu.VMEM((hidden, width), jnp.bfloat16),
            pltpu.VMEM((8, LANES), jnp.float32),
        ],
        scratch_shapes=[pltpu.SemaphoreType.DMA((3,))],
        compiler_params=params(VMEM_MOST),
        cost_estimate=pl.CostEstimate(flops=0, bytes_accessed=12 * width * hidden, transcendentals=0),
        name="load",
    )(gate, up, down)


def relay_kernel(block_ref, done_ref, out_ref):
    out_ref[...] = block_ref[:, : out_ref.shape[1]]


def relay(block, cols, done):
    return pl.pallas_call(
        relay_kernel,
        out_shape=jax.ShapeDtypeStruct((block.shape[0], cols), block.dtype),
        compiler_params=params(),
        name="relay",
    )(block, done)


def choices(ids, peers, slots):
    rows = ids[0].shape[1]
    me = lax.axis_index("ep")
    named = []
    for one in ids:
        for k in range(peers):
            hits = [jnp.where(one[p : p + 1, :] == me ^ k, 1.0, 0.0) for p in range(one.shape[0])]
            named.append(sum(hits))
    earlier = lax.broadcasted_iota(jnp.int32, (rows, rows), 0) < lax.broadcasted_iota(jnp.int32, (rows, rows), 1)
    ahead = jnp.dot(
        jnp.concatenate(named, axis=0).astype(jnp.bfloat16),
        jnp.where(earlier, 1.0, 0.0).astype(jnp.bfloat16),
        preferred_element_type=jnp.float32,
    ).astype(jnp.int32)
    slot = lax.broadcasted_iota(jnp.int32, (slots, rows), 0)
    holds = [jnp.where((ahead[i : i + 1, :] == slot) & (row > 0.5), 1.0, 0.0) for i, row in enumerate(named)]
    return [jnp.concatenate(holds[s * peers : (s + 1) * peers], axis=0) for s in range(len(ids))]


def narrow(x):
    return x.astype(jnp.bfloat16)


def product(x, y):
    return jnp.dot(narrow(x), narrow(y), preferred_element_type=jnp.float32)


def named_experts(ids, held, experts):
    rows = ids[0].shape[1]
    flags = []
    for s, one in enumerate(ids):
        lane = lax.broadcasted_iota(jnp.int32, (LANES, rows), 0)
        hits = [jnp.where(one[p : p + 1, :] + s * experts == lane, 1.0, 0.0) for p in range(one.shape[0])]
        over_rows = (((1,), (1,)), ((), ()))
        flags.append(
            lax.dot_general(narrow(held[s]), narrow(sum(hits)), over_rows, preferred_element_type=jnp.float32)
        )
    return sum(flags)


def pack_kernel(experts, tokens_ref, ids_ref, *refs):
    *out_refs, own_ref, half_ref, held_ref, sems = refs
    quarter = tokens_ref.shape[1] // 4
    half = 2 * quarter
    where = lax.axis_index("et")
    copies = [
        pltpu.make_async_copy(ids_ref, held_ref, sems.at[0]),
        pltpu.make_async_copy(tokens_ref.at[:, aligned(where & 1, quarter)], half_ref.at[:, :quarter], sems.at[1]),
        pltpu.make_async_copy(tokens_ref.at[:, aligned(where & 1 | 2, quarter)], half_ref.at[:, quarter:], sems.at[2]),
    ]
    for copy in copies:
        copy.start()
    copies[0].wait()
    ids = [held_ref[s] for s in range(held_ref.shape[0])]
    slots, peers = out_refs[0].shape[0], 1 + len(out_refs)
    held = choices(ids, peers, slots)
    flags = named_experts(ids, held, experts)
    copies[1].wait()
    copies[2].wait()
    own_ref[...] = half_ref[:, aligned(where >> 1, quarter)]
    picked = product(held[0][slots:], half_ref[...])
    for k, out_ref in enumerate(out_refs):
        out_ref[:, :half] = narrow(picked[k * slots : (k + 1) * slots])
        out_ref[:, half:] = narrow(flags[(k + 1) * slots : (k + 2) * slots])


def pack(tokens, ids, experts, slots):
    rows, width = tokens.shape
    others = lax.axis_size("ep") - 1
    shapes = [(slots, width // 2 + LANES)] * others + [(rows, width // 4)]
    return pl.pallas_call(
        functools.partial(pack_kernel, experts),
        in_specs=[ANY] * 2,
        out_specs=[VMEM] * len(shapes),
        out_shape=[pltpu.VMEM(s, jnp.bfloat16) for s in shapes],
        scratch_shapes=[
            pltpu.VMEM((rows, width // 2), jnp.bfloat16),
            pltpu.VMEM(ids.shape, jnp.int32),
            pltpu.SemaphoreType.DMA((3,)),
        ],
        compiler_params=params(VMEM_ALL),
        name="pack",
    )(tokens, ids)


def own_kernel(experts, tokens_ref, ids_ref, done_ref, out_ref, flags_ref, *choice_refs):
    ids = [ids_ref[s] for s in range(ids_ref.shape[0])]
    slots = out_ref.shape[0]
    held = choices(ids, choice_refs[0].shape[0] // slots, slots)
    flags_ref[...] = narrow(named_experts(ids, held, experts)[:slots])
    out_ref[...] = narrow(product(held[0][:slots], tokens_ref[...]))
    for s, one in enumerate(held):
        choice_refs[2 * s][...] = narrow(one)
        choice_refs[2 * s + 1][...] = narrow(one.T)


def own_rows(tokens, ids, experts, slots, done):
    rows, width = tokens.shape
    total = lax.axis_size("ep") * slots
    shapes = [(slots, width), (slots, LANES)] + [(total, rows), (rows, total)] * ids.shape[0]
    return pl.pallas_call(
        functools.partial(own_kernel, experts),
        out_shape=[jax.ShapeDtypeStruct(s, jnp.bfloat16) for s in shapes],
        compiler_params=params(),
        name="own_rows",
    )(tokens, ids, done)


def front_kernel(layout, order, flips, section, experts, *refs):
    n = sum(len(block) for block in layout)
    x_refs = list(refs[:n])
    mod_ref, router_ref, pair_ref, *rest = refs[n:]
    width = pair_ref.shape[0]
    quarter = width // 4
    et = lax.axis_index("et")
    blocks = {}
    for k in order:
        blocks[k] = [(x_refs.pop(0), cols, flip) for cols, flip in layout[k]]

    def part(block, flip):
        for ref, cols, at in block:
            if cols == quarter and at == flip:
                return ref[...].astype(jnp.float32)
            if cols == 2 * quarter and at == flip & 1:
                return ref[:, aligned((et ^ flip) >> 1, quarter)].astype(jnp.float32)
            if cols == width:
                return ref[:, aligned(et ^ flip, quarter)].astype(jnp.float32)

    units, logits, squares = 0.0, 0.0, 0.0
    for flip in flips:
        xf = jnp.concatenate([part(blocks[k], flip) for k in range(len(layout))], axis=0)
        squares += jnp.sum(xf * xf, axis=1, keepdims=True)
        where = aligned(et ^ flip, quarter)
        shift = mod_ref[section, 1:2, where]
        head = narrow(shift).astype(jnp.float32)
        blank = jnp.zeros((6, quarter), jnp.float32)
        lhs = [xf * (1.0 + mod_ref[section, 0:1, where]), head, shift - head, blank]
        lhs = narrow(jnp.concatenate(lhs, axis=0))
        units += jnp.dot(lhs, pair_ref[where, :], preferred_element_type=jnp.float32)
        logits += lax.dot_general(
            lhs, router_ref[:, where], (((1,), (1,)), ((), ())), preferred_element_type=jnp.float32
        )
    if len(rest) == 3:
        rest[0][...], rest[1][...], rest[2][...] = units, logits, squares
        return
    *flag_refs, units_ref, logits_ref, squares_ref, out_ref = rest
    rows, hidden = out_ref.shape
    scale = lax.rsqrt((squares + squares_ref[...]) / width + 1e-06)

    def scaled(x):
        return x[:rows] * scale + (x[rows : rows + 1] + x[rows + 1 : rows + 2])

    units, logits = scaled(units + units_ref[...]), scaled(logits + logits_ref[...])
    count = logits.shape[1]
    lane = lax.broadcasted_iota(jnp.int32, logits.shape, 1)
    flags = [flag_refs[order.index(k)] for k in range(len(layout))]
    flags = [f[:, f.shape[1] - LANES :].astype(jnp.float32) for f in flags]
    flags = jnp.concatenate(flags, axis=0)[:, section * experts : section * experts + count]
    chosen = jnp.where(flags > 0.5, jax.nn.sigmoid(logits), 0.0)
    mine = jnp.sum(jnp.where(lane == lax.axis_index("ep"), chosen, 0.0), axis=1, keepdims=True)
    used = jnp.max(flags, axis=1, keepdims=True) > 0.5
    weight = jnp.where(used, mine / jnp.sum(chosen, axis=1, keepdims=True), 0.0)
    gate, upper = units[:, :hidden], units[:, hidden:]
    out = jnp.where(used, gate / (1.0 + jnp.exp(-gate)) * upper * weight, 0.0)
    out_ref[...] = narrow(out)


def half_front(blocks, flips, extra, shapes, order, section, mod, router, pair):
    xs = [x for k in order for x, _, _ in blocks[k]]
    layout = [[piece[1:] for piece in block] for block in blocks]
    rows, (width, units) = shapes[0].shape[0], pair.shape
    return pl.pallas_call(
        functools.partial(front_kernel, layout, order, flips, section, router.shape[0]),
        in_specs=[VMEM] * (len(xs) + 3 + len(extra)),
        out_shape=shapes,
        compiler_params=params(),
        cost_estimate=pl.CostEstimate(
            flops=rows * width * units, bytes_accessed=width * units, transcendentals=0
        ),
        name="front",
    )(*xs, mod, router, pair, *extra)


def front(blocks, flags, order, section, mod, router, pair):
    rows = sum(f.shape[0] for f in flags)
    units, experts = pair.shape[1], router.shape[0]
    width = pair.shape[0]
    common = (order, section, mod, router, pair)
    here = [[p for p in block if p[1] == width or p[2] & 1 == 0] for block in blocks]
    there = [[p for p in block if p[1] == width or p[2] & 1] for block in blocks]
    shapes = [jax.ShapeDtypeStruct(s, jnp.float32) for s in ((rows + 8, units), (rows + 8, experts), (rows, 1))]
    sums = half_front(here, (0, 2), [], shapes, *common)
    shapes = [jax.ShapeDtypeStruct((rows, units // 2), jnp.bfloat16)]
    return half_front(there, (1, 3), [flags[k] for k in order] + list(sums), shapes, *common)[0]


def store_blocks(total, groups, outs):
    rows = total.shape[0] // sum(len(group) for group in groups)
    for group, out in zip(groups, outs):
        blocks = [total[k * rows : (k + 1) * rows] for k in group]
        out[...] = jnp.concatenate(blocks, axis=0).astype(out.dtype)


def shapes_of(rows, cols, groups, types):
    slots = rows // sum(len(group) for group in groups)
    return [jax.ShapeDtypeStruct((slots * len(group), cols), t) for group, t in zip(groups, types)]


def down_kernel(flip, n_adds, groups, hidden_ref, down_ref, *refs):
    adds, outs = refs[:n_adds], refs[n_adds:]
    quarter = outs[0].shape[1]
    weights = down_ref[:, aligned(lax.axis_index("et") ^ flip, quarter)]
    total = jnp.dot(hidden_ref[...], weights, preferred_element_type=jnp.float32)
    for ref in adds:
        total += ref[...].astype(jnp.float32)
    store_blocks(total, groups, outs)


def down(hidden, w_down, flip, adds=(), groups=((0,),), types=(jnp.bfloat16,)):
    units, width = w_down.shape
    rows, quarter = hidden.shape[0], width // 4
    return pl.pallas_call(
        functools.partial(down_kernel, flip, len(adds), groups),
        in_specs=[VMEM] * (2 + len(adds)),
        out_shape=shapes_of(rows, quarter, groups, types),
        compiler_params=params(),
        cost_estimate=pl.CostEstimate(
            flops=2 * rows * units * quarter, bytes_accessed=2 * units * quarter, transcendentals=0
        ),
        name="down",
    )(hidden, w_down, *adds)


def add_kernel(groups, keep_ref, came_ref, *outs):
    store_blocks(keep_ref[...] + came_ref[...].astype(jnp.float32), groups, outs)


def add(keep, came, groups):
    return pl.pallas_call(
        functools.partial(add_kernel, groups),
        out_shape=shapes_of(*keep.shape, groups, [jnp.bfloat16] * len(groups)),
        compiler_params=params(),
        name="add",
    )(keep, came)


def diagonal(x, k, flip):
    n_ep, n_et = lax.axis_size("ep"), lax.axis_size("et")
    pairs = [(e * n_et + t, (e ^ k) * n_et + (t ^ flip)) for e in range(n_ep) for t in range(n_et)]
    return lax.ppermute(x, ("ep", "et"), pairs)


def move_kernel(order, last, own_ref, back_ref, pick_ref, extra_ref, *refs):
    came, outs = refs[: len(order)], refs[len(order) :]
    rows = [came[order.index(k)][...].astype(jnp.float32) for k in range(len(order))]
    rows[DIRECT] += extra_ref[...].astype(jnp.float32)
    velocity = product(back_ref[...], jnp.concatenate(rows, axis=0))
    moved = narrow(own_ref[...].astype(jnp.float32) - 0.5 * velocity)
    outs[0][...] = moved
    if last:
        outs[1][...] = narrow(velocity)
    else:
        slots = came[0].shape[0]
        picked = product(pick_ref[...], moved)
        for k, out in enumerate(outs[1:]):
            out[...] = narrow(picked[k * slots : (k + 1) * slots])


def move(own, back, pick, extra, came, order, last):
    shapes = [own.shape] + ([own.shape] if last else [c.shape for c in came])
    return pl.pallas_call(
        functools.partial(move_kernel, order, last),
        out_shape=[jax.ShapeDtypeStruct(s, jnp.bfloat16) for s in shapes],
        compiler_params=params(),
        name="move",
    )(own, back, pick, extra, *[came[k] for k in order])


DIRECT = 3


def sum_back(hidden, w_down, own, back, pick, last):
    peers = lax.axis_size("ep")
    rest = tuple(k for k in range(peers) if k != DIRECT)
    groups = (rest, (DIRECT,))
    (far,), (near,) = down(hidden, w_down, 3), down(hidden, w_down, 1)
    far, near = swap(far, "et", 1), swap(near, "et", 1)
    (crossing,) = down(hidden, w_down, 2, types=[jnp.float32])
    crossing, beside = add(crossing, far, groups)
    crossed, extra = swap(crossing, "et", 2), diagonal(beside, DIRECT, 2)
    kept, straight = down(hidden, w_down, 0, (near,), groups, [jnp.float32, jnp.bfloat16])
    blocks = dict(zip(rest, add(kept, crossed, [(i,) for i in range(len(rest))])))
    blocks[DIRECT] = straight
    came = [swap(blocks[k], "ep", k) if k else blocks[k] for k in range(peers)]
    order = [*range(2, peers), 1, 0]
    return move(own, back, pick, extra, came, order, last)


def spread(block, quarter):
    side = swap(block, "et", 2)
    near, far = swap(block, "et", 1), swap(side, "et", 1)
    return [(block, quarter, 0), (side, quarter, 2), (near, quarter, 1), (far, quarter, 3)]


def dense_body(tokens, modulation, router, gate_weight, up_weight, down_weight, expert_ids):
    rows, width = tokens.shape
    half, quarter = width // 2, width // 4
    router = router.T
    experts = router.shape[0]
    peers = lax.axis_size("ep")
    slots = 3 * rows * expert_ids.shape[2] // (2 * experts)
    ids = expert_ids.transpose(0, 2, 1)

    *packed, own = pack(tokens, ids, experts, slots)
    pair, w_down, done = load(gate_weight, up_weight, down_weight)
    mine, flags, *choice = own_rows(tokens, ids, experts, slots, done)
    pick, back = choice[2], choice[1::2]
    order = [*range(2, len(packed) + 1), 1]
    came = {k: swap(packed[k - 1], "ep", k) for k in order}
    halves = {k: relay(came[k], half, flags) for k in order}
    others = {k: swap(halves[k], "et", 1) for k in order}
    flags = [flags] + [came[k] for k in sorted(order)]
    blocks = [[(mine, width, 0)]] + [[(halves[k], half, 0), (others[k], half, 1)] for k in sorted(order)]
    hidden = front(blocks, flags, order + [0], 0, modulation, router, pair)
    own, *sent = sum_back(hidden, w_down, own, back[0], pick, False)

    blocks = [spread(swap(b, "ep", k) if k else b, quarter) for k, b in enumerate(sent)]
    hidden = front(blocks, flags, order + [0], 1, modulation, router, pair)
    return tuple(sum_back(hidden, w_down, own, back[1], pick, True))


def solution(mesh):
    in_specs = (
        P(("grp", "ep"), None),
        P(),
        P(),
        P("ep", None, "et"),
        P("ep", None, "et"),
        P("ep", "et", None),
        P(None, ("grp", "ep"), None),
    )
    out_specs = (P(("grp", "ep"), "et"), P(("grp", "ep"), "et"))

    def body(*args):
        experts, picks = args[2].shape[1], args[6].shape[2]
        peers = lax.axis_size("ep")
        fits = lax.axis_size("et") == 4 and peers >= 4 and peers & (peers - 1) == 0
        chosen = dense_body if fits and experts <= 2 * picks else routed_body
        return chosen(*args)

    return jax.shard_map(body, mesh=mesh, in_specs=in_specs, out_specs=out_specs, check_vma=False)
```

```python
import functools

import jax
import jax.numpy as jnp
from jax import lax
from jax.experimental import pallas as pl
from jax.experimental.pallas import tpu as pltpu
from jax.sharding import PartitionSpec as P


def normalize(x, mod):
    xf = x.astype(jnp.float32)
    scaled = xf * lax.rsqrt(jnp.mean(xf * xf, axis=-1, keepdims=True) + 1e-06)
    return (scaled * (1.0 + mod[0]) + mod[1]).astype(jnp.bfloat16)


def routed_section(x_full, x_cols, mod, ids, router, gate_weight, up_weight, down_weight):
    tok_rows = x_full.shape[0]
    width = x_full.shape[1]
    experts = router.shape[1]
    picks = ids.shape[1]
    n_peers = lax.axis_size("ep")
    quarter = width // lax.axis_size("et")
    slot_count = 3 * tok_rows * picks // (2 * experts)
    normed = normalize(x_full, mod)
    logits = jnp.dot(normed, router, preferred_element_type=jnp.float32)
    chosen = jax.nn.sigmoid(jnp.take_along_axis(logits, ids, axis=1))
    weight = chosen / jnp.sum(chosen, axis=1, keepdims=True)
    flat_e = ids.reshape(-1)
    onehot = (flat_e[:, None] == jnp.arange(experts, dtype=jnp.int32)).astype(jnp.int32)
    counted = jnp.cumsum(onehot, axis=0)
    slot = jnp.sum(onehot * (counted - 1), axis=1)
    repeated = jnp.repeat(normed, picks, axis=0)
    outbox = jnp.zeros((experts, slot_count, width), jnp.bfloat16).at[flat_e, slot].set(repeated)
    arrived = lax.all_to_all(outbox, "ep", split_axis=0, concat_axis=0, tiled=True)
    in_rows = arrived.reshape(n_peers * slot_count, width)
    gate = jnp.dot(in_rows, gate_weight[0], preferred_element_type=jnp.float32)
    upper = jnp.dot(in_rows, up_weight[0], preferred_element_type=jnp.float32)
    hidden = (jax.nn.silu(gate) * upper).astype(jnp.bfloat16)
    partial_out = jnp.dot(hidden, down_weight[0], preferred_element_type=jnp.float32)
    summed = lax.psum_scatter(
        partial_out.astype(jnp.bfloat16), "et", scatter_dimension=1, tiled=True
    )
    returned = lax.all_to_all(
        summed.reshape(n_peers, slot_count, quarter), "ep", split_axis=0, concat_axis=0, tiled=True
    )
    picked = returned[flat_e, slot].astype(jnp.float32).reshape(tok_rows, picks, quarter)
    velocity = jnp.sum(picked * weight[:, :, None], axis=1)
    moved = (x_cols.astype(jnp.float32) - 0.5 * velocity).astype(jnp.bfloat16)
    return (moved, velocity)


def routed_body(tokens, modulation, router, gate_weight, up_weight, down_weight, expert_ids):
    quarter = tokens.shape[1] // lax.axis_size("et")
    column_start = lax.axis_index("et") * quarter
    cols = lax.dynamic_slice_in_dim(tokens, column_start, quarter, 1)
    weights = (router, gate_weight, up_weight, down_weight)
    first, _ = routed_section(tokens, cols, modulation[0], expert_ids[0], *weights)
    full = lax.all_gather(first, "et", axis=1, tiled=True)
    second, velocity = routed_section(full, first, modulation[1], expert_ids[1], *weights)
    return (second, velocity.astype(jnp.bfloat16))


def swap(x, axis, bit):
    size = lax.axis_size(axis)
    return lax.ppermute(x, axis, [(i, i ^ bit) for i in range(size)])


LANES = 128
VMEM_LIMIT = 32 * 1024 * 1024
VMEM_MOST = 52 * 1024 * 1024
VMEM_ALL = 63 * 1024 * 1024
VMEM = pl.BlockSpec(memory_space=pltpu.VMEM)
ANY = pl.BlockSpec(memory_space=pl.ANY)


def params(limit=VMEM_LIMIT):
    return pltpu.CompilerParams(vmem_limit_bytes=limit)


def aligned(index, size):
    return pl.ds(pl.multiple_of(index * size, size), size)


def load_kernel(gate_ref, up_ref, down_ref, pair_ref, out_ref, done_ref, sems):
    hidden = gate_ref.shape[2]
    copies = [
        pltpu.make_async_copy(gate_ref.at[0], pair_ref.at[:, :hidden], sems.at[0]),
        pltpu.make_async_copy(up_ref.at[0], pair_ref.at[:, hidden:], sems.at[1]),
        pltpu.make_async_copy(down_ref.at[0], out_ref, sems.at[2]),
    ]
    for copy in copies:
        copy.start()
    for copy in copies:
        copy.wait()
    done_ref[...] = jnp.zeros_like(done_ref)


def load(gate, up, down):
    _, width, hidden = gate.shape
    return pl.pallas_call(
        load_kernel,
        in_specs=[ANY] * 3,
        out_specs=[VMEM] * 3,
        out_shape=[
            pltpu.VMEM((width, 2 * hidden), jnp.bfloat16),
            pltpu.VMEM((hidden, width), jnp.bfloat16),
            pltpu.VMEM((8, LANES), jnp.float32),
        ],
        scratch_shapes=[pltpu.SemaphoreType.DMA((3,))],
        compiler_params=params(VMEM_MOST),
        cost_estimate=pl.CostEstimate(flops=0, bytes_accessed=12 * width * hidden, transcendentals=0),
        name="load",
    )(gate, up, down)


def relay_kernel(block_ref, done_ref, out_ref):
    out_ref[...] = block_ref[:, : out_ref.shape[1]]


def relay(block, cols, done):
    return pl.pallas_call(
        relay_kernel,
        out_shape=jax.ShapeDtypeStruct((block.shape[0], cols), block.dtype),
        compiler_params=params(),
        name="relay",
    )(block, done)


def choices(ids, peers, slots):
    rows = ids[0].shape[1]
    me = lax.axis_index("ep")
    named = []
    for one in ids:
        for k in range(peers):
            hits = [jnp.where(one[p : p + 1, :] == me ^ k, 1.0, 0.0) for p in range(one.shape[0])]
            named.append(sum(hits))
    earlier = lax.broadcasted_iota(jnp.int32, (rows, rows), 0) < lax.broadcasted_iota(jnp.int32, (rows, rows), 1)
    ahead = jnp.dot(
        jnp.concatenate(named, axis=0).astype(jnp.bfloat16),
        jnp.where(earlier, 1.0, 0.0).astype(jnp.bfloat16),
        preferred_element_type=jnp.float32,
    ).astype(jnp.int32)
    slot = lax.broadcasted_iota(jnp.int32, (slots, rows), 0)
    holds = [jnp.where((ahead[i : i + 1, :] == slot) & (row > 0.5), 1.0, 0.0) for i, row in enumerate(named)]
    return [jnp.concatenate(holds[s * peers : (s + 1) * peers], axis=0) for s in range(len(ids))]


def narrow(x):
    return x.astype(jnp.bfloat16)


def product(x, y):
    return jnp.dot(narrow(x), narrow(y), preferred_element_type=jnp.float32)


def named_experts(ids, held, experts):
    rows = ids[0].shape[1]
    flags = []
    for s, one in enumerate(ids):
        lane = lax.broadcasted_iota(jnp.int32, (LANES, rows), 0)
        hits = [jnp.where(one[p : p + 1, :] + s * experts == lane, 1.0, 0.0) for p in range(one.shape[0])]
        flags.append(product(held[s], sum(hits).T))
    return sum(flags)


def pack_kernel(experts, tokens_ref, ids_ref, *refs):
    *out_refs, own_ref, half_ref, held_ref, sems = refs
    quarter = tokens_ref.shape[1] // 4
    half = 2 * quarter
    where = lax.axis_index("et")
    copies = [
        pltpu.make_async_copy(ids_ref, held_ref, sems.at[0]),
        pltpu.make_async_copy(tokens_ref.at[:, aligned(where & 1, quarter)], half_ref.at[:, :quarter], sems.at[1]),
        pltpu.make_async_copy(tokens_ref.at[:, aligned(where & 1 | 2, quarter)], half_ref.at[:, quarter:], sems.at[2]),
    ]
    for copy in copies:
        copy.start()
    copies[0].wait()
    ids = [held_ref[s] for s in range(held_ref.shape[0])]
    slots, peers = out_refs[0].shape[0], 1 + len(out_refs)
    held = choices(ids, peers, slots)
    flags = named_experts(ids, held, experts)
    copies[1].wait()
    copies[2].wait()
    own_ref[...] = half_ref[:, aligned(where >> 1, quarter)]
    picked = product(held[0][slots:], half_ref[...])
    for k, out_ref in enumerate(out_refs):
        out_ref[:, :half] = narrow(picked[k * slots : (k + 1) * slots])
        out_ref[:, half:] = narrow(flags[(k + 1) * slots : (k + 2) * slots])


def pack(tokens, ids, experts, slots):
    rows, width = tokens.shape
    others = lax.axis_size("ep") - 1
    shapes = [(slots, width // 2 + LANES)] * others + [(rows, width // 4)]
    return pl.pallas_call(
        functools.partial(pack_kernel, experts),
        in_specs=[ANY] * 2,
        out_specs=[VMEM] * len(shapes),
        out_shape=[pltpu.VMEM(s, jnp.bfloat16) for s in shapes],
        scratch_shapes=[
            pltpu.VMEM((rows, width // 2), jnp.bfloat16),
            pltpu.VMEM(ids.shape, jnp.int32),
            pltpu.SemaphoreType.DMA((3,)),
        ],
        compiler_params=params(VMEM_ALL),
        name="pack",
    )(tokens, ids)


def own_kernel(experts, tokens_ref, ids_ref, done_ref, out_ref, flags_ref, *choice_refs):
    ids = [ids_ref[s] for s in range(ids_ref.shape[0])]
    slots = out_ref.shape[0]
    held = choices(ids, choice_refs[0].shape[0] // slots, slots)
    flags_ref[...] = narrow(named_experts(ids, held, experts)[:slots])
    out_ref[...] = narrow(product(held[0][:slots], tokens_ref[...]))
    for s, one in enumerate(held):
        choice_refs[2 * s][...] = narrow(one)
        choice_refs[2 * s + 1][...] = narrow(one.T)


def own_rows(tokens, ids, experts, slots, done):
    rows, width = tokens.shape
    total = lax.axis_size("ep") * slots
    shapes = [(slots, width), (slots, LANES)] + [(total, rows), (rows, total)] * ids.shape[0]
    return pl.pallas_call(
        functools.partial(own_kernel, experts),
        out_shape=[jax.ShapeDtypeStruct(s, jnp.bfloat16) for s in shapes],
        compiler_params=params(),
        name="own_rows",
    )(tokens, ids, done)


def front_kernel(layout, order, flips, section, experts, *refs):
    n = sum(len(block) for block in layout)
    x_refs = list(refs[:n])
    mod_ref, router_ref, pair_ref, *rest = refs[n:]
    width = pair_ref.shape[0]
    quarter = width // 4
    et = lax.axis_index("et")
    blocks = {}
    for k in order:
        blocks[k] = [(x_refs.pop(0), cols, flip) for cols, flip in layout[k]]

    def part(block, flip):
        for ref, cols, at in block:
            if cols == quarter and at == flip:
                return ref[...].astype(jnp.float32)
            if cols == 2 * quarter and at == flip & 1:
                return ref[:, aligned((et ^ flip) >> 1, quarter)].astype(jnp.float32)
            if cols == width:
                return ref[:, aligned(et ^ flip, quarter)].astype(jnp.float32)

    units, logits, squares = 0.0, 0.0, 0.0
    for flip in flips:
        xf = jnp.concatenate([part(blocks[k], flip) for k in range(len(layout))], axis=0)
        squares += jnp.sum(xf * xf, axis=1, keepdims=True)
        where = aligned(et ^ flip, quarter)
        shift = mod_ref[section, 1:2, where]
        head = narrow(shift).astype(jnp.float32)
        blank = jnp.zeros((6, quarter), jnp.float32)
        lhs = [xf * (1.0 + mod_ref[section, 0:1, where]), head, shift - head, blank]
        lhs = narrow(jnp.concatenate(lhs, axis=0))
        units += jnp.dot(lhs, pair_ref[where, :], preferred_element_type=jnp.float32)
        logits += lax.dot_general(
            lhs, router_ref[:, where], (((1,), (1,)), ((), ())), preferred_element_type=jnp.float32
        )
    if len(rest) == 3:
        rest[0][...], rest[1][...], rest[2][...] = units, logits, squares
        return
    *flag_refs, units_ref, logits_ref, squares_ref, out_ref = rest
    rows, hidden = out_ref.shape
    scale = lax.rsqrt((squares + squares_ref[...]) / width + 1e-06)

    def scaled(x):
        return x[:rows] * scale + (x[rows : rows + 1] + x[rows + 1 : rows + 2])

    units, logits = scaled(units + units_ref[...]), scaled(logits + logits_ref[...])
    count = logits.shape[1]
    lane = lax.broadcasted_iota(jnp.int32, logits.shape, 1)
    flags = [flag_refs[order.index(k)] for k in range(len(layout))]
    flags = [f[:, f.shape[1] - LANES :].astype(jnp.float32) for f in flags]
    flags = jnp.concatenate(flags, axis=0)[:, section * experts : section * experts + count]
    chosen = jnp.where(flags > 0.5, jax.nn.sigmoid(logits), 0.0)
    mine = jnp.sum(jnp.where(lane == lax.axis_index("ep"), chosen, 0.0), axis=1, keepdims=True)
    used = jnp.max(flags, axis=1, keepdims=True) > 0.5
    weight = jnp.where(used, mine / jnp.sum(chosen, axis=1, keepdims=True), 0.0)
    gate, upper = units[:, :hidden], units[:, hidden:]
    out = jnp.where(used, gate / (1.0 + jnp.exp(-gate)) * upper * weight, 0.0)
    out_ref[...] = narrow(out)


def half_front(blocks, flips, extra, shapes, order, section, mod, router, pair):
    xs = [x for k in order for x, _, _ in blocks[k]]
    layout = [[piece[1:] for piece in block] for block in blocks]
    rows, (width, units) = shapes[0].shape[0], pair.shape
    return pl.pallas_call(
        functools.partial(front_kernel, layout, order, flips, section, router.shape[0]),
        in_specs=[VMEM] * (len(xs) + 3 + len(extra)),
        out_shape=shapes,
        compiler_params=params(),
        cost_estimate=pl.CostEstimate(
            flops=rows * width * units, bytes_accessed=width * units, transcendentals=0
        ),
        name="front",
    )(*xs, mod, router, pair, *extra)


def front(blocks, flags, order, section, mod, router, pair):
    rows = sum(f.shape[0] for f in flags)
    units, experts = pair.shape[1], router.shape[0]
    width = pair.shape[0]
    common = (order, section, mod, router, pair)
    here = [[p for p in block if p[1] == width or p[2] & 1 == 0] for block in blocks]
    there = [[p for p in block if p[1] == width or p[2] & 1] for block in blocks]
    shapes = [jax.ShapeDtypeStruct(s, jnp.float32) for s in ((rows + 8, units), (rows + 8, experts), (rows, 1))]
    sums = half_front(here, (0, 2), [], shapes, *common)
    shapes = [jax.ShapeDtypeStruct((rows, units // 2), jnp.bfloat16)]
    return half_front(there, (1, 3), [flags[k] for k in order] + list(sums), shapes, *common)[0]


def store_blocks(total, groups, outs):
    rows = total.shape[0] // sum(len(group) for group in groups)
    for group, out in zip(groups, outs):
        blocks = [total[k * rows : (k + 1) * rows] for k in group]
        out[...] = jnp.concatenate(blocks, axis=0).astype(out.dtype)


def shapes_of(rows, cols, groups, types):
    slots = rows // sum(len(group) for group in groups)
    return [jax.ShapeDtypeStruct((slots * len(group), cols), t) for group, t in zip(groups, types)]


def down_kernel(flip, n_adds, groups, hidden_ref, down_ref, *refs):
    adds, outs = refs[:n_adds], refs[n_adds:]
    quarter = outs[0].shape[1]
    weights = down_ref[:, aligned(lax.axis_index("et") ^ flip, quarter)]
    total = jnp.dot(hidden_ref[...], weights, preferred_element_type=jnp.float32)
    for ref in adds:
        total += ref[...].astype(jnp.float32)
    store_blocks(total, groups, outs)


def down(hidden, w_down, flip, adds=(), groups=((0,),), types=(jnp.bfloat16,)):
    units, width = w_down.shape
    rows, quarter = hidden.shape[0], width // 4
    return pl.pallas_call(
        functools.partial(down_kernel, flip, len(adds), groups),
        in_specs=[VMEM] * (2 + len(adds)),
        out_shape=shapes_of(rows, quarter, groups, types),
        compiler_params=params(),
        cost_estimate=pl.CostEstimate(
            flops=2 * rows * units * quarter, bytes_accessed=2 * units * quarter, transcendentals=0
        ),
        name="down",
    )(hidden, w_down, *adds)


def add_kernel(groups, keep_ref, came_ref, *outs):
    store_blocks(keep_ref[...] + came_ref[...].astype(jnp.float32), groups, outs)


def add(keep, came, groups):
    return pl.pallas_call(
        functools.partial(add_kernel, groups),
        out_shape=shapes_of(*keep.shape, groups, [jnp.bfloat16] * len(groups)),
        compiler_params=params(),
        name="add",
    )(keep, came)


def diagonal(x, k, flip):
    n_ep, n_et = lax.axis_size("ep"), lax.axis_size("et")
    pairs = [(e * n_et + t, (e ^ k) * n_et + (t ^ flip)) for e in range(n_ep) for t in range(n_et)]
    return lax.ppermute(x, ("ep", "et"), pairs)


def move_kernel(order, last, own_ref, back_ref, pick_ref, extra_ref, *refs):
    came, outs = refs[: len(order)], refs[len(order) :]
    rows = [came[order.index(k)][...].astype(jnp.float32) for k in range(len(order))]
    rows[DIRECT] += extra_ref[...].astype(jnp.float32)
    velocity = product(back_ref[...], jnp.concatenate(rows, axis=0))
    moved = narrow(own_ref[...].astype(jnp.float32) - 0.5 * velocity)
    outs[0][...] = moved
    if last:
        outs[1][...] = narrow(velocity)
    else:
        slots = came[0].shape[0]
        picked = product(pick_ref[...], moved)
        for k, out in enumerate(outs[1:]):
            out[...] = narrow(picked[k * slots : (k + 1) * slots])


def move(own, back, pick, extra, came, order, last):
    shapes = [own.shape] + ([own.shape] if last else [c.shape for c in came])
    return pl.pallas_call(
        functools.partial(move_kernel, order, last),
        out_shape=[jax.ShapeDtypeStruct(s, jnp.bfloat16) for s in shapes],
        compiler_params=params(),
        name="move",
    )(own, back, pick, extra, *[came[k] for k in order])


DIRECT = 3


def sum_back(hidden, w_down, own, back, pick, last):
    peers = lax.axis_size("ep")
    rest = tuple(k for k in range(peers) if k != DIRECT)
    groups = (rest, (DIRECT,))
    (far,), (near,) = down(hidden, w_down, 3), down(hidden, w_down, 1)
    far, near = swap(far, "et", 1), swap(near, "et", 1)
    (crossing,) = down(hidden, w_down, 2, types=[jnp.float32])
    crossing, beside = add(crossing, far, groups)
    crossed, extra = swap(crossing, "et", 2), diagonal(beside, DIRECT, 2)
    kept, straight = down(hidden, w_down, 0, (near,), groups, [jnp.float32, jnp.bfloat16])
    blocks = dict(zip(rest, add(kept, crossed, [(i,) for i in range(len(rest))])))
    blocks[DIRECT] = straight
    came = [swap(blocks[k], "ep", k) if k else blocks[k] for k in range(peers)]
    order = [*range(2, peers), 1, 0]
    return move(own, back, pick, extra, came, order, last)


def spread(block, quarter):
    side = swap(block, "et", 2)
    near, far = swap(block, "et", 1), swap(side, "et", 1)
    return [(block, quarter, 0), (side, quarter, 2), (near, quarter, 1), (far, quarter, 3)]


def dense_body(tokens, modulation, router, gate_weight, up_weight, down_weight, expert_ids):
    rows, width = tokens.shape
    half, quarter = width // 2, width // 4
    router = router.T
    experts = router.shape[0]
    peers = lax.axis_size("ep")
    slots = 3 * rows * expert_ids.shape[2] // (2 * experts)
    ids = expert_ids.transpose(0, 2, 1)

    *packed, own = pack(tokens, ids, experts, slots)
    pair, w_down, done = load(gate_weight, up_weight, down_weight)
    mine, flags, *choice = own_rows(tokens, ids, experts, slots, done)
    pick, back = choice[2], choice[1::2]
    order = [*range(2, len(packed) + 1), 1]
    came = {k: swap(packed[k - 1], "ep", k) for k in order}
    halves = {k: relay(came[k], half, flags) for k in order}
    others = {k: swap(halves[k], "et", 1) for k in order}
    flags = [flags] + [came[k] for k in sorted(order)]
    blocks = [[(mine, width, 0)]] + [[(halves[k], half, 0), (others[k], half, 1)] for k in sorted(order)]
    hidden = front(blocks, flags, order + [0], 0, modulation, router, pair)
    own, *sent = sum_back(hidden, w_down, own, back[0], pick, False)

    blocks = [spread(swap(b, "ep", k) if k else b, quarter) for k, b in enumerate(sent)]
    hidden = front(blocks, flags, [order[0], 1, *order[1:-1], 0], 1, modulation, router, pair)
    return tuple(sum_back(hidden, w_down, own, back[1], pick, True))


def solution(mesh):
    in_specs = (
        P(("grp", "ep"), None),
        P(),
        P(),
        P("ep", None, "et"),
        P("ep", None, "et"),
        P("ep", "et", None),
        P(None, ("grp", "ep"), None),
    )
    out_specs = (P(("grp", "ep"), "et"), P(("grp", "ep"), "et"))

    def body(*args):
        experts, picks = args[2].shape[1], args[6].shape[2]
        peers = lax.axis_size("ep")
        fits = lax.axis_size("et") == 4 and peers >= 4 and peers & (peers - 1) == 0
        chosen = dense_body if fits and experts <= 2 * picks else routed_body
        return chosen(*args)

    return jax.shard_map(body, mesh=mesh, in_specs=in_specs, out_specs=out_specs, check_vma=False)
```
